32 devices in a mesh: node: 8 (over y, x, core), chan: 4 (over z).
Axes of the slice: x: 2, y: 2, z: 4, core: 2. Of those that a mesh axis runs over, the one named last changes fastest.
Arguments:
- features: bfloat16 [14336, 1024], P('node', 'chan'), may hold values from -0.0625 to 0.0625
- weight: bfloat16 [1024, 1024], P('node', 'chan'), may hold values from -0.25 to 0.25
- pre_clean: bfloat16 [14336, 1024], P('node', 'chan'), may hold values from -6 to 6
- pre_corrupt: bfloat16 [14336, 1024], P('node', 'chan'), may hold values from -6 to 6
- grad_clean: bfloat16 [14336, 1024], P('node', 'chan'), may hold values from -6 to 6
- grad_corrupt: bfloat16 [14336, 1024], P('node', 'chan'), may hold values from -6 to 6
- slopes: float32 [1024], P('chan'), may hold values from 0.05 to 0.5
- adj_vals: bfloat16 [112, 5, 128, 128], P('node'), may hold values from 0 to 0.07861328
- adj_cols: int32 [112, 5], P('node'), may hold values from 0 to 111, as said below
- adj_count: int32 [112], P('node'), may hold values from 1 to 5, as said below
- shuffle_from: int32 [112], replicated, may hold values from 0 to 111, as said below
Outputs:
- grad_weight: float32 [1024, 1024], P('node', 'chan')
- grad_features: bfloat16 [14336, 1024], P('node', 'chan')
The draws below stay inside these ranges and needn't reach their ends.
Inputs may be any that keep to these rules, and one draw needn't show every extreme that they name: `adj_cols`: entry [b, k] is a block within 2 of b, and entry [b, 0] is b itself. Slots k < adj_count[b] of row block b hold edge tiles; the other slots are padding and are not read. `shuffle_from`: A permutation of the blocks. The 14 blocks of one index of node take their rows from exactly 7 distinct indices of node, 2 blocks from each; among these are the index just after it and the index 4 away, counted round.
All inputs are finite; a program needn't handle non-finite values.
Results may differ from the reference program's by a relative error of at most 0.023.
Values may be sent and summed in bfloat16 or wider, within the bound.
No kernel may reach another device: no remote copies, remote signals or barrier semaphores. Data moves between devices by JAX's collectives and lax.ppermute only.
A program may use at most 128 MiB of HBM per device.

```python
import math
import jax
import jax.numpy as jnp
from jax import lax

F = 1024
TB = 128
BAND = 2
KMAX = 5
BLK_DEV = 14
CAP = 2
NBLK = 112
NODES = 14336
N_CHAN = 4


def draw_adj_cols(key, part):
    scores = jax.random.randint(key, (NBLK, 2 * BAND), 0, 1 << 20) * (2 * BAND) + jnp.arange(2 * BAND)[None, :]
    shuffled = jnp.argsort(scores, axis=1)
    nonzero = jnp.concatenate([jnp.arange(-BAND, 0), jnp.arange(1, BAND + 1)])
    offsets = jnp.concatenate([jnp.zeros((NBLK, 1), jnp.int32), nonzero[shuffled].astype(jnp.int32)], axis=1)
    columns = jnp.arange(NBLK)[:, None] + offsets
    columns = jnp.where(columns < 0, -columns, columns)
    columns = jnp.where(columns > NBLK - 1, 2 * (NBLK - 1) - columns, columns)
    return columns.astype(jnp.int32)


def draw_adj_count(key, part):
    dev_count = NBLK // BLK_DEV
    key_one, key_two, key_three = jax.random.split(key, 3)
    largest = jax.random.randint(key_one, (dev_count,), 1, KMAX + 1)
    largest_rows = jnp.repeat(largest, BLK_DEV)
    picked = jax.random.randint(key_two, (NBLK,), 0, 1 << 20)
    counts = 1 + picked % largest_rows
    full_row = jax.random.randint(key_three, (), 0, NBLK)
    counts = jnp.where(jnp.arange(NBLK) == full_row, KMAX, counts)
    return counts.astype(jnp.int32)


def draw_shuffle_from(key, part):
    key = jax.random.fold_in(key, 7)
    dev_count = NBLK // BLK_DEV
    groups = BLK_DEV // CAP
    key_one, key_two, key_three = jax.random.split(key, 3)
    values = jnp.arange(dev_count - 2)
    rest = jnp.where(values == 0, 0, values + 1)
    rest = jnp.where((values > 0) & (rest >= dev_count // 2), rest + 1, rest)
    rest = rest[jax.random.permutation(key_one, dev_count - 2)]
    shifts = jnp.concatenate([jnp.array([1, dev_count // 2], jnp.int32), rest.astype(jnp.int32)])[:groups]
    base = jax.random.permutation(key_two, BLK_DEV)
    scores = jax.random.randint(key_three, (dev_count, BLK_DEV), 0, 1 << 20) * BLK_DEV + jnp.arange(BLK_DEV)[None, :]
    order = jnp.argsort(scores, axis=1)
    device_of = jnp.arange(NBLK) // BLK_DEV
    position = jnp.arange(NBLK) % BLK_DEV
    slot = order[device_of, position]
    source_dev = (device_of + shifts[slot // CAP]) % dev_count
    return (source_dev * BLK_DEV + base[slot]).astype(jnp.int32)


def raised(result, key, source, target, shards_of, factor):
    def block_of(dim):
        return (jnp.arange(result.shape[dim]) // (result.shape[dim] // shards_of)).reshape((-1,) + (1,) * (result.ndim - 1 - dim))

    near = jax.random.permutation(key, shards_of)[block_of(target)]
    other_side = (block_of(target) + shards_of // 2) % shards_of
    return jnp.where((block_of(source) == near) | (block_of(source) == other_side), factor * result, result)


def level_of(own_key, extent, cuts, smallest, high):
    gain = 1.0
    for axis_at, shards_of in cuts:
        heights = jax.random.uniform(jax.random.fold_in(jax.random.fold_in(own_key, 6), axis_at), (shards_of,), jnp.float32, smallest / len(cuts), high / len(cuts))
        gain = gain * jnp.repeat(jnp.exp(heights), extent[axis_at] // shards_of).reshape((-1,) + (1,) * (len(extent) - 1 - axis_at))
    return gain


def normal_values(stream_key, shape, scale, reach, shards=(), held_as=jnp.bfloat16):
    level = level_of(stream_key, shape, shards, -0.22, 0.18) if shards else 1.0
    entries = jax.random.normal(stream_key, shape, jnp.float32) * scale * level
    return jnp.minimum(jnp.maximum(entries, -reach), reach).astype(held_as)


def bell_draw_with(rng, dims, deviation, limit, cuts, heavy, kind=jnp.bfloat16):
    drawn = deviation * jax.random.normal(rng, dims, jnp.float32)
    if cuts:
        drawn = drawn * level_of(rng, dims, cuts, -0.22, 0.18)
    return jnp.clip(raised(drawn, jax.random.fold_in(rng, 3), *heavy), -limit, limit).astype(kind)


def setup_inputs(seed: int = 0) -> dict:
    arg_keys = jax.random.split(jax.random.key(seed), 12)
    features = bell_draw_with(arg_keys[0], (NODES, F), (NODES ** -0.5), 0.0625, ((0, 8), (1, 4)), (0, 1, 8, 2.0))
    weight = bell_draw_with(arg_keys[1], (F, F), F ** -0.5, 0.25, ((0, 8), (1, 4)), (1, 0, 8, 2.0))
    pre_clean = normal_values(arg_keys[2], (NODES, F), 1.0, 6.0, ((0, 8), (1, 4)))
    pre_corrupt = normal_values(arg_keys[3], (NODES, F), 1.0, 6.0, ((0, 8), (1, 4)))
    grad_clean = normal_values(arg_keys[4], (NODES, F), 1.0, 6.0, ((0, 8), (1, 4)))
    grad_corrupt = normal_values(arg_keys[5], (NODES, F), 1.0, 6.0, ((0, 8), (1, 4)))
    slopes = jnp.clip(jnp.exp(math.log(0.5) - 2.3025851 * jax.random.uniform(arg_keys[6], (F,), jnp.float32) ** level_of(arg_keys[6], (F,), ((0, 4),), -0.2, 0.2)), 0.05, 0.5)
    adj_vals = jnp.clip(0.07861328 * jax.random.uniform(arg_keys[7], (NBLK, KMAX, TB, TB), jnp.float32) ** level_of(arg_keys[7], (NBLK, KMAX, TB, TB), ((0, 8),), -0.2, 0.2), 0.0, 0.07861328).astype(jnp.bfloat16)
    adj_cols = draw_adj_cols(jax.random.fold_in(arg_keys[11], 71), 0)
    adj_count = draw_adj_count(jax.random.fold_in(arg_keys[11], 71), 0)
    shuffle_from = draw_shuffle_from(jax.random.fold_in(arg_keys[11], 71), 0)
    return dict(features=features, weight=weight, pre_clean=pre_clean, pre_corrupt=pre_corrupt, grad_clean=grad_clean, grad_corrupt=grad_corrupt, slopes=slopes, adj_vals=adj_vals, adj_cols=adj_cols, adj_count=adj_count, shuffle_from=shuffle_from)


def local_grad(grad_part, pre_part, slopes):
    factor = jnp.where(pre_part > 0, 1.0, slopes[None, :])
    return (grad_part.astype(jnp.float32) * factor).astype(jnp.bfloat16)

def reference(features, weight, pre_clean, pre_corrupt, grad_clean, grad_corrupt, slopes, adj_vals, adj_cols, adj_count, shuffle_from):
    d_clean = local_grad(grad_clean, pre_clean, slopes)
    d_corrupt = local_grad(grad_corrupt, pre_corrupt, slopes)
    block_count = adj_cols.shape[0]
    tile_rows = adj_vals.shape[2]
    stacked = jnp.concatenate([d_clean, d_corrupt], axis=1).reshape(block_count, tile_rows, 2 * F)

    def one_block(summed, inputs):
        tile_vals, columns, tile_count, rhs_block = inputs
        contrib = jnp.einsum('kpq,pc->kqc', tile_vals.astype(jnp.float32), rhs_block.astype(jnp.float32))
        live_mask = (jnp.arange(tile_vals.shape[0], dtype=jnp.int32) < tile_count).astype(jnp.float32)
        return (summed.at[columns].add(contrib * live_mask[:, None, None]), None)
    start_sum = jnp.zeros((block_count, tile_rows, 2 * F), jnp.float32)
    summed, _ = lax.scan(one_block, start_sum, (adj_vals, adj_cols, adj_count, stacked))
    backprop = summed.astype(jnp.bfloat16)
    back_clean = backprop[:, :, :F].reshape(block_count * tile_rows, F)
    back_corrupt = backprop[:, :, F:]
    unshuffled = jnp.zeros_like(back_corrupt).at[shuffle_from].set(back_corrupt).reshape(block_count * tile_rows, F)
    grad_weight = jnp.dot(features.T, back_clean, preferred_element_type=jnp.float32) + jnp.dot(features.T, unshuffled, preferred_element_type=jnp.float32)
    chan_width = F // N_CHAN

    def add_partial(block_index, running):
        start_col = (block_index * chan_width).astype(jnp.int32)
        first_part = lax.dynamic_slice_in_dim(back_clean, start_col, chan_width, 1)
        second_part = lax.dynamic_slice_in_dim(unshuffled, start_col, chan_width, 1)
        weight_part = lax.dynamic_slice_in_dim(weight, start_col, chan_width, 1)
        partial_value = jnp.dot(first_part, weight_part.T, preferred_element_type=jnp.float32) + jnp.dot(second_part, weight_part.T, preferred_element_type=jnp.float32)
        rounded = lax.optimization_barrier(partial_value.astype(jnp.bfloat16))
        return running + rounded.astype(jnp.float32)
    running = lax.fori_loop(0, N_CHAN, add_partial, jnp.zeros((block_count * tile_rows, F), jnp.float32))
    return (grad_weight, running.astype(jnp.bfloat16))
```

```python
import functools

import jax
import jax.numpy as jnp
from jax import lax
from jax.experimental import pallas as pl
from jax.experimental.pallas import tpu as pltpu
from jax.sharding import PartitionSpec as P

VMEM_LIMIT = 48 * 1024 * 1024


def params():
    return pltpu.CompilerParams(vmem_limit_bytes=VMEM_LIMIT)


def shifted(value, axis, by):
    size = lax.axis_size(axis)
    pairs = [(i, i + by) for i in range(size) if 0 <= i + by < size]
    return lax.ppermute(value, axis, pairs)


def swapped(value, axis, bit):
    size = lax.axis_size(axis)
    return lax.ppermute(value, axis, [(i, i ^ bit) for i in range(size)])


def exchanged(value, axis):
    return lax.all_to_all(value, axis, split_axis=0, concat_axis=0, tiled=True)


def masked_grad(grad_ref, pre_ref, slope):
    factor = jnp.where(pre_ref[...].astype(jnp.float32) > 0, 1.0, slope)
    return (grad_ref[...].astype(jnp.float32) * factor).astype(jnp.bfloat16)


def both_grads(gc, pc, gx, px, slopes):
    slope = slopes[...]
    return jnp.concatenate([masked_grad(gc, pc, slope), masked_grad(gx, px, slope)], axis=1)


def tile_product(tile, rhs):
    return lax.dot_general(
        tile, rhs, (((0,), (0,)), ((), ())), preferred_element_type=jnp.float32
    )


def border_kernel(reach, blocks, slots, width, targets, gc, pc, gx, px, slopes, adj, down, up, acc):
    step = pl.program_id(0)
    row = jnp.where(step < reach, step, step + blocks - 2 * reach)

    @pl.when(step == 0)
    def _():
        acc[...] = jnp.zeros_like(acc)

    rhs = both_grads(gc, pc, gx, px, slopes)
    for k in range(slots):
        target = targets[row, k]

        @pl.when((target >= 0) & ((target < reach) | (target >= reach + blocks)))
        def _():
            place = jnp.where(target < reach, target, target - blocks)
            acc[place] += tile_product(adj[0, k], rhs)

    @pl.when(step == 2 * reach - 1)
    def _():
        for which in range(2):
            part = acc[:, :, which * width : (which + 1) * width].astype(jnp.bfloat16)
            down[which] = part[:reach]
            up[which] = part[reach:]


def border(targets, gc, pc, gx, px, slopes, adj, reach):
    blocks, slots, rows, _ = adj.shape
    width = gc.shape[1]

    def row_of(i):
        return jnp.where(i < reach, i, i + blocks - 2 * reach)

    data = pl.BlockSpec((rows, width), lambda i, *_: (row_of(i), 0))
    halo = pl.BlockSpec((2, reach, rows, width), lambda i, *_: (0, 0, 0, 0))
    halo_shape = jax.ShapeDtypeStruct((2, reach, rows, width), jnp.bfloat16)
    return pl.pallas_call(
        functools.partial(border_kernel, reach, blocks, slots, width),
        grid_spec=pltpu.PrefetchScalarGridSpec(
            num_scalar_prefetch=1,
            grid=(2 * reach,),
            in_specs=[
                data,
                data,
                data,
                data,
                pl.BlockSpec((1, width), lambda i, *_: (0, 0)),
                pl.BlockSpec((1, slots, rows, rows), lambda i, *_: (row_of(i), 0, 0, 0)),
            ],
            out_specs=[halo, halo],
            scratch_shapes=[pltpu.VMEM((2 * reach, rows, 2 * width), jnp.float32)],
        ),
        out_shape=[halo_shape, halo_shape],
        compiler_params=params(),
        name="border",
    )(targets, gc, pc, gx, px, slopes, adj)


def inner_kernel(
    reach, blocks, slots, width, targets, places, gc, pc, gx, px, slopes, adj, clean, outgoing, acc
):
    step = pl.program_id(0)

    @pl.when(step == 0)
    def _():
        acc[...] = jnp.zeros_like(acc)

    rhs = both_grads(gc, pc, gx, px, slopes)
    for k in range(slots):
        target = targets[step, k] - reach

        @pl.when((target >= 0) & (target < blocks))
        def _():
            acc[target] += tile_product(adj[0, k], rhs)

    def finish(block):
        clean[block] = acc[block, :, :width].astype(jnp.bfloat16)
        outgoing[places[block]] = acc[block, :, width:].astype(jnp.bfloat16)

    @pl.when(step >= reach)
    def _():
        finish(step - reach)

    @pl.when(step == blocks - 1)
    def _():
        for j in range(reach):
            finish(blocks - reach + j)


def inner(targets, places, gc, pc, gx, px, slopes, adj, reach, sent):
    blocks, slots, rows, _ = adj.shape
    width = gc.shape[1]
    data = pl.BlockSpec((rows, width), lambda i, *_: (i, 0))
    return pl.pallas_call(
        functools.partial(inner_kernel, reach, blocks, slots, width),
        grid_spec=pltpu.PrefetchScalarGridSpec(
            num_scalar_prefetch=2,
            grid=(blocks,),
            in_specs=[
                data,
                data,
                data,
                data,
                pl.BlockSpec((1, width), lambda i, *_: (0, 0)),
                pl.BlockSpec((1, slots, rows, rows), lambda i, *_: (i, 0, 0, 0)),
            ],
            out_specs=[
                pl.BlockSpec((blocks, rows, width), lambda i, *_: (0, 0, 0)),
                pl.BlockSpec((sent, rows, width), lambda i, *_: (0, 0, 0)),
            ],
            scratch_shapes=[pltpu.VMEM((blocks, rows, 2 * width), jnp.float32)],
        ),
        out_shape=[
            jax.ShapeDtypeStruct((blocks, rows, width), jnp.bfloat16),
            jax.ShapeDtypeStruct((sent, rows, width), jnp.bfloat16),
        ],
        compiler_params=params(),
        cost_estimate=pl.CostEstimate(
            flops=4 * blocks * slots * rows * rows * width,
            bytes_accessed=12 * blocks * rows * width + 2 * blocks * slots * rows * rows,
            transcendentals=0,
        ),
        name="inner",
    )(targets, places, gc, pc, gx, px, slopes, adj)


def patch_kernel(reach, places, block, low, high, out):
    step = pl.program_id(0)

    @pl.when(step < reach)
    def _():
        out[...] = (block[...].astype(jnp.float32) + low[0].astype(jnp.float32)).astype(jnp.bfloat16)

    @pl.when(step >= reach)
    def _():
        out[...] = (block[...].astype(jnp.float32) + high[0].astype(jnp.float32)).astype(jnp.bfloat16)


def patch(places, outgoing, low, high, blocks):
    sent, rows, width = outgoing.shape
    reach = low.shape[1]

    def place_of(i, places):
        return places[jnp.where(i < reach, i, i + blocks - 2 * reach)]

    spot = pl.BlockSpec((1, rows, width), lambda i, places: (place_of(i, places), 0, 0))
    return pl.pallas_call(
        functools.partial(patch_kernel, reach),
        grid_spec=pltpu.PrefetchScalarGridSpec(
            num_scalar_prefetch=1,
            grid=(2 * reach,),
            in_specs=[
                spot,
                pl.BlockSpec(
                    (1, 1, rows, width), lambda i, _: (1, jnp.minimum(i, reach - 1), 0, 0)
                ),
                pl.BlockSpec(
                    (1, 1, rows, width), lambda i, _: (1, jnp.maximum(i - reach, 0), 0, 0)
                ),
            ],
            out_specs=spot,
        ),
        out_shape=jax.ShapeDtypeStruct(outgoing.shape, jnp.bfloat16),
        input_output_aliases={1: 0},
        compiler_params=params(),
        name="patch",
    )(places, outgoing, low, high)


def merge_kernel(reach, blocks, sources, clean, low, high, incoming, out):
    step = pl.program_id(0)
    total = clean[0].astype(jnp.float32) + incoming[0].astype(jnp.float32)
    out[...] = total.astype(jnp.bfloat16)

    @pl.when(step < reach)
    def _():
        out[...] = (total + low[0, 0].astype(jnp.float32)).astype(jnp.bfloat16)

    @pl.when(step >= blocks - reach)
    def _():
        out[...] = (total + high[0, 0].astype(jnp.float32)).astype(jnp.bfloat16)


def merge(sources, clean, low, high, incoming):
    blocks, rows, width = clean.shape
    reach = low.shape[1]
    return pl.pallas_call(
        functools.partial(merge_kernel, reach, blocks),
        grid_spec=pltpu.PrefetchScalarGridSpec(
            num_scalar_prefetch=1,
            grid=(blocks,),
            in_specs=[
                pl.BlockSpec((1, rows, width), lambda i, _: (i, 0, 0)),
                pl.BlockSpec(
                    (1, 1, rows, width), lambda i, _: (0, jnp.minimum(i, reach - 1), 0, 0)
                ),
                pl.BlockSpec(
                    (1, 1, rows, width),
                    lambda i, _: (0, jnp.maximum(i - (blocks - reach), 0), 0, 0),
                ),
                pl.BlockSpec((1, rows, width), lambda i, sources: (sources[i], 0, 0)),
            ],
            out_specs=pl.BlockSpec((rows, width), lambda i, _: (i, 0)),
        ),
        out_shape=jax.ShapeDtypeStruct((blocks * rows, width), jnp.bfloat16),
        compiler_params=params(),
        name="merge",
    )(sources, clean, low, high, incoming)


def weight_kernel(groups, shares, bits, me, feats, summed, keep, send):
    step = pl.program_id(0)
    height = keep.shape[2]
    for group in range(groups):
        product = lax.dot_general(
            feats[0], summed[group], (((0,), (0,)), ((), ())), preferred_element_type=jnp.float32
        ).astype(jnp.bfloat16)
        for share in range(shares):
            relative = (step * shares + share) ^ me[0]
            place = jnp.int32(0)
            for j in range(1, bits):
                place += ((relative >> j) & 1) << (bits - 1 - j)
            part = product[share * height : (share + 1) * height]

            @pl.when((relative & 1) == 0)
            def _():
                keep[place, group] = part

            @pl.when((relative & 1) == 1)
            def _():
                send[place, group] = part


def weight_partial(me, feats, summed, devs):
    groups, rows, width = feats.shape
    shares = devs // groups
    height = groups * width // devs
    bits = devs.bit_length() - 1
    half = (devs // 2, groups, height, width)
    out = pl.BlockSpec(half, lambda i, _: (0, 0, 0, 0))
    return pl.pallas_call(
        functools.partial(weight_kernel, groups, shares, bits),
        grid_spec=pltpu.PrefetchScalarGridSpec(
            num_scalar_prefetch=1,
            grid=(groups,),
            in_specs=[
                pl.BlockSpec((1, rows, width), lambda i, _: (i, 0, 0)),
                pl.BlockSpec((groups, rows, width), lambda i, _: (0, 0, 0)),
            ],
            out_specs=[out, out],
        ),
        out_shape=[jax.ShapeDtypeStruct(half, jnp.bfloat16)] * 2,
        compiler_params=params(),
        cost_estimate=pl.CostEstimate(
            flops=2 * rows * (groups * width) ** 2,
            bytes_accessed=2 * (groups * width) ** 2 + 4 * groups * rows * width,
            transcendentals=0,
        ),
        name="weight_partial",
    )(me, feats, summed)


def feature_kernel(groups, shares, summed, weight, out):
    total = None
    for group in range(groups):
        tile = jnp.concatenate([weight[share, group] for share in range(shares)], axis=0)
        product = lax.dot_general(
            summed[group], tile, (((1,), (1,)), ((), ())), preferred_element_type=jnp.float32
        )
        total = product if total is None else total + product
    out[0] = total.astype(jnp.bfloat16)


def feature_rows(summed, weight):
    groups, rows, width = summed.shape
    devs, _, height, _ = weight.shape
    shares = devs // groups
    return pl.pallas_call(
        functools.partial(feature_kernel, groups, shares),
        grid=(groups,),
        in_specs=[
            pl.BlockSpec((groups, rows, width), lambda i: (0, 0, 0)),
            pl.BlockSpec((shares, groups, height, width), lambda i: (i, 0, 0, 0)),
        ],
        out_specs=pl.BlockSpec((1, rows, width), lambda i: (i, 0, 0)),
        out_shape=jax.ShapeDtypeStruct((groups, rows, width), jnp.bfloat16),
        compiler_params=params(),
        cost_estimate=pl.CostEstimate(
            flops=2 * rows * (groups * width) ** 2,
            bytes_accessed=2 * (groups * width) ** 2 + 4 * groups * rows * width,
            transcendentals=0,
        ),
        name="feature_rows",
    )(summed, weight)


def routes(shuffle_from, my_index, blocks, devs, slots):
    owner = (shuffle_from // blocks).reshape(devs, blocks)
    earlier = jnp.arange(blocks)[None, :] < jnp.arange(blocks)[:, None]
    slot = jnp.sum(((owner[:, None, :] == owner[:, :, None]) & earlier[None]).astype(jnp.int32), axis=2)
    sender = jnp.arange(devs, dtype=jnp.int32)[:, None]
    places = lax.dynamic_slice_in_dim(owner * slots + slot, my_index, 1, 0)[0]
    landing = (sender * slots + slot).reshape(-1)
    mine = my_index * blocks + jnp.arange(blocks, dtype=jnp.int32)
    found = shuffle_from[None, :] == mine[:, None]
    sources = jnp.sum(jnp.where(found, landing[None, :], 0), axis=1)
    return places, sources


def local(
    features,
    weight,
    pre_clean,
    pre_corrupt,
    grad_clean,
    grad_corrupt,
    slopes,
    adj_vals,
    adj_cols,
    adj_count,
    shuffle_from,
):
    row_count, width = features.shape
    blocks, tile_slots, tile_rows, _ = adj_vals.shape
    reach = (tile_slots - 1) // 2
    my_index = lax.axis_index("node")
    devs = lax.axis_size("node")
    groups = lax.axis_size("chan")
    slots = -(-blocks // devs)

    live = jnp.arange(tile_slots)[None, :] < adj_count[:, None]
    targets = jnp.where(live, adj_cols - (my_index * blocks - reach), -1)
    slopes = slopes[None, :]
    down, up = border(
        targets, grad_clean, pre_clean, grad_corrupt, pre_corrupt, slopes, adj_vals, reach
    )
    from_prev = shifted(up, "node", 1)
    from_next = shifted(down, "node", -1)
    feature_cols = exchanged(features.reshape(groups, -1, width), "chan")
    whole_weight = lax.all_gather(weight, ("node", "chan"), axis=0)
    whole_weight = whole_weight.reshape(devs, groups, *weight.shape)

    places, sources = routes(shuffle_from, my_index, blocks, devs, slots)
    clean, outgoing = inner(
        targets,
        places,
        grad_clean,
        pre_clean,
        grad_corrupt,
        pre_corrupt,
        slopes,
        adj_vals,
        reach,
        devs * slots,
    )
    outgoing = patch(places, outgoing, from_prev, from_next, blocks)
    incoming = exchanged(outgoing, "node")
    summed = merge(sources, clean, from_prev, from_next, incoming)
    summed = exchanged(summed.reshape(groups, -1, width), "chan")

    keep, send = weight_partial(my_index[None], feature_cols, summed, devs)
    rows_out = feature_rows(summed, whole_weight)
    grad_features = exchanged(rows_out, "chan").reshape(row_count, width)

    bit = 1
    while True:
        total = keep.astype(jnp.float32) + swapped(send, "node", bit).astype(jnp.float32)
        bit *= 2
        if bit == devs:
            break
        half = total.shape[0] // 2
        keep, send = total[:half], total[half:].astype(jnp.bfloat16)
    parts = exchanged(total[0].astype(jnp.bfloat16), "chan")
    grad_weight = jnp.sum(parts.astype(jnp.float32), axis=0)
    return (grad_weight, grad_features)


def solution(mesh):
    placed = (
        P("node", "chan"),
        P("node", "chan"),
        P("node", "chan"),
        P("node", "chan"),
        P("node", "chan"),
        P("node", "chan"),
        P("chan"),
        P("node", None, None, None),
        P("node", None),
        P("node"),
        P(),
    )
    return jax.shard_map(
        local,
        mesh=mesh,
        in_specs=placed,
        out_specs=(P("node", "chan"), P("node", "chan")),
        check_vma=False,
    )
```

```python
import functools
import math

import jax
import jax.numpy as jnp
from jax import lax
from jax.experimental import pallas as pl
from jax.experimental.pallas import tpu as pltpu
from jax.sharding import PartitionSpec as P

VMEM_LIMIT = 32 * 1024 * 1024
VMEM_ALL = 61 * 1024 * 1024
IN_VMEM = pl.BlockSpec(memory_space=pltpu.VMEM)
IN_SMEM = pl.BlockSpec(memory_space=pltpu.SMEM)
IN_HBM = pl.BlockSpec(memory_space=pltpu.HBM)


def params(limit=VMEM_LIMIT):
    return pltpu.CompilerParams(vmem_limit_bytes=limit)


def bf16(*shape):
    return jax.ShapeDtypeStruct(shape, jnp.bfloat16)


def wide(value):
    return value.astype(jnp.float32)


def shifted(value, axis, by):
    size = lax.axis_size(axis)
    pairs = [(i, i + by) for i in range(size) if 0 <= i + by < size]
    return lax.ppermute(value, axis, pairs)


def swapped(value, axis, by):
    size = lax.axis_size(axis)
    return lax.ppermute(value, axis, [(i, i ^ by) for i in range(size)])


def masked_grad(grad, pre, slope):
    return (wide(grad) * jnp.where(wide(pre) > 0, 1.0, slope)).astype(jnp.bfloat16)


def add_products(block, slot, slots, place, data, tiles, slopes, acc):
    gc, pc, gx, px = (data[i, slot] for i in range(4))
    slope = slopes[...]
    rhs = jnp.concatenate([masked_grad(gc, pc, slope), masked_grad(gx, px, slope)], axis=1)
    rows = tiles.shape[2]
    lhs = jnp.concatenate([tiles[slot, k].T for k in range(slots)], axis=0)
    product = jnp.dot(lhs, rhs, preferred_element_type=jnp.float32)
    for k in range(slots):
        acc[place(block, k)] += product[k * rows : (k + 1) * rows]


def block_copies(block, slot, rows, inputs, adj, data, tiles, sems):
    span = pl.ds(pl.multiple_of(block * rows, rows), rows)
    copies = [
        pltpu.make_async_copy(ref.at[span], data.at[i, slot], sems.at[i, slot])
        for i, ref in enumerate(inputs)
    ]
    return copies + [pltpu.make_async_copy(adj.at[block], tiles.at[slot], sems.at[4, slot])]


def border_kernel(
    reach, me, cols, count, gc, pc, gx, px, slopes, adj, down, up, data, tiles, acc, sems
):
    blocks, slots, rows, _ = adj.shape
    width = gc.shape[1]
    border = [*range(reach), *range(blocks - reach, blocks)]

    def copies(i):
        return block_copies(border[i], i, rows, (gc, pc, gx, px), adj, data, tiles, sems)

    for i in range(2 * reach):
        for copy in copies(i):
            copy.start()
    acc[...] = jnp.zeros_like(acc)

    def place(block, k):
        target = cols[k, block] - me[0] * blocks
        live = k < count[block]
        below = live & (target < 0)
        above = live & (target >= blocks)
        return jnp.where(below, target + reach, jnp.where(above, target - blocks + reach, 2 * reach))

    for i in range(2 * reach):
        for copy in copies(i):
            copy.wait()
        add_products(border[i], i, slots, place, data, tiles, slopes, acc)
    for which in range(2):
        part = acc[: 2 * reach, :, which * width : (which + 1) * width].astype(jnp.bfloat16)
        down[which] = part[:reach]
        up[which] = part[reach:]


def border(me, cols, count, gc, pc, gx, px, slopes, adj, reach):
    _, slots, rows, _ = adj.shape
    width = gc.shape[1]
    return pl.pallas_call(
        functools.partial(border_kernel, reach),
        in_specs=[IN_SMEM] * 3 + [IN_HBM] * 4 + [IN_VMEM, IN_HBM],
        out_specs=[IN_VMEM] * 2,
        out_shape=[bf16(2, reach, rows, width)] * 2,
        scratch_shapes=[
            pltpu.VMEM((4, 2 * reach, rows, width), jnp.bfloat16),
            pltpu.VMEM((2 * reach, slots, rows, rows), jnp.bfloat16),
            pltpu.VMEM((2 * reach + 1, rows, 2 * width), jnp.float32),
            pltpu.SemaphoreType.DMA((5, 2 * reach)),
        ],
        compiler_params=params(VMEM_ALL),
        cost_estimate=pl.CostEstimate(
            flops=8 * reach * slots * rows * rows * width,
            bytes_accessed=16 * reach * rows * width + 4 * reach * slots * rows * rows,
            transcendentals=0,
        ),
        name="border",
    )(me, cols, count, gc, pc, gx, px, slopes, adj)


def inner_kernel(me, cols, count, gc, pc, gx, px, slopes, adj, clean, corrupt, data, tiles, acc, sems):
    blocks, slots, rows, _ = adj.shape
    width = gc.shape[1]

    def copies(block):
        return block_copies(block, block, rows, (gc, pc, gx, px), adj, data, tiles, sems)

    for block in range(blocks):
        for copy in copies(block):
            copy.start()
    acc[...] = jnp.zeros_like(acc)

    def place(block, k):
        target = cols[k, block] - me[0] * blocks
        inside = (k < count[block]) & (target >= 0) & (target < blocks)
        return jnp.where(inside, target, blocks)

    per_step = 2 - blocks % 2

    @pl.loop(0, blocks // per_step)
    def _(step):
        for i in range(per_step):
            for copy in copies(step * per_step + i):
                copy.wait()
        for i in range(per_step):
            block = step * per_step + i
            add_products(block, block, slots, place, data, tiles, slopes, acc)

    @pl.loop(0, blocks)
    def _(block):
        clean[block] = acc[block, :, :width].astype(jnp.bfloat16)
        corrupt[block] = acc[block, :, width:].astype(jnp.bfloat16)


def inner(me, cols, count, gc, pc, gx, px, slopes, adj):
    blocks, slots, rows, _ = adj.shape
    width = gc.shape[1]
    return pl.pallas_call(
        inner_kernel,
        in_specs=[IN_SMEM] * 3 + [IN_HBM] * 4 + [IN_VMEM, IN_HBM],
        out_specs=[IN_VMEM] * 2,
        out_shape=[bf16(blocks, rows, width)] * 2,
        scratch_shapes=[
            pltpu.VMEM((4, blocks, rows, width), jnp.bfloat16),
            pltpu.VMEM((blocks, slots, rows, rows), jnp.bfloat16),
            pltpu.VMEM((blocks + 1, rows, 2 * width), jnp.float32),
            pltpu.SemaphoreType.DMA((5, blocks)),
        ],
        compiler_params=params(),
        cost_estimate=pl.CostEstimate(
            flops=4 * blocks * slots * rows * rows * width,
            bytes_accessed=12 * blocks * rows * width + 2 * blocks * slots * rows * rows,
            transcendentals=0,
        ),
        name="inner",
    )(me, cols, count, gc, pc, gx, px, slopes, adj)


def route_kernel(reach, slots, me, shuffle, clean, corrupt, low, high, whole, outgoing, used):
    blocks = clean.shape[0]
    for i in range(outgoing.shape[0] // slots):
        used[i] = 0
    for block in range(blocks):
        owner = shuffle[me[0] * blocks + block] // blocks
        slot = used[owner]
        used[owner] = slot + 1
        mine, theirs = clean[block], corrupt[block]
        if block < reach:
            mine = (wide(mine) + wide(low[0, block])).astype(jnp.bfloat16)
            theirs = (wide(theirs) + wide(low[1, block])).astype(jnp.bfloat16)
        elif block >= blocks - reach:
            at = block - (blocks - reach)
            mine = (wide(mine) + wide(high[0, at])).astype(jnp.bfloat16)
            theirs = (wide(theirs) + wide(high[1, at])).astype(jnp.bfloat16)
        whole[block] = mine
        outgoing[owner * slots + slot] = theirs


def route(me, shuffle, clean, corrupt, low, high, devs, slots):
    blocks, rows, width = clean.shape
    return pl.pallas_call(
        functools.partial(route_kernel, low.shape[1], slots),
        in_specs=[IN_SMEM] * 2 + [IN_VMEM] * 4,
        out_specs=[IN_VMEM] * 2,
        out_shape=[bf16(blocks, rows, width), bf16(devs * slots, rows, width)],
        scratch_shapes=[pltpu.SMEM((devs,), jnp.int32)],
        compiler_params=params(),
        name="route",
    )(me, shuffle, clean, corrupt, low, high)


def merge_kernel(quarter, index, landing, clean, incoming, out):
    _, rows, _ = clean.shape
    group = index[1]
    piece = math.gcd(rows, quarter)
    for place in range(incoming.shape[0]):
        block = landing[place]

        @pl.when(block >= 0)
        def _():
            total = (wide(clean[block]) + wide(incoming[place])).astype(jnp.bfloat16)
            for part in range(rows // piece):
                at = block * (rows // piece) + part
                owner = at // (quarter // piece)
                offset = (at - owner * (quarter // piece)) * piece
                out[owner ^ group, pl.ds(pl.multiple_of(offset, piece), piece)] = total[
                    part * piece : (part + 1) * piece
                ]


def merge(index, landing, clean, incoming, groups):
    blocks, rows, width = clean.shape
    quarter = blocks * rows // groups
    return pl.pallas_call(
        functools.partial(merge_kernel, quarter),
        in_specs=[IN_SMEM] * 2 + [IN_VMEM] * 2,
        out_specs=IN_VMEM,
        out_shape=bf16(groups, quarter, width),
        compiler_params=params(),
        name="merge",
    )(index, landing, clean, incoming)


def halving_orders(devs):
    bits = list(range(1, devs.bit_length() - 1))
    return bits, bits[::-1]


def weight_kernel(devs, index, *refs):
    groups = (len(refs) - 2) // 2
    feats, summed, (keep, send) = refs[:groups], refs[groups : 2 * groups], refs[2 * groups :]
    me, group = index[0], index[1]
    shares = devs // groups
    height, width = keep.shape[3:]
    rhs = jnp.concatenate([piece[...] for piece in summed], axis=1)
    for relative in range(groups):
        product = lax.dot_general(
            feats[relative][...],
            rhs,
            (((0,), (0,)), ((), ())),
            preferred_element_type=jnp.float32,
        ).astype(jnp.bfloat16)
        for share in range(shares):
            node = ((group ^ relative) * shares + share) ^ me
            for half, order in enumerate(halving_orders(devs)):
                place = jnp.int32(0)
                for bit in order:
                    place = place * 2 + ((node >> bit) & 1)
                for i in range(groups // 2):
                    column = (half * (groups // 2) + i) * width
                    part = product[share * height : (share + 1) * height, column : column + width]

                    @pl.when((node & 1) == 0)
                    def _():
                        keep[half, place, i] = part

                    @pl.when((node & 1) == 1)
                    def _():
                        send[half, place, i] = part


def weight_partial(index, feats, summed, devs):
    groups = len(feats)
    rows, width = feats[0].shape
    height = groups * width // devs
    return pl.pallas_call(
        functools.partial(weight_kernel, devs),
        in_specs=[IN_SMEM] + [IN_VMEM] * (2 * groups),
        out_specs=[IN_VMEM] * 2,
        out_shape=[bf16(2, devs // 2, groups // 2, height, width)] * 2,
        compiler_params=params(),
        cost_estimate=pl.CostEstimate(
            flops=2 * rows * (groups * width) ** 2,
            bytes_accessed=2 * (groups * width) ** 2 + 4 * groups * rows * width,
            transcendentals=0,
        ),
        name="weight_partial",
    )(index, *feats, *summed)


def feature_kernel(index, *refs):
    *summed, low, high, out = refs
    groups = len(summed)
    devs = low.shape[0]
    me, group = index[0], index[1]
    shares = devs // groups
    lhs = jnp.concatenate([piece[...] for piece in summed], axis=1)
    for relative in range(groups):
        rows = []
        for share in range(shares):
            node = ((group ^ relative) * shares + share) ^ me
            parts = []
            for half, order in zip((low, high), halving_orders(devs)):
                place = jnp.int32(0)
                for j, bit in enumerate([*order, 0]):
                    place += ((node >> bit) & 1) << j
                parts += [half[place, i] for i in range(groups // 2)]
            rows.append(jnp.concatenate(parts, axis=1))
        out[relative] = lax.dot_general(
            lhs,
            jnp.concatenate(rows, axis=0),
            (((1,), (1,)), ((), ())),
            preferred_element_type=jnp.float32,
        ).astype(jnp.bfloat16)


def feature_rows(index, summed, halves):
    groups = len(summed)
    rows, width = summed[0].shape
    return pl.pallas_call(
        feature_kernel,
        in_specs=[IN_SMEM] + [IN_VMEM] * (groups + 2),
        out_specs=IN_VMEM,
        out_shape=bf16(groups, rows, width),
        compiler_params=params(),
        cost_estimate=pl.CostEstimate(
            flops=2 * rows * (groups * width) ** 2,
            bytes_accessed=2 * (groups * width) ** 2 + 4 * groups * rows * width,
            transcendentals=0,
        ),
        name="feature_rows",
    )(index, *summed, *halves)


def gather_kernel(index, *refs):
    *pieces, out, sems = refs
    rows = pieces[0].shape[0]
    copies = [
        pltpu.make_async_copy(
            piece, out.at[pl.ds(pl.multiple_of((index[1] ^ i) * rows, rows), rows)], sems.at[i]
        )
        for i, piece in enumerate(pieces)
    ]
    for copy in copies:
        copy.start()
    for copy in copies:
        copy.wait()


def laid_out(index, pieces):
    rows, width = pieces[0].shape
    return pl.pallas_call(
        gather_kernel,
        in_specs=[IN_SMEM] + [IN_VMEM] * len(pieces),
        out_specs=IN_HBM,
        out_shape=bf16(len(pieces) * rows, width),
        scratch_shapes=[pltpu.SemaphoreType.DMA((len(pieces),))],
        compiler_params=params(),
        name="laid_out",
    )(index, *pieces)


def landing_blocks(shuffle_from, me, blocks, devs, slots):
    owner = (shuffle_from // blocks).reshape(devs, blocks)
    within = (shuffle_from % blocks).reshape(devs, blocks)
    for_me = owner == me
    earlier = jnp.arange(blocks)[None, :] < jnp.arange(blocks)[:, None]
    rank = jnp.sum((for_me[:, None, :] & earlier[None]).astype(jnp.int32), axis=2)
    picked = for_me[:, None, :] & (rank[:, None, :] == jnp.arange(slots)[None, :, None])
    return (jnp.sum(jnp.where(picked, within[:, None, :] + 1, 0), axis=2) - 1).reshape(-1)


def exchange_order(groups):
    return sorted(range(1, groups), reverse=True)


def local(
    features,
    weight,
    pre_clean,
    pre_corrupt,
    grad_clean,
    grad_corrupt,
    slopes,
    adj_vals,
    adj_cols,
    adj_count,
    shuffle_from,
):
    row_count, width = features.shape
    blocks, tile_slots, tile_rows, _ = adj_vals.shape
    reach = (tile_slots - 1) // 2
    me = lax.axis_index("node")
    group = lax.axis_index("chan")
    devs = lax.axis_size("node")
    groups = lax.axis_size("chan")
    slots = -(-blocks // devs)
    quarter = row_count // groups
    index = jnp.stack([me, group])

    args = (index, adj_cols.T, adj_count, grad_clean, pre_clean, grad_corrupt, pre_corrupt)
    args += (slopes[None, :], adj_vals)
    down, up = border(*args, reach)
    from_prev = shifted(up, "node", 1)
    from_next = shifted(down, "node", -1)

    tiles = [weight] + [swapped(weight, "chan", i) for i in range(1, groups)]
    clean, corrupt = inner(*args)
    clean, corrupt, tiles = lax.optimization_barrier((clean, corrupt, tiles))
    clean, outgoing = route(
        index, shuffle_from, clean, corrupt, from_prev, from_next, devs, slots
    )

    feats = [None] * groups
    by_quarter = features.reshape(groups, quarter, width)
    for i in [0, *exchange_order(groups)]:
        piece = lax.dynamic_index_in_dim(by_quarter, group ^ i, 0, keepdims=False)
        feats[i] = swapped(piece, "chan", i) if i else piece
    shuffle_from, outgoing = lax.optimization_barrier((shuffle_from, outgoing))
    landing = landing_blocks(shuffle_from, me, blocks, devs, slots)
    incoming = lax.all_to_all(outgoing, "node", split_axis=0, concat_axis=0, tiled=True)
    orders = halving_orders(devs)
    halves = [jnp.stack(part)[None] for part in (tiles[: groups // 2], tiles[groups // 2 :])]

    def gather_hop(halves, hop):
        return [
            jnp.concatenate([part, swapped(part, "node", 1 << order[hop])], axis=0)
            for part, order in zip(halves, orders)
        ]

    halves = gather_hop(halves, 0)
    incoming, feats, halves = lax.optimization_barrier((incoming, feats, halves))
    merged = merge(index, landing, clean, incoming, groups)
    summed = [merged[0]] + [None] * (groups - 1)
    for i in exchange_order(groups):
        summed[i] = swapped(merged[i], "chan", i)
    for hop in range(1, len(orders[0])):
        halves = gather_hop(halves, hop)
    summed, halves = lax.optimization_barrier((summed, halves))
    halves = [jnp.concatenate([part, swapped(part, "node", 1)], axis=0) for part in halves]

    rows_out = feature_rows(index, summed, halves)
    pieces = [rows_out[0]] + [None] * (groups - 1)
    for i in exchange_order(groups):
        pieces[i] = swapped(rows_out[i], "chan", i)

    keep, send = weight_partial(index, feats, summed, devs)
    total = wide(keep) + wide(swapped(send, "node", 1))
    shares = []
    for part, order in zip((total[0], total[1]), halving_orders(devs)):
        for bit in order:
            size = part.shape[0] // 2
            arrived = swapped(part[size:].astype(jnp.bfloat16), "node", 1 << bit)
            part = part[:size] + wide(arrived)
        shares.append(part[0])
    shares = jnp.concatenate(shares, axis=0)
    grad_weight = shares[0]
    for i in range(1, groups):
        grad_weight = grad_weight + wide(swapped(shares[i].astype(jnp.bfloat16), "chan", i))

    grad_features = laid_out(index, pieces)
    return (grad_weight, grad_features)


def solution(mesh):
    placed = (
        P("node", "chan"),
        P("node", "chan"),
        P("node", "chan"),
        P("node", "chan"),
        P("node", "chan"),
        P("node", "chan"),
        P("chan"),
        P("node", None, None, None),
        P("node", None),
        P("node"),
        P(),
    )
    return jax.shard_map(
        local,
        mesh=mesh,
        in_specs=placed,
        out_specs=(P("node", "chan"), P("node", "chan")),
        check_vma=False,
    )
```

```python
import functools
import math

import jax
import jax.numpy as jnp
from jax import lax
from jax.experimental import pallas as pl
from jax.experimental.pallas import tpu as pltpu
from jax.sharding import PartitionSpec as P

VMEM_LIMIT = 32 * 1024 * 1024
VMEM_ALL = 61 * 1024 * 1024
IN_VMEM = pl.BlockSpec(memory_space=pltpu.VMEM)
IN_SMEM = pl.BlockSpec(memory_space=pltpu.SMEM)
IN_HBM = pl.BlockSpec(memory_space=pltpu.HBM)


def params(limit=VMEM_LIMIT):
    return pltpu.CompilerParams(vmem_limit_bytes=limit)


def bf16(*shape):
    return jax.ShapeDtypeStruct(shape, jnp.bfloat16)


def wide(value):
    return value.astype(jnp.float32)


def shifted(value, axis, by):
    size = lax.axis_size(axis)
    pairs = [(i, i + by) for i in range(size) if 0 <= i + by < size]
    return lax.ppermute(value, axis, pairs)


def swapped(value, axis, by):
    size = lax.axis_size(axis)
    return lax.ppermute(value, axis, [(i, i ^ by) for i in range(size)])


def exchanged(value, axis):
    return lax.all_to_all(value, axis, split_axis=0, concat_axis=0, tiled=True)


def masked_grad(grad, pre, slope):
    return (wide(grad) * jnp.where(wide(pre) > 0, 1.0, slope)).astype(jnp.bfloat16)


def aggregate_kernel(
    reach, me, cols, count, gc, pc, gx, px, slopes, adj, clean, corrupt, down, up, data, tiles, rhs, stage, sems
):
    blocks, slots, rows, _ = adj.shape
    width = gc.shape[1]
    spare = blocks + 2 * reach
    pad = 2 * reach * rows

    def copies(block):
        span = pl.ds(pl.multiple_of(block * rows, rows), rows)
        out = [
            pltpu.make_async_copy(ref.at[span], data.at[i, block], sems.at[i, block])
            for i, ref in enumerate((gc, pc, gx, px))
        ]
        return out + [pltpu.make_async_copy(adj.at[block], tiles.at[block], sems.at[4, block])]

    for block in range(blocks):
        for copy in copies(block):
            copy.start()
    stage[...] = jnp.zeros_like(stage)
    rhs[:pad] = jnp.zeros((pad, 2 * width), jnp.bfloat16)
    rhs[pad + blocks * rows :] = jnp.zeros((pad, 2 * width), jnp.bfloat16)
    shape = (rows, rows)
    identity = (
        lax.broadcasted_iota(jnp.int32, shape, 0) == lax.broadcasted_iota(jnp.int32, shape, 1)
    ).astype(jnp.float32).astype(jnp.bfloat16)
    slope = slopes[...]

    def take(block):
        gradients = [masked_grad(data[i, block], data[i + 1, block], slope) for i in (0, 2)]
        span = pl.ds(pl.multiple_of(pad + block * rows, rows), rows)
        rhs[span] = jnp.concatenate(gradients, axis=1)
        turned = lax.dot_general(
            identity,
            tiles[block].reshape(slots * rows, rows),
            (((1,), (1,)), ((), ())),
            preferred_element_type=jnp.float32,
        )
        for k in range(slots):
            live = k < count[block]
            target = cols[k, block] - me[0] * blocks
            place = jnp.where(live, target + reach, spare)
            distance = jnp.where(live, block - target + reach, 0)
            part = turned[:, k * rows : (k + 1) * rows]
            stage[place, distance] = (wide(stage[place, distance]) + part).astype(jnp.bfloat16)

    per_step = 2 - blocks % 2

    @pl.loop(0, blocks // per_step)
    def _(step):
        for i in range(per_step):
            for copy in copies(step * per_step + i):
                copy.wait()
        for i in range(per_step):
            take(step * per_step + i)

    blank = jnp.zeros(shape, jnp.bfloat16)

    def pair(first):
        lhs = jnp.concatenate(
            [
                jnp.concatenate(
                    [blank] * i + [stage[first + i, j] for j in range(2 * reach + 1)] + [blank] * (1 - i),
                    axis=1,
                )
                for i in range(2)
            ],
            axis=0,
        )
        span = pl.ds(pl.multiple_of(first * rows, rows), (2 * reach + 2) * rows)
        product = jnp.dot(lhs, rhs[span], preferred_element_type=jnp.float32)
        product = product.astype(jnp.bfloat16).reshape(2, rows, 2 * width)
        return product[:, :, :width], product[:, :, width:]

    for i in range(0, reach, 2):
        down[0, i : i + 2], down[1, i : i + 2] = pair(i)
        up[0, i : i + 2], up[1, i : i + 2] = pair(blocks + reach + i)

    @pl.loop(0, blocks // 2)
    def _(step):
        span = pl.ds(2 * step, 2)
        clean[span], corrupt[span] = pair(reach + 2 * step)


def aggregate(me, cols, count, gc, pc, gx, px, slopes, adj, reach):
    blocks, slots, rows, _ = adj.shape
    width = gc.shape[1]
    assert reach % 2 == 0 and blocks % 2 == 0
    return pl.pallas_call(
        functools.partial(aggregate_kernel, reach),
        in_specs=[IN_SMEM] * 3 + [IN_HBM] * 4 + [IN_VMEM, IN_HBM],
        out_specs=[IN_VMEM] * 4,
        out_shape=[bf16(blocks, rows, width)] * 2 + [bf16(2, reach, rows, width)] * 2,
        scratch_shapes=[
            pltpu.VMEM((4, blocks, rows, width), jnp.bfloat16),
            pltpu.VMEM((blocks, slots, rows, rows), jnp.bfloat16),
            pltpu.VMEM(((blocks + 4 * reach) * rows, 2 * width), jnp.bfloat16),
            pltpu.VMEM((blocks + 2 * reach + 1, 2 * reach + 1, rows, rows), jnp.bfloat16),
            pltpu.SemaphoreType.DMA((5, blocks)),
        ],
        compiler_params=params(VMEM_ALL),
        cost_estimate=pl.CostEstimate(
            flops=4 * blocks * slots * rows * rows * width,
            bytes_accessed=12 * blocks * rows * width + 2 * blocks * slots * rows * rows,
            transcendentals=0,
        ),
        name="aggregate",
    )(me, cols, count, gc, pc, gx, px, slopes, adj)


def route_kernel(reach, slots, me, shuffle, clean, corrupt, low, high, whole, outgoing, used):
    blocks = clean.shape[0]
    for i in range(outgoing.shape[0] // slots):
        used[i] = 0
    for block in range(blocks):
        owner = shuffle[me[0] * blocks + block] // blocks
        slot = used[owner]
        used[owner] = slot + 1
        mine, theirs = clean[block], corrupt[block]
        if block < reach:
            mine = (wide(mine) + wide(low[0, block])).astype(jnp.bfloat16)
            theirs = (wide(theirs) + wide(low[1, block])).astype(jnp.bfloat16)
        elif block >= blocks - reach:
            at = block - (blocks - reach)
            mine = (wide(mine) + wide(high[0, at])).astype(jnp.bfloat16)
            theirs = (wide(theirs) + wide(high[1, at])).astype(jnp.bfloat16)
        whole[block] = mine
        outgoing[owner * slots + slot] = theirs


def route(me, shuffle, clean, corrupt, low, high, devs, slots):
    blocks, rows, width = clean.shape
    return pl.pallas_call(
        functools.partial(route_kernel, low.shape[1], slots),
        in_specs=[IN_SMEM] * 2 + [IN_VMEM] * 4,
        out_specs=[IN_VMEM] * 2,
        out_shape=[bf16(blocks, rows, width), bf16(devs * slots, rows, width)],
        scratch_shapes=[pltpu.SMEM((devs,), jnp.int32)],
        compiler_params=params(),
        name="route",
    )(me, shuffle, clean, corrupt, low, high)


def merge_kernel(quarter, index, landing, clean, incoming, out):
    _, rows, _ = clean.shape
    group = index[1]
    piece = math.gcd(rows, quarter)
    for place in range(incoming.shape[0]):
        block = landing[place]

        @pl.when(block >= 0)
        def _():
            total = (wide(clean[block]) + wide(incoming[place])).astype(jnp.bfloat16)
            for part in range(rows // piece):
                at = block * (rows // piece) + part
                owner = at // (quarter // piece)
                offset = (at - owner * (quarter // piece)) * piece
                out[owner ^ group, pl.ds(pl.multiple_of(offset, piece), piece)] = total[
                    part * piece : (part + 1) * piece
                ]


def merge(index, landing, clean, incoming, groups):
    blocks, rows, width = clean.shape
    quarter = blocks * rows // groups
    return pl.pallas_call(
        functools.partial(merge_kernel, quarter),
        in_specs=[IN_SMEM] * 2 + [IN_VMEM] * 2,
        out_specs=IN_VMEM,
        out_shape=bf16(groups, quarter, width),
        compiler_params=params(),
        name="merge",
    )(index, landing, clean, incoming)


def halving_orders(devs):
    bits = list(range(1, devs.bit_length() - 1))
    return bits, bits[::-1]


def weight_kernel(devs, index, *refs):
    groups = (len(refs) - 2) // 2
    feats, summed, (keep, send) = refs[:groups], refs[groups : 2 * groups], refs[2 * groups :]
    me, group = index[0], index[1]
    shares = devs // groups
    height, width = keep.shape[3:]
    rhs = jnp.concatenate([piece[...] for piece in summed], axis=1)
    for relative in range(groups):
        product = lax.dot_general(
            feats[relative][...],
            rhs,
            (((0,), (0,)), ((), ())),
            preferred_element_type=jnp.float32,
        ).astype(jnp.bfloat16)
        for share in range(shares):
            node = ((group ^ relative) * shares + share) ^ me
            for half, order in enumerate(halving_orders(devs)):
                place = jnp.int32(0)
                for bit in order:
                    place = place * 2 + ((node >> bit) & 1)
                for i in range(groups // 2):
                    column = (half * (groups // 2) + i) * width
                    part = product[share * height : (share + 1) * height, column : column + width]

                    @pl.when((node & 1) == 0)
                    def _():
                        keep[half, place, i] = part

                    @pl.when((node & 1) == 1)
                    def _():
                        send[half, place, i] = part


def weight_partial(index, feats, summed, devs):
    groups = len(feats)
    rows, width = feats[0].shape
    height = groups * width // devs
    return pl.pallas_call(
        functools.partial(weight_kernel, devs),
        in_specs=[IN_SMEM] + [IN_VMEM] * (2 * groups),
        out_specs=[IN_VMEM] * 2,
        out_shape=[bf16(2, devs // 2, groups // 2, height, width)] * 2,
        compiler_params=params(),
        cost_estimate=pl.CostEstimate(
            flops=2 * rows * (groups * width) ** 2,
            bytes_accessed=2 * (groups * width) ** 2 + 4 * groups * rows * width,
            transcendentals=0,
        ),
        name="weight_partial",
    )(index, *feats, *summed)


def feature_kernel(index, *refs):
    *summed, low, high, out = refs
    groups = len(summed)
    devs = low.shape[0]
    me = index[0]
    shares = devs // groups
    lhs = jnp.concatenate([piece[...] for piece in summed], axis=1)
    for target in range(groups):
        rows = []
        for share in range(shares):
            node = (target * shares + share) ^ me
            parts = []
            for half, order in zip((low, high), halving_orders(devs)):
                place = jnp.int32(0)
                for j, bit in enumerate([*order, 0]):
                    place += ((node >> bit) & 1) << j
                parts += [half[place, i] for i in range(groups // 2)]
            rows.append(jnp.concatenate(parts, axis=1))
        out[target] = lax.dot_general(
            lhs,
            jnp.concatenate(rows, axis=0),
            (((1,), (1,)), ((), ())),
            preferred_element_type=jnp.float32,
        ).astype(jnp.bfloat16)


def feature_rows(index, summed, halves):
    groups = len(summed)
    rows, width = summed[0].shape
    return pl.pallas_call(
        feature_kernel,
        in_specs=[IN_SMEM] + [IN_VMEM] * (groups + 2),
        out_specs=IN_VMEM,
        out_shape=bf16(groups, rows, width),
        compiler_params=params(),
        cost_estimate=pl.CostEstimate(
            flops=2 * rows * (groups * width) ** 2,
            bytes_accessed=2 * (groups * width) ** 2 + 4 * groups * rows * width,
            transcendentals=0,
        ),
        name="feature_rows",
    )(index, *summed, *halves)


def landing_blocks(shuffle_from, me, blocks, devs, slots):
    owner = (shuffle_from // blocks).reshape(devs, blocks)
    within = (shuffle_from % blocks).reshape(devs, blocks)
    for_me = owner == me
    earlier = jnp.arange(blocks)[None, :] < jnp.arange(blocks)[:, None]
    rank = jnp.sum((for_me[:, None, :] & earlier[None]).astype(jnp.int32), axis=2)
    picked = for_me[:, None, :] & (rank[:, None, :] == jnp.arange(slots)[None, :, None])
    return (jnp.sum(jnp.where(picked, within[:, None, :] + 1, 0), axis=2) - 1).reshape(-1)


def exchange_order(groups):
    return sorted(range(1, groups), reverse=True)


def local(
    features,
    weight,
    pre_clean,
    pre_corrupt,
    grad_clean,
    grad_corrupt,
    slopes,
    adj_vals,
    adj_cols,
    adj_count,
    shuffle_from,
):
    row_count, width = features.shape
    blocks, tile_slots, tile_rows, _ = adj_vals.shape
    reach = (tile_slots - 1) // 2
    me = lax.axis_index("node")
    group = lax.axis_index("chan")
    devs = lax.axis_size("node")
    groups = lax.axis_size("chan")
    slots = -(-blocks // devs)
    quarter = row_count // groups
    index = jnp.stack([me, group])

    args = (index, adj_cols.T, adj_count, grad_clean, pre_clean, grad_corrupt, pre_corrupt)
    args += (slopes[None, :], adj_vals)
    clean, corrupt, down, up = aggregate(*args, reach)
    from_prev = shifted(up, "node", 1)
    from_next = shifted(down, "node", -1)
    tiles = [weight] + [swapped(weight, "chan", i) for i in range(1, groups)]

    feats = [None] * groups
    by_quarter = features.reshape(groups, quarter, width)
    for i in [0, *exchange_order(groups)]:
        piece = lax.dynamic_index_in_dim(by_quarter, group ^ i, 0, keepdims=False)
        feats[i] = swapped(piece, "chan", i) if i else piece

    clean, outgoing = route(
        index, shuffle_from, clean, corrupt, from_prev, from_next, devs, slots
    )
    shuffle_from, outgoing, tiles = lax.optimization_barrier((shuffle_from, outgoing, tiles))
    landing = landing_blocks(shuffle_from, me, blocks, devs, slots)
    incoming = exchanged(outgoing, "node")

    halves = [jnp.stack(part)[None] for part in (tiles[: groups // 2], tiles[groups // 2 :])]
    orders = halving_orders(devs)
    for hop in range(len(orders[0])):
        halves = [
            jnp.concatenate([part, swapped(part, "node", 1 << order[hop])], axis=0)
            for part, order in zip(halves, orders)
        ]
    incoming, feats, halves = lax.optimization_barrier((incoming, feats, halves))

    merged = merge(index, landing, clean, incoming, groups)
    summed = [merged[0]] + [None] * (groups - 1)
    for i in exchange_order(groups):
        summed[i] = swapped(merged[i], "chan", i)
    halves = [jnp.concatenate([part, swapped(part, "node", 1)], axis=0) for part in halves]
    summed, halves = lax.optimization_barrier((summed, halves))

    rows_out = feature_rows(index, summed, halves)
    grad_features = exchanged(rows_out, "chan").reshape(row_count, width)

    feats, summed, rows_out = lax.optimization_barrier((feats, summed, rows_out))
    keep, send = weight_partial(index, feats, summed, devs)
    total = wide(keep) + wide(swapped(send, "node", 1))
    shares = []
    for part, order in zip((total[0], total[1]), halving_orders(devs)):
        for bit in order:
            size = part.shape[0] // 2
            arrived = swapped(part[size:].astype(jnp.bfloat16), "node", 1 << bit)
            part = part[:size] + wide(arrived)
        shares.append(part[0])
    shares = jnp.concatenate(shares, axis=0)
    grad_weight = shares[0]
    for i in range(1, groups):
        grad_weight = grad_weight + wide(swapped(shares[i].astype(jnp.bfloat16), "chan", i))

    return (grad_weight, grad_features)


def solution(mesh):
    placed = (
        P("node", "chan"),
        P("node", "chan"),
        P("node", "chan"),
        P("node", "chan"),
        P("node", "chan"),
        P("node", "chan"),
        P("chan"),
        P("node", None, None, None),
        P("node", None),
        P("node"),
        P(),
    )
    return jax.shard_map(
        local,
        mesh=mesh,
        in_specs=placed,
        out_specs=(P("node", "chan"), P("node", "chan")),
        check_vma=False,
    )
```

```python
import functools
import math

import jax
import jax.numpy as jnp
from jax import lax
from jax.experimental import pallas as pl
from jax.experimental.pallas import tpu as pltpu
from jax.sharding import PartitionSpec as P

VMEM_LIMIT = 32 * 1024 * 1024
VMEM_ALL = 61 * 1024 * 1024
IN_VMEM = pl.BlockSpec(memory_space=pltpu.VMEM)
IN_SMEM = pl.BlockSpec(memory_space=pltpu.SMEM)
IN_HBM = pl.BlockSpec(memory_space=pltpu.HBM)


def params(limit=VMEM_LIMIT):
    return pltpu.CompilerParams(vmem_limit_bytes=limit)


def bf16(*shape):
    return jax.ShapeDtypeStruct(shape, jnp.bfloat16)


def wide(value):
    return value.astype(jnp.float32)


def shifted(value, axis, by):
    size = lax.axis_size(axis)
    pairs = [(i, i + by) for i in range(size) if 0 <= i + by < size]
    return lax.ppermute(value, axis, pairs)


def swapped(value, axis, by):
    size = lax.axis_size(axis)
    return lax.ppermute(value, axis, [(i, i ^ by) for i in range(size)])


def exchanged(value, axis):
    return lax.all_to_all(value, axis, split_axis=0, concat_axis=0, tiled=True)


def masked_grad(grad, pre, slope):
    return (wide(grad) * jnp.where(wide(pre) > 0, 1.0, slope)).astype(jnp.bfloat16)


def aggregate_kernel(
    reach, groups, me, cols, count, gc, pc, gx, px, slopes, adj, features, weight, *refs
):
    clean, corrupt, down, up, *refs = refs
    packed, (data, tiles, rhs, stage, sems, pack_sems) = refs[:groups], refs[groups:]
    blocks, slots, rows, _ = adj.shape
    width = gc.shape[1]
    quarter = features.shape[0] // groups
    spare = blocks + 2 * reach
    pad = 2 * reach * rows

    def copies(block):
        span = pl.ds(pl.multiple_of(block * rows, rows), rows)
        out = [
            pltpu.make_async_copy(ref.at[span], data.at[i, block], sems.at[i, block])
            for i, ref in enumerate((gc, pc, gx, px))
        ]
        return out + [pltpu.make_async_copy(adj.at[block], tiles.at[block], sems.at[4, block])]

    packs = []
    for i in range(groups):
        span = pl.ds(pl.multiple_of((me[1] ^ i) * quarter, quarter), quarter)
        packs.append(
            pltpu.make_async_copy(features.at[span], packed[i].at[:quarter], pack_sems.at[0, i])
        )
        packs.append(pltpu.make_async_copy(weight, packed[i].at[quarter:], pack_sems.at[1, i]))
    for block in range(blocks):
        for copy in copies(block):
            copy.start()
    for copy in packs:
        copy.start()
    stage[...] = jnp.zeros_like(stage)
    rhs[:pad] = jnp.zeros((pad, 2 * width), jnp.bfloat16)
    rhs[pad + blocks * rows :] = jnp.zeros((pad, 2 * width), jnp.bfloat16)
    shape = (rows, rows)
    identity = (
        lax.broadcasted_iota(jnp.int32, shape, 0) == lax.broadcasted_iota(jnp.int32, shape, 1)
    ).astype(jnp.float32).astype(jnp.bfloat16)
    slope = slopes[...]

    def take(block):
        gradients = [masked_grad(data[i, block], data[i + 1, block], slope) for i in (0, 2)]
        span = pl.ds(pl.multiple_of(pad + block * rows, rows), rows)
        rhs[span] = jnp.concatenate(gradients, axis=1)
        turned = lax.dot_general(
            identity,
            tiles[block].reshape(slots * rows, rows),
            (((1,), (1,)), ((), ())),
            preferred_element_type=jnp.float32,
        )
        for k in range(slots):
            live = k < count[block]
            target = cols[k, block] - me[0] * blocks
            place = jnp.where(live, target + reach, spare)
            distance = jnp.where(live, block - target + reach, 0)
            part = turned[:, k * rows : (k + 1) * rows]
            stage[place, distance] = (wide(stage[place, distance]) + part).astype(jnp.bfloat16)

    per_step = 2 - blocks % 2

    @pl.loop(0, blocks // per_step)
    def _(step):
        for i in range(per_step):
            for copy in copies(step * per_step + i):
                copy.wait()
        for i in range(per_step):
            take(step * per_step + i)

    blank = jnp.zeros(shape, jnp.bfloat16)

    def pair(first):
        lhs = jnp.concatenate(
            [
                jnp.concatenate(
                    [blank] * i + [stage[first + i, j] for j in range(2 * reach + 1)] + [blank] * (1 - i),
                    axis=1,
                )
                for i in range(2)
            ],
            axis=0,
        )
        span = pl.ds(pl.multiple_of(first * rows, rows), (2 * reach + 2) * rows)
        product = jnp.dot(lhs, rhs[span], preferred_element_type=jnp.float32)
        product = product.astype(jnp.bfloat16).reshape(2, rows, 2 * width)
        return product[:, :, :width], product[:, :, width:]

    for i in range(0, reach, 2):
        down[0, i : i + 2], down[1, i : i + 2] = pair(i)
        up[0, i : i + 2], up[1, i : i + 2] = pair(blocks + reach + i)

    @pl.loop(0, blocks // 2)
    def _(step):
        span = pl.ds(2 * step, 2)
        clean[span], corrupt[span] = pair(reach + 2 * step)

    for copy in packs:
        copy.wait()


def aggregate(me, cols, count, gc, pc, gx, px, slopes, adj, features, weight, reach, groups):
    blocks, slots, rows, _ = adj.shape
    width = gc.shape[1]
    assert reach % 2 == 0 and blocks % 2 == 0
    packed = features.shape[0] // groups + weight.shape[0]
    return pl.pallas_call(
        functools.partial(aggregate_kernel, reach, groups),
        in_specs=[IN_SMEM] * 3 + [IN_HBM] * 4 + [IN_VMEM] + [IN_HBM] * 3,
        out_specs=[IN_VMEM] * 4 + [IN_HBM] * groups,
        out_shape=[bf16(blocks, rows, width)] * 2
        + [bf16(2, reach, rows, width)] * 2
        + [bf16(packed, width)] * groups,
        scratch_shapes=[
            pltpu.VMEM((4, blocks, rows, width), jnp.bfloat16),
            pltpu.VMEM((blocks, slots, rows, rows), jnp.bfloat16),
            pltpu.VMEM(((blocks + 4 * reach) * rows, 2 * width), jnp.bfloat16),
            pltpu.VMEM((blocks + 2 * reach + 1, 2 * reach + 1, rows, rows), jnp.bfloat16),
            pltpu.SemaphoreType.DMA((5, blocks)),
            pltpu.SemaphoreType.DMA((2, groups)),
        ],
        compiler_params=params(VMEM_ALL),
        cost_estimate=pl.CostEstimate(
            flops=4 * blocks * slots * rows * rows * width,
            bytes_accessed=12 * blocks * rows * width + 2 * blocks * slots * rows * rows,
            transcendentals=0,
        ),
        name="aggregate",
    )(me, cols, count, gc, pc, gx, px, slopes, adj, features, weight)


def route_kernel(reach, slots, me, shuffle, clean, corrupt, low, high, whole, outgoing, used):
    blocks = clean.shape[0]
    for i in range(outgoing.shape[0] // slots):
        used[i] = 0
    for block in range(blocks):
        owner = shuffle[me[0] * blocks + block] // blocks
        slot = used[owner]
        used[owner] = slot + 1
        mine, theirs = clean[block], corrupt[block]
        if block < reach:
            mine = (wide(mine) + wide(low[0, block])).astype(jnp.bfloat16)
            theirs = (wide(theirs) + wide(low[1, block])).astype(jnp.bfloat16)
        elif block >= blocks - reach:
            at = block - (blocks - reach)
            mine = (wide(mine) + wide(high[0, at])).astype(jnp.bfloat16)
            theirs = (wide(theirs) + wide(high[1, at])).astype(jnp.bfloat16)
        whole[block] = mine
        outgoing[owner * slots + slot] = theirs


def route(me, shuffle, clean, corrupt, low, high, devs, slots):
    blocks, rows, width = clean.shape
    return pl.pallas_call(
        functools.partial(route_kernel, low.shape[1], slots),
        in_specs=[IN_SMEM] * 2 + [IN_VMEM] * 4,
        out_specs=[IN_VMEM] * 2,
        out_shape=[bf16(blocks, rows, width), bf16(devs * slots, rows, width)],
        scratch_shapes=[pltpu.SMEM((devs,), jnp.int32)],
        compiler_params=params(),
        name="route",
    )(me, shuffle, clean, corrupt, low, high)


def merge_kernel(quarter, index, landing, clean, incoming, *refs):
    *packed, out, tiles = refs
    for i, piece in enumerate(packed):
        tiles[i] = piece[quarter:]
    _, rows, _ = clean.shape
    group = index[1]
    piece = math.gcd(rows, quarter)
    for place in range(incoming.shape[0]):
        block = landing[place]

        @pl.when(block >= 0)
        def _():
            total = (wide(clean[block]) + wide(incoming[place])).astype(jnp.bfloat16)
            for part in range(rows // piece):
                at = block * (rows // piece) + part
                owner = at // (quarter // piece)
                offset = (at - owner * (quarter // piece)) * piece
                out[owner ^ group, pl.ds(pl.multiple_of(offset, piece), piece)] = total[
                    part * piece : (part + 1) * piece
                ]


def merge(index, landing, clean, incoming, packed):
    blocks, rows, width = clean.shape
    groups = len(packed)
    quarter = blocks * rows // groups
    height = packed[0].shape[0] - quarter
    return pl.pallas_call(
        functools.partial(merge_kernel, quarter),
        in_specs=[IN_SMEM] * 2 + [IN_VMEM] * (2 + groups),
        out_specs=[IN_VMEM] * 2,
        out_shape=[bf16(groups, quarter, width), bf16(groups, height, width)],
        compiler_params=params(),
        name="merge",
    )(index, landing, clean, incoming, *packed)


def weight_kernel(devs, index, *refs):
    groups = (len(refs) - 2) // 2
    packed, summed, (keep, send) = refs[:groups], refs[groups : 2 * groups], refs[2 * groups :]
    me, group = index[0], index[1]
    shares = devs // groups
    height, width = keep.shape[2:]
    rhs = jnp.concatenate([piece[...] for piece in summed], axis=1)
    for relative in range(groups):
        product = lax.dot_general(
            packed[relative][: rhs.shape[0]],
            rhs,
            (((0,), (0,)), ((), ())),
            preferred_element_type=jnp.float32,
        ).astype(jnp.bfloat16)
        for share in range(shares):
            node = ((group ^ relative) * shares + share) ^ me
            rows = product[share * height : (share + 1) * height]

            def store(out):
                for i in range(groups):
                    out[node >> 1, i] = rows[:, i * width : (i + 1) * width]

            pl.when((node & 1) == 0)(functools.partial(store, keep))
            pl.when((node & 1) == 1)(functools.partial(store, send))


def weight_partial(index, packed, summed, devs):
    groups = len(packed)
    rows, width = summed[0].shape
    height = groups * width // devs
    return pl.pallas_call(
        functools.partial(weight_kernel, devs),
        in_specs=[IN_SMEM] + [IN_VMEM] * (2 * groups),
        out_specs=[IN_VMEM] * 2,
        out_shape=[bf16(devs // 2, groups, height, width)] * 2,
        compiler_params=params(),
        cost_estimate=pl.CostEstimate(
            flops=2 * rows * (groups * width) ** 2,
            bytes_accessed=2 * (groups * width) ** 2 + 4 * groups * rows * width,
            transcendentals=0,
        ),
        name="weight_partial",
    )(index, *packed, *summed)


def feature_kernel(index, *refs):
    *summed, even, odd, out = refs
    groups = len(summed)
    devs = 2 * even.shape[0]
    me, group = index[0], index[1]
    shares = devs // groups
    height = even.shape[2]
    low = me & (shares - 1)
    lhs = jnp.concatenate([piece[...] for piece in summed], axis=1)
    for relative in range(groups):
        rows = []
        for i in range(shares):
            node = (((group ^ relative) * shares) ^ (me - low)) + i
            half = odd if i % 2 else even
            rows.append(jnp.concatenate([half[node >> 1, j] for j in range(groups)], axis=1))
        product = lax.dot_general(
            lhs,
            jnp.concatenate(rows, axis=0),
            (((1,), (1,)), ((), ())),
            preferred_element_type=jnp.float32,
        ).astype(jnp.bfloat16)
        parts = [product[:, i * height : (i + 1) * height] for i in range(shares)]

        def store(flip):
            out[relative] = jnp.concatenate([parts[i ^ flip] for i in range(shares)], axis=1)

        for flip in range(shares):
            pl.when(low == flip)(functools.partial(store, flip))


def feature_rows(index, summed, even, odd):
    groups = len(summed)
    rows, width = summed[0].shape
    return pl.pallas_call(
        feature_kernel,
        in_specs=[IN_SMEM] + [IN_VMEM] * (groups + 2),
        out_specs=IN_VMEM,
        out_shape=bf16(groups, rows, width),
        compiler_params=params(),
        cost_estimate=pl.CostEstimate(
            flops=2 * rows * (groups * width) ** 2,
            bytes_accessed=2 * (groups * width) ** 2 + 4 * groups * rows * width,
            transcendentals=0,
        ),
        name="feature_rows",
    )(index, *summed, even, odd)


def gather_kernel(index, *refs):
    *pieces, out, sems = refs
    rows = pieces[0].shape[0]
    copies = [
        pltpu.make_async_copy(
            piece, out.at[pl.ds(pl.multiple_of((index[1] ^ i) * rows, rows), rows)], sems.at[i]
        )
        for i, piece in enumerate(pieces)
    ]
    for copy in copies:
        copy.start()
    for copy in copies:
        copy.wait()


def laid_out(index, pieces):
    rows, width = pieces[0].shape
    return pl.pallas_call(
        gather_kernel,
        in_specs=[IN_SMEM] + [IN_VMEM] * len(pieces),
        out_specs=IN_HBM,
        out_shape=bf16(len(pieces) * rows, width),
        scratch_shapes=[pltpu.SemaphoreType.DMA((len(pieces),))],
        compiler_params=params(),
        name="laid_out",
    )(index, *pieces)


def landing_blocks(shuffle_from, me, blocks, devs, slots):
    owner = (shuffle_from // blocks).reshape(devs, blocks)
    within = (shuffle_from % blocks).reshape(devs, blocks)
    for_me = owner == me
    earlier = jnp.arange(blocks)[None, :] < jnp.arange(blocks)[:, None]
    rank = jnp.sum((for_me[:, None, :] & earlier[None]).astype(jnp.int32), axis=2)
    picked = for_me[:, None, :] & (rank[:, None, :] == jnp.arange(slots)[None, :, None])
    return (jnp.sum(jnp.where(picked, within[:, None, :] + 1, 0), axis=2) - 1).reshape(-1)


def exchange_order(groups):
    return sorted(range(1, groups), reverse=True)


def local(
    features,
    weight,
    pre_clean,
    pre_corrupt,
    grad_clean,
    grad_corrupt,
    slopes,
    adj_vals,
    adj_cols,
    adj_count,
    shuffle_from,
):
    blocks, tile_slots, tile_rows, _ = adj_vals.shape
    reach = (tile_slots - 1) // 2
    me = lax.axis_index("node")
    group = lax.axis_index("chan")
    devs = lax.axis_size("node")
    groups = lax.axis_size("chan")
    slots = -(-blocks // devs)
    index = jnp.stack([me, group])

    args = (index, adj_cols.T, adj_count, grad_clean, pre_clean, grad_corrupt, pre_corrupt)
    args += (slopes[None, :], adj_vals)
    clean, corrupt, down, up, *packed = aggregate(*args, features, weight, reach, groups)
    from_prev = shifted(up, "node", 1)
    from_next = shifted(down, "node", -1)
    for i in exchange_order(groups):
        packed[i] = swapped(packed[i], "chan", i)

    clean, outgoing = route(
        index, shuffle_from, clean, corrupt, from_prev, from_next, devs, slots
    )
    shuffle_from, outgoing = lax.optimization_barrier((shuffle_from, outgoing))
    landing = landing_blocks(shuffle_from, me, blocks, devs, slots)
    incoming = exchanged(outgoing, "node")
    merged, tiles = merge(index, landing, clean, incoming, packed)

    summed = [merged[0]] + [None] * (groups - 1)
    for i in exchange_order(groups):
        summed[i] = swapped(merged[i], "chan", i)
    even = [tiles] + [swapped(tiles, "node", 2 * i) for i in range(1, devs // 2)]
    summed, even = lax.optimization_barrier((summed, even))
    even = jnp.stack(even)
    odd = swapped(even, "node", 1)

    keep, send = weight_partial(index, packed, summed, devs)
    odd, send = lax.optimization_barrier((odd, send))
    arrived = swapped(send, "node", 1)
    rows_out = feature_rows(index, summed, even, odd)
    arrived, rows_out = lax.optimization_barrier((arrived, rows_out))
    pieces = [rows_out[0]] + [None] * (groups - 1)
    for i in exchange_order(groups):
        pieces[i] = swapped(rows_out[i], "chan", i)

    total = wide(keep) + wide(arrived)
    share = total[0]
    for i in range(1, devs // 2):
        share = share + wide(swapped(total[i].astype(jnp.bfloat16), "node", 2 * i))
    pieces, share = lax.optimization_barrier((pieces, share))
    grad_weight = share[0]
    for i in range(1, groups):
        grad_weight = grad_weight + wide(swapped(share[i].astype(jnp.bfloat16), "chan", i))

    return (grad_weight, laid_out(index, pieces))


def solution(mesh):
    placed = (
        P("node", "chan"),
        P("node", "chan"),
        P("node", "chan"),
        P("node", "chan"),
        P("node", "chan"),
        P("node", "chan"),
        P("chan"),
        P("node", None, None, None),
        P("node", None),
        P("node"),
        P(),
    )
    return jax.shard_map(
        local,
        mesh=mesh,
        in_specs=placed,
        out_specs=(P("node", "chan"), P("node", "chan")),
        check_vma=False,
    )
```

```python
import functools
import math

import jax
import jax.numpy as jnp
from jax import lax
from jax.experimental import pallas as pl
from jax.experimental.pallas import tpu as pltpu
from jax.sharding import PartitionSpec as P

VMEM_LIMIT = 32 * 1024 * 1024
VMEM_ALL = 61 * 1024 * 1024
IN_VMEM = pl.BlockSpec(memory_space=pltpu.VMEM)
IN_SMEM = pl.BlockSpec(memory_space=pltpu.SMEM)
IN_HBM = pl.BlockSpec(memory_space=pltpu.HBM)


def params(limit=VMEM_LIMIT):
    return pltpu.CompilerParams(vmem_limit_bytes=limit)


def bf16(*shape):
    return jax.ShapeDtypeStruct(shape, jnp.bfloat16)


def wide(value):
    return value.astype(jnp.float32)


def shifted(value, axis, by):
    size = lax.axis_size(axis)
    pairs = [(i, i + by) for i in range(size) if 0 <= i + by < size]
    return lax.ppermute(value, axis, pairs)


def swapped(value, axis, by):
    size = lax.axis_size(axis)
    return lax.ppermute(value, axis, [(i, i ^ by) for i in range(size)])


def exchanged(value, axis):
    return lax.all_to_all(value, axis, split_axis=0, concat_axis=0, tiled=True)


def masked_grad(grad, pre, slope):
    return (wide(grad) * jnp.where(wide(pre) > 0, 1.0, slope)).astype(jnp.bfloat16)


def find_places(index, shuffle, blocks, slots, places, used):
    for i in range(used.shape[0]):
        used[i] = 0
    for block in range(blocks):
        owner = shuffle[index[0] * blocks + block] // blocks
        slot = used[owner]
        used[owner] = slot + 1
        places[block] = owner * slots + slot


def aggregate_kernel(
    reach, groups, send_slots, me, shuffle, cols, count, gc, pc, gx, px, slopes, adj, features, weight, *refs
):
    clean, outgoing, down, up, *refs = refs
    packed, (data, tiles, rhs, stage, places, used, sems, pack_sems) = refs[:groups], refs[groups:]
    blocks, slots, rows, _ = adj.shape
    width = gc.shape[1]
    quarter = features.shape[0] // groups
    spare = blocks + 2 * reach
    pad = 2 * reach * rows

    def copies(block):
        span = pl.ds(pl.multiple_of(block * rows, rows), rows)
        out = [
            pltpu.make_async_copy(ref.at[span], data.at[i, block], sems.at[i, block])
            for i, ref in enumerate((gc, pc, gx, px))
        ]
        return out + [pltpu.make_async_copy(adj.at[block], tiles.at[block], sems.at[4, block])]

    packs = []
    for i in range(groups):
        span = pl.ds(pl.multiple_of((me[1] ^ i) * quarter, quarter), quarter)
        packs.append(
            pltpu.make_async_copy(features.at[span], packed[i].at[:quarter], pack_sems.at[0, i])
        )
        packs.append(pltpu.make_async_copy(weight, packed[i].at[quarter:], pack_sems.at[1, i]))
    for block in range(blocks):
        for copy in copies(block):
            copy.start()
    for copy in packs:
        copy.start()
    stage[...] = jnp.zeros_like(stage)
    rhs[:pad] = jnp.zeros((pad, 2 * width), jnp.bfloat16)
    rhs[pad + blocks * rows :] = jnp.zeros((pad, 2 * width), jnp.bfloat16)
    shape = (rows, rows)
    identity = (
        lax.broadcasted_iota(jnp.int32, shape, 0) == lax.broadcasted_iota(jnp.int32, shape, 1)
    ).astype(jnp.float32).astype(jnp.bfloat16)
    slope = slopes[...]

    def take(block):
        gradients = [masked_grad(data[i, block], data[i + 1, block], slope) for i in (0, 2)]
        span = pl.ds(pl.multiple_of(pad + block * rows, rows), rows)
        rhs[span] = jnp.concatenate(gradients, axis=1)
        turned = lax.dot_general(
            identity,
            tiles[block].reshape(slots * rows, rows),
            (((1,), (1,)), ((), ())),
            preferred_element_type=jnp.float32,
        )
        for k in range(slots):
            live = k < count[block]
            target = cols[k, block] - me[0] * blocks
            place = jnp.where(live, target + reach, spare)
            distance = jnp.where(live, block - target + reach, 0)
            part = turned[:, k * rows : (k + 1) * rows]
            stage[place, distance] = (wide(stage[place, distance]) + part).astype(jnp.bfloat16)

    find_places(me, shuffle, blocks, send_slots, places, used)
    per_step = blocks // 2

    @pl.loop(0, blocks // per_step)
    def _(step):
        for i in range(per_step):
            for copy in copies(step * per_step + i):
                copy.wait()
        for i in range(per_step):
            take(step * per_step + i)

    blank = jnp.zeros(shape, jnp.bfloat16)

    def pair(first):
        lhs = jnp.concatenate(
            [
                jnp.concatenate(
                    [blank] * i + [stage[first + i, j] for j in range(2 * reach + 1)] + [blank] * (1 - i),
                    axis=1,
                )
                for i in range(2)
            ],
            axis=0,
        )
        span = pl.ds(pl.multiple_of(first * rows, rows), (2 * reach + 2) * rows)
        product = jnp.dot(lhs, rhs[span], preferred_element_type=jnp.float32)
        product = product.astype(jnp.bfloat16).reshape(2, rows, 2 * width)
        return product[:, :, :width], product[:, :, width:]

    for i in range(0, reach, 2):
        down[0, i : i + 2], down[1, i : i + 2] = pair(i)
        up[0, i : i + 2], up[1, i : i + 2] = pair(blocks + reach + i)

    for first in range(0, blocks, 2):
        clean[first : first + 2], sent = pair(reach + first)
        for i in range(2):
            outgoing[places[first + i]] = sent[i]

    for copy in packs:
        copy.wait()


def aggregate(index, shuffle, cols, count, gc, pc, gx, px, slopes, adj, features, weight, reach, devs, groups):
    blocks, slots, rows, _ = adj.shape
    width = gc.shape[1]
    send_slots = -(-blocks // devs)
    assert reach % 2 == 0 and blocks % 2 == 0
    packed = features.shape[0] // groups + weight.shape[0]
    return pl.pallas_call(
        functools.partial(aggregate_kernel, reach, groups, send_slots),
        in_specs=[IN_SMEM] * 4 + [IN_HBM] * 4 + [IN_VMEM] + [IN_HBM] * 3,
        out_specs=[IN_VMEM] * (4 + groups),
        out_shape=[bf16(blocks, rows, width), bf16(devs * send_slots, rows, width)]
        + [bf16(2, reach, rows, width)] * 2
        + [bf16(packed, width)] * groups,
        scratch_shapes=[
            pltpu.VMEM((4, blocks, rows, width), jnp.bfloat16),
            pltpu.VMEM((blocks, slots, rows, rows), jnp.bfloat16),
            pltpu.VMEM(((blocks + 4 * reach) * rows, 2 * width), jnp.bfloat16),
            pltpu.VMEM((blocks + 2 * reach + 1, 2 * reach + 1, rows, rows), jnp.bfloat16),
            pltpu.SMEM((blocks,), jnp.int32),
            pltpu.SMEM((devs,), jnp.int32),
            pltpu.SemaphoreType.DMA((5, blocks)),
            pltpu.SemaphoreType.DMA((2, groups)),
        ],
        compiler_params=params(VMEM_ALL),
        cost_estimate=pl.CostEstimate(
            flops=4 * blocks * slots * rows * rows * width,
            bytes_accessed=12 * blocks * rows * width + 2 * blocks * slots * rows * rows,
            transcendentals=0,
        ),
        name="aggregate",
    )(index, shuffle, cols, count, gc, pc, gx, px, slopes, adj, features, weight)


def patch_kernel(reach, slots, index, shuffle, clean, outgoing, low, high, clean_out, outgoing_out, *scratch):
    held, ready, places, used, sems = scratch
    blocks = clean.shape[0]
    find_places(index, shuffle, blocks, slots, places, used)
    border = [*range(reach), *range(blocks - reach, blocks)]

    def spots(i, first, second):
        return (first.at[border[i]], second.at[places[border[i]]])

    reads, writes = [], []
    for i in range(2 * reach):
        for which in range(2):
            source = spots(i, clean, outgoing)[which]
            reads.append(pltpu.make_async_copy(source, held.at[which, i], sems.at[0, which, i]))
            target = spots(i, clean_out, outgoing_out)[which]
            writes.append(pltpu.make_async_copy(ready.at[which, i], target, sems.at[1, which, i]))
    for copy in reads:
        copy.start()
    for i in range(2 * reach):
        for which in range(2):
            reads[2 * i + which].wait()
            other = low[which, i] if i < reach else high[which, i - reach]
            ready[which, i] = (wide(held[which, i]) + wide(other)).astype(jnp.bfloat16)
            writes[2 * i + which].start()
    for copy in writes:
        copy.wait()


def patch(index, shuffle, clean, outgoing, low, high, slots):
    blocks, rows, width = clean.shape
    reach = low.shape[1]
    return pl.pallas_call(
        functools.partial(patch_kernel, reach, slots),
        in_specs=[IN_SMEM] * 2 + [IN_HBM] * 2 + [IN_VMEM] * 2,
        out_specs=[IN_HBM] * 2,
        out_shape=[bf16(*clean.shape), bf16(*outgoing.shape)],
        input_output_aliases={2: 0, 3: 1},
        scratch_shapes=[
            pltpu.VMEM((2, 2 * reach, rows, width), jnp.bfloat16),
            pltpu.VMEM((2, 2 * reach, rows, width), jnp.bfloat16),
            pltpu.SMEM((blocks,), jnp.int32),
            pltpu.SMEM((outgoing.shape[0] // slots,), jnp.int32),
            pltpu.SemaphoreType.DMA((2, 2, 2 * reach)),
        ],
        compiler_params=params(VMEM_ALL),
        name="patch",
    )(index, shuffle, clean, outgoing, low, high)


def merge_kernel(quarter, index, landing, clean, incoming, out):
    _, rows, _ = clean.shape
    group = index[1]
    piece = math.gcd(rows, quarter)
    for place in range(incoming.shape[0]):
        block = landing[place]

        @pl.when(block >= 0)
        def _():
            total = (wide(clean[block]) + wide(incoming[place])).astype(jnp.bfloat16)
            for part in range(rows // piece):
                at = block * (rows // piece) + part
                owner = at // (quarter // piece)
                offset = (at - owner * (quarter // piece)) * piece
                out[owner ^ group, pl.ds(pl.multiple_of(offset, piece), piece)] = total[
                    part * piece : (part + 1) * piece
                ]


def merge(index, landing, clean, incoming, groups):
    blocks, rows, width = clean.shape
    quarter = blocks * rows // groups
    return pl.pallas_call(
        functools.partial(merge_kernel, quarter),
        in_specs=[IN_SMEM] * 2 + [IN_VMEM] * 2,
        out_specs=IN_VMEM,
        out_shape=bf16(groups, quarter, width),
        compiler_params=params(),
        name="merge",
    )(index, landing, clean, incoming)


def weight_kernel(devs, index, *refs):
    groups = (len(refs) - 2) // 2
    packed, summed, (keep, send) = refs[:groups], refs[groups : 2 * groups], refs[2 * groups :]
    me, group = index[0], index[1]
    shares = devs // groups
    height, width = keep.shape[2:]
    rhs = jnp.concatenate([piece[...] for piece in summed], axis=1)
    for relative in range(groups):
        product = lax.dot_general(
            packed[relative][: rhs.shape[0]],
            rhs,
            (((0,), (0,)), ((), ())),
            preferred_element_type=jnp.float32,
        ).astype(jnp.bfloat16)
        for share in range(shares):
            node = ((group ^ relative) * shares + share) ^ me
            rows = product[share * height : (share + 1) * height]

            def store(out):
                for i in range(groups):
                    out[node >> 1, i] = rows[:, i * width : (i + 1) * width]

            pl.when((node & 1) == 0)(functools.partial(store, keep))
            pl.when((node & 1) == 1)(functools.partial(store, send))


def weight_partial(index, packed, summed, devs):
    groups = len(packed)
    rows, width = summed[0].shape
    height = groups * width // devs
    return pl.pallas_call(
        functools.partial(weight_kernel, devs),
        in_specs=[IN_SMEM] + [IN_VMEM] * (2 * groups),
        out_specs=[IN_VMEM] * 2,
        out_shape=[bf16(devs // 2, groups, height, width)] * 2,
        compiler_params=params(),
        cost_estimate=pl.CostEstimate(
            flops=2 * rows * (groups * width) ** 2,
            bytes_accessed=2 * (groups * width) ** 2 + 4 * groups * rows * width,
            transcendentals=0,
        ),
        name="weight_partial",
    )(index, *packed, *summed)


def feature_kernel(index, *refs):
    *summed, even, odd, out = refs
    groups = len(summed)
    devs = 2 * even.shape[0]
    me, group = index[0], index[1]
    shares = devs // groups
    height = even.shape[2]
    low = me & (shares - 1)
    lhs = jnp.concatenate([piece[...] for piece in summed], axis=1)
    for relative in range(groups):
        rows = []
        for i in range(shares):
            node = (((group ^ relative) * shares) ^ (me - low)) + i
            half = odd if i % 2 else even
            rows.append(jnp.concatenate([half[node >> 1, j] for j in range(groups)], axis=1))
        product = lax.dot_general(
            lhs,
            jnp.concatenate(rows, axis=0),
            (((1,), (1,)), ((), ())),
            preferred_element_type=jnp.float32,
        ).astype(jnp.bfloat16)
        parts = [product[:, i * height : (i + 1) * height] for i in range(shares)]

        def store(flip):
            out[relative] = jnp.concatenate([parts[i ^ flip] for i in range(shares)], axis=1)

        for flip in range(shares):
            pl.when(low == flip)(functools.partial(store, flip))


def feature_rows(index, summed, even, odd):
    groups = len(summed)
    rows, width = summed[0].shape
    return pl.pallas_call(
        feature_kernel,
        in_specs=[IN_SMEM] + [IN_VMEM] * (groups + 2),
        out_specs=IN_VMEM,
        out_shape=bf16(groups, rows, width),
        compiler_params=params(),
        cost_estimate=pl.CostEstimate(
            flops=2 * rows * (groups * width) ** 2,
            bytes_accessed=2 * (groups * width) ** 2 + 4 * groups * rows * width,
            transcendentals=0,
        ),
        name="feature_rows",
    )(index, *summed, even, odd)


def gather_kernel(index, *refs):
    *parts, out, sems = refs
    groups = len(parts) // 2
    sizes = [parts[0].shape[0], out.shape[0] // groups - parts[0].shape[0]]
    copies = []
    for i in range(groups):
        for which, size in enumerate(sizes):
            start = (index[1] ^ i) * sum(sizes) + which * sizes[0]
            copies.append(
                pltpu.make_async_copy(
                    parts[which * groups + i].at[:size],
                    out.at[pl.ds(pl.multiple_of(start, 16), size)],
                    sems.at[which, i],
                )
            )
    for copy in copies:
        copy.start()
    for copy in copies:
        copy.wait()


def laid_out(index, heads, tails, rows):
    groups = len(heads)
    return pl.pallas_call(
        gather_kernel,
        in_specs=[IN_SMEM] + [IN_VMEM] * (2 * groups),
        out_specs=IN_HBM,
        out_shape=bf16(rows, heads[0].shape[1]),
        scratch_shapes=[pltpu.SemaphoreType.DMA((2, groups))],
        compiler_params=params(),
        name="laid_out",
    )(index, *heads, *tails)


def landing_blocks(shuffle_from, me, blocks, devs, slots):
    owner = (shuffle_from // blocks).reshape(devs, blocks)
    within = (shuffle_from % blocks).reshape(devs, blocks)
    for_me = owner == me
    earlier = jnp.arange(blocks)[None, :] < jnp.arange(blocks)[:, None]
    rank = jnp.sum((for_me[:, None, :] & earlier[None]).astype(jnp.int32), axis=2)
    picked = for_me[:, None, :] & (rank[:, None, :] == jnp.arange(slots)[None, :, None])
    return (jnp.sum(jnp.where(picked, within[:, None, :] + 1, 0), axis=2) - 1).reshape(-1)


def exchange_order(groups):
    return sorted(range(1, groups), reverse=True)


def local(
    features,
    weight,
    pre_clean,
    pre_corrupt,
    grad_clean,
    grad_corrupt,
    slopes,
    adj_vals,
    adj_cols,
    adj_count,
    shuffle_from,
):
    row_count = features.shape[0]
    blocks, tile_slots, _, _ = adj_vals.shape
    reach = (tile_slots - 1) // 2
    me = lax.axis_index("node")
    group = lax.axis_index("chan")
    devs = lax.axis_size("node")
    groups = lax.axis_size("chan")
    slots = -(-blocks // devs)
    index = jnp.stack([me, group])

    args = (index, shuffle_from, adj_cols.T, adj_count)
    args += (grad_clean, pre_clean, grad_corrupt, pre_corrupt, slopes[None, :], adj_vals)
    clean, outgoing, down, up, *packed = aggregate(*args, features, weight, reach, devs, groups)
    from_prev = shifted(up, "node", 1)
    from_next = shifted(down, "node", -1)
    for i in exchange_order(groups):
        packed[i] = swapped(packed[i], "chan", i)

    clean, outgoing = patch(index, shuffle_from, clean, outgoing, from_prev, from_next, slots)
    shuffle_from, outgoing = lax.optimization_barrier((shuffle_from, outgoing))
    landing = landing_blocks(shuffle_from, me, blocks, devs, slots)
    incoming = exchanged(outgoing, "node")
    incoming, packed = lax.optimization_barrier((incoming, packed))
    merged = merge(index, landing, clean, incoming, groups)

    quarter = row_count // groups
    summed = [merged[0]] + [None] * (groups - 1)
    for i in exchange_order(groups):
        summed[i] = swapped(merged[i], "chan", i)
    even = jnp.stack([piece[quarter:] for piece in packed])[None]
    for bit in range(1, devs.bit_length() - 1):
        even = jnp.concatenate([even, swapped(even, "node", 1 << bit)], axis=0)
    summed, even = lax.optimization_barrier((summed, even))
    odd = swapped(even, "node", 1)

    keep, send = weight_partial(index, packed, summed, devs)
    odd, send = lax.optimization_barrier((odd, send))
    arrived = swapped(send, "node", 1)
    rows_out = feature_rows(index, summed, even, odd)
    arrived, rows_out = lax.optimization_barrier((arrived, rows_out))

    cut = quarter - quarter // 64 * 16
    heads = [rows_out[0]] + [None] * (groups - 1)
    for i in exchange_order(groups):
        heads[i] = swapped(rows_out[i, :cut], "chan", i)
    total = wide(keep) + wide(arrived)
    share = total[0]
    for i in range(1, devs // 2):
        share = share + wide(swapped(total[i].astype(jnp.bfloat16), "node", 2 * i))
    heads, share = lax.optimization_barrier((heads, share))
    grad_weight = share[0]
    tails = [rows_out[0, cut:]] + [None] * (groups - 1)
    for i in exchange_order(groups):
        tail = jnp.concatenate([rows_out[i, cut:], share[i].astype(jnp.bfloat16)], axis=0)
        tails[i] = swapped(tail, "chan", i)
        grad_weight = grad_weight + wide(tails[i][quarter - cut :])

    heads[0] = rows_out[0, :cut]
    return (grad_weight, laid_out(index, heads, tails, row_count))


def solution(mesh):
    placed = (
        P("node", "chan"),
        P("node", "chan"),
        P("node", "chan"),
        P("node", "chan"),
        P("node", "chan"),
        P("node", "chan"),
        P("chan"),
        P("node", None, None, None),
        P("node", None),
        P("node"),
        P(),
    )
    return jax.shard_map(
        local,
        mesh=mesh,
        in_specs=placed,
        out_specs=(P("node", "chan"), P("node", "chan")),
        check_vma=False,
    )
```

```python
import functools
import math

import jax
import jax.numpy as jnp
from jax import lax
from jax.experimental import pallas as pl
from jax.experimental.pallas import tpu as pltpu
from jax.sharding import PartitionSpec as P

VMEM_LIMIT = 32 * 1024 * 1024
VMEM_ALL = 61 * 1024 * 1024
IN_VMEM = pl.BlockSpec(memory_space=pltpu.VMEM)
IN_SMEM = pl.BlockSpec(memory_space=pltpu.SMEM)
IN_HBM = pl.BlockSpec(memory_space=pltpu.HBM)


def params(limit=VMEM_LIMIT):
    return pltpu.CompilerParams(vmem_limit_bytes=limit)


def bf16(*shape):
    return jax.ShapeDtypeStruct(shape, jnp.bfloat16)


def wide(value):
    return value.astype(jnp.float32)


def shifted(value, axis, by):
    size = lax.axis_size(axis)
    pairs = [(i, i + by) for i in range(size) if 0 <= i + by < size]
    return lax.ppermute(value, axis, pairs)


def swapped(value, axis, by):
    size = lax.axis_size(axis)
    return lax.ppermute(value, axis, [(i, i ^ by) for i in range(size)])


def exchanged(value, axis):
    return lax.all_to_all(value, axis, split_axis=0, concat_axis=0, tiled=True)


def masked_grad(grad, pre, slope):
    return (wide(grad) * jnp.where(wide(pre) > 0, 1.0, slope)).astype(jnp.bfloat16)


def find_places(index, shuffle, blocks, slots, places, used):
    for i in range(used.shape[0]):
        used[i] = 0
    for block in range(blocks):
        owner = shuffle[index[0] * blocks + block] // blocks
        slot = used[owner]
        used[owner] = slot + 1
        places[block] = owner * slots + slot


def aggregate_kernel(
    reach, groups, send_slots, me, shuffle, cols, count, gc, pc, gx, px, slopes, adj, features, weight, *refs
):
    clean, outgoing, down, up, *refs = refs
    packed, refs = refs[:groups], refs[groups:]
    data, tiles, rhs, stage, results, halos, packs, places, used, sems, tile_sems, pack_sems, out_sems = refs
    blocks, slots, rows, _ = adj.shape
    width = gc.shape[1]
    quarter = features.shape[0] // groups
    spare = blocks + 2 * reach
    pad = 2 * reach * rows

    def copies(block):
        span = pl.ds(pl.multiple_of(block * rows, rows), rows)
        return [
            pltpu.make_async_copy(ref.at[span], data.at[i, block], sems.at[i, block])
            for i, ref in enumerate((gc, pc, gx, px))
        ]

    def each_tile(block, act):
        for k in range(slots):
            pl.when(k < count[block])(
                lambda k=k: act(
                    pltpu.make_async_copy(adj.at[block, k], tiles.at[block, k], tile_sems.at[block, k])
                )
            )

    for block in range(blocks):
        for copy in copies(block):
            copy.start()
        each_tile(block, lambda copy: copy.start())
    to_vmem, to_hbm = [], []
    for i in range(groups):
        span = pl.ds(pl.multiple_of((me[1] ^ i) * quarter, quarter), quarter)
        to_vmem.append(
            pltpu.make_async_copy(features.at[span], packs.at[i, :quarter], pack_sems.at[0, i])
        )
        to_vmem.append(pltpu.make_async_copy(weight, packs.at[i, quarter:], pack_sems.at[1, i]))
        to_hbm.append(pltpu.make_async_copy(packs.at[i], packed[i], pack_sems.at[2, i]))
    for copy in to_vmem:
        copy.start()
    stage[...] = jnp.zeros_like(stage)
    rhs[:pad] = jnp.zeros((pad, 2 * width), jnp.bfloat16)
    rhs[pad + blocks * rows :] = jnp.zeros((pad, 2 * width), jnp.bfloat16)
    shape = (rows, rows)
    identity = (
        lax.broadcasted_iota(jnp.int32, shape, 0) == lax.broadcasted_iota(jnp.int32, shape, 1)
    ).astype(jnp.float32).astype(jnp.bfloat16)
    slope = slopes[...]
    find_places(me, shuffle, blocks, send_slots, places, used)

    def take(block):
        gradients = [masked_grad(data[i, block], data[i + 1, block], slope) for i in (0, 2)]
        span = pl.ds(pl.multiple_of(pad + block * rows, rows), rows)
        rhs[span] = jnp.concatenate(gradients, axis=1)
        turned = lax.dot_general(
            identity,
            tiles[block].reshape(slots * rows, rows),
            (((1,), (1,)), ((), ())),
            preferred_element_type=jnp.float32,
        )
        for k in range(slots):
            live = k < count[block]
            target = cols[k, block] - me[0] * blocks
            place = jnp.where(live, target + reach, spare)
            distance = jnp.where(live, block - target + reach, 0)
            part = turned[:, k * rows : (k + 1) * rows]
            stage[place, distance] = (wide(stage[place, distance]) + part).astype(jnp.bfloat16)

    per_step = blocks // 2

    @pl.loop(0, blocks // per_step)
    def _(step):
        for i in range(per_step):
            block = step * per_step + i
            for copy in copies(block):
                copy.wait()
            each_tile(block, lambda copy: copy.wait())
        for i in range(per_step):
            take(step * per_step + i)

    for copy in to_vmem:
        copy.wait()
    for copy in to_hbm:
        copy.start()
    blank = jnp.zeros(shape, jnp.bfloat16)

    def pair(first):
        lhs = jnp.concatenate(
            [
                jnp.concatenate(
                    [blank] * i + [stage[first + i, j] for j in range(2 * reach + 1)] + [blank] * (1 - i),
                    axis=1,
                )
                for i in range(2)
            ],
            axis=0,
        )
        span = pl.ds(pl.multiple_of(first * rows, rows), (2 * reach + 2) * rows)
        product = jnp.dot(lhs, rhs[span], preferred_element_type=jnp.float32)
        product = product.astype(jnp.bfloat16).reshape(2, rows, 2 * width)
        return product[:, :, :width], product[:, :, width:]

    for i in range(0, reach, 2):
        halos[0, 0, i : i + 2], halos[0, 1, i : i + 2] = pair(i)
        halos[1, 0, i : i + 2], halos[1, 1, i : i + 2] = pair(blocks + reach + i)
    writes = [
        pltpu.make_async_copy(halos.at[0], down, out_sems.at[2, 0]),
        pltpu.make_async_copy(halos.at[1], up, out_sems.at[2, 1]),
    ]
    for copy in writes:
        copy.start()
    for first in range(0, blocks, 2):
        span = pl.ds(first, 2)
        results[0, span], results[1, span] = pair(reach + first)
        done = [pltpu.make_async_copy(results.at[0, span], clean.at[span], out_sems.at[0, first])]
        for block in range(first, first + 2):
            target = outgoing.at[places[block]]
            done.append(pltpu.make_async_copy(results.at[1, block], target, out_sems.at[1, block]))
        for copy in done:
            copy.start()
        writes += done
    for copy in writes + to_hbm:
        copy.wait()


def aggregate(index, shuffle, cols, count, gc, pc, gx, px, slopes, adj, features, weight, reach, devs, groups):
    blocks, slots, rows, _ = adj.shape
    width = gc.shape[1]
    send_slots = -(-blocks // devs)
    assert reach % 2 == 0 and blocks % 2 == 0
    packed = features.shape[0] // groups + weight.shape[0]
    return pl.pallas_call(
        functools.partial(aggregate_kernel, reach, groups, send_slots),
        in_specs=[IN_SMEM] * 4 + [IN_HBM] * 4 + [IN_VMEM] + [IN_HBM] * 3,
        out_specs=[IN_HBM] * (4 + groups),
        out_shape=[bf16(blocks, rows, width), bf16(devs * send_slots, rows, width)]
        + [bf16(2, reach, rows, width)] * 2
        + [bf16(packed, width)] * groups,
        scratch_shapes=[
            pltpu.VMEM((4, blocks, rows, width), jnp.bfloat16),
            pltpu.VMEM((blocks, slots, rows, rows), jnp.bfloat16),
            pltpu.VMEM(((blocks + 4 * reach) * rows, 2 * width), jnp.bfloat16),
            pltpu.VMEM((blocks + 2 * reach + 1, 2 * reach + 1, rows, rows), jnp.bfloat16),
            pltpu.VMEM((2, blocks, rows, width), jnp.bfloat16),
            pltpu.VMEM((2, 2, reach, rows, width), jnp.bfloat16),
            pltpu.VMEM((groups, packed, width), jnp.bfloat16),
            pltpu.SMEM((blocks,), jnp.int32),
            pltpu.SMEM((devs,), jnp.int32),
            pltpu.SemaphoreType.DMA((4, blocks)),
            pltpu.SemaphoreType.DMA((blocks, slots)),
            pltpu.SemaphoreType.DMA((3, groups)),
            pltpu.SemaphoreType.DMA((3, blocks)),
        ],
        compiler_params=params(VMEM_ALL),
        cost_estimate=pl.CostEstimate(
            flops=4 * blocks * slots * rows * rows * width,
            bytes_accessed=12 * blocks * rows * width + 2 * blocks * slots * rows * rows,
            transcendentals=0,
        ),
        name="aggregate",
    )(index, shuffle, cols, count, gc, pc, gx, px, slopes, adj, features, weight)


def patch_kernel(reach, slots, index, shuffle, clean, outgoing, low, high, clean_out, outgoing_out, *scratch):
    held, other, ready, places, used, sems = scratch
    blocks = clean.shape[0]
    border = [*range(reach), *range(blocks - reach, blocks)]
    arrivals = [
        pltpu.make_async_copy(low, other.at[0], sems.at[2, 0, 0]),
        pltpu.make_async_copy(high, other.at[1], sems.at[2, 0, 1]),
    ]
    for copy in arrivals:
        copy.start()
    find_places(index, shuffle, blocks, slots, places, used)

    def spot(i, which, first, second):
        return second.at[places[border[i]]] if which else first.at[border[i]]

    order = [(i, which) for i in range(2 * reach) for which in range(2)]
    reads, writes = [], []
    for i, which in order:
        source, target = spot(i, which, clean, outgoing), spot(i, which, clean_out, outgoing_out)
        reads.append(pltpu.make_async_copy(source, held.at[which, i], sems.at[0, which, i]))
        writes.append(pltpu.make_async_copy(ready.at[which, i], target, sems.at[1, which, i]))
    for copy in reads:
        copy.start()
    for copy in arrivals:
        copy.wait()
    for (i, which), read, write in zip(order, reads, writes):
        read.wait()
        total = wide(held[which, i]) + wide(other[i // reach, which, i % reach])
        ready[which, i] = total.astype(jnp.bfloat16)
        write.start()
    for copy in writes:
        copy.wait()


def patch(index, shuffle, clean, outgoing, low, high, slots):
    blocks, rows, width = clean.shape
    reach = low.shape[1]
    blocks_shape = (2, 2 * reach, rows, width)
    return pl.pallas_call(
        functools.partial(patch_kernel, reach, slots),
        in_specs=[IN_SMEM] * 2 + [IN_HBM] * 4,
        out_specs=[IN_HBM] * 2,
        out_shape=[bf16(*clean.shape), bf16(*outgoing.shape)],
        input_output_aliases={2: 0, 3: 1},
        scratch_shapes=[
            pltpu.VMEM(blocks_shape, jnp.bfloat16),
            pltpu.VMEM((2, 2, reach, rows, width), jnp.bfloat16),
            pltpu.VMEM(blocks_shape, jnp.bfloat16),
            pltpu.SMEM((blocks,), jnp.int32),
            pltpu.SMEM((outgoing.shape[0] // slots,), jnp.int32),
            pltpu.SemaphoreType.DMA((3, 2, 2 * reach)),
        ],
        compiler_params=params(VMEM_ALL),
        name="patch",
    )(index, shuffle, clean, outgoing, low, high)


def merge_kernel(quarter, index, landing, clean, incoming, out):
    _, rows, _ = clean.shape
    group = index[1]
    piece = math.gcd(rows, quarter)
    for place in range(incoming.shape[0]):
        block = landing[place]

        @pl.when(block >= 0)
        def _():
            total = (wide(clean[block]) + wide(incoming[place])).astype(jnp.bfloat16)
            for part in range(rows // piece):
                at = block * (rows // piece) + part
                owner = at // (quarter // piece)
                offset = (at - owner * (quarter // piece)) * piece
                out[owner ^ group, pl.ds(pl.multiple_of(offset, piece), piece)] = total[
                    part * piece : (part + 1) * piece
                ]


def merge(index, landing, clean, incoming, groups):
    blocks, rows, width = clean.shape
    quarter = blocks * rows // groups
    return pl.pallas_call(
        functools.partial(merge_kernel, quarter),
        in_specs=[IN_SMEM] * 2 + [IN_VMEM] * 2,
        out_specs=IN_VMEM,
        out_shape=bf16(groups, quarter, width),
        compiler_params=params(),
        name="merge",
    )(index, landing, clean, incoming)


def weight_kernel(devs, index, *refs):
    groups = (len(refs) - 2) // 2
    packed, summed, (keep, send) = refs[:groups], refs[groups : 2 * groups], refs[2 * groups :]
    me, group = index[0], index[1]
    shares = devs // groups
    height, width = keep.shape[2:]
    rhs = jnp.concatenate([piece[...] for piece in summed], axis=1)
    for relative in range(groups):
        product = lax.dot_general(
            packed[relative][: rhs.shape[0]],
            rhs,
            (((0,), (0,)), ((), ())),
            preferred_element_type=jnp.float32,
        ).astype(jnp.bfloat16)
        for share in range(shares):
            node = ((group ^ relative) * shares + share) ^ me
            rows = product[share * height : (share + 1) * height]

            def store(out):
                for i in range(groups):
                    out[node >> 1, i] = rows[:, i * width : (i + 1) * width]

            pl.when((node & 1) == 0)(functools.partial(store, keep))
            pl.when((node & 1) == 1)(functools.partial(store, send))


def weight_partial(index, packed, summed, devs):
    groups = len(packed)
    rows, width = summed[0].shape
    height = groups * width // devs
    return pl.pallas_call(
        functools.partial(weight_kernel, devs),
        in_specs=[IN_SMEM] + [IN_VMEM] * (2 * groups),
        out_specs=[IN_VMEM] * 2,
        out_shape=[bf16(devs // 2, groups, height, width)] * 2,
        compiler_params=params(),
        cost_estimate=pl.CostEstimate(
            flops=2 * rows * (groups * width) ** 2,
            bytes_accessed=2 * (groups * width) ** 2 + 4 * groups * rows * width,
            transcendentals=0,
        ),
        name="weight_partial",
    )(index, *packed, *summed)


def feature_kernel(index, *refs):
    *summed, even, odd, out = refs
    groups = len(summed)
    devs = 2 * even.shape[0]
    me, group = index[0], index[1]
    shares = devs // groups
    height = even.shape[2]
    low = me & (shares - 1)
    lhs = jnp.concatenate([piece[...] for piece in summed], axis=1)
    for relative in range(groups):
        rows = []
        for i in range(shares):
            node = (((group ^ relative) * shares) ^ (me - low)) + i
            half = odd if i % 2 else even
            rows.append(jnp.concatenate([half[node >> 1, j] for j in range(groups)], axis=1))
        product = lax.dot_general(
            lhs,
            jnp.concatenate(rows, axis=0),
            (((1,), (1,)), ((), ())),
            preferred_element_type=jnp.float32,
        ).astype(jnp.bfloat16)
        parts = [product[:, i * height : (i + 1) * height] for i in range(shares)]

        def store(flip):
            out[relative] = jnp.concatenate([parts[i ^ flip] for i in range(shares)], axis=1)

        for flip in range(shares):
            pl.when(low == flip)(functools.partial(store, flip))


def feature_rows(index, summed, even, odd):
    groups = len(summed)
    rows, width = summed[0].shape
    return pl.pallas_call(
        feature_kernel,
        in_specs=[IN_SMEM] + [IN_VMEM] * (groups + 2),
        out_specs=IN_VMEM,
        out_shape=bf16(groups, rows, width),
        compiler_params=params(),
        cost_estimate=pl.CostEstimate(
            flops=2 * rows * (groups * width) ** 2,
            bytes_accessed=2 * (groups * width) ** 2 + 4 * groups * rows * width,
            transcendentals=0,
        ),
        name="feature_rows",
    )(index, *summed, even, odd)


def gather_kernel(index, *refs):
    *parts, out, sems = refs
    groups = len(parts) // 2
    sizes = [parts[0].shape[0], out.shape[0] // groups - parts[0].shape[0]]
    copies = []
    for i in range(groups):
        for which, size in enumerate(sizes):
            start = (index[1] ^ i) * sum(sizes) + which * sizes[0]
            copies.append(
                pltpu.make_async_copy(
                    parts[which * groups + i].at[:size],
                    out.at[pl.ds(pl.multiple_of(start, 16), size)],
                    sems.at[which, i],
                )
            )
    for copy in copies:
        copy.start()
    for copy in copies:
        copy.wait()


def laid_out(index, heads, tails, rows):
    groups = len(heads)
    return pl.pallas_call(
        gather_kernel,
        in_specs=[IN_SMEM] + [IN_VMEM] * (2 * groups),
        out_specs=IN_HBM,
        out_shape=bf16(rows, heads[0].shape[1]),
        scratch_shapes=[pltpu.SemaphoreType.DMA((2, groups))],
        compiler_params=params(),
        name="laid_out",
    )(index, *heads, *tails)


def landing_blocks(shuffle_from, me, blocks, devs, slots):
    owner = (shuffle_from // blocks).reshape(devs, blocks)
    within = (shuffle_from % blocks).reshape(devs, blocks)
    for_me = owner == me
    earlier = jnp.arange(blocks)[None, :] < jnp.arange(blocks)[:, None]
    rank = jnp.sum((for_me[:, None, :] & earlier[None]).astype(jnp.int32), axis=2)
    picked = for_me[:, None, :] & (rank[:, None, :] == jnp.arange(slots)[None, :, None])
    return (jnp.sum(jnp.where(picked, within[:, None, :] + 1, 0), axis=2) - 1).reshape(-1)


def exchange_order(groups):
    return sorted(range(1, groups), reverse=True)


def local(
    features,
    weight,
    pre_clean,
    pre_corrupt,
    grad_clean,
    grad_corrupt,
    slopes,
    adj_vals,
    adj_cols,
    adj_count,
    shuffle_from,
):
    row_count = features.shape[0]
    blocks, tile_slots, _, _ = adj_vals.shape
    reach = (tile_slots - 1) // 2
    me = lax.axis_index("node")
    group = lax.axis_index("chan")
    devs = lax.axis_size("node")
    groups = lax.axis_size("chan")
    slots = -(-blocks // devs)
    index = jnp.stack([me, group])

    args = (index, shuffle_from, adj_cols.T, adj_count)
    args += (grad_clean, pre_clean, grad_corrupt, pre_corrupt, slopes[None, :], adj_vals)
    clean, outgoing, down, up, *packed = aggregate(*args, features, weight, reach, devs, groups)
    from_prev = shifted(up, "node", 1)
    from_next = shifted(down, "node", -1)
    for i in exchange_order(groups):
        packed[i] = swapped(packed[i], "chan", i)

    clean, outgoing = patch(index, shuffle_from, clean, outgoing, from_prev, from_next, slots)
    shuffle_from, outgoing = lax.optimization_barrier((shuffle_from, outgoing))
    landing = landing_blocks(shuffle_from, me, blocks, devs, slots)
    incoming = exchanged(outgoing, "node")
    incoming, packed = lax.optimization_barrier((incoming, packed))
    merged = merge(index, landing, clean, incoming, groups)

    quarter = row_count // groups
    summed = [merged[0]] + [None] * (groups - 1)
    for i in exchange_order(groups):
        summed[i] = swapped(merged[i], "chan", i)
    tiles = jnp.stack([piece[quarter:] for piece in packed])
    even = [tiles] + [swapped(tiles, "node", 2 * i) for i in range(1, devs // 2)]
    early = devs // 2 - 1
    summed, even[:early] = lax.optimization_barrier((summed, even[:early]))
    even = jnp.stack(even)
    odd = swapped(even, "node", 1)

    keep, send = weight_partial(index, packed, summed, devs)
    odd, send = lax.optimization_barrier((odd, send))
    arrived = swapped(send, "node", 1)
    rows_out = feature_rows(index, summed, even, odd)
    arrived, rows_out = lax.optimization_barrier((arrived, rows_out))

    cut = quarter - quarter // 64 * 16
    heads = [rows_out[0]] + [None] * (groups - 1)
    for i in exchange_order(groups):
        heads[i] = swapped(rows_out[i, :cut], "chan", i)
    total = wide(keep) + wide(arrived)
    sums = [
        swapped(total[i].astype(jnp.bfloat16), "node", 2 * i) for i in range(1, devs // 2)
    ]
    heads, sums = lax.optimization_barrier((heads, sums))
    share = total[0]
    for part in sums:
        share = share + wide(part)
    grad_weight = share[0]
    tails = [rows_out[0, cut:]] + [None] * (groups - 1)
    for i in exchange_order(groups):
        tail = jnp.concatenate([rows_out[i, cut:], share[i].astype(jnp.bfloat16)], axis=0)
        tails[i] = swapped(tail, "chan", i)
        grad_weight = grad_weight + wide(tails[i][quarter - cut :])

    heads[0] = rows_out[0, :cut]
    return (grad_weight, laid_out(index, heads, tails, row_count))


def solution(mesh):
    placed = (
        P("node", "chan"),
        P("node", "chan"),
        P("node", "chan"),
        P("node", "chan"),
        P("node", "chan"),
        P("node", "chan"),
        P("chan"),
        P("node", None, None, None),
        P("node", None),
        P("node"),
        P(),
    )
    return jax.shard_map(
        local,
        mesh=mesh,
        in_specs=placed,
        out_specs=(P("node", "chan"), P("node", "chan")),
        check_vma=False,
    )
```

```python
import functools
import math

import jax
import jax.numpy as jnp
from jax import lax
from jax.experimental import pallas as pl
from jax.experimental.pallas import tpu as pltpu
from jax.sharding import PartitionSpec as P

VMEM_LIMIT = 32 * 1024 * 1024
VMEM_ALL = 61 * 1024 * 1024
IN_VMEM = pl.BlockSpec(memory_space=pltpu.VMEM)
IN_SMEM = pl.BlockSpec(memory_space=pltpu.SMEM)
IN_HBM = pl.BlockSpec(memory_space=pltpu.HBM)


def params(limit=VMEM_LIMIT):
    return pltpu.CompilerParams(vmem_limit_bytes=limit)


def bf16(*shape):
    return jax.ShapeDtypeStruct(shape, jnp.bfloat16)


def wide(value):
    return value.astype(jnp.float32)


def shifted(value, axis, by):
    size = lax.axis_size(axis)
    pairs = [(i, i + by) for i in range(size) if 0 <= i + by < size]
    return lax.ppermute(value, axis, pairs)


def swapped(value, axis, by):
    size = lax.axis_size(axis)
    return lax.ppermute(value, axis, [(i, i ^ by) for i in range(size)])


def exchanged(value, axis):
    return lax.all_to_all(value, axis, split_axis=0, concat_axis=0, tiled=True)


def masked_grad(grad, pre, slope):
    return (wide(grad) * jnp.where(wide(pre) > 0, 1.0, slope)).astype(jnp.bfloat16)


def find_places(index, shuffle, blocks, slots, places, used):
    for i in range(used.shape[0]):
        used[i] = 0
    for block in range(blocks):
        owner = shuffle[index[0] * blocks + block] // blocks
        slot = used[owner]
        used[owner] = slot + 1
        places[block] = owner * slots + slot


def identity_of(size):
    shape = (size, size)
    same = lax.broadcasted_iota(jnp.int32, shape, 0) == lax.broadcasted_iota(jnp.int32, shape, 1)
    return same.astype(jnp.float32).astype(jnp.bfloat16)


def both_grads(data, block, slope):
    return jnp.concatenate(
        [masked_grad(data[i, block], data[i + 1, block], slope) for i in (0, 2)], axis=1
    )


def turned_tiles(identity, tiles):
    slots, rows, _ = tiles.shape
    return lax.dot_general(
        identity,
        tiles.reshape(slots * rows, rows),
        (((1,), (1,)), ((), ())),
        preferred_element_type=jnp.float32,
    )


def border_kernel(reach, groups, index, cols, count, gc, pc, gx, px, slopes, adj, features, weight, *refs):
    down, up, *refs = refs
    packed, refs = refs[:groups], refs[groups:]
    data, tiles, rhs, stage, halos, packs, held, sems, tile_sems, pack_sems, out_sems = refs
    blocks, slots, rows, _ = adj.shape
    quarter = features.shape[0] // groups
    height, width = weight.shape
    spare = 2 * reach
    border = [*range(reach), *range(blocks - reach, blocks)]

    def target_of(block, k):
        target = cols[k, block] - index[0] * blocks
        outside = (k < count[block]) & ((target < 0) | (target >= blocks))
        return outside, jnp.where(target < 0, target + reach, target - blocks + reach)

    def each_tile(i, act):
        for k in range(slots):
            copy = pltpu.make_async_copy(adj.at[border[i], k], tiles.at[i, k], tile_sems.at[i, k])
            pl.when(target_of(border[i], k)[0])(functools.partial(act, copy))

    inputs = []
    for i, block in enumerate(border):
        for j, ref in enumerate((gc, pc, gx, px)):
            source = ref.at[block * rows : (block + 1) * rows]
            inputs.append(pltpu.make_async_copy(source, data.at[j, i], sems.at[j, i]))
    for copy in inputs:
        copy.start()
    for i in range(2 * reach):
        each_tile(i, lambda copy: copy.start())
    to_vmem, to_hbm = [pltpu.make_async_copy(weight, held, pack_sems.at[1, 0])], []
    for i in range(groups):
        span = pl.ds(pl.multiple_of((index[1] ^ i) * quarter, quarter), quarter)
        to_vmem.append(
            pltpu.make_async_copy(features.at[span], packs.at[i, :quarter], pack_sems.at[0, i])
        )
        to_hbm.append(pltpu.make_async_copy(packs.at[i], packed[i], pack_sems.at[2, i]))
    for copy in to_vmem:
        copy.start()

    stage[...] = jnp.zeros_like(stage)
    identity = identity_of(rows)
    slope = slopes[...]
    for copy in inputs:
        copy.wait()
    for i in range(2 * reach):
        each_tile(i, lambda copy: copy.wait())
    for i in range(2 * reach):
        rhs[i * rows : (i + 1) * rows] = both_grads(data, i, slope)
        turned = turned_tiles(identity, tiles[i])
        for k in range(slots):
            outside, place = target_of(border[i], k)
            place = jnp.where(outside, place, spare)
            part = turned[:, k * rows : (k + 1) * rows]
            stage[place, i % reach] = (wide(stage[place, i % reach]) + part).astype(jnp.bfloat16)
    writes = []
    for side, out in enumerate((down, up)):
        lhs = jnp.concatenate(
            [
                jnp.concatenate([stage[side * reach + t, j] for j in range(reach)], axis=1)
                for t in range(reach)
            ],
            axis=0,
        )
        span = slice(side * reach * rows, (side + 1) * reach * rows)
        product = jnp.dot(lhs, rhs[span], preferred_element_type=jnp.float32)
        product = product.astype(jnp.bfloat16).reshape(reach, rows, 2 * width)
        halos[side, 0] = product[:, :, :width]
        halos[side, 1] = product[:, :, width:]
        writes.append(pltpu.make_async_copy(halos.at[side], out, out_sems.at[side]))
        writes[-1].start()

    for copy in to_vmem:
        copy.wait()
    turned = wide(held[...]).T.astype(jnp.bfloat16)
    tile = jnp.concatenate(
        [turned[i * height : (i + 1) * height] for i in range(width // height)], axis=1
    )
    for i in range(groups):
        packs[i, quarter:] = tile
        to_hbm[i].start()
    for copy in writes + to_hbm:
        copy.wait()


def border(index, cols, count, gc, pc, gx, px, slopes, adj, features, weight, reach, groups):
    _, slots, rows, _ = adj.shape
    width = gc.shape[1]
    packed = features.shape[0] // groups + weight.shape[0]
    return pl.pallas_call(
        functools.partial(border_kernel, reach, groups),
        in_specs=[IN_SMEM] * 3 + [IN_HBM] * 4 + [IN_VMEM] + [IN_HBM] * 3,
        out_specs=[IN_HBM] * (2 + groups),
        out_shape=[bf16(2, reach, rows, width)] * 2 + [bf16(packed, width)] * groups,
        scratch_shapes=[
            pltpu.VMEM((4, 2 * reach, rows, width), jnp.bfloat16),
            pltpu.VMEM((2 * reach, slots, rows, rows), jnp.bfloat16),
            pltpu.VMEM((2 * reach * rows, 2 * width), jnp.bfloat16),
            pltpu.VMEM((2 * reach + 1, reach, rows, rows), jnp.bfloat16),
            pltpu.VMEM((2, 2, reach, rows, width), jnp.bfloat16),
            pltpu.VMEM((groups, packed, width), jnp.bfloat16),
            pltpu.VMEM(weight.shape, jnp.bfloat16),
            pltpu.SemaphoreType.DMA((4, 2 * reach)),
            pltpu.SemaphoreType.DMA((2 * reach, slots)),
            pltpu.SemaphoreType.DMA((3, groups)),
            pltpu.SemaphoreType.DMA((2,)),
        ],
        compiler_params=params(VMEM_ALL),
        name="border",
    )(index, cols, count, gc, pc, gx, px, slopes, adj, features, weight)


def inner_kernel(
    reach, send_slots, index, shuffle, cols, count, gc, pc, gx, px, slopes, adj, clean, outgoing, *refs
):
    data, tiles, rhs, stage, results, places, used, sems, tile_sems, out_sems = refs
    blocks, slots, rows, _ = adj.shape
    width = gc.shape[1]
    pad = reach * rows

    def copies(block):
        span = pl.ds(pl.multiple_of(block * rows, rows), rows)
        return [
            pltpu.make_async_copy(ref.at[span], data.at[i, block], sems.at[i, block])
            for i, ref in enumerate((gc, pc, gx, px))
        ]

    def each_tile(block, act):
        for k in range(slots):
            copy = pltpu.make_async_copy(adj.at[block, k], tiles.at[block, k], tile_sems.at[block, k])
            pl.when(k < count[block])(functools.partial(act, copy))

    for block in range(blocks):
        for copy in copies(block):
            copy.start()
        each_tile(block, lambda copy: copy.start())
    stage[...] = jnp.zeros_like(stage)
    rhs[:pad] = jnp.zeros((pad, 2 * width), jnp.bfloat16)
    rhs[pad + blocks * rows :] = jnp.zeros((pad, 2 * width), jnp.bfloat16)
    identity = identity_of(rows)
    slope = slopes[...]
    find_places(index, shuffle, blocks, send_slots, places, used)

    def take(block):
        span = pl.ds(pl.multiple_of(pad + block * rows, rows), rows)
        rhs[span] = both_grads(data, block, slope)
        turned = turned_tiles(identity, tiles[block])
        for k in range(slots):
            target = cols[k, block] - index[0] * blocks
            inside = (k < count[block]) & (target >= 0) & (target < blocks)
            place = jnp.where(inside, target, blocks)
            distance = jnp.where(inside, block - target + reach, 0)
            part = turned[:, k * rows : (k + 1) * rows]
            stage[place, distance] = (wide(stage[place, distance]) + part).astype(jnp.bfloat16)

    blank = jnp.zeros((rows, rows), jnp.bfloat16)

    def writes(first):
        span = pl.ds(first, 2)
        out = [pltpu.make_async_copy(results.at[0, span], clean.at[span], out_sems.at[0, first])]
        for i in range(2):
            source, target = results.at[1, first + i], outgoing.at[places[first + i]]
            out.append(pltpu.make_async_copy(source, target, out_sems.at[1, first + i]))
        return out

    def pair(first):
        lhs = jnp.concatenate(
            [
                jnp.concatenate(
                    [blank] * i + [stage[first + i, j] for j in range(2 * reach + 1)] + [blank] * (1 - i),
                    axis=1,
                )
                for i in range(2)
            ],
            axis=0,
        )
        span = pl.ds(pl.multiple_of(first * rows, rows), (2 * reach + 2) * rows)
        product = jnp.dot(lhs, rhs[span], preferred_element_type=jnp.float32)
        product = product.astype(jnp.bfloat16).reshape(2, rows, 2 * width)
        for i in range(2):
            results[0, first + i] = product[i, :, :width]
            results[1, first + i] = product[i, :, width:]
        for copy in writes(first):
            copy.start()

    lag = reach // 2

    @pl.loop(0, blocks // 2)
    def _(step):
        for i in range(2):
            for copy in copies(2 * step + i):
                copy.wait()
            each_tile(2 * step + i, lambda copy: copy.wait())
        for i in range(2):
            take(2 * step + i)

        @pl.when(step >= lag)
        def _():
            pair(2 * (step - lag))

    for i in range(lag):
        pair(blocks - 2 * (lag - i))
    for first in range(0, blocks, 2):
        for copy in writes(first):
            copy.wait()


def inner(index, shuffle, cols, count, gc, pc, gx, px, slopes, adj, reach, devs):
    blocks, slots, rows, _ = adj.shape
    width = gc.shape[1]
    send_slots = -(-blocks // devs)
    assert reach % 2 == 0 and blocks % 2 == 0
    return pl.pallas_call(
        functools.partial(inner_kernel, reach, send_slots),
        in_specs=[IN_SMEM] * 4 + [IN_HBM] * 4 + [IN_VMEM, IN_HBM],
        out_specs=[IN_HBM] * 2,
        out_shape=[bf16(blocks, rows, width), bf16(devs * send_slots, rows, width)],
        scratch_shapes=[
            pltpu.VMEM((4, blocks, rows, width), jnp.bfloat16),
            pltpu.VMEM((blocks, slots, rows, rows), jnp.bfloat16),
            pltpu.VMEM(((blocks + 2 * reach) * rows, 2 * width), jnp.bfloat16),
            pltpu.VMEM((blocks + 1, 2 * reach + 1, rows, rows), jnp.bfloat16),
            pltpu.VMEM((2, blocks, rows, width), jnp.bfloat16),
            pltpu.SMEM((blocks,), jnp.int32),
            pltpu.SMEM((devs,), jnp.int32),
            pltpu.SemaphoreType.DMA((4, blocks)),
            pltpu.SemaphoreType.DMA((blocks, slots)),
            pltpu.SemaphoreType.DMA((2, blocks)),
        ],
        compiler_params=params(VMEM_ALL),
        cost_estimate=pl.CostEstimate(
            flops=4 * blocks * slots * rows * rows * width,
            bytes_accessed=12 * blocks * rows * width + 2 * blocks * slots * rows * rows,
            transcendentals=0,
        ),
        name="inner",
    )(index, shuffle, cols, count, gc, pc, gx, px, slopes, adj)


def patch_kernel(reach, slots, index, shuffle, clean, outgoing, low, high, clean_out, outgoing_out, *scratch):
    held, other, ready, places, used, sems = scratch
    blocks = clean.shape[0]
    border = [*range(reach), *range(blocks - reach, blocks)]
    arrivals = [
        pltpu.make_async_copy(low, other.at[0], sems.at[2, 0, 0]),
        pltpu.make_async_copy(high, other.at[1], sems.at[2, 0, 1]),
    ]
    for copy in arrivals:
        copy.start()
    find_places(index, shuffle, blocks, slots, places, used)

    def spot(i, which, first, second):
        return second.at[places[border[i]]] if which else first.at[border[i]]

    order = [(i, which) for i in range(2 * reach) for which in range(2)]
    reads, writes = [], []
    for i, which in order:
        source, target = spot(i, which, clean, outgoing), spot(i, which, clean_out, outgoing_out)
        reads.append(pltpu.make_async_copy(source, held.at[which, i], sems.at[0, which, i]))
        writes.append(pltpu.make_async_copy(ready.at[which, i], target, sems.at[1, which, i]))
    for copy in reads:
        copy.start()
    for copy in arrivals:
        copy.wait()
    for (i, which), read, write in zip(order, reads, writes):
        read.wait()
        total = wide(held[which, i]) + wide(other[i // reach, which, i % reach])
        ready[which, i] = total.astype(jnp.bfloat16)
        write.start()
    for copy in writes:
        copy.wait()


def patch(index, shuffle, clean, outgoing, low, high, slots):
    blocks, rows, width = clean.shape
    reach = low.shape[1]
    blocks_shape = (2, 2 * reach, rows, width)
    return pl.pallas_call(
        functools.partial(patch_kernel, reach, slots),
        in_specs=[IN_SMEM] * 2 + [IN_HBM] * 4,
        out_specs=[IN_HBM] * 2,
        out_shape=[bf16(*clean.shape), bf16(*outgoing.shape)],
        input_output_aliases={2: 0, 3: 1},
        scratch_shapes=[
            pltpu.VMEM(blocks_shape, jnp.bfloat16),
            pltpu.VMEM((2, 2, reach, rows, width), jnp.bfloat16),
            pltpu.VMEM(blocks_shape, jnp.bfloat16),
            pltpu.SMEM((blocks,), jnp.int32),
            pltpu.SMEM((outgoing.shape[0] // slots,), jnp.int32),
            pltpu.SemaphoreType.DMA((3, 2, 2 * reach)),
        ],
        compiler_params=params(VMEM_ALL),
        name="patch",
    )(index, shuffle, clean, outgoing, low, high)


def slot_of(target, group):
    relative = target ^ group
    return jnp.where(relative < 2, target & 1, relative)


def arrived_piece(pair, others, group, relative):
    return pair[(group & 1) ^ relative] if relative < 2 else others[relative - 2][...]


def merge_kernel(quarter, index, landing, clean, incoming, out):
    _, rows, _ = clean.shape
    group = index[1]
    piece = math.gcd(rows, quarter)
    for place in range(incoming.shape[0]):
        block = landing[place]

        @pl.when(block >= 0)
        def _():
            total = (wide(clean[block]) + wide(incoming[place])).astype(jnp.bfloat16)
            for part in range(rows // piece):
                at = block * (rows // piece) + part
                owner = at // (quarter // piece)
                offset = (at - owner * (quarter // piece)) * piece
                out[slot_of(owner, group), pl.ds(pl.multiple_of(offset, piece), piece)] = total[
                    part * piece : (part + 1) * piece
                ]


def merge(index, landing, clean, incoming, groups):
    blocks, rows, width = clean.shape
    quarter = blocks * rows // groups
    return pl.pallas_call(
        functools.partial(merge_kernel, quarter),
        in_specs=[IN_SMEM] * 2 + [IN_VMEM] * 2,
        out_specs=IN_VMEM,
        out_shape=bf16(groups, quarter, width),
        compiler_params=params(),
        name="merge",
    )(index, landing, clean, incoming)


def weight_kernel(devs, index, *refs):
    groups = len(refs) // 2
    packed, (pair, *others), (keep, send) = refs[:groups], refs[groups:-2], refs[-2:]
    me, group = index[0], index[1]
    shares = devs // groups
    height, width = keep.shape[2:]
    rhs = jnp.concatenate([arrived_piece(pair, others, group, i) for i in range(groups)], axis=1)
    for relative in range(groups):
        product = lax.dot_general(
            packed[relative][: rhs.shape[0]],
            rhs,
            (((0,), (0,)), ((), ())),
            preferred_element_type=jnp.float32,
        ).astype(jnp.bfloat16)
        for share in range(shares):
            node = ((group ^ relative) * shares + share) ^ me
            rows = product[share * height : (share + 1) * height]

            def store(out):
                for i in range(groups):
                    out[node >> 1, i] = rows[:, i * width : (i + 1) * width]

            pl.when((node & 1) == 0)(functools.partial(store, keep))
            pl.when((node & 1) == 1)(functools.partial(store, send))


def weight_partial(index, packed, pair, others, devs):
    groups = len(packed)
    _, rows, width = pair.shape
    height = groups * width // devs
    return pl.pallas_call(
        functools.partial(weight_kernel, devs),
        in_specs=[IN_SMEM] + [IN_VMEM] * (2 * groups - 1),
        out_specs=[IN_VMEM] * 2,
        out_shape=[bf16(devs // 2, groups, height, width)] * 2,
        compiler_params=params(),
        cost_estimate=pl.CostEstimate(
            flops=2 * rows * (groups * width) ** 2,
            bytes_accessed=2 * (groups * width) ** 2 + 4 * groups * rows * width,
            transcendentals=0,
        ),
        name="weight_partial",
    )(index, *packed, pair, *others)


def feature_kernel(index, *refs):
    pair, *others, even, odd, heads, tails = refs
    groups = even.shape[1]
    devs = 2 * even.shape[0]
    me, group = index[0], index[1]
    shares = devs // groups
    height, width = even.shape[2:]
    low = me & (shares - 1)
    cut = heads.shape[1]
    lhs = jnp.concatenate([arrived_piece(pair, others, group, i) for i in range(groups)], axis=1)

    def tile(half, place, i):
        held = half[place, i]
        parts = [held[:, j * height : (j + 1) * height] for j in range(width // height)]
        return jnp.concatenate(parts, axis=0)

    for relative in range(groups):
        columns = []
        for i in range(shares):
            node = (((group ^ relative) * shares) ^ (me - low)) + i
            half = odd if i % 2 else even
            columns.append(jnp.concatenate([tile(half, node >> 1, j) for j in range(groups)], axis=0))
        product = jnp.dot(
            lhs, jnp.concatenate(columns, axis=1), preferred_element_type=jnp.float32
        ).astype(jnp.bfloat16)
        parts = [product[:, i * height : (i + 1) * height] for i in range(shares)]

        def store(flip):
            ordered = jnp.concatenate([parts[i ^ flip] for i in range(shares)], axis=1)
            heads[slot_of(group ^ relative, group)] = ordered[:cut]
            tails[relative] = ordered[cut:]

        for flip in range(shares):
            pl.when(low == flip)(functools.partial(store, flip))


def feature_rows(index, pair, others, even, odd, cut):
    groups = len(others) + 2
    _, rows, width = pair.shape
    return pl.pallas_call(
        feature_kernel,
        in_specs=[IN_SMEM] + [IN_VMEM] * (groups + 1),
        out_specs=[IN_VMEM] * 2,
        out_shape=[bf16(groups, cut, width), bf16(groups, rows - cut, width)],
        compiler_params=params(),
        cost_estimate=pl.CostEstimate(
            flops=2 * rows * (groups * width) ** 2,
            bytes_accessed=2 * (groups * width) ** 2 + 4 * groups * rows * width,
            transcendentals=0,
        ),
        name="feature_rows",
    )(index, pair, *others, even, odd)


def heads_kernel(quarter, index, pair, *refs):
    *others, out, sems = refs
    group = index[1]
    cut = pair.shape[1]
    copies = []
    for i in range(len(others) + 2):
        source = pair.at[i] if i < 2 else others[i - 2]
        owner = (group & ~1) + i if i < 2 else group ^ i
        span = pl.ds(pl.multiple_of(owner * quarter, 16), cut)
        copies.append(pltpu.make_async_copy(source, out.at[span], sems.at[i]))
    for copy in copies:
        copy.start()
    for copy in copies:
        copy.wait()


def place_heads(index, pair, others, rows):
    groups = len(others) + 2
    return pl.pallas_call(
        functools.partial(heads_kernel, rows // groups),
        in_specs=[IN_SMEM] + [IN_VMEM] * (groups - 1),
        out_specs=IN_HBM,
        out_shape=bf16(rows, pair.shape[2]),
        scratch_shapes=[pltpu.SemaphoreType.DMA((groups,))],
        compiler_params=params(),
        name="place_heads",
    )(index, pair, *others)


def tails_kernel(index, head_rows, own, share, *refs):
    *others, out, total, sems = refs
    groups = len(others) + 1
    size = own.shape[0]
    quarter = out.shape[0] // groups
    copies = []
    for i, source in enumerate([own, *others]):
        span = pl.ds(pl.multiple_of((index[1] ^ i) * quarter + quarter - size, 16), size)
        copies.append(pltpu.make_async_copy(source.at[:size], out.at[span], sems.at[i]))
    for copy in copies:
        copy.start()
    sum_of = share[...]
    for other in others:
        sum_of = sum_of + wide(other[size:])
    total[...] = sum_of
    for copy in copies:
        copy.wait()


def place_tails(index, head_rows, own, share, others):
    groups = len(others) + 1
    return pl.pallas_call(
        tails_kernel,
        in_specs=[IN_SMEM, IN_HBM] + [IN_VMEM] * (groups + 1),
        out_specs=[IN_HBM, IN_VMEM],
        out_shape=[bf16(*head_rows.shape), jax.ShapeDtypeStruct(share.shape, jnp.float32)],
        input_output_aliases={1: 0},
        scratch_shapes=[pltpu.SemaphoreType.DMA((groups,))],
        compiler_params=params(),
        name="place_tails",
    )(index, head_rows, own, share, *others)


def landing_blocks(shuffle_from, me, blocks, devs, slots):
    owner = (shuffle_from // blocks).reshape(devs, blocks)
    within = (shuffle_from % blocks).reshape(devs, blocks)
    for_me = owner == me
    earlier = jnp.arange(blocks)[None, :] < jnp.arange(blocks)[:, None]
    rank = jnp.sum((for_me[:, None, :] & earlier[None]).astype(jnp.int32), axis=2)
    picked = for_me[:, None, :] & (rank[:, None, :] == jnp.arange(slots)[None, :, None])
    return (jnp.sum(jnp.where(picked, within[:, None, :] + 1, 0), axis=2) - 1).reshape(-1)


def exchange_order(groups, first):
    return range(groups - 1, first - 1, -1)


def chan_exchanged(value, groups):
    pairs = [[i, i + 1] for i in range(0, groups, 2)]
    others = [None] * (groups - 2)
    for i in exchange_order(groups, 2):
        others[i - 2] = swapped(value[i], "chan", i)
    pair = lax.all_to_all(
        value[:2], "chan", split_axis=0, concat_axis=0, tiled=True, axis_index_groups=pairs
    )
    return pair, others


def local(
    features,
    weight,
    pre_clean,
    pre_corrupt,
    grad_clean,
    grad_corrupt,
    slopes,
    adj_vals,
    adj_cols,
    adj_count,
    shuffle_from,
):
    row_count = features.shape[0]
    blocks, tile_slots, _, _ = adj_vals.shape
    reach = (tile_slots - 1) // 2
    me = lax.axis_index("node")
    group = lax.axis_index("chan")
    devs = lax.axis_size("node")
    groups = lax.axis_size("chan")
    slots = -(-blocks // devs)
    index = jnp.stack([me, group])

    args = (adj_cols.T, adj_count, grad_clean, pre_clean, grad_corrupt, pre_corrupt)
    args += (slopes[None, :], adj_vals)
    down, up, *packed = border(index, *args, features, weight, reach, groups)
    from_prev = shifted(up, "node", 1)
    from_next = shifted(down, "node", -1)
    clean, outgoing = inner(index, shuffle_from, *args, reach, devs)
    for i in exchange_order(groups, 1):
        packed[i] = swapped(packed[i], "chan", i)

    clean, outgoing = patch(index, shuffle_from, clean, outgoing, from_prev, from_next, slots)
    shuffle_from, outgoing = lax.optimization_barrier((shuffle_from, outgoing))
    landing = landing_blocks(shuffle_from, me, blocks, devs, slots)
    incoming = exchanged(outgoing, "node")
    incoming, packed = lax.optimization_barrier((incoming, packed))
    merged = merge(index, landing, clean, incoming, groups)

    quarter = row_count // groups
    pair, others = chan_exchanged(merged, groups)
    tiles = jnp.stack([piece[quarter:] for piece in packed])
    even = [tiles] + [swapped(tiles, "node", 2 * i) for i in range(1, devs // 2)]
    pair, others, even = lax.optimization_barrier((pair, others, even))
    even = jnp.stack(even)
    odd = swapped(even, "node", 1)

    keep, send = weight_partial(index, packed, pair, others, devs)
    odd, send = lax.optimization_barrier((odd, send))
    arrived = swapped(send, "node", 1)
    cut = quarter - quarter // 64 * 16
    heads, tails = feature_rows(index, pair, others, even, odd, cut)
    arrived, heads, tails = lax.optimization_barrier((arrived, heads, tails))
    pair, others = chan_exchanged(heads, groups)
    total = wide(keep) + wide(arrived)
    sums = [
        swapped(total[i].astype(jnp.bfloat16), "node", 2 * i) for i in range(1, devs // 2)
    ]
    pair, others, sums = lax.optimization_barrier((pair, others, sums))
    share = total[0]
    for part in sums:
        share = share + wide(part)
    last = [None] * (groups - 1)
    for i in exchange_order(groups, 1):
        tail = jnp.concatenate([tails[i], share[i].astype(jnp.bfloat16)], axis=0)
        last[i - 1] = swapped(tail, "chan", i)
    head_rows = place_heads(index, pair, others, row_count)
    grad_features, grad_weight = place_tails(index, head_rows, tails[0], share[0], last)
    return (grad_weight, grad_features)


def solution(mesh):
    placed = (
        P("node", "chan"),
        P("node", "chan"),
        P("node", "chan"),
        P("node", "chan"),
        P("node", "chan"),
        P("node", "chan"),
        P("chan"),
        P("node", None, None, None),
        P("node", None),
        P("node"),
        P(),
    )
    return jax.shard_map(
        local,
        mesh=mesh,
        in_specs=placed,
        out_specs=(P("node", "chan"), P("node", "chan")),
        check_vma=False,
    )
```

```python
import functools
import math

import jax
import jax.numpy as jnp
from jax import lax
from jax.experimental import pallas as pl
from jax.experimental.pallas import tpu as pltpu
from jax.sharding import PartitionSpec as P

VMEM_LIMIT = 32 * 1024 * 1024
VMEM_ALL = 61 * 1024 * 1024
VMEM_MOST = 52 * 1024 * 1024
IN_VMEM = pl.BlockSpec(memory_space=pltpu.VMEM)
IN_SMEM = pl.BlockSpec(memory_space=pltpu.SMEM)
IN_HBM = pl.BlockSpec(memory_space=pltpu.HBM)


def params(limit=VMEM_LIMIT):
    return pltpu.CompilerParams(vmem_limit_bytes=limit)


def bf16(*shape):
    return jax.ShapeDtypeStruct(shape, jnp.bfloat16)


def wide(value):
    return value.astype(jnp.float32)


def shifted(value, axis, by):
    size = lax.axis_size(axis)
    pairs = [(i, i + by) for i in range(size) if 0 <= i + by < size]
    return lax.ppermute(value, axis, pairs)


def swapped(value, axis, by):
    size = lax.axis_size(axis)
    return lax.ppermute(value, axis, [(i, i ^ by) for i in range(size)])


def exchanged(value, axis):
    return lax.all_to_all(value, axis, split_axis=0, concat_axis=0, tiled=True)


def masked_grad(grad, pre, slope):
    return (wide(grad) * jnp.where(wide(pre) > 0, 1.0, slope)).astype(jnp.bfloat16)


def find_places(index, shuffle, blocks, slots, places, used):
    for i in range(used.shape[0]):
        used[i] = 0
    for block in range(blocks):
        owner = shuffle[index[0] * blocks + block] // blocks
        slot = used[owner]
        used[owner] = slot + 1
        places[block] = owner * slots + slot


def aggregate_kernel(
    reach, groups, send_slots, me, shuffle, cols, count, gc, pc, gx, px, slopes, adj, features, weight, *refs
):
    clean, outgoing, down, up, *refs = refs
    packed, refs = refs[:groups], refs[groups:]
    data, tiles, rhs, stage, results, halos, packs, places, used, sems, pack_sems, out_sems = refs
    blocks, slots, rows, _ = adj.shape
    width = gc.shape[1]
    quarter = features.shape[0] // groups
    spare = blocks + 2 * reach
    pad = 2 * reach * rows

    def copies(step):
        span = slice(2 * step, 2 * step + 2)
        out = [
            pltpu.make_async_copy(
                ref.at[2 * step * rows : (2 * step + 2) * rows], data.at[i, step], sems.at[i, step]
            )
            for i, ref in enumerate((gc, pc, gx, px))
        ]
        return out + [pltpu.make_async_copy(adj.at[span], tiles.at[span], sems.at[4, step])]

    inputs = [copies(step) for step in range(blocks // 2)]
    for copy in sum(inputs, []):
        copy.start()
    to_vmem, to_hbm = [], []
    for i in range(groups):
        span = pl.ds(pl.multiple_of((me[1] ^ i) * quarter, quarter), quarter)
        to_vmem.append(
            pltpu.make_async_copy(features.at[span], packs.at[i, :quarter], pack_sems.at[0, i])
        )
        to_vmem.append(pltpu.make_async_copy(weight, packs.at[i, quarter:], pack_sems.at[1, i]))
        to_hbm.append(pltpu.make_async_copy(packs.at[i], packed[i], pack_sems.at[2, i]))
    for copy in to_vmem:
        copy.start()
    stage[...] = jnp.zeros_like(stage)
    rhs[:pad] = jnp.zeros((pad, 2 * width), jnp.bfloat16)
    rhs[pad + blocks * rows :] = jnp.zeros((pad, 2 * width), jnp.bfloat16)
    shape = (rows, rows)
    identity = (
        lax.broadcasted_iota(jnp.int32, shape, 0) == lax.broadcasted_iota(jnp.int32, shape, 1)
    ).astype(jnp.float32).astype(jnp.bfloat16)
    slope = slopes[...]
    find_places(me, shuffle, blocks, send_slots, places, used)

    def take(step):
        gradients = [masked_grad(data[i, step], data[i + 1, step], slope) for i in (0, 2)]
        rhs[pad + 2 * step * rows : pad + (2 * step + 2) * rows] = jnp.concatenate(gradients, axis=1)
        turned = lax.dot_general(
            identity,
            tiles[2 * step : 2 * step + 2].reshape(2 * slots * rows, rows),
            (((1,), (1,)), ((), ())),
            preferred_element_type=jnp.float32,
        )
        for i in range(2 * slots):
            block, k = 2 * step + i // slots, i % slots
            live = k < count[block]
            target = cols[k, block] - me[0] * blocks
            place = jnp.where(live, target + reach, spare)
            distance = jnp.where(live, block - target + reach, 0)
            part = turned[:, i * rows : (i + 1) * rows]
            stage[place, distance] = (wide(stage[place, distance]) + part).astype(jnp.bfloat16)

    blank = jnp.zeros(shape, jnp.bfloat16)

    def pair(first):
        lhs = jnp.concatenate(
            [
                jnp.concatenate(
                    [blank] * i + [stage[first + i, j] for j in range(2 * reach + 1)] + [blank] * (1 - i),
                    axis=1,
                )
                for i in range(2)
            ],
            axis=0,
        )
        span = slice(first * rows, (first + 2 * reach + 2) * rows)
        product = jnp.dot(lhs, rhs[span], preferred_element_type=jnp.float32)
        product = product.astype(jnp.bfloat16).reshape(2, rows, 2 * width)
        return product[:, :, :width], product[:, :, width:]

    writes = []

    def finish(first):
        block = first - reach
        if 0 <= block < blocks:
            span = slice(block, block + 2)
            results[0, span], results[1, span] = pair(first)
            done = [pltpu.make_async_copy(results.at[0, span], clean.at[span], out_sems.at[0, block])]
            for i in range(block, block + 2):
                target = outgoing.at[places[i]]
                done.append(pltpu.make_async_copy(results.at[1, i], target, out_sems.at[1, i]))
        else:
            side, at = int(block >= 0), first % (blocks + reach)
            halos[side, 0, at : at + 2], halos[side, 1, at : at + 2] = pair(first)
            out = (down, up)[side]
            done = []
            for i in range(2):
                source, target = halos.at[side, i, at : at + 2], out.at[i, at : at + 2]
                done.append(pltpu.make_async_copy(source, target, out_sems.at[2 + i, first]))
        for copy in done:
            copy.start()
        writes.extend(done)

    for step in range(blocks // 2):
        for copy in inputs[step]:
            copy.wait()
        take(step)
        finish(2 * step)
    for copy in to_vmem:
        copy.wait()
    for copy in to_hbm:
        copy.start()
    for first in range(blocks, blocks + 2 * reach, 2):
        finish(first)
    for copy in writes + to_hbm:
        copy.wait()


def aggregate(index, shuffle, cols, count, gc, pc, gx, px, slopes, adj, features, weight, reach, devs, groups):
    blocks, slots, rows, _ = adj.shape
    width = gc.shape[1]
    send_slots = -(-blocks // devs)
    assert reach % 2 == 0 and blocks % 2 == 0
    packed = features.shape[0] // groups + weight.shape[0]
    return pl.pallas_call(
        functools.partial(aggregate_kernel, reach, groups, send_slots),
        in_specs=[IN_SMEM] * 4 + [IN_HBM] * 4 + [IN_VMEM] + [IN_HBM] * 3,
        out_specs=[IN_HBM] * (4 + groups),
        out_shape=[bf16(blocks, rows, width), bf16(devs * send_slots, rows, width)]
        + [bf16(2, reach, rows, width)] * 2
        + [bf16(packed, width)] * groups,
        scratch_shapes=[
            pltpu.VMEM((4, blocks // 2, 2 * rows, width), jnp.bfloat16),
            pltpu.VMEM((blocks, slots, rows, rows), jnp.bfloat16),
            pltpu.VMEM(((blocks + 4 * reach) * rows, 2 * width), jnp.bfloat16),
            pltpu.VMEM((blocks + 2 * reach + 1, 2 * reach + 1, rows, rows), jnp.bfloat16),
            pltpu.VMEM((2, blocks, rows, width), jnp.bfloat16),
            pltpu.VMEM((2, 2, reach, rows, width), jnp.bfloat16),
            pltpu.VMEM((groups, packed, width), jnp.bfloat16),
            pltpu.SMEM((blocks,), jnp.int32),
            pltpu.SMEM((devs,), jnp.int32),
            pltpu.SemaphoreType.DMA((5, blocks // 2)),
            pltpu.SemaphoreType.DMA((3, groups)),
            pltpu.SemaphoreType.DMA((4, blocks + 2 * reach)),
        ],
        compiler_params=params(VMEM_ALL),
        cost_estimate=pl.CostEstimate(
            flops=4 * blocks * slots * rows * rows * width,
            bytes_accessed=12 * blocks * rows * width + 2 * blocks * slots * rows * rows,
            transcendentals=0,
        ),
        name="aggregate",
    )(index, shuffle, cols, count, gc, pc, gx, px, slopes, adj, features, weight)


def patch_kernel(reach, blocks, slots, index, shuffle, outgoing, low, high, out, held, ready, places, used, sems):
    find_places(index, shuffle, blocks, slots, places, used)
    border = [*range(reach), *range(blocks - reach, blocks)]
    reads, writes = [], []
    for i, block in enumerate(border):
        place = places[block]
        reads.append(pltpu.make_async_copy(outgoing.at[place], held.at[i], sems.at[0, i]))
        writes.append(pltpu.make_async_copy(ready.at[i], out.at[place], sems.at[1, i]))
    for copy in reads:
        copy.start()
    for i, (read, write) in enumerate(zip(reads, writes)):
        read.wait()
        other = low[1, i] if i < reach else high[1, i - reach]
        ready[i] = (wide(held[i]) + wide(other)).astype(jnp.bfloat16)
        write.start()
    for copy in writes:
        copy.wait()


def patch(index, shuffle, outgoing, low, high, blocks, slots):
    sent, rows, width = outgoing.shape
    reach = low.shape[1]
    border = pltpu.VMEM((2 * reach, rows, width), jnp.bfloat16)
    return pl.pallas_call(
        functools.partial(patch_kernel, reach, blocks, slots),
        in_specs=[IN_SMEM] * 2 + [IN_HBM] + [IN_VMEM] * 2,
        out_specs=IN_HBM,
        out_shape=bf16(*outgoing.shape),
        input_output_aliases={2: 0},
        scratch_shapes=[
            border,
            border,
            pltpu.SMEM((blocks,), jnp.int32),
            pltpu.SMEM((sent // slots,), jnp.int32),
            pltpu.SemaphoreType.DMA((2, 2 * reach)),
        ],
        compiler_params=params(VMEM_MOST),
        name="patch",
    )(index, shuffle, outgoing, low, high)


def merge_kernel(quarter, index, landing, clean, low, high, incoming, out, whole):
    blocks, rows, _ = clean.shape
    reach = low.shape[1]
    group = index[1]
    piece = math.gcd(rows, quarter)
    for block in range(blocks):
        whole[block] = wide(clean[block])
    for i in range(reach):
        whole[i] += wide(low[0, i])
        whole[blocks - reach + i] += wide(high[0, i])
    for place in range(incoming.shape[0]):
        block = landing[place]

        @pl.when(block >= 0)
        def _():
            total = (whole[block] + wide(incoming[place])).astype(jnp.bfloat16)
            for part in range(rows // piece):
                at = block * (rows // piece) + part
                owner = at // (quarter // piece)
                offset = (at - owner * (quarter // piece)) * piece
                out[owner ^ group, pl.ds(pl.multiple_of(offset, piece), piece)] = total[
                    part * piece : (part + 1) * piece
                ]


def merge(index, landing, clean, low, high, incoming, groups):
    blocks, rows, width = clean.shape
    quarter = blocks * rows // groups
    return pl.pallas_call(
        functools.partial(merge_kernel, quarter),
        in_specs=[IN_SMEM] * 2 + [IN_VMEM] * 4,
        out_specs=IN_VMEM,
        out_shape=bf16(groups, quarter, width),
        scratch_shapes=[pltpu.VMEM((blocks, rows, width), jnp.float32)],
        compiler_params=params(),
        name="merge",
    )(index, landing, clean, low, high, incoming)


def weight_kernel(devs, index, *refs):
    groups = (len(refs) - 2) // 2
    packed, summed, (keep, send) = refs[:groups], refs[groups : 2 * groups], refs[2 * groups :]
    me, group = index[0], index[1]
    shares = devs // groups
    height, width = keep.shape[2:]
    rhs = jnp.concatenate([piece[...] for piece in summed], axis=1)
    for relative in range(groups):
        product = lax.dot_general(
            packed[relative][: rhs.shape[0]],
            rhs,
            (((0,), (0,)), ((), ())),
            preferred_element_type=jnp.float32,
        ).astype(jnp.bfloat16)
        for share in range(shares):
            node = ((group ^ relative) * shares + share) ^ me
            rows = product[share * height : (share + 1) * height]

            def store(out):
                for i in range(groups):
                    out[node >> 1, i] = rows[:, i * width : (i + 1) * width]

            pl.when((node & 1) == 0)(functools.partial(store, keep))
            pl.when((node & 1) == 1)(functools.partial(store, send))


def weight_partial(index, packed, summed, devs):
    groups = len(packed)
    rows, width = summed[0].shape
    height = groups * width // devs
    return pl.pallas_call(
        functools.partial(weight_kernel, devs),
        in_specs=[IN_SMEM] + [IN_VMEM] * (2 * groups),
        out_specs=[IN_VMEM] * 2,
        out_shape=[bf16(devs // 2, groups, height, width)] * 2,
        compiler_params=params(),
        cost_estimate=pl.CostEstimate(
            flops=2 * rows * (groups * width) ** 2,
            bytes_accessed=2 * (groups * width) ** 2 + 4 * groups * rows * width,
            transcendentals=0,
        ),
        name="weight_partial",
    )(index, *packed, *summed)


def feature_kernel(index, *refs):
    *summed, even, odd, out = refs
    groups = len(summed)
    devs = 2 * even.shape[0]
    me, group = index[0], index[1]
    shares = devs // groups
    height = even.shape[2]
    low = me & (shares - 1)
    lhs = jnp.concatenate([piece[...] for piece in summed], axis=1)
    for relative in range(groups):
        rows = []
        for i in range(shares):
            node = (((group ^ relative) * shares) ^ (me - low)) + i
            half = odd if i % 2 else even
            rows.append(jnp.concatenate([half[node >> 1, j] for j in range(groups)], axis=1))
        product = lax.dot_general(
            lhs,
            jnp.concatenate(rows, axis=0),
            (((1,), (1,)), ((), ())),
            preferred_element_type=jnp.float32,
        ).astype(jnp.bfloat16)
        parts = [product[:, i * height : (i + 1) * height] for i in range(shares)]

        def store(flip):
            out[relative] = jnp.concatenate([parts[i ^ flip] for i in range(shares)], axis=1)

        for flip in range(shares):
            pl.when(low == flip)(functools.partial(store, flip))


def feature_rows(index, summed, even, odd):
    groups = len(summed)
    rows, width = summed[0].shape
    return pl.pallas_call(
        feature_kernel,
        in_specs=[IN_SMEM] + [IN_VMEM] * (groups + 2),
        out_specs=IN_VMEM,
        out_shape=bf16(groups, rows, width),
        compiler_params=params(),
        cost_estimate=pl.CostEstimate(
            flops=2 * rows * (groups * width) ** 2,
            bytes_accessed=2 * (groups * width) ** 2 + 4 * groups * rows * width,
            transcendentals=0,
        ),
        name="feature_rows",
    )(index, *summed, even, odd)


def gather_kernel(index, *refs):
    *parts, out, sems = refs
    groups = len(parts) // 2
    sizes = [parts[0].shape[0], out.shape[0] // groups - parts[0].shape[0]]
    copies = []
    for i in range(groups):
        for which, size in enumerate(sizes):
            start = (index[1] ^ i) * sum(sizes) + which * sizes[0]
            copies.append(
                pltpu.make_async_copy(
                    parts[which * groups + i].at[:size],
                    out.at[pl.ds(pl.multiple_of(start, 16), size)],
                    sems.at[which, i],
                )
            )
    for copy in copies:
        copy.start()
    for copy in copies:
        copy.wait()


def laid_out(index, heads, tails, rows):
    groups = len(heads)
    return pl.pallas_call(
        gather_kernel,
        in_specs=[IN_SMEM] + [IN_VMEM] * (2 * groups),
        out_specs=IN_HBM,
        out_shape=bf16(rows, heads[0].shape[1]),
        scratch_shapes=[pltpu.SemaphoreType.DMA((2, groups))],
        compiler_params=params(),
        name="laid_out",
    )(index, *heads, *tails)


def landing_blocks(shuffle_from, me, blocks, devs, slots):
    owner = (shuffle_from // blocks).reshape(devs, blocks)
    within = (shuffle_from % blocks).reshape(devs, blocks)
    for_me = owner == me
    earlier = jnp.arange(blocks)[None, :] < jnp.arange(blocks)[:, None]
    rank = jnp.sum((for_me[:, None, :] & earlier[None]).astype(jnp.int32), axis=2)
    picked = for_me[:, None, :] & (rank[:, None, :] == jnp.arange(slots)[None, :, None])
    return (jnp.sum(jnp.where(picked, within[:, None, :] + 1, 0), axis=2) - 1).reshape(-1)


def exchange_order(groups):
    return sorted(range(1, groups), reverse=True)


def local(
    features,
    weight,
    pre_clean,
    pre_corrupt,
    grad_clean,
    grad_corrupt,
    slopes,
    adj_vals,
    adj_cols,
    adj_count,
    shuffle_from,
):
    row_count = features.shape[0]
    blocks, tile_slots, _, _ = adj_vals.shape
    reach = (tile_slots - 1) // 2
    me = lax.axis_index("node")
    group = lax.axis_index("chan")
    devs = lax.axis_size("node")
    groups = lax.axis_size("chan")
    slots = -(-blocks // devs)
    index = jnp.stack([me, group])

    args = (index, shuffle_from, adj_cols.T, adj_count)
    args += (grad_clean, pre_clean, grad_corrupt, pre_corrupt, slopes[None, :], adj_vals)
    clean, outgoing, down, up, *packed = aggregate(*args, features, weight, reach, devs, groups)
    from_prev = shifted(up, "node", 1)
    from_next = shifted(down, "node", -1)
    for i in exchange_order(groups):
        packed[i] = swapped(packed[i], "chan", i)

    outgoing = patch(index, shuffle_from, outgoing, from_prev, from_next, blocks, slots)
    shuffle_from, outgoing = lax.optimization_barrier((shuffle_from, outgoing))
    landing = landing_blocks(shuffle_from, me, blocks, devs, slots)
    incoming = exchanged(outgoing, "node")
    incoming, packed = lax.optimization_barrier((incoming, packed))
    merged = merge(index, landing, clean, from_prev, from_next, incoming, groups)

    quarter = row_count // groups
    summed = [merged[0]] + [None] * (groups - 1)
    for i in [1, *exchange_order(groups)[:-1]]:
        summed[i] = swapped(merged[i], "chan", i)
    tiles = jnp.stack([piece[quarter:] for piece in packed])
    even = [tiles] + [swapped(tiles, "node", 2 * i) for i in range(1, devs // 2)]
    early = devs // 2 - 1
    rest, even[:early] = lax.optimization_barrier((summed[::-1], even[:early]))
    summed = rest[::-1]
    even = jnp.stack(even)
    odd = swapped(even, "node", 1)

    keep, send = weight_partial(index, packed, summed, devs)
    odd, send = lax.optimization_barrier((odd, send))
    arrived = swapped(send, "node", 1)
    rows_out = feature_rows(index, summed, even, odd)
    arrived, rows_out = lax.optimization_barrier((arrived, rows_out))

    cut = quarter - quarter // 64 * 16
    heads = [rows_out[0]] + [None] * (groups - 1)
    for i in exchange_order(groups):
        heads[i] = swapped(rows_out[i, :cut], "chan", i)
    total = wide(keep) + wide(arrived)
    sums = [
        swapped(total[i].astype(jnp.bfloat16), "node", 2 * i) for i in range(1, devs // 2)
    ]
    heads, sums = lax.optimization_barrier((heads, sums))
    share = total[0]
    for part in sums:
        share = share + wide(part)
    grad_weight = share[0]
    tails = [rows_out[0, cut:]] + [None] * (groups - 1)
    for i in exchange_order(groups):
        tail = jnp.concatenate([rows_out[i, cut:], share[i].astype(jnp.bfloat16)], axis=0)
        tails[i] = swapped(tail, "chan", i)
        grad_weight = grad_weight + wide(tails[i][quarter - cut :])

    heads[0] = rows_out[0, :cut]
    return (grad_weight, laid_out(index, heads, tails, row_count))


def solution(mesh):
    placed = (
        P("node", "chan"),
        P("node", "chan"),
        P("node", "chan"),
        P("node", "chan"),
        P("node", "chan"),
        P("node", "chan"),
        P("chan"),
        P("node", None, None, None),
        P("node", None),
        P("node"),
        P(),
    )
    return jax.shard_map(
        local,
        mesh=mesh,
        in_specs=placed,
        out_specs=(P("node", "chan"), P("node", "chan")),
        check_vma=False,
    )
```

```python
import functools
import math

import jax
import jax.numpy as jnp
from jax import lax
from jax.experimental import pallas as pl
from jax.experimental.pallas import tpu as pltpu
from jax.sharding import PartitionSpec as P

VMEM_LIMIT = 32 * 1024 * 1024
VMEM_ALL = 61 * 1024 * 1024
VMEM_MOST = 52 * 1024 * 1024
IN_VMEM = pl.BlockSpec(memory_space=pltpu.VMEM)
IN_SMEM = pl.BlockSpec(memory_space=pltpu.SMEM)
IN_HBM = pl.BlockSpec(memory_space=pltpu.HBM)


def params(limit=VMEM_LIMIT):
    return pltpu.CompilerParams(vmem_limit_bytes=limit)


def bf16(*shape):
    return jax.ShapeDtypeStruct(shape, jnp.bfloat16)


def wide(value):
    return value.astype(jnp.float32)


def shifted(value, axis, by):
    size = lax.axis_size(axis)
    pairs = [(i, i + by) for i in range(size) if 0 <= i + by < size]
    return lax.ppermute(value, axis, pairs)


def swapped(value, axis, by):
    size = lax.axis_size(axis)
    return lax.ppermute(value, axis, [(i, i ^ by) for i in range(size)])


def exchanged(value, axis):
    return lax.all_to_all(value, axis, split_axis=0, concat_axis=0, tiled=True)


def masked_grad(grad, pre, slope):
    return jnp.where(pre > 0, grad, (wide(grad) * slope).astype(jnp.bfloat16))


def find_places(index, shuffle, blocks, slots, places, used):
    for i in range(used.shape[0]):
        used[i] = 0
    for block in range(blocks):
        owner = shuffle[index[0] * blocks + block] // blocks
        slot = used[owner]
        used[owner] = slot + 1
        places[block] = owner * slots + slot


def aggregate_kernel(
    reach, groups, send_slots, me, shuffle, cols, count, gc, pc, gx, px, slopes, adj, features, weight, *refs
):
    clean, outgoing, down, up, *refs = refs
    packed, refs = refs[:groups], refs[groups:]
    data, tiles, rhs, stage, results, halos, packs, places, used, sems, pack_sems, out_sems = refs
    blocks, slots, rows, _ = adj.shape
    width = gc.shape[1]
    quarter = features.shape[0] // groups
    spare = blocks + 2 * reach
    pad = 2 * reach * rows

    def copies(step):
        span = slice(2 * step, 2 * step + 2)
        out = [
            pltpu.make_async_copy(
                ref.at[2 * step * rows : (2 * step + 2) * rows], data.at[i, step], sems.at[i, step]
            )
            for i, ref in enumerate((gc, pc, gx, px))
        ]
        return out + [pltpu.make_async_copy(adj.at[span], tiles.at[span], sems.at[4, step])]

    inputs = [copies(step) for step in range(blocks // 2)]
    for copy in sum(inputs, []):
        copy.start()
    to_vmem, to_hbm = [], []
    for i in range(groups):
        span = pl.ds(pl.multiple_of((me[1] ^ i) * quarter, quarter), quarter)
        to_vmem.append(
            pltpu.make_async_copy(features.at[span], packs.at[i, :quarter], pack_sems.at[0, i])
        )
        to_vmem.append(pltpu.make_async_copy(weight, packs.at[i, quarter:], pack_sems.at[1, i]))
        to_hbm.append(pltpu.make_async_copy(packs.at[i], packed[i], pack_sems.at[2, i]))
    for copy in to_vmem:
        copy.start()
    stage[...] = jnp.zeros_like(stage)
    rhs[:pad] = jnp.zeros((pad, 2 * width), jnp.bfloat16)
    rhs[pad + blocks * rows :] = jnp.zeros((pad, 2 * width), jnp.bfloat16)
    shape = (rows, rows)
    identity = (
        lax.broadcasted_iota(jnp.int32, shape, 0) == lax.broadcasted_iota(jnp.int32, shape, 1)
    ).astype(jnp.float32).astype(jnp.bfloat16)
    slope = slopes[...]
    find_places(me, shuffle, blocks, send_slots, places, used)

    def take(step):
        gradients = [masked_grad(data[i, step], data[i + 1, step], slope) for i in (0, 2)]
        rhs[pad + 2 * step * rows : pad + (2 * step + 2) * rows] = jnp.concatenate(gradients, axis=1)
        turned = lax.dot_general(
            identity,
            tiles[2 * step : 2 * step + 2].reshape(2 * slots * rows, rows),
            (((1,), (1,)), ((), ())),
            preferred_element_type=jnp.float32,
        )
        for i in range(2 * slots):
            block, k = 2 * step + i // slots, i % slots
            live = k < count[block]
            target = cols[k, block] - me[0] * blocks
            place = jnp.where(live, target + reach, spare)
            distance = jnp.where(live, block - target + reach, 0)
            part = turned[:, i * rows : (i + 1) * rows]
            stage[place, distance] = (wide(stage[place, distance]) + part).astype(jnp.bfloat16)

    blank = jnp.zeros(shape, jnp.bfloat16)

    def pair(first):
        lhs = jnp.concatenate(
            [
                jnp.concatenate(
                    [blank] * i + [stage[first + i, j] for j in range(2 * reach + 1)] + [blank] * (1 - i),
                    axis=1,
                )
                for i in range(2)
            ],
            axis=0,
        )
        span = slice(first * rows, (first + 2 * reach + 2) * rows)
        product = jnp.dot(lhs, rhs[span], preferred_element_type=jnp.float32)
        product = product.astype(jnp.bfloat16).reshape(2, rows, 2 * width)
        return product[:, :, :width], product[:, :, width:]

    writes = []

    def finish(first):
        block = first - reach
        if 0 <= block < blocks:
            span = slice(block, block + 2)
            results[0, span], results[1, span] = pair(first)
            done = [pltpu.make_async_copy(results.at[0, span], clean.at[span], out_sems.at[0, block])]
            for i in range(block, block + 2):
                target = outgoing.at[places[i]]
                done.append(pltpu.make_async_copy(results.at[1, i], target, out_sems.at[1, i]))
        else:
            side, at = int(block >= 0), first % (blocks + reach)
            halos[side, 0, at : at + 2], halos[side, 1, at : at + 2] = pair(first)
            out = (down, up)[side]
            done = []
            for i in range(2):
                source, target = halos.at[side, i, at : at + 2], out.at[i, at : at + 2]
                done.append(pltpu.make_async_copy(source, target, out_sems.at[2 + i, first]))
        for copy in done:
            copy.start()
        writes.extend(done)

    for step in range(blocks // 2):
        for copy in inputs[step]:
            copy.wait()
        take(step)
        finish(2 * step)
    for copy in to_vmem:
        copy.wait()
    for copy in to_hbm:
        copy.start()
    for first in range(blocks, blocks + 2 * reach, 2):
        finish(first)
    for copy in writes + to_hbm:
        copy.wait()


def aggregate(index, shuffle, cols, count, gc, pc, gx, px, slopes, adj, features, weight, reach, devs, groups):
    blocks, slots, rows, _ = adj.shape
    width = gc.shape[1]
    send_slots = -(-blocks // devs)
    assert reach % 2 == 0 and blocks % 2 == 0
    packed = features.shape[0] // groups + weight.shape[0]
    return pl.pallas_call(
        functools.partial(aggregate_kernel, reach, groups, send_slots),
        in_specs=[IN_SMEM] * 4 + [IN_HBM] * 4 + [IN_VMEM] + [IN_HBM] * 3,
        out_specs=[IN_HBM] * (4 + groups),
        out_shape=[bf16(blocks, rows, width), bf16(devs * send_slots, rows, width)]
        + [bf16(2, reach, rows, width)] * 2
        + [bf16(packed, width)] * groups,
        scratch_shapes=[
            pltpu.VMEM((4, blocks // 2, 2 * rows, width), jnp.bfloat16),
            pltpu.VMEM((blocks, slots, rows, rows), jnp.bfloat16),
            pltpu.VMEM(((blocks + 4 * reach) * rows, 2 * width), jnp.bfloat16),
            pltpu.VMEM((blocks + 2 * reach + 1, 2 * reach + 1, rows, rows), jnp.bfloat16),
            pltpu.VMEM((2, blocks, rows, width), jnp.bfloat16),
            pltpu.VMEM((2, 2, reach, rows, width), jnp.bfloat16),
            pltpu.VMEM((groups, packed, width), jnp.bfloat16),
            pltpu.SMEM((blocks,), jnp.int32),
            pltpu.SMEM((devs,), jnp.int32),
            pltpu.SemaphoreType.DMA((5, blocks // 2)),
            pltpu.SemaphoreType.DMA((3, groups)),
            pltpu.SemaphoreType.DMA((4, blocks + 2 * reach)),
        ],
        compiler_params=params(VMEM_ALL),
        cost_estimate=pl.CostEstimate(
            flops=4 * blocks * slots * rows * rows * width,
            bytes_accessed=12 * blocks * rows * width + 2 * blocks * slots * rows * rows,
            transcendentals=0,
        ),
        name="aggregate",
    )(index, shuffle, cols, count, gc, pc, gx, px, slopes, adj, features, weight)


def patch_kernel(reach, blocks, slots, index, shuffle, outgoing, low, high, out, held, ready, places, used, sems):
    find_places(index, shuffle, blocks, slots, places, used)
    border = [*range(reach), *range(blocks - reach, blocks)]
    reads, writes = [], []
    for i, block in enumerate(border):
        place = places[block]
        reads.append(pltpu.make_async_copy(outgoing.at[place], held.at[i], sems.at[0, i]))
        writes.append(pltpu.make_async_copy(ready.at[i], out.at[place], sems.at[1, i]))
    for copy in reads:
        copy.start()
    for i, (read, write) in enumerate(zip(reads, writes)):
        read.wait()
        other = low[1, i] if i < reach else high[1, i - reach]
        ready[i] = (wide(held[i]) + wide(other)).astype(jnp.bfloat16)
        write.start()
    for copy in writes:
        copy.wait()


def patch(index, shuffle, outgoing, low, high, blocks, slots):
    sent, rows, width = outgoing.shape
    reach = low.shape[1]
    border = pltpu.VMEM((2 * reach, rows, width), jnp.bfloat16)
    return pl.pallas_call(
        functools.partial(patch_kernel, reach, blocks, slots),
        in_specs=[IN_SMEM] * 2 + [IN_HBM] + [IN_VMEM] * 2,
        out_specs=IN_HBM,
        out_shape=bf16(*outgoing.shape),
        input_output_aliases={2: 0},
        scratch_shapes=[
            border,
            border,
            pltpu.SMEM((blocks,), jnp.int32),
            pltpu.SMEM((sent // slots,), jnp.int32),
            pltpu.SemaphoreType.DMA((2, 2 * reach)),
        ],
        compiler_params=params(VMEM_MOST),
        name="patch",
    )(index, shuffle, outgoing, low, high)


def merge_kernel(quarter, index, landing, clean, low, high, incoming, out, whole):
    blocks, rows, _ = clean.shape
    reach = low.shape[1]
    group = index[1]
    piece = math.gcd(rows, quarter)
    for block in range(blocks):
        whole[block] = wide(clean[block])
    for i in range(reach):
        whole[i] += wide(low[0, i])
        whole[blocks - reach + i] += wide(high[0, i])
    for place in range(incoming.shape[0]):
        block = landing[place]

        @pl.when(block >= 0)
        def _():
            total = (whole[block] + wide(incoming[place])).astype(jnp.bfloat16)
            for part in range(rows // piece):
                at = block * (rows // piece) + part
                owner = at // (quarter // piece)
                offset = (at - owner * (quarter // piece)) * piece
                out[owner ^ group, pl.ds(pl.multiple_of(offset, piece), piece)] = total[
                    part * piece : (part + 1) * piece
                ]


def merge(index, landing, clean, low, high, incoming, groups):
    blocks, rows, width = clean.shape
    quarter = blocks * rows // groups
    return pl.pallas_call(
        functools.partial(merge_kernel, quarter),
        in_specs=[IN_SMEM] * 2 + [IN_VMEM] * 4,
        out_specs=IN_VMEM,
        out_shape=bf16(groups, quarter, width),
        scratch_shapes=[pltpu.VMEM((blocks, rows, width), jnp.float32)],
        compiler_params=params(),
        name="merge",
    )(index, landing, clean, low, high, incoming)


def weight_kernel(devs, index, *refs):
    groups = (len(refs) - 2) // 2
    packed, summed, (keep, send) = refs[:groups], refs[groups : 2 * groups], refs[2 * groups :]
    me, group = index[0], index[1]
    shares = devs // groups
    height, width = keep.shape[2:]
    rhs = jnp.concatenate([piece[...] for piece in summed], axis=1)
    for relative in range(groups):
        product = lax.dot_general(
            packed[relative][: rhs.shape[0]],
            rhs,
            (((0,), (0,)), ((), ())),
            preferred_element_type=jnp.float32,
        ).astype(jnp.bfloat16)
        for share in range(shares):
            node = ((group ^ relative) * shares + share) ^ me
            rows = product[share * height : (share + 1) * height]

            def store(out):
                for i in range(groups):
                    out[node >> 1, i] = rows[:, i * width : (i + 1) * width]

            pl.when((node & 1) == 0)(functools.partial(store, keep))
            pl.when((node & 1) == 1)(functools.partial(store, send))


def weight_partial(index, packed, summed, devs):
    groups = len(packed)
    rows, width = summed[0].shape
    height = groups * width // devs
    return pl.pallas_call(
        functools.partial(weight_kernel, devs),
        in_specs=[IN_SMEM] + [IN_VMEM] * (2 * groups),
        out_specs=[IN_VMEM] * 2,
        out_shape=[bf16(devs // 2, groups, height, width)] * 2,
        compiler_params=params(),
        cost_estimate=pl.CostEstimate(
            flops=2 * rows * (groups * width) ** 2,
            bytes_accessed=2 * (groups * width) ** 2 + 4 * groups * rows * width,
            transcendentals=0,
        ),
        name="weight_partial",
    )(index, *packed, *summed)


def feature_kernel(index, *refs):
    *summed, even, odd, out = refs
    groups = len(summed)
    devs = 2 * even.shape[0]
    me, group = index[0], index[1]
    shares = devs // groups
    height = even.shape[2]
    low = me & (shares - 1)
    lhs = jnp.concatenate([piece[...] for piece in summed], axis=1)
    for relative in range(groups):
        rows = []
        for i in range(shares):
            node = (((group ^ relative) * shares) ^ (me - low)) + i
            half = odd if i % 2 else even
            rows.append(jnp.concatenate([half[node >> 1, j] for j in range(groups)], axis=1))
        product = lax.dot_general(
            lhs,
            jnp.concatenate(rows, axis=0),
            (((1,), (1,)), ((), ())),
            preferred_element_type=jnp.float32,
        ).astype(jnp.bfloat16)
        parts = [product[:, i * height : (i + 1) * height] for i in range(shares)]

        def store(flip):
            out[relative] = jnp.concatenate([parts[i ^ flip] for i in range(shares)], axis=1)

        for flip in range(shares):
            pl.when(low == flip)(functools.partial(store, flip))


def feature_rows(index, summed, even, odd):
    groups = len(summed)
    rows, width = summed[0].shape
    return pl.pallas_call(
        feature_kernel,
        in_specs=[IN_SMEM] + [IN_VMEM] * (groups + 2),
        out_specs=IN_VMEM,
        out_shape=bf16(groups, rows, width),
        compiler_params=params(),
        cost_estimate=pl.CostEstimate(
            flops=2 * rows * (groups * width) ** 2,
            bytes_accessed=2 * (groups * width) ** 2 + 4 * groups * rows * width,
            transcendentals=0,
        ),
        name="feature_rows",
    )(index, *summed, even, odd)


def gather_kernel(index, *refs):
    *pieces, out, sems = refs
    rows = pieces[0].shape[0]
    copies = [
        pltpu.make_async_copy(
            piece, out.at[pl.ds(pl.multiple_of((index[1] ^ i) * rows, rows), rows)], sems.at[i]
        )
        for i, piece in enumerate(pieces)
    ]
    for copy in copies:
        copy.start()
    for copy in copies:
        copy.wait()


def laid_out(index, pieces):
    rows, width = pieces[0].shape
    return pl.pallas_call(
        gather_kernel,
        in_specs=[IN_SMEM] + [IN_VMEM] * len(pieces),
        out_specs=IN_HBM,
        out_shape=bf16(len(pieces) * rows, width),
        scratch_shapes=[pltpu.SemaphoreType.DMA((len(pieces),))],
        compiler_params=params(),
        name="laid_out",
    )(index, *pieces)


def landing_blocks(shuffle_from, me, blocks, devs, slots):
    owner = (shuffle_from // blocks).reshape(devs, blocks)
    within = (shuffle_from % blocks).reshape(devs, blocks)
    for_me = owner == me
    earlier = jnp.arange(blocks)[None, :] < jnp.arange(blocks)[:, None]
    rank = jnp.sum((for_me[:, None, :] & earlier[None]).astype(jnp.int32), axis=2)
    picked = for_me[:, None, :] & (rank[:, None, :] == jnp.arange(slots)[None, :, None])
    return (jnp.sum(jnp.where(picked, within[:, None, :] + 1, 0), axis=2) - 1).reshape(-1)


def exchange_order(groups):
    return sorted(range(1, groups), reverse=True)


def local(
    features,
    weight,
    pre_clean,
    pre_corrupt,
    grad_clean,
    grad_corrupt,
    slopes,
    adj_vals,
    adj_cols,
    adj_count,
    shuffle_from,
):
    row_count = features.shape[0]
    blocks, tile_slots, _, _ = adj_vals.shape
    reach = (tile_slots - 1) // 2
    me = lax.axis_index("node")
    group = lax.axis_index("chan")
    devs = lax.axis_size("node")
    groups = lax.axis_size("chan")
    slots = -(-blocks // devs)
    index = jnp.stack([me, group])

    args = (index, shuffle_from, adj_cols.T, adj_count)
    args += (grad_clean, pre_clean, grad_corrupt, pre_corrupt, slopes[None, :], adj_vals)
    clean, outgoing, down, up, *packed = aggregate(*args, features, weight, reach, devs, groups)
    from_prev = shifted(up, "node", 1)
    from_next = shifted(down, "node", -1)
    for i in exchange_order(groups):
        packed[i] = swapped(packed[i], "chan", i)

    outgoing = patch(index, shuffle_from, outgoing, from_prev, from_next, blocks, slots)
    shuffle_from, outgoing, clean = lax.optimization_barrier((shuffle_from, outgoing, clean))
    landing = landing_blocks(shuffle_from, me, blocks, devs, slots)
    incoming = exchanged(outgoing, "node")
    incoming, packed = lax.optimization_barrier((incoming, packed))
    merged = merge(index, landing, clean, from_prev, from_next, incoming, groups)

    quarter = row_count // groups
    summed = [merged[0]] + [None] * (groups - 1)
    for i in [1, *exchange_order(groups)[:-1]]:
        summed[i] = swapped(merged[i], "chan", i)
    tiles = jnp.stack([piece[quarter:] for piece in packed])
    even = [tiles] + [swapped(tiles, "node", 2 * i) for i in range(1, devs // 2)]
    summed, even = lax.optimization_barrier((summed, even))
    even = jnp.stack(even)
    odd = swapped(even, "node", 1)

    keep, send = weight_partial(index, packed, summed, devs)
    odd, send = lax.optimization_barrier((odd, send))
    arrived = swapped(send, "node", 1)
    rows_out = feature_rows(index, summed, even, odd)
    arrived, rows_out = lax.optimization_barrier((arrived, rows_out))

    pieces = [rows_out[0]] + [None] * (groups - 1)
    for i in exchange_order(groups):
        pieces[i] = swapped(rows_out[i], "chan", i)
    total = wide(keep) + wide(arrived)
    share = total[0]
    for i in range(1, devs // 2):
        share = share + wide(swapped(total[i].astype(jnp.bfloat16), "node", 2 * i))
    grad_weight = share[0]
    for i in range(1, groups):
        grad_weight = grad_weight + wide(swapped(share[i].astype(jnp.bfloat16), "chan", i))
    return (grad_weight, laid_out(index, pieces))


def solution(mesh):
    placed = (
        P("node", "chan"),
        P("node", "chan"),
        P("node", "chan"),
        P("node", "chan"),
        P("node", "chan"),
        P("node", "chan"),
        P("chan"),
        P("node", None, None, None),
        P("node", None),
        P("node"),
        P(),
    )
    return jax.shard_map(
        local,
        mesh=mesh,
        in_specs=placed,
        out_specs=(P("node", "chan"), P("node", "chan")),
        check_vma=False,
    )
```

```python
import functools
import math

import jax
import jax.numpy as jnp
from jax import lax
from jax.experimental import pallas as pl
from jax.experimental.pallas import tpu as pltpu
from jax.sharding import PartitionSpec as P

VMEM_LIMIT = 32 * 1024 * 1024
VMEM_ALL = 61 * 1024 * 1024
VMEM_MOST = 52 * 1024 * 1024
IN_VMEM = pl.BlockSpec(memory_space=pltpu.VMEM)
IN_SMEM = pl.BlockSpec(memory_space=pltpu.SMEM)
IN_HBM = pl.BlockSpec(memory_space=pltpu.HBM)


def params(limit=VMEM_LIMIT):
    return pltpu.CompilerParams(vmem_limit_bytes=limit)


def bf16(*shape):
    return jax.ShapeDtypeStruct(shape, jnp.bfloat16)


def wide(value):
    return value.astype(jnp.float32)


def shifted(value, axis, by):
    size = lax.axis_size(axis)
    pairs = [(i, i + by) for i in range(size) if 0 <= i + by < size]
    return lax.ppermute(value, axis, pairs)


def swapped(value, axis, by):
    size = lax.axis_size(axis)
    return lax.ppermute(value, axis, [(i, i ^ by) for i in range(size)])


def exchanged(value, axis):
    return lax.all_to_all(value, axis, split_axis=0, concat_axis=0, tiled=True)


def masked_grad(grad, pre, slope):
    return jnp.where(pre > 0, grad, (wide(grad) * slope).astype(jnp.bfloat16))


def find_places(index, shuffle, blocks, slots, places, used):
    for i in range(used.shape[0]):
        used[i] = 0
    for block in range(blocks):
        owner = shuffle[index[0] * blocks + block] // blocks
        slot = used[owner]
        used[owner] = slot + 1
        places[block] = owner * slots + slot


def aggregate_kernel(
    reach, groups, send_slots, me, shuffle, cols, count, gc, pc, gx, px, slopes, adj, features, weight, *refs
):
    clean, outgoing, *refs = refs
    sides, packed, refs = refs[:4], refs[4 : 4 + groups], refs[4 + groups :]
    data, tiles, rhs, stage, results, halos, packs, places, used, sems, pack_sems, out_sems = refs
    blocks, slots, rows, _ = adj.shape
    width = gc.shape[1]
    quarter = features.shape[0] // groups
    spare = blocks + 2 * reach
    pad = 2 * reach * rows

    def copies(step):
        span = slice(2 * step, 2 * step + 2)
        out = [
            pltpu.make_async_copy(
                ref.at[2 * step * rows : (2 * step + 2) * rows], data.at[i, step], sems.at[i, step]
            )
            for i, ref in enumerate((gc, pc, gx, px))
        ]
        return out + [pltpu.make_async_copy(adj.at[span], tiles.at[span], sems.at[4, step])]

    inputs = [copies(step) for step in range(blocks // 2)]
    for copy in sum(inputs, []):
        copy.start()
    to_vmem, to_hbm = [], []
    for i in range(groups):
        span = pl.ds(pl.multiple_of((me[1] ^ i) * quarter, quarter), quarter)
        to_vmem.append(
            pltpu.make_async_copy(features.at[span], packs.at[i, :quarter], pack_sems.at[0, i])
        )
        to_vmem.append(pltpu.make_async_copy(weight, packs.at[i, quarter:], pack_sems.at[1, i]))
        to_hbm.append(pltpu.make_async_copy(packs.at[i], packed[i], pack_sems.at[2, i]))
    for copy in to_vmem:
        copy.start()
    stage[...] = jnp.zeros_like(stage)
    rhs[:pad] = jnp.zeros((pad, 2 * width), jnp.bfloat16)
    rhs[pad + blocks * rows :] = jnp.zeros((pad, 2 * width), jnp.bfloat16)
    shape = (rows, rows)
    identity = (
        lax.broadcasted_iota(jnp.int32, shape, 0) == lax.broadcasted_iota(jnp.int32, shape, 1)
    ).astype(jnp.float32).astype(jnp.bfloat16)
    slope = slopes[...]
    find_places(me, shuffle, blocks, send_slots, places, used)

    def take(step):
        gradients = [masked_grad(data[i, step], data[i + 1, step], slope) for i in (0, 2)]
        rhs[pad + 2 * step * rows : pad + (2 * step + 2) * rows] = jnp.concatenate(gradients, axis=1)
        turned = lax.dot_general(
            identity,
            tiles[2 * step : 2 * step + 2].reshape(2 * slots * rows, rows),
            (((1,), (1,)), ((), ())),
            preferred_element_type=jnp.float32,
        )
        for i in range(2 * slots):
            block, k = 2 * step + i // slots, i % slots
            live = k < count[block]
            target = cols[k, block] - me[0] * blocks
            place = jnp.where(live, target + reach, spare)
            distance = jnp.where(live, block - target + reach, 0)
            part = turned[:, i * rows : (i + 1) * rows]
            stage[place, distance] = (wide(stage[place, distance]) + part).astype(jnp.bfloat16)

    blank = jnp.zeros(shape, jnp.bfloat16)

    def pair(first):
        lhs = jnp.concatenate(
            [
                jnp.concatenate(
                    [blank] * i + [stage[first + i, j] for j in range(2 * reach + 1)] + [blank] * (1 - i),
                    axis=1,
                )
                for i in range(2)
            ],
            axis=0,
        )
        span = slice(first * rows, (first + 2 * reach + 2) * rows)
        product = jnp.dot(lhs, rhs[span], preferred_element_type=jnp.float32)
        product = product.astype(jnp.bfloat16).reshape(2, rows, 2 * width)
        return product[:, :, :width], product[:, :, width:]

    writes = []

    def finish(first):
        block = first - reach
        if 0 <= block < blocks:
            span = slice(block, block + 2)
            results[0, span], results[1, span] = pair(first)
            done = [pltpu.make_async_copy(results.at[0, span], clean.at[span], out_sems.at[0, block])]
            for i in range(block, block + 2):
                target = outgoing.at[places[i]]
                done.append(pltpu.make_async_copy(results.at[1, i], target, out_sems.at[1, i]))
        else:
            side, at = int(block >= 0), first % (blocks + reach)
            halos[side, 0, at : at + 2], halos[side, 1, at : at + 2] = pair(first)
            done = []
            for i in range(2):
                source, target = halos.at[side, i, at : at + 2], sides[2 * i + side].at[at : at + 2]
                done.append(pltpu.make_async_copy(source, target, out_sems.at[2 + i, first]))
        for copy in done:
            copy.start()
        writes.extend(done)

    for step in range(blocks // 2):
        for copy in inputs[step]:
            copy.wait()
        if step:
            finish(2 * step - 2)
        take(step)
    for copy in to_vmem:
        copy.wait()
    for copy in to_hbm:
        copy.start()
    for first in range(blocks + 2 * reach - 2, blocks - 4, -2):
        finish(first)
    for copy in writes + to_hbm:
        copy.wait()


def aggregate(index, shuffle, cols, count, gc, pc, gx, px, slopes, adj, features, weight, reach, devs, groups):
    blocks, slots, rows, _ = adj.shape
    width = gc.shape[1]
    send_slots = -(-blocks // devs)
    assert reach % 2 == 0 and blocks % 2 == 0
    packed = features.shape[0] // groups + weight.shape[0]
    return pl.pallas_call(
        functools.partial(aggregate_kernel, reach, groups, send_slots),
        in_specs=[IN_SMEM] * 4 + [IN_HBM] * 4 + [IN_VMEM] + [IN_HBM] * 3,
        out_specs=[IN_HBM] * (6 + groups),
        out_shape=[bf16(blocks, rows, width), bf16(devs * send_slots, rows, width)]
        + [bf16(reach, rows, width)] * 4
        + [bf16(packed, width)] * groups,
        scratch_shapes=[
            pltpu.VMEM((4, blocks // 2, 2 * rows, width), jnp.bfloat16),
            pltpu.VMEM((blocks, slots, rows, rows), jnp.bfloat16),
            pltpu.VMEM(((blocks + 4 * reach) * rows, 2 * width), jnp.bfloat16),
            pltpu.VMEM((blocks + 2 * reach + 1, 2 * reach + 1, rows, rows), jnp.bfloat16),
            pltpu.VMEM((2, blocks, rows, width), jnp.bfloat16),
            pltpu.VMEM((2, 2, reach, rows, width), jnp.bfloat16),
            pltpu.VMEM((groups, packed, width), jnp.bfloat16),
            pltpu.SMEM((blocks,), jnp.int32),
            pltpu.SMEM((devs,), jnp.int32),
            pltpu.SemaphoreType.DMA((5, blocks // 2)),
            pltpu.SemaphoreType.DMA((3, groups)),
            pltpu.SemaphoreType.DMA((4, blocks + 2 * reach)),
        ],
        compiler_params=params(VMEM_ALL),
        cost_estimate=pl.CostEstimate(
            flops=4 * blocks * slots * rows * rows * width,
            bytes_accessed=12 * blocks * rows * width + 2 * blocks * slots * rows * rows,
            transcendentals=0,
        ),
        name="aggregate",
    )(index, shuffle, cols, count, gc, pc, gx, px, slopes, adj, features, weight)


def patch_kernel(reach, blocks, slots, index, shuffle, outgoing, low, high, out, held, ready, places, used, sems):
    find_places(index, shuffle, blocks, slots, places, used)
    border = [*range(reach), *range(blocks - reach, blocks)]
    reads, writes = [], []
    for i, block in enumerate(border):
        place = places[block]
        reads.append(pltpu.make_async_copy(outgoing.at[place], held.at[i], sems.at[0, i]))
        writes.append(pltpu.make_async_copy(ready.at[i], out.at[place], sems.at[1, i]))
    for copy in reads:
        copy.start()
    for i, (read, write) in enumerate(zip(reads, writes)):
        read.wait()
        other = low[i] if i < reach else high[i - reach]
        ready[i] = (wide(held[i]) + wide(other)).astype(jnp.bfloat16)
        write.start()
    for copy in writes:
        copy.wait()


def patch(index, shuffle, outgoing, low, high, blocks, slots):
    sent, rows, width = outgoing.shape
    reach = low.shape[0]
    border = pltpu.VMEM((2 * reach, rows, width), jnp.bfloat16)
    return pl.pallas_call(
        functools.partial(patch_kernel, reach, blocks, slots),
        in_specs=[IN_SMEM] * 2 + [IN_HBM] + [IN_VMEM] * 2,
        out_specs=IN_HBM,
        out_shape=bf16(*outgoing.shape),
        input_output_aliases={2: 0},
        scratch_shapes=[
            border,
            border,
            pltpu.SMEM((blocks,), jnp.int32),
            pltpu.SMEM((sent // slots,), jnp.int32),
            pltpu.SemaphoreType.DMA((2, 2 * reach)),
        ],
        compiler_params=params(VMEM_MOST),
        name="patch",
    )(index, shuffle, outgoing, low, high)


def merge_kernel(quarter, index, landing, clean, low, high, incoming, out, whole):
    blocks, rows, _ = clean.shape
    reach = low.shape[0]
    group = index[1]
    piece = math.gcd(rows, quarter)
    for block in range(blocks):
        whole[block] = wide(clean[block])
    for i in range(reach):
        whole[i] += wide(low[i])
        whole[blocks - reach + i] += wide(high[i])
    for place in range(incoming.shape[0]):
        block = landing[place]

        @pl.when(block >= 0)
        def _():
            total = (whole[block] + wide(incoming[place])).astype(jnp.bfloat16)
            for part in range(rows // piece):
                at = block * (rows // piece) + part
                owner = at // (quarter // piece)
                offset = (at - owner * (quarter // piece)) * piece
                out[owner ^ group, pl.ds(pl.multiple_of(offset, piece), piece)] = total[
                    part * piece : (part + 1) * piece
                ]


def merge(index, landing, clean, low, high, incoming, groups):
    blocks, rows, width = clean.shape
    quarter = blocks * rows // groups
    return pl.pallas_call(
        functools.partial(merge_kernel, quarter),
        in_specs=[IN_SMEM] * 2 + [IN_VMEM] * 4,
        out_specs=IN_VMEM,
        out_shape=bf16(groups, quarter, width),
        scratch_shapes=[pltpu.VMEM((blocks, rows, width), jnp.float32)],
        compiler_params=params(),
        name="merge",
    )(index, landing, clean, low, high, incoming)


def weight_kernel(devs, index, *refs):
    groups = (len(refs) - 2) // 2
    packed, summed, (keep, send) = refs[:groups], refs[groups : 2 * groups], refs[2 * groups :]
    me, group = index[0], index[1]
    shares = devs // groups
    height, width = keep.shape[2:]
    rhs = jnp.concatenate([piece[...] for piece in summed], axis=1)
    for relative in range(groups):
        product = lax.dot_general(
            packed[relative][: rhs.shape[0]],
            rhs,
            (((0,), (0,)), ((), ())),
            preferred_element_type=jnp.float32,
        ).astype(jnp.bfloat16)
        for share in range(shares):
            node = ((group ^ relative) * shares + share) ^ me
            rows = product[share * height : (share + 1) * height]

            def store(out):
                for i in range(groups):
                    out[node >> 1, i] = rows[:, i * width : (i + 1) * width]

            pl.when((node & 1) == 0)(functools.partial(store, keep))
            pl.when((node & 1) == 1)(functools.partial(store, send))


def weight_partial(index, packed, summed, devs):
    groups = len(packed)
    rows, width = summed[0].shape
    height = groups * width // devs
    return pl.pallas_call(
        functools.partial(weight_kernel, devs),
        in_specs=[IN_SMEM] + [IN_VMEM] * (2 * groups),
        out_specs=[IN_VMEM] * 2,
        out_shape=[bf16(devs // 2, groups, height, width)] * 2,
        compiler_params=params(),
        cost_estimate=pl.CostEstimate(
            flops=2 * rows * (groups * width) ** 2,
            bytes_accessed=2 * (groups * width) ** 2 + 4 * groups * rows * width,
            transcendentals=0,
        ),
        name="weight_partial",
    )(index, *packed, *summed)


def feature_kernel(index, *refs):
    *summed, even, odd, out = refs
    groups = len(summed)
    devs = 2 * even.shape[0]
    me, group = index[0], index[1]
    shares = devs // groups
    height = even.shape[2]
    low = me & (shares - 1)
    lhs = jnp.concatenate([piece[...] for piece in summed], axis=1)
    for relative in range(groups):
        rows = []
        for i in range(shares):
            node = (((group ^ relative) * shares) ^ (me - low)) + i
            half = odd if i % 2 else even
            rows.append(jnp.concatenate([half[node >> 1, j] for j in range(groups)], axis=1))
        product = lax.dot_general(
            lhs,
            jnp.concatenate(rows, axis=0),
            (((1,), (1,)), ((), ())),
            preferred_element_type=jnp.float32,
        ).astype(jnp.bfloat16)
        parts = [product[:, i * height : (i + 1) * height] for i in range(shares)]

        def store(flip):
            out[relative] = jnp.concatenate([parts[i ^ flip] for i in range(shares)], axis=1)

        for flip in range(shares):
            pl.when(low == flip)(functools.partial(store, flip))


def feature_rows(index, summed, even, odd):
    groups = len(summed)
    rows, width = summed[0].shape
    return pl.pallas_call(
        feature_kernel,
        in_specs=[IN_SMEM] + [IN_VMEM] * (groups + 2),
        out_specs=IN_VMEM,
        out_shape=bf16(groups, rows, width),
        compiler_params=params(),
        cost_estimate=pl.CostEstimate(
            flops=2 * rows * (groups * width) ** 2,
            bytes_accessed=2 * (groups * width) ** 2 + 4 * groups * rows * width,
            transcendentals=0,
        ),
        name="feature_rows",
    )(index, *summed, even, odd)


def finish_kernel(index, share, *refs):
    *refs, out, total, sems = refs
    groups = (len(refs) + 1) // 2
    pieces, others = refs[:groups], refs[groups:]
    rows = pieces[0].shape[0]
    copies = [
        pltpu.make_async_copy(
            piece, out.at[pl.ds(pl.multiple_of((index[1] ^ i) * rows, rows), rows)], sems.at[i]
        )
        for i, piece in enumerate(pieces)
    ]
    for copy in copies:
        copy.start()
    sum_of = share[...]
    for other in others:
        sum_of = sum_of + wide(other[...])
    total[...] = sum_of
    for copy in copies:
        copy.wait()


def finish(index, pieces, share, others):
    rows, width = pieces[0].shape
    return pl.pallas_call(
        finish_kernel,
        in_specs=[IN_SMEM] + [IN_VMEM] * (2 * len(pieces)),
        out_specs=[IN_HBM, IN_VMEM],
        out_shape=[
            bf16(len(pieces) * rows, width),
            jax.ShapeDtypeStruct(share.shape, jnp.float32),
        ],
        scratch_shapes=[pltpu.SemaphoreType.DMA((len(pieces),))],
        compiler_params=params(),
        name="finish",
    )(index, share, *pieces, *others)


def landing_blocks(shuffle_from, me, blocks, devs, slots):
    owner = (shuffle_from // blocks).reshape(devs, blocks)
    within = (shuffle_from % blocks).reshape(devs, blocks)
    for_me = owner == me
    earlier = jnp.arange(blocks)[None, :] < jnp.arange(blocks)[:, None]
    rank = jnp.sum((for_me[:, None, :] & earlier[None]).astype(jnp.int32), axis=2)
    picked = for_me[:, None, :] & (rank[:, None, :] == jnp.arange(slots)[None, :, None])
    return (jnp.sum(jnp.where(picked, within[:, None, :] + 1, 0), axis=2) - 1).reshape(-1)


def exchange_order(groups):
    return sorted(range(1, groups), reverse=True)


def local(
    features,
    weight,
    pre_clean,
    pre_corrupt,
    grad_clean,
    grad_corrupt,
    slopes,
    adj_vals,
    adj_cols,
    adj_count,
    shuffle_from,
):
    row_count = features.shape[0]
    blocks, tile_slots, _, _ = adj_vals.shape
    reach = (tile_slots - 1) // 2
    me = lax.axis_index("node")
    group = lax.axis_index("chan")
    devs = lax.axis_size("node")
    groups = lax.axis_size("chan")
    slots = -(-blocks // devs)
    index = jnp.stack([me, group])

    args = (index, shuffle_from, adj_cols.T, adj_count)
    args += (grad_clean, pre_clean, grad_corrupt, pre_corrupt, slopes[None, :], adj_vals)
    clean, outgoing, *sides = aggregate(*args, features, weight, reach, devs, groups)
    sides, packed = sides[:4], sides[4:]
    low, high = shifted(sides[3], "node", 1), shifted(sides[2], "node", -1)
    for i in exchange_order(groups):
        packed[i] = swapped(packed[i], "chan", i)

    outgoing = patch(index, shuffle_from, outgoing, low, high, blocks, slots)
    shuffle_from, outgoing, clean, sides = lax.optimization_barrier(
        (shuffle_from, outgoing, clean, sides)
    )
    low, high = shifted(sides[1], "node", 1), shifted(sides[0], "node", -1)
    landing = landing_blocks(shuffle_from, me, blocks, devs, slots)
    incoming = exchanged(outgoing, "node")
    incoming, packed = lax.optimization_barrier((incoming, packed))
    merged = merge(index, landing, clean, low, high, incoming, groups)

    quarter = row_count // groups
    summed = [merged[0]] + [None] * (groups - 1)
    for i in exchange_order(groups):
        summed[i] = swapped(merged[i], "chan", i)
    tiles = jnp.stack([piece[quarter:] for piece in packed])
    even = [tiles] + [swapped(tiles, "node", 2 * i) for i in range(1, devs // 2)]
    order = [0, *range(2, groups - 1), 1, groups - 1]
    listed, even = lax.optimization_barrier(([summed[i] for i in order], even))
    summed = [listed[order.index(i)] for i in range(groups)]
    even = jnp.stack(even)
    odd = swapped(even, "node", 1)

    keep, send = weight_partial(index, packed, summed, devs)
    odd, send = lax.optimization_barrier((odd, send))
    arrived = swapped(send, "node", 1)
    rows_out = feature_rows(index, summed, even, odd)
    arrived, rows_out = lax.optimization_barrier((arrived, rows_out))

    pieces = [rows_out[0]] + [None] * (groups - 1)
    for i in exchange_order(groups):
        pieces[i] = swapped(rows_out[i], "chan", i)
    total = wide(keep) + wide(arrived)
    share = total[0]
    for i in range(1, devs // 2):
        share = share + wide(swapped(total[i].astype(jnp.bfloat16), "node", 2 * i))
    others = [swapped(share[i].astype(jnp.bfloat16), "chan", i) for i in range(1, groups)]
    grad_features, grad_weight = finish(index, pieces, share[0], others)
    return (grad_weight, grad_features)


def solution(mesh):
    placed = (
        P("node", "chan"),
        P("node", "chan"),
        P("node", "chan"),
        P("node", "chan"),
        P("node", "chan"),
        P("node", "chan"),
        P("chan"),
        P("node", None, None, None),
        P("node", None),
        P("node"),
        P(),
    )
    return jax.shard_map(
        local,
        mesh=mesh,
        in_specs=placed,
        out_specs=(P("node", "chan"), P("node", "chan")),
        check_vma=False,
    )
```

```python
import functools
import math

import jax
import jax.numpy as jnp
from jax import lax
from jax.experimental import pallas as pl
from jax.experimental.pallas import tpu as pltpu
from jax.sharding import PartitionSpec as P

VMEM_LIMIT = 32 * 1024 * 1024
VMEM_ALL = 61 * 1024 * 1024
VMEM_MOST = 52 * 1024 * 1024
IN_VMEM = pl.BlockSpec(memory_space=pltpu.VMEM)
IN_SMEM = pl.BlockSpec(memory_space=pltpu.SMEM)
IN_HBM = pl.BlockSpec(memory_space=pltpu.HBM)


def params(limit=VMEM_LIMIT):
    return pltpu.CompilerParams(vmem_limit_bytes=limit)


def bf16(*shape):
    return jax.ShapeDtypeStruct(shape, jnp.bfloat16)


def wide(value):
    return value.astype(jnp.float32)


def shifted(value, axis, by):
    size = lax.axis_size(axis)
    pairs = [(i, i + by) for i in range(size) if 0 <= i + by < size]
    return lax.ppermute(value, axis, pairs)


def swapped(value, axis, by):
    size = lax.axis_size(axis)
    return lax.ppermute(value, axis, [(i, i ^ by) for i in range(size)])


def exchanged(value, axis):
    return lax.all_to_all(value, axis, split_axis=0, concat_axis=0, tiled=True)


def masked_grad(grad, pre, slope):
    return jnp.where(pre > 0, grad, (wide(grad) * slope).astype(jnp.bfloat16))


def find_places(index, shuffle, blocks, slots, places, used):
    for i in range(used.shape[0]):
        used[i] = 0
    for block in range(blocks):
        owner = shuffle[index[0] * blocks + block] // blocks
        slot = used[owner]
        used[owner] = slot + 1
        places[block] = owner * slots + slot


def aggregate_kernel(
    reach, send_slots, me, shuffle, cols, count, gc, pc, gx, px, slopes, adj, clean, outgoing, *refs
):
    sides, refs = refs[:4], refs[4:]
    data, tiles, rhs, stage, results, halos, places, used, sems, out_sems = refs
    blocks, slots, rows, _ = adj.shape
    width = gc.shape[1]
    spare = blocks + 2 * reach
    pad = 2 * reach * rows

    def copies(step):
        span = slice(2 * step, 2 * step + 2)
        out = [
            pltpu.make_async_copy(
                ref.at[2 * step * rows : (2 * step + 2) * rows], data.at[i, step], sems.at[i, step]
            )
            for i, ref in enumerate((gc, pc, gx, px))
        ]
        return out + [pltpu.make_async_copy(adj.at[span], tiles.at[span], sems.at[4, step])]

    inputs = [copies(step) for step in range(blocks // 2)]
    for copy in sum(inputs, []):
        copy.start()
    stage[...] = jnp.zeros_like(stage)
    rhs[:pad] = jnp.zeros((pad, 2 * width), jnp.bfloat16)
    rhs[pad + blocks * rows :] = jnp.zeros((pad, 2 * width), jnp.bfloat16)
    shape = (rows, rows)
    identity = (
        lax.broadcasted_iota(jnp.int32, shape, 0) == lax.broadcasted_iota(jnp.int32, shape, 1)
    ).astype(jnp.float32).astype(jnp.bfloat16)
    slope = slopes[...]
    find_places(me, shuffle, blocks, send_slots, places, used)

    def take(step):
        gradients = [masked_grad(data[i, step], data[i + 1, step], slope) for i in (0, 2)]
        rhs[pad + 2 * step * rows : pad + (2 * step + 2) * rows] = jnp.concatenate(gradients, axis=1)
        turned = lax.dot_general(
            identity,
            tiles[2 * step : 2 * step + 2].reshape(2 * slots * rows, rows),
            (((1,), (1,)), ((), ())),
            preferred_element_type=jnp.float32,
        )
        for i in range(2 * slots):
            block, k = 2 * step + i // slots, i % slots
            live = k < count[block]
            target = cols[k, block] - me[0] * blocks
            place = jnp.where(live, target + reach, spare)
            distance = jnp.where(live, block - target + reach, 0)
            part = turned[:, i * rows : (i + 1) * rows]
            stage[place, distance] = (wide(stage[place, distance]) + part).astype(jnp.bfloat16)

    blank = jnp.zeros(shape, jnp.bfloat16)

    def pair(first):
        lhs = jnp.concatenate(
            [
                jnp.concatenate(
                    [blank] * i + [stage[first + i, j] for j in range(2 * reach + 1)] + [blank] * (1 - i),
                    axis=1,
                )
                for i in range(2)
            ],
            axis=0,
        )
        span = slice(first * rows, (first + 2 * reach + 2) * rows)
        product = jnp.dot(lhs, rhs[span], preferred_element_type=jnp.float32)
        product = product.astype(jnp.bfloat16).reshape(2, rows, 2 * width)
        return product[:, :, :width], product[:, :, width:]

    writes = []

    def finish(first):
        block = first - reach
        if 0 <= block < blocks:
            span = slice(block, block + 2)
            results[0, span], results[1, span] = pair(first)
            done = [pltpu.make_async_copy(results.at[0, span], clean.at[span], out_sems.at[0, block])]
            for i in range(block, block + 2):
                target = outgoing.at[places[i]]
                done.append(pltpu.make_async_copy(results.at[1, i], target, out_sems.at[1, i]))
        else:
            side, at = int(block >= 0), first % (blocks + reach)
            halos[side, 0, at : at + 2], halos[side, 1, at : at + 2] = pair(first)
            done = []
            for i in range(2):
                source, target = halos.at[side, i, at : at + 2], sides[2 * i + side].at[at : at + 2]
                done.append(pltpu.make_async_copy(source, target, out_sems.at[2 + i, first]))
        for copy in done:
            copy.start()
        writes.extend(done)

    for step in range(blocks // 2):
        for copy in inputs[step]:
            copy.wait()
        if step:
            finish(2 * step - 2)
        take(step)
    for first in range(blocks + 2 * reach - 2, blocks - 4, -2):
        finish(first)
    for copy in writes:
        copy.wait()


def aggregate(index, shuffle, cols, count, gc, pc, gx, px, slopes, adj, reach, devs):
    blocks, slots, rows, _ = adj.shape
    width = gc.shape[1]
    send_slots = -(-blocks // devs)
    assert reach % 2 == 0 and blocks % 2 == 0
    return pl.pallas_call(
        functools.partial(aggregate_kernel, reach, send_slots),
        in_specs=[IN_SMEM] * 4 + [IN_HBM] * 4 + [IN_VMEM, IN_HBM],
        out_specs=[IN_HBM] * 6,
        out_shape=[bf16(blocks, rows, width), bf16(devs * send_slots, rows, width)]
        + [bf16(reach, rows, width)] * 4,
        scratch_shapes=[
            pltpu.VMEM((4, blocks // 2, 2 * rows, width), jnp.bfloat16),
            pltpu.VMEM((blocks, slots, rows, rows), jnp.bfloat16),
            pltpu.VMEM(((blocks + 4 * reach) * rows, 2 * width), jnp.bfloat16),
            pltpu.VMEM((blocks + 2 * reach + 1, 2 * reach + 1, rows, rows), jnp.bfloat16),
            pltpu.VMEM((2, blocks, rows, width), jnp.bfloat16),
            pltpu.VMEM((2, 2, reach, rows, width), jnp.bfloat16),
            pltpu.SMEM((blocks,), jnp.int32),
            pltpu.SMEM((devs,), jnp.int32),
            pltpu.SemaphoreType.DMA((5, blocks // 2)),
            pltpu.SemaphoreType.DMA((4, blocks + 2 * reach)),
        ],
        compiler_params=params(VMEM_ALL),
        cost_estimate=pl.CostEstimate(
            flops=4 * blocks * slots * rows * rows * width,
            bytes_accessed=12 * blocks * rows * width + 2 * blocks * slots * rows * rows,
            transcendentals=0,
        ),
        name="aggregate",
    )(index, shuffle, cols, count, gc, pc, gx, px, slopes, adj)


def patch_kernel(reach, blocks, slots, index, shuffle, outgoing, low, high, out, held, ready, places, used, sems):
    find_places(index, shuffle, blocks, slots, places, used)
    border = [*range(reach), *range(blocks - reach, blocks)]
    reads, writes = [], []
    for i, block in enumerate(border):
        place = places[block]
        reads.append(pltpu.make_async_copy(outgoing.at[place], held.at[i], sems.at[0, i]))
        writes.append(pltpu.make_async_copy(ready.at[i], out.at[place], sems.at[1, i]))
    for copy in reads:
        copy.start()
    for i, (read, write) in enumerate(zip(reads, writes)):
        read.wait()
        other = low[i] if i < reach else high[i - reach]
        ready[i] = (wide(held[i]) + wide(other)).astype(jnp.bfloat16)
        write.start()
    for copy in writes:
        copy.wait()


def patch(index, shuffle, outgoing, low, high, blocks, slots):
    sent, rows, width = outgoing.shape
    reach = low.shape[0]
    border = pltpu.VMEM((2 * reach, rows, width), jnp.bfloat16)
    return pl.pallas_call(
        functools.partial(patch_kernel, reach, blocks, slots),
        in_specs=[IN_SMEM] * 2 + [IN_HBM] + [IN_VMEM] * 2,
        out_specs=IN_HBM,
        out_shape=bf16(*outgoing.shape),
        input_output_aliases={2: 0},
        scratch_shapes=[
            border,
            border,
            pltpu.SMEM((blocks,), jnp.int32),
            pltpu.SMEM((sent // slots,), jnp.int32),
            pltpu.SemaphoreType.DMA((2, 2 * reach)),
        ],
        compiler_params=params(VMEM_MOST),
        name="patch",
    )(index, shuffle, outgoing, low, high)


def merge_kernel(quarter, index, landing, clean, low, high, incoming, out, whole):
    blocks, rows, _ = clean.shape
    reach = low.shape[0]
    group = index[1]
    piece = math.gcd(rows, quarter)
    for block in range(blocks):
        whole[block] = wide(clean[block])
    for i in range(reach):
        whole[i] += wide(low[i])
        whole[blocks - reach + i] += wide(high[i])
    for place in range(incoming.shape[0]):
        block = landing[place]

        @pl.when(block >= 0)
        def _():
            total = (whole[block] + wide(incoming[place])).astype(jnp.bfloat16)
            for part in range(rows // piece):
                at = block * (rows // piece) + part
                owner = at // (quarter // piece)
                offset = (at - owner * (quarter // piece)) * piece
                out[owner ^ group, pl.ds(pl.multiple_of(offset, piece), piece)] = total[
                    part * piece : (part + 1) * piece
                ]


def merge(index, landing, clean, low, high, incoming, groups):
    blocks, rows, width = clean.shape
    quarter = blocks * rows // groups
    return pl.pallas_call(
        functools.partial(merge_kernel, quarter),
        in_specs=[IN_SMEM] * 2 + [IN_VMEM] * 4,
        out_specs=IN_VMEM,
        out_shape=bf16(groups, quarter, width),
        scratch_shapes=[pltpu.VMEM((blocks, rows, width), jnp.float32)],
        compiler_params=params(),
        name="merge",
    )(index, landing, clean, low, high, incoming)


def weight_kernel(devs, index, feats, *refs):
    *summed, keep, send = refs
    groups = len(summed)
    me, group = index[0], index[1]
    shares = devs // groups
    height, width = keep.shape[2:]
    rhs = jnp.concatenate([piece[...] for piece in summed], axis=1)
    for relative in range(groups):
        product = lax.dot_general(
            feats[group ^ relative],
            rhs,
            (((0,), (0,)), ((), ())),
            preferred_element_type=jnp.float32,
        ).astype(jnp.bfloat16)
        for share in range(shares):
            node = ((group ^ relative) * shares + share) ^ me
            rows = product[share * height : (share + 1) * height]

            def store(out):
                for i in range(groups):
                    out[node >> 1, i] = rows[:, i * width : (i + 1) * width]

            pl.when((node & 1) == 0)(functools.partial(store, keep))
            pl.when((node & 1) == 1)(functools.partial(store, send))


def weight_partial(index, feats, summed, devs):
    groups = len(summed)
    rows, width = summed[0].shape
    height = groups * width // devs
    return pl.pallas_call(
        functools.partial(weight_kernel, devs),
        in_specs=[IN_SMEM] + [IN_VMEM] * (1 + groups),
        out_specs=[IN_VMEM] * 2,
        out_shape=[bf16(devs // 2, groups, height, width)] * 2,
        compiler_params=params(),
        cost_estimate=pl.CostEstimate(
            flops=2 * rows * (groups * width) ** 2,
            bytes_accessed=2 * (groups * width) ** 2 + 4 * groups * rows * width,
            transcendentals=0,
        ),
        name="weight_partial",
    )(index, feats, *summed)


def feature_kernel(index, *refs):
    *summed, even, odd, out = refs
    groups = len(summed)
    devs = 2 * even.shape[0]
    me, group = index[0], index[1]
    shares = devs // groups
    height = even.shape[2]
    low = me & (shares - 1)
    lhs = jnp.concatenate([piece[...] for piece in summed], axis=1)
    for relative in range(groups):
        rows = []
        for i in range(shares):
            node = (((group ^ relative) * shares) ^ (me - low)) + i
            half = odd if i % 2 else even
            rows.append(jnp.concatenate([half[node >> 1, j] for j in range(groups)], axis=1))
        product = lax.dot_general(
            lhs,
            jnp.concatenate(rows, axis=0),
            (((1,), (1,)), ((), ())),
            preferred_element_type=jnp.float32,
        ).astype(jnp.bfloat16)
        parts = [product[:, i * height : (i + 1) * height] for i in range(shares)]

        def store(flip):
            out[relative] = jnp.concatenate([parts[i ^ flip] for i in range(shares)], axis=1)

        for flip in range(shares):
            pl.when(low == flip)(functools.partial(store, flip))


def feature_rows(index, summed, even, odd):
    groups = len(summed)
    rows, width = summed[0].shape
    return pl.pallas_call(
        feature_kernel,
        in_specs=[IN_SMEM] + [IN_VMEM] * (groups + 2),
        out_specs=IN_VMEM,
        out_shape=bf16(groups, rows, width),
        compiler_params=params(),
        cost_estimate=pl.CostEstimate(
            flops=2 * rows * (groups * width) ** 2,
            bytes_accessed=2 * (groups * width) ** 2 + 4 * groups * rows * width,
            transcendentals=0,
        ),
        name="feature_rows",
    )(index, *summed, even, odd)


def finish_kernel(index, share, *refs):
    *refs, out, total, sems = refs
    groups = (len(refs) + 1) // 2
    pieces, others = refs[:groups], refs[groups:]
    rows = pieces[0].shape[0]
    copies = [
        pltpu.make_async_copy(
            piece, out.at[pl.ds(pl.multiple_of((index[1] ^ i) * rows, rows), rows)], sems.at[i]
        )
        for i, piece in enumerate(pieces)
    ]
    for copy in copies:
        copy.start()
    sum_of = share[...]
    for other in others:
        sum_of = sum_of + wide(other[...])
    total[...] = sum_of
    for copy in copies:
        copy.wait()


def finish(index, pieces, share, others):
    rows, width = pieces[0].shape
    return pl.pallas_call(
        finish_kernel,
        in_specs=[IN_SMEM] + [IN_VMEM] * (2 * len(pieces)),
        out_specs=[IN_HBM, IN_VMEM],
        out_shape=[
            bf16(len(pieces) * rows, width),
            jax.ShapeDtypeStruct(share.shape, jnp.float32),
        ],
        scratch_shapes=[pltpu.SemaphoreType.DMA((len(pieces),))],
        compiler_params=params(),
        name="finish",
    )(index, share, *pieces, *others)


def landing_blocks(shuffle_from, me, blocks, devs, slots):
    owner = (shuffle_from // blocks).reshape(devs, blocks)
    within = (shuffle_from % blocks).reshape(devs, blocks)
    for_me = owner == me
    earlier = jnp.arange(blocks)[None, :] < jnp.arange(blocks)[:, None]
    rank = jnp.sum((for_me[:, None, :] & earlier[None]).astype(jnp.int32), axis=2)
    picked = for_me[:, None, :] & (rank[:, None, :] == jnp.arange(slots)[None, :, None])
    return (jnp.sum(jnp.where(picked, within[:, None, :] + 1, 0), axis=2) - 1).reshape(-1)


def exchange_order(groups):
    return sorted(range(1, groups), reverse=True)


def local(
    features,
    weight,
    pre_clean,
    pre_corrupt,
    grad_clean,
    grad_corrupt,
    slopes,
    adj_vals,
    adj_cols,
    adj_count,
    shuffle_from,
):
    row_count, width = features.shape
    blocks, tile_slots, _, _ = adj_vals.shape
    reach = (tile_slots - 1) // 2
    me = lax.axis_index("node")
    group = lax.axis_index("chan")
    devs = lax.axis_size("node")
    groups = lax.axis_size("chan")
    slots = -(-blocks // devs)
    index = jnp.stack([me, group])

    args = (index, shuffle_from, adj_cols.T, adj_count)
    args += (grad_clean, pre_clean, grad_corrupt, pre_corrupt, slopes[None, :], adj_vals)
    quarter = row_count // groups
    feats = exchanged(features.reshape(groups, quarter, width), "chan")
    clean, outgoing, *sides = aggregate(*args, reach, devs)
    low, high = shifted(sides[3], "node", 1), shifted(sides[2], "node", -1)
    outgoing = patch(index, shuffle_from, outgoing, low, high, blocks, slots)
    shuffle_from, weight, outgoing, feats, clean, sides = lax.optimization_barrier(
        (shuffle_from, weight, outgoing, feats, clean, sides)
    )
    low, high = shifted(sides[1], "node", 1), shifted(sides[0], "node", -1)
    tiles = [weight] + [swapped(weight, "chan", i) for i in range(1, groups)]
    landing = landing_blocks(shuffle_from, me, blocks, devs, slots)
    incoming = exchanged(outgoing, "node")
    incoming, tiles = lax.optimization_barrier((incoming, tiles))
    merged = merge(index, landing, clean, low, high, incoming, groups)

    summed = [merged[0]] + [None] * (groups - 1)
    for i in exchange_order(groups):
        summed[i] = swapped(merged[i], "chan", i)
    tiles = jnp.stack(tiles)
    even = [tiles] + [swapped(tiles, "node", 2 * i) for i in range(1, devs // 2)]
    order = [0, *range(2, groups - 1), 1, groups - 1]
    listed, even = lax.optimization_barrier(([summed[i] for i in order], even))
    summed = [listed[order.index(i)] for i in range(groups)]
    even = jnp.stack(even)
    odd = swapped(even, "node", 1)

    keep, send = weight_partial(index, feats, summed, devs)
    odd, send = lax.optimization_barrier((odd, send))
    arrived = swapped(send, "node", 1)
    rows_out = feature_rows(index, summed, even, odd)
    arrived, rows_out = lax.optimization_barrier((arrived, rows_out))

    pieces = [rows_out[0]] + [None] * (groups - 1)
    for i in exchange_order(groups):
        pieces[i] = swapped(rows_out[i], "chan", i)
    total = wide(keep) + wide(arrived)
    share = total[0]
    for i in range(1, devs // 2):
        share = share + wide(swapped(total[i].astype(jnp.bfloat16), "node", 2 * i))
    others = [swapped(share[i].astype(jnp.bfloat16), "chan", i) for i in range(1, groups)]
    grad_features, grad_weight = finish(index, pieces, share[0], others)
    return (grad_weight, grad_features)


def solution(mesh):
    placed = (
        P("node", "chan"),
        P("node", "chan"),
        P("node", "chan"),
        P("node", "chan"),
        P("node", "chan"),
        P("node", "chan"),
        P("chan"),
        P("node", None, None, None),
        P("node", None),
        P("node"),
        P(),
    )
    return jax.shard_map(
        local,
        mesh=mesh,
        in_specs=placed,
        out_specs=(P("node", "chan"), P("node", "chan")),
        check_vma=False,
    )
```

```python
import functools
import math

import jax
import jax.numpy as jnp
from jax import lax
from jax.experimental import pallas as pl
from jax.experimental.pallas import tpu as pltpu
from jax.sharding import PartitionSpec as P

VMEM_LIMIT = 32 * 1024 * 1024
VMEM_ALL = 61 * 1024 * 1024
IN_VMEM = pl.BlockSpec(memory_space=pltpu.VMEM)
IN_SMEM = pl.BlockSpec(memory_space=pltpu.SMEM)
IN_HBM = pl.BlockSpec(memory_space=pltpu.HBM)


def params(limit=VMEM_LIMIT):
    return pltpu.CompilerParams(vmem_limit_bytes=limit)


def bf16(*shape):
    return jax.ShapeDtypeStruct(shape, jnp.bfloat16)


def wide(value):
    return value.astype(jnp.float32)


def shifted(value, axis, by):
    size = lax.axis_size(axis)
    pairs = [(i, i + by) for i in range(size) if 0 <= i + by < size]
    return lax.ppermute(value, axis, pairs)


def swapped(value, axis, by):
    size = lax.axis_size(axis)
    return lax.ppermute(value, axis, [(i, i ^ by) for i in range(size)])


def exchanged(value, axis):
    return lax.all_to_all(value, axis, split_axis=0, concat_axis=0, tiled=True)


def masked_grad(grad, pre, slope):
    return jnp.where(pre > 0, grad, (wide(grad) * slope).astype(jnp.bfloat16))


def find_places(index, shuffle, blocks, slots, places, used):
    for i in range(used.shape[0]):
        used[i] = 0
    for block in range(blocks):
        owner = shuffle[index[0] * blocks + block] // blocks
        slot = used[owner]
        used[owner] = slot + 1
        places[block] = owner * slots + slot


def aggregate_kernel(
    reach, groups, send_slots, me, shuffle, cols, count, gc, pc, gx, px, slopes, adj, features, weight, *refs
):
    clean, outgoing, *refs = refs
    sides, packed, refs = refs[:4], refs[4 : 4 + groups], refs[4 + groups :]
    data, tiles, rhs, stage, results, halos, packs, places, used, sems, pack_sems, out_sems = refs
    blocks, slots, rows, _ = adj.shape
    width = gc.shape[1]
    quarter = features.shape[0] // groups
    spare = blocks + 2 * reach
    pad = 2 * reach * rows

    def copies(step):
        span = slice(2 * step, 2 * step + 2)
        out = [
            pltpu.make_async_copy(
                ref.at[2 * step * rows : (2 * step + 2) * rows], data.at[i, step], sems.at[i, step]
            )
            for i, ref in enumerate((gc, pc, gx, px))
        ]
        return out + [pltpu.make_async_copy(adj.at[span], tiles.at[span], sems.at[4, step])]

    inputs = [copies(step) for step in range(blocks // 2)]
    for copy in sum(inputs, []):
        copy.start()
    to_vmem, to_hbm = [], []
    for i in range(groups):
        span = pl.ds(pl.multiple_of((me[1] ^ i) * quarter, quarter), quarter)
        to_vmem.append(
            pltpu.make_async_copy(features.at[span], packs.at[i, :quarter], pack_sems.at[0, i])
        )
        to_vmem.append(pltpu.make_async_copy(weight, packs.at[i, quarter:], pack_sems.at[1, i]))
        to_hbm.append(pltpu.make_async_copy(packs.at[i], packed[i], pack_sems.at[2, i]))
    for copy in to_vmem:
        copy.start()
    stage[...] = jnp.zeros_like(stage)
    rhs[:pad] = jnp.zeros((pad, 2 * width), jnp.bfloat16)
    rhs[pad + blocks * rows :] = jnp.zeros((pad, 2 * width), jnp.bfloat16)
    shape = (rows, rows)
    identity = (
        lax.broadcasted_iota(jnp.int32, shape, 0) == lax.broadcasted_iota(jnp.int32, shape, 1)
    ).astype(jnp.float32).astype(jnp.bfloat16)
    slope = slopes[...]
    find_places(me, shuffle, blocks, send_slots, places, used)

    def take(step):
        gradients = [masked_grad(data[i, step], data[i + 1, step], slope) for i in (0, 2)]
        rhs[pad + 2 * step * rows : pad + (2 * step + 2) * rows] = jnp.concatenate(gradients, axis=1)
        turned = lax.dot_general(
            identity,
            tiles[2 * step : 2 * step + 2].reshape(2 * slots * rows, rows),
            (((1,), (1,)), ((), ())),
            preferred_element_type=jnp.float32,
        )
        for i in range(2 * slots):
            block, k = 2 * step + i // slots, i % slots
            live = k < count[block]
            target = cols[k, block] - me[0] * blocks
            place = jnp.where(live, target + reach, spare)
            distance = jnp.where(live, block - target + reach, 0)
            part = turned[:, i * rows : (i + 1) * rows]
            stage[place, distance] = (wide(stage[place, distance]) + part).astype(jnp.bfloat16)

    blank = jnp.zeros(shape, jnp.bfloat16)

    def pair(first):
        lhs = jnp.concatenate(
            [
                jnp.concatenate(
                    [blank] * i + [stage[first + i, j] for j in range(2 * reach + 1)] + [blank] * (1 - i),
                    axis=1,
                )
                for i in range(2)
            ],
            axis=0,
        )
        span = slice(first * rows, (first + 2 * reach + 2) * rows)
        product = jnp.dot(lhs, rhs[span], preferred_element_type=jnp.float32)
        product = product.astype(jnp.bfloat16).reshape(2, rows, 2 * width)
        return product[:, :, :width], product[:, :, width:]

    writes = []

    def finish(first):
        block = first - reach
        if 0 <= block < blocks:
            span = slice(block, block + 2)
            results[0, span], results[1, span] = pair(first)
            done = [pltpu.make_async_copy(results.at[0, span], clean.at[span], out_sems.at[0, block])]
            for i in range(block, block + 2):
                target = outgoing.at[places[i]]
                done.append(pltpu.make_async_copy(results.at[1, i], target, out_sems.at[1, i]))
        else:
            side, at = int(block >= 0), first % (blocks + reach)
            halos[side, 0, at : at + 2], halos[side, 1, at : at + 2] = pair(first)
            done = []
            for i in range(2):
                source, target = halos.at[side, i, at : at + 2], sides[2 * i + side].at[at : at + 2]
                done.append(pltpu.make_async_copy(source, target, out_sems.at[2 + i, first]))
        for copy in done:
            copy.start()
        writes.extend(done)

    for step in range(blocks // 2):
        for copy in inputs[step]:
            copy.wait()
        if step:
            finish(2 * step - 2)
        take(step)
    for copy in to_vmem:
        copy.wait()
    for copy in to_hbm:
        copy.start()
    for first in range(blocks + 2 * reach - 2, blocks - 4, -2):
        finish(first)
    for copy in writes + to_hbm:
        copy.wait()


def aggregate(index, shuffle, cols, count, gc, pc, gx, px, slopes, adj, features, weight, reach, devs, groups):
    blocks, slots, rows, _ = adj.shape
    width = gc.shape[1]
    send_slots = -(-blocks // devs)
    assert reach % 2 == 0 and blocks % 2 == 0
    packed = features.shape[0] // groups + weight.shape[0]
    return pl.pallas_call(
        functools.partial(aggregate_kernel, reach, groups, send_slots),
        in_specs=[IN_SMEM] * 4 + [IN_HBM] * 4 + [IN_VMEM] + [IN_HBM] * 3,
        out_specs=[IN_HBM] * (6 + groups),
        out_shape=[bf16(blocks, rows, width), bf16(devs * send_slots, rows, width)]
        + [bf16(reach, rows, width)] * 4
        + [bf16(packed, width)] * groups,
        scratch_shapes=[
            pltpu.VMEM((4, blocks // 2, 2 * rows, width), jnp.bfloat16),
            pltpu.VMEM((blocks, slots, rows, rows), jnp.bfloat16),
            pltpu.VMEM(((blocks + 4 * reach) * rows, 2 * width), jnp.bfloat16),
            pltpu.VMEM((blocks + 2 * reach + 1, 2 * reach + 1, rows, rows), jnp.bfloat16),
            pltpu.VMEM((2, blocks, rows, width), jnp.bfloat16),
            pltpu.VMEM((2, 2, reach, rows, width), jnp.bfloat16),
            pltpu.VMEM((groups, packed, width), jnp.bfloat16),
            pltpu.SMEM((blocks,), jnp.int32),
            pltpu.SMEM((devs,), jnp.int32),
            pltpu.SemaphoreType.DMA((5, blocks // 2)),
            pltpu.SemaphoreType.DMA((3, groups)),
            pltpu.SemaphoreType.DMA((4, blocks + 2 * reach)),
        ],
        compiler_params=params(VMEM_ALL),
        cost_estimate=pl.CostEstimate(
            flops=4 * blocks * slots * rows * rows * width,
            bytes_accessed=12 * blocks * rows * width + 2 * blocks * slots * rows * rows,
            transcendentals=0,
        ),
        name="aggregate",
    )(index, shuffle, cols, count, gc, pc, gx, px, slopes, adj, features, weight)


def patch_kernel(reach, blocks, slots, index, shuffle, outgoing, low, high, out, *scratch):
    held, other, ready, places, used, sems = scratch
    arrivals = [
        pltpu.make_async_copy(side, other.at[i * reach : (i + 1) * reach], sems.at[2, i])
        for i, side in enumerate((low, high))
    ]
    for copy in arrivals:
        copy.start()
    find_places(index, shuffle, blocks, slots, places, used)
    border = [*range(reach), *range(blocks - reach, blocks)]
    reads, writes = [], []
    for i, block in enumerate(border):
        place = places[block]
        reads.append(pltpu.make_async_copy(outgoing.at[place], held.at[i], sems.at[0, i]))
        writes.append(pltpu.make_async_copy(ready.at[i], out.at[place], sems.at[1, i]))
    for copy in reads:
        copy.start()
    for copy in arrivals:
        copy.wait()
    for i, (read, write) in enumerate(zip(reads, writes)):
        read.wait()
        ready[i] = (wide(held[i]) + wide(other[i])).astype(jnp.bfloat16)
        write.start()
    for copy in writes:
        copy.wait()


def patch(index, shuffle, outgoing, low, high, blocks, slots):
    sent, rows, width = outgoing.shape
    reach = low.shape[0]
    border = pltpu.VMEM((2 * reach, rows, width), jnp.bfloat16)
    return pl.pallas_call(
        functools.partial(patch_kernel, reach, blocks, slots),
        in_specs=[IN_SMEM] * 2 + [IN_HBM] * 3,
        out_specs=IN_HBM,
        out_shape=bf16(*outgoing.shape),
        input_output_aliases={2: 0},
        scratch_shapes=[
            border,
            border,
            border,
            pltpu.SMEM((blocks,), jnp.int32),
            pltpu.SMEM((sent // slots,), jnp.int32),
            pltpu.SemaphoreType.DMA((3, 2 * reach)),
        ],
        compiler_params=params(VMEM_ALL),
        name="patch",
    )(index, shuffle, outgoing, low, high)


def merge_kernel(quarter, index, landing, clean, low, high, incoming, out, whole):
    blocks, rows, _ = clean.shape
    reach = low.shape[0]
    group = index[1]
    piece = math.gcd(rows, quarter)
    for block in range(blocks):
        whole[block] = wide(clean[block])
    for i in range(reach):
        whole[i] += wide(low[i])
        whole[blocks - reach + i] += wide(high[i])
    for place in range(incoming.shape[0]):
        block = landing[place]

        @pl.when(block >= 0)
        def _():
            total = (whole[block] + wide(incoming[place])).astype(jnp.bfloat16)
            for part in range(rows // piece):
                at = block * (rows // piece) + part
                owner = at // (quarter // piece)
                offset = (at - owner * (quarter // piece)) * piece
                out[owner ^ group, pl.ds(pl.multiple_of(offset, piece), piece)] = total[
                    part * piece : (part + 1) * piece
                ]


def merge(index, landing, clean, low, high, incoming, groups):
    blocks, rows, width = clean.shape
    quarter = blocks * rows // groups
    return pl.pallas_call(
        functools.partial(merge_kernel, quarter),
        in_specs=[IN_SMEM] * 2 + [IN_VMEM] * 4,
        out_specs=IN_VMEM,
        out_shape=bf16(groups, quarter, width),
        scratch_shapes=[pltpu.VMEM((blocks, rows, width), jnp.float32)],
        compiler_params=params(),
        name="merge",
    )(index, landing, clean, low, high, incoming)


def weight_kernel(devs, index, *refs):
    groups = (len(refs) - 2) // 2
    packed, summed, (keep, send) = refs[:groups], refs[groups : 2 * groups], refs[2 * groups :]
    me, group = index[0], index[1]
    shares = devs // groups
    height, width = keep.shape[2:]
    rhs = jnp.concatenate([piece[...] for piece in summed], axis=1)
    for relative in range(groups):
        product = lax.dot_general(
            packed[relative][: rhs.shape[0]],
            rhs,
            (((0,), (0,)), ((), ())),
            preferred_element_type=jnp.float32,
        ).astype(jnp.bfloat16)
        for share in range(shares):
            node = ((group ^ relative) * shares + share) ^ me
            rows = product[share * height : (share + 1) * height]

            def store(out):
                for i in range(groups):
                    out[node >> 1, i] = rows[:, i * width : (i + 1) * width]

            pl.when((node & 1) == 0)(functools.partial(store, keep))
            pl.when((node & 1) == 1)(functools.partial(store, send))


def weight_partial(index, packed, summed, devs):
    groups = len(packed)
    rows, width = summed[0].shape
    height = groups * width // devs
    return pl.pallas_call(
        functools.partial(weight_kernel, devs),
        in_specs=[IN_SMEM] + [IN_VMEM] * (2 * groups),
        out_specs=[IN_VMEM] * 2,
        out_shape=[bf16(devs // 2, groups, height, width)] * 2,
        compiler_params=params(),
        cost_estimate=pl.CostEstimate(
            flops=2 * rows * (groups * width) ** 2,
            bytes_accessed=2 * (groups * width) ** 2 + 4 * groups * rows * width,
            transcendentals=0,
        ),
        name="weight_partial",
    )(index, *packed, *summed)


def feature_kernel(first, index, *refs):
    *summed, even, odd, out = refs
    groups = len(summed)
    devs = 2 * even.shape[0]
    me, group = index[0], index[1]
    shares = devs // groups
    height = even.shape[2]
    low = me & (shares - 1)
    lhs = jnp.concatenate([piece[...] for piece in summed], axis=1)
    for relative in range(first, first + out.shape[0]):
        rows = []
        for i in range(shares):
            node = (((group ^ relative) * shares) ^ (me - low)) + i
            half = odd if i % 2 else even
            rows.append(jnp.concatenate([half[node >> 1, j] for j in range(groups)], axis=1))
        product = lax.dot_general(
            lhs,
            jnp.concatenate(rows, axis=0),
            (((1,), (1,)), ((), ())),
            preferred_element_type=jnp.float32,
        ).astype(jnp.bfloat16)
        parts = [product[:, i * height : (i + 1) * height] for i in range(shares)]

        def store(flip):
            out[relative - first] = jnp.concatenate([parts[i ^ flip] for i in range(shares)], axis=1)

        for flip in range(shares):
            pl.when(low == flip)(functools.partial(store, flip))


def feature_rows(index, summed, even, odd, first, count):
    groups = len(summed)
    rows, width = summed[0].shape
    return pl.pallas_call(
        functools.partial(feature_kernel, first),
        in_specs=[IN_SMEM] + [IN_VMEM] * (groups + 2),
        out_specs=IN_VMEM,
        out_shape=bf16(count, rows, width),
        compiler_params=params(),
        cost_estimate=pl.CostEstimate(
            flops=2 * rows * groups * count * width**2,
            bytes_accessed=2 * groups * count * width**2 + 2 * (groups + count) * rows * width,
            transcendentals=0,
        ),
        name="feature_rows",
    )(index, *summed, even, odd)


def gather_kernel(index, *refs):
    *pieces, out, sems = refs
    rows = pieces[0].shape[0]
    copies = [
        pltpu.make_async_copy(
            piece, out.at[pl.ds(pl.multiple_of((index[1] ^ i) * rows, rows), rows)], sems.at[i]
        )
        for i, piece in enumerate(pieces)
    ]
    for copy in copies:
        copy.start()
    for copy in copies:
        copy.wait()


def laid_out(index, pieces):
    rows, width = pieces[0].shape
    return pl.pallas_call(
        gather_kernel,
        in_specs=[IN_SMEM] + [IN_VMEM] * len(pieces),
        out_specs=IN_HBM,
        out_shape=bf16(len(pieces) * rows, width),
        scratch_shapes=[pltpu.SemaphoreType.DMA((len(pieces),))],
        compiler_params=params(),
        name="laid_out",
    )(index, *pieces)


def landing_blocks(shuffle_from, me, blocks, devs, slots):
    owner = (shuffle_from // blocks).reshape(devs, blocks)
    within = (shuffle_from % blocks).reshape(devs, blocks)
    for_me = owner == me
    earlier = jnp.arange(blocks)[None, :] < jnp.arange(blocks)[:, None]
    rank = jnp.sum((for_me[:, None, :] & earlier[None]).astype(jnp.int32), axis=2)
    picked = for_me[:, None, :] & (rank[:, None, :] == jnp.arange(slots)[None, :, None])
    return (jnp.sum(jnp.where(picked, within[:, None, :] + 1, 0), axis=2) - 1).reshape(-1)


def exchange_order(groups):
    return sorted(range(1, groups), reverse=True)


def local(
    features,
    weight,
    pre_clean,
    pre_corrupt,
    grad_clean,
    grad_corrupt,
    slopes,
    adj_vals,
    adj_cols,
    adj_count,
    shuffle_from,
):
    row_count = features.shape[0]
    blocks, tile_slots, _, _ = adj_vals.shape
    reach = (tile_slots - 1) // 2
    me = lax.axis_index("node")
    group = lax.axis_index("chan")
    devs = lax.axis_size("node")
    groups = lax.axis_size("chan")
    slots = -(-blocks // devs)
    index = jnp.stack([me, group])

    args = (index, shuffle_from, adj_cols.T, adj_count)
    args += (grad_clean, pre_clean, grad_corrupt, pre_corrupt, slopes[None, :], adj_vals)
    clean, outgoing, *sides = aggregate(*args, features, weight, reach, devs, groups)
    sides, packed = sides[:4], sides[4:]
    low, high = shifted(sides[3], "node", 1), shifted(sides[2], "node", -1)
    for i in exchange_order(groups):
        packed[i] = swapped(packed[i], "chan", i)

    outgoing = patch(index, shuffle_from, outgoing, low, high, blocks, slots)
    shuffle_from, outgoing, clean, sides = lax.optimization_barrier(
        (shuffle_from, outgoing, clean, sides)
    )
    low, high = shifted(sides[1], "node", 1), shifted(sides[0], "node", -1)
    landing = landing_blocks(shuffle_from, me, blocks, devs, slots)
    incoming = exchanged(outgoing, "node")
    incoming, packed = lax.optimization_barrier((incoming, packed))
    merged = merge(index, landing, clean, low, high, incoming, groups)

    quarter = row_count // groups
    summed = [merged[0]] + [None] * (groups - 1)
    for i in exchange_order(groups):
        summed[i] = swapped(merged[i], "chan", i)
    tiles = jnp.stack([piece[quarter:] for piece in packed])
    even = [tiles] + [swapped(tiles, "node", 2 * i) for i in range(1, devs // 2)]
    order = [0, *range(2, groups - 1), 1, groups - 1]
    listed, even = lax.optimization_barrier(([summed[i] for i in order], even))
    summed = [listed[order.index(i)] for i in range(groups)]
    even = jnp.stack(even)
    odd = swapped(even, "node", 1)

    keep, send = weight_partial(index, packed, summed, devs)
    odd, send = lax.optimization_barrier((odd, send))
    arrived = swapped(send, "node", 1)
    sent = feature_rows(index, summed, even, odd, 1, groups - 1)
    arrived, sent, summed, even, odd = lax.optimization_barrier((arrived, sent, summed, even, odd))
    pieces = [feature_rows(index, summed, even, odd, 0, 1)[0]] + [None] * (groups - 1)
    for i in exchange_order(groups):
        pieces[i] = swapped(sent[i - 1], "chan", i)
    total = wide(keep) + wide(arrived)
    share = total[0]
    for i in range(1, devs // 2):
        share = share + wide(swapped(total[i].astype(jnp.bfloat16), "node", 2 * i))
    grad_weight = share[0]
    for i in range(1, groups):
        grad_weight = grad_weight + wide(swapped(share[i].astype(jnp.bfloat16), "chan", i))
    return (grad_weight, laid_out(index, pieces))


def solution(mesh):
    placed = (
        P("node", "chan"),
        P("node", "chan"),
        P("node", "chan"),
        P("node", "chan"),
        P("node", "chan"),
        P("node", "chan"),
        P("chan"),
        P("node", None, None, None),
        P("node", None),
        P("node"),
        P(),
    )
    return jax.shard_map(
        local,
        mesh=mesh,
        in_specs=placed,
        out_specs=(P("node", "chan"), P("node", "chan")),
        check_vma=False,
    )
```

```python
import functools
import math

import jax
import jax.numpy as jnp
from jax import lax
from jax.experimental import pallas as pl
from jax.experimental.pallas import tpu as pltpu
from jax.sharding import PartitionSpec as P

VMEM_LIMIT = 32 * 1024 * 1024
VMEM_ALL = 61 * 1024 * 1024
IN_VMEM = pl.BlockSpec(memory_space=pltpu.VMEM)
IN_SMEM = pl.BlockSpec(memory_space=pltpu.SMEM)
IN_HBM = pl.BlockSpec(memory_space=pltpu.HBM)


def params(limit=VMEM_LIMIT):
    return pltpu.CompilerParams(vmem_limit_bytes=limit)


def bf16(*shape):
    return jax.ShapeDtypeStruct(shape, jnp.bfloat16)


def wide(value):
    return value.astype(jnp.float32)


def shifted(value, axis, by):
    size = lax.axis_size(axis)
    pairs = [(i, i + by) for i in range(size) if 0 <= i + by < size]
    return lax.ppermute(value, axis, pairs)


def swapped(value, axis, by):
    size = lax.axis_size(axis)
    return lax.ppermute(value, axis, [(i, i ^ by) for i in range(size)])


def exchanged(value, axis):
    return lax.all_to_all(value, axis, split_axis=0, concat_axis=0, tiled=True)


def masked_grad(grad, pre, slope):
    return jnp.where(pre > 0, grad, (wide(grad) * slope).astype(jnp.bfloat16))


def find_places(index, shuffle, blocks, slots, places, used):
    for i in range(used.shape[0]):
        used[i] = 0
    for block in range(blocks):
        owner = shuffle[index[0] * blocks + block] // blocks
        slot = used[owner]
        used[owner] = slot + 1
        places[block] = owner * slots + slot


def aggregate_kernel(
    reach, groups, send_slots, me, shuffle, cols, count, gc, pc, gx, px, slopes, adj, features, weight, *refs
):
    clean, outgoing, *refs = refs
    sides, packed, refs = refs[:4], refs[4 : 4 + groups], refs[4 + groups :]
    data, tiles, rhs, stage, results, halos, packs, places, used, sems, pack_sems, out_sems = refs
    blocks, slots, rows, _ = adj.shape
    width = gc.shape[1]
    quarter = features.shape[0] // groups
    spare = blocks + 2 * reach
    pad = 2 * reach * rows

    def copies(step):
        span = slice(2 * step, 2 * step + 2)
        out = [
            pltpu.make_async_copy(
                ref.at[2 * step * rows : (2 * step + 2) * rows], data.at[i, step], sems.at[i, step]
            )
            for i, ref in enumerate((gc, pc, gx, px))
        ]
        return out + [pltpu.make_async_copy(adj.at[span], tiles.at[span], sems.at[4, step])]

    inputs = [copies(step) for step in range(blocks // 2)]
    for copy in sum(inputs, []):
        copy.start()
    to_vmem, to_hbm = [], []
    for i in range(groups):
        span = pl.ds(pl.multiple_of((me[1] ^ i) * quarter, quarter), quarter)
        to_vmem.append(
            pltpu.make_async_copy(features.at[span], packs.at[i, :quarter], pack_sems.at[0, i])
        )
        to_vmem.append(pltpu.make_async_copy(weight, packs.at[i, quarter:], pack_sems.at[1, i]))
        to_hbm.append(pltpu.make_async_copy(packs.at[i], packed[i], pack_sems.at[2, i]))
    for copy in to_vmem:
        copy.start()
    stage[...] = jnp.zeros_like(stage)
    rhs[:pad] = jnp.zeros((pad, 2 * width), jnp.bfloat16)
    rhs[pad + blocks * rows :] = jnp.zeros((pad, 2 * width), jnp.bfloat16)
    shape = (rows, rows)
    identity = (
        lax.broadcasted_iota(jnp.int32, shape, 0) == lax.broadcasted_iota(jnp.int32, shape, 1)
    ).astype(jnp.float32).astype(jnp.bfloat16)
    slope = slopes[...]
    find_places(me, shuffle, blocks, send_slots, places, used)

    def take(step):
        gradients = [masked_grad(data[i, step], data[i + 1, step], slope) for i in (0, 2)]
        rhs[pad + 2 * step * rows : pad + (2 * step + 2) * rows] = jnp.concatenate(gradients, axis=1)
        turned = lax.dot_general(
            identity,
            tiles[2 * step : 2 * step + 2].reshape(2 * slots * rows, rows),
            (((1,), (1,)), ((), ())),
            preferred_element_type=jnp.float32,
        )
        for i in range(2 * slots):
            block, k = 2 * step + i // slots, i % slots
            live = k < count[block]
            target = cols[k, block] - me[0] * blocks
            place = jnp.where(live, target + reach, spare)
            distance = jnp.where(live, block - target + reach, 0)
            part = turned[:, i * rows : (i + 1) * rows]
            stage[place, distance] = (wide(stage[place, distance]) + part).astype(jnp.bfloat16)

    blank = jnp.zeros(shape, jnp.bfloat16)

    def pair(first):
        lhs = jnp.concatenate(
            [
                jnp.concatenate(
                    [blank] * i + [stage[first + i, j] for j in range(2 * reach + 1)] + [blank] * (1 - i),
                    axis=1,
                )
                for i in range(2)
            ],
            axis=0,
        )
        span = slice(first * rows, (first + 2 * reach + 2) * rows)
        product = jnp.dot(lhs, rhs[span], preferred_element_type=jnp.float32)
        product = product.astype(jnp.bfloat16).reshape(2, rows, 2 * width)
        return product[:, :, :width], product[:, :, width:]

    writes = []

    def finish(first):
        block = first - reach
        if 0 <= block < blocks:
            span = slice(block, block + 2)
            results[0, span], results[1, span] = pair(first)
            done = [pltpu.make_async_copy(results.at[0, span], clean.at[span], out_sems.at[0, block])]
            for i in range(block, block + 2):
                target = outgoing.at[places[i]]
                done.append(pltpu.make_async_copy(results.at[1, i], target, out_sems.at[1, i]))
        else:
            side, at = int(block >= 0), first % (blocks + reach)
            halos[side, 0, at : at + 2], halos[side, 1, at : at + 2] = pair(first)
            done = []
            for i in range(2):
                source, target = halos.at[side, i, at : at + 2], sides[2 * i + side].at[at : at + 2]
                done.append(pltpu.make_async_copy(source, target, out_sems.at[2 + i, first]))
        for copy in done:
            copy.start()
        writes.extend(done)

    for step in range(blocks // 2):
        for copy in inputs[step]:
            copy.wait()
        if step:
            finish(2 * step - 2)
        take(step)
    for copy in to_vmem:
        copy.wait()
    for copy in to_hbm:
        copy.start()
    for first in range(blocks + 2 * reach - 2, blocks - 4, -2):
        finish(first)
    for copy in writes + to_hbm:
        copy.wait()


def aggregate(index, shuffle, cols, count, gc, pc, gx, px, slopes, adj, features, weight, reach, devs, groups):
    blocks, slots, rows, _ = adj.shape
    width = gc.shape[1]
    send_slots = -(-blocks // devs)
    assert reach % 2 == 0 and blocks % 2 == 0
    packed = features.shape[0] // groups + weight.shape[0]
    return pl.pallas_call(
        functools.partial(aggregate_kernel, reach, groups, send_slots),
        in_specs=[IN_SMEM] * 4 + [IN_HBM] * 4 + [IN_VMEM] + [IN_HBM] * 3,
        out_specs=[IN_HBM] * (6 + groups),
        out_shape=[bf16(blocks, rows, width), bf16(devs * send_slots, rows, width)]
        + [bf16(reach, rows, width)] * 4
        + [bf16(packed, width)] * groups,
        scratch_shapes=[
            pltpu.VMEM((4, blocks // 2, 2 * rows, width), jnp.bfloat16),
            pltpu.VMEM((blocks, slots, rows, rows), jnp.bfloat16),
            pltpu.VMEM(((blocks + 4 * reach) * rows, 2 * width), jnp.bfloat16),
            pltpu.VMEM((blocks + 2 * reach + 1, 2 * reach + 1, rows, rows), jnp.bfloat16),
            pltpu.VMEM((2, blocks, rows, width), jnp.bfloat16),
            pltpu.VMEM((2, 2, reach, rows, width), jnp.bfloat16),
            pltpu.VMEM((groups, packed, width), jnp.bfloat16),
            pltpu.SMEM((blocks,), jnp.int32),
            pltpu.SMEM((devs,), jnp.int32),
            pltpu.SemaphoreType.DMA((5, blocks // 2)),
            pltpu.SemaphoreType.DMA((3, groups)),
            pltpu.SemaphoreType.DMA((4, blocks + 2 * reach)),
        ],
        compiler_params=params(VMEM_ALL),
        cost_estimate=pl.CostEstimate(
            flops=4 * blocks * slots * rows * rows * width,
            bytes_accessed=12 * blocks * rows * width + 2 * blocks * slots * rows * rows,
            transcendentals=0,
        ),
        name="aggregate",
    )(index, shuffle, cols, count, gc, pc, gx, px, slopes, adj, features, weight)


def patch_kernel(reach, blocks, slots, index, shuffle, outgoing, low, high, out, *scratch):
    held, other, ready, places, used, sems = scratch
    arrivals = [
        pltpu.make_async_copy(side, other.at[i * reach : (i + 1) * reach], sems.at[2, i])
        for i, side in enumerate((low, high))
    ]
    for copy in arrivals:
        copy.start()
    find_places(index, shuffle, blocks, slots, places, used)
    border = [*range(reach), *range(blocks - reach, blocks)]
    reads, writes = [], []
    for i, block in enumerate(border):
        place = places[block]
        reads.append(pltpu.make_async_copy(outgoing.at[place], held.at[i], sems.at[0, i]))
        writes.append(pltpu.make_async_copy(ready.at[i], out.at[place], sems.at[1, i]))
    for copy in reads:
        copy.start()
    for copy in arrivals:
        copy.wait()
    for i, (read, write) in enumerate(zip(reads, writes)):
        read.wait()
        ready[i] = (wide(held[i]) + wide(other[i])).astype(jnp.bfloat16)
        write.start()
    for copy in writes:
        copy.wait()


def patch(index, shuffle, outgoing, low, high, blocks, slots):
    sent, rows, width = outgoing.shape
    reach = low.shape[0]
    border = pltpu.VMEM((2 * reach, rows, width), jnp.bfloat16)
    return pl.pallas_call(
        functools.partial(patch_kernel, reach, blocks, slots),
        in_specs=[IN_SMEM] * 2 + [IN_HBM] * 3,
        out_specs=IN_HBM,
        out_shape=bf16(*outgoing.shape),
        input_output_aliases={2: 0},
        scratch_shapes=[
            border,
            border,
            border,
            pltpu.SMEM((blocks,), jnp.int32),
            pltpu.SMEM((sent // slots,), jnp.int32),
            pltpu.SemaphoreType.DMA((3, 2 * reach)),
        ],
        compiler_params=params(VMEM_ALL),
        name="patch",
    )(index, shuffle, outgoing, low, high)


def merge_kernel(quarter, index, landing, clean, low, high, incoming, out, whole):
    blocks, rows, _ = clean.shape
    reach = low.shape[0]
    group = index[1]
    piece = math.gcd(rows, quarter)
    for block in range(blocks):
        whole[block] = wide(clean[block])
    for i in range(reach):
        whole[i] += wide(low[i])
        whole[blocks - reach + i] += wide(high[i])
    for place in range(incoming.shape[0]):
        block = landing[place]

        @pl.when(block >= 0)
        def _():
            total = (whole[block] + wide(incoming[place])).astype(jnp.bfloat16)
            for part in range(rows // piece):
                at = block * (rows // piece) + part
                owner = at // (quarter // piece)
                offset = (at - owner * (quarter // piece)) * piece
                out[owner ^ group, pl.ds(pl.multiple_of(offset, piece), piece)] = total[
                    part * piece : (part + 1) * piece
                ]


def merge(index, landing, clean, low, high, incoming, groups):
    blocks, rows, width = clean.shape
    quarter = blocks * rows // groups
    return pl.pallas_call(
        functools.partial(merge_kernel, quarter),
        in_specs=[IN_SMEM] * 2 + [IN_VMEM] * 4,
        out_specs=IN_VMEM,
        out_shape=bf16(groups, quarter, width),
        scratch_shapes=[pltpu.VMEM((blocks, rows, width), jnp.float32)],
        compiler_params=params(),
        name="merge",
    )(index, landing, clean, low, high, incoming)


def weight_kernel(devs, index, *refs):
    groups = (len(refs) - 2) // 2
    packed, summed, (keep, send) = refs[:groups], refs[groups : 2 * groups], refs[2 * groups :]
    me, group = index[0], index[1]
    shares = devs // groups
    height, width = keep.shape[2:]
    rhs = jnp.concatenate([piece[...] for piece in summed], axis=1)
    for relative in range(groups):
        product = lax.dot_general(
            packed[relative][: rhs.shape[0]],
            rhs,
            (((0,), (0,)), ((), ())),
            preferred_element_type=jnp.float32,
        ).astype(jnp.bfloat16)
        for share in range(shares):
            node = ((group ^ relative) * shares + share) ^ me
            rows = product[share * height : (share + 1) * height]

            def store(out):
                for i in range(groups):
                    out[node >> 1, i] = rows[:, i * width : (i + 1) * width]

            pl.when((node & 1) == 0)(functools.partial(store, keep))
            pl.when((node & 1) == 1)(functools.partial(store, send))


def weight_partial(index, packed, summed, devs):
    groups = len(packed)
    rows, width = summed[0].shape
    height = groups * width // devs
    return pl.pallas_call(
        functools.partial(weight_kernel, devs),
        in_specs=[IN_SMEM] + [IN_VMEM] * (2 * groups),
        out_specs=[IN_VMEM] * 2,
        out_shape=[bf16(devs // 2, groups, height, width)] * 2,
        compiler_params=params(),
        cost_estimate=pl.CostEstimate(
            flops=2 * rows * (groups * width) ** 2,
            bytes_accessed=2 * (groups * width) ** 2 + 4 * groups * rows * width,
            transcendentals=0,
        ),
        name="weight_partial",
    )(index, *packed, *summed)


def feature_kernel(first, index, *refs):
    *summed, even, odd, out = refs
    groups = len(summed)
    devs = 2 * even.shape[0]
    me, group = index[0], index[1]
    shares = devs // groups
    height = even.shape[2]
    low = me & (shares - 1)
    lhs = jnp.concatenate([piece[...] for piece in summed], axis=1)
    for relative in range(first, first + out.shape[0]):
        rows = []
        for i in range(shares):
            node = (((group ^ relative) * shares) ^ (me - low)) + i
            half = odd if i % 2 else even
            rows.append(jnp.concatenate([half[node >> 1, j] for j in range(groups)], axis=1))
        product = lax.dot_general(
            lhs,
            jnp.concatenate(rows, axis=0),
            (((1,), (1,)), ((), ())),
            preferred_element_type=jnp.float32,
        ).astype(jnp.bfloat16)
        parts = [product[:, i * height : (i + 1) * height] for i in range(shares)]

        def store(flip):
            out[relative - first] = jnp.concatenate([parts[i ^ flip] for i in range(shares)], axis=1)

        for flip in range(shares):
            pl.when(low == flip)(functools.partial(store, flip))


def feature_rows(index, summed, even, odd, first, count):
    groups = len(summed)
    rows, width = summed[0].shape
    return pl.pallas_call(
        functools.partial(feature_kernel, first),
        in_specs=[IN_SMEM] + [IN_VMEM] * (groups + 2),
        out_specs=IN_VMEM,
        out_shape=bf16(count, rows, width),
        compiler_params=params(),
        cost_estimate=pl.CostEstimate(
            flops=2 * rows * groups * count * width**2,
            bytes_accessed=2 * groups * count * width**2 + 2 * (groups + count) * rows * width,
            transcendentals=0,
        ),
        name="feature_rows",
    )(index, *summed, even, odd)


def gather_kernel(index, *refs):
    *pieces, out, sems = refs
    rows = pieces[0].shape[0]
    copies = [
        pltpu.make_async_copy(
            piece, out.at[pl.ds(pl.multiple_of((index[1] ^ i) * rows, rows), rows)], sems.at[i]
        )
        for i, piece in enumerate(pieces)
    ]
    for copy in copies:
        copy.start()
    for copy in copies:
        copy.wait()


def laid_out(index, pieces):
    rows, width = pieces[0].shape
    return pl.pallas_call(
        gather_kernel,
        in_specs=[IN_SMEM] + [IN_VMEM] * len(pieces),
        out_specs=IN_HBM,
        out_shape=bf16(len(pieces) * rows, width),
        scratch_shapes=[pltpu.SemaphoreType.DMA((len(pieces),))],
        compiler_params=params(),
        name="laid_out",
    )(index, *pieces)


def landing_blocks(shuffle_from, me, blocks, devs, slots):
    owner = (shuffle_from // blocks).reshape(devs, blocks)
    within = (shuffle_from % blocks).reshape(devs, blocks)
    for_me = owner == me
    earlier = jnp.arange(blocks)[None, :] < jnp.arange(blocks)[:, None]
    rank = jnp.sum((for_me[:, None, :] & earlier[None]).astype(jnp.int32), axis=2)
    picked = for_me[:, None, :] & (rank[:, None, :] == jnp.arange(slots)[None, :, None])
    return (jnp.sum(jnp.where(picked, within[:, None, :] + 1, 0), axis=2) - 1).reshape(-1)


def exchange_order(groups):
    return sorted(range(1, groups), reverse=True)


def local(
    features,
    weight,
    pre_clean,
    pre_corrupt,
    grad_clean,
    grad_corrupt,
    slopes,
    adj_vals,
    adj_cols,
    adj_count,
    shuffle_from,
):
    row_count = features.shape[0]
    blocks, tile_slots, _, _ = adj_vals.shape
    reach = (tile_slots - 1) // 2
    me = lax.axis_index("node")
    group = lax.axis_index("chan")
    devs = lax.axis_size("node")
    groups = lax.axis_size("chan")
    slots = -(-blocks // devs)
    index = jnp.stack([me, group])

    args = (index, shuffle_from, adj_cols.T, adj_count)
    args += (grad_clean, pre_clean, grad_corrupt, pre_corrupt, slopes[None, :], adj_vals)
    clean, outgoing, *sides = aggregate(*args, features, weight, reach, devs, groups)
    sides, packed = sides[:4], sides[4:]
    low, high = shifted(sides[3], "node", 1), shifted(sides[2], "node", -1)
    for i in exchange_order(groups):
        packed[i] = swapped(packed[i], "chan", i)

    outgoing = patch(index, shuffle_from, outgoing, low, high, blocks, slots)
    shuffle_from, outgoing, clean, sides = lax.optimization_barrier(
        (shuffle_from, outgoing, clean, sides)
    )
    low, high = shifted(sides[1], "node", 1), shifted(sides[0], "node", -1)
    landing = landing_blocks(shuffle_from, me, blocks, devs, slots)
    incoming = exchanged(outgoing, "node")
    incoming, packed = lax.optimization_barrier((incoming, packed))
    merged = merge(index, landing, clean, low, high, incoming, groups)

    quarter = row_count // groups
    summed = [merged[0]] + [None] * (groups - 1)
    for i in exchange_order(groups):
        summed[i] = swapped(merged[i], "chan", i)
    tiles = jnp.stack([piece[quarter:] for piece in packed])
    even = [tiles] + [swapped(tiles, "node", 2 * i) for i in range(1, devs // 2)]
    even = jnp.stack(even)
    summed, even = lax.optimization_barrier((summed, even))
    odd = swapped(even, "node", 1)

    keep, send = weight_partial(index, packed, summed, devs)
    odd, send = lax.optimization_barrier((odd, send))
    arrived = swapped(send, "node", 1)
    sent = feature_rows(index, summed, even, odd, 1, groups - 1)
    arrived, sent, summed, even, odd = lax.optimization_barrier((arrived, sent, summed, even, odd))
    pieces = [feature_rows(index, summed, even, odd, 0, 1)[0]] + [None] * (groups - 1)
    for i in exchange_order(groups):
        pieces[i] = swapped(sent[i - 1], "chan", i)
    total = wide(keep) + wide(arrived)
    share = total[0]
    for i in range(1, devs // 2):
        share = share + wide(swapped(total[i].astype(jnp.bfloat16), "node", 2 * i))
    grad_weight = share[0]
    for i in range(1, groups):
        grad_weight = grad_weight + wide(swapped(share[i].astype(jnp.bfloat16), "chan", i))
    return (grad_weight, laid_out(index, pieces))


def solution(mesh):
    placed = (
        P("node", "chan"),
        P("node", "chan"),
        P("node", "chan"),
        P("node", "chan"),
        P("node", "chan"),
        P("node", "chan"),
        P("chan"),
        P("node", None, None, None),
        P("node", None),
        P("node"),
        P(),
    )
    return jax.shard_map(
        local,
        mesh=mesh,
        in_specs=placed,
        out_specs=(P("node", "chan"), P("node", "chan")),
        check_vma=False,
    )
```

```python
import functools
import math

import jax
import jax.numpy as jnp
from jax import lax
from jax.experimental import pallas as pl
from jax.experimental.pallas import tpu as pltpu
from jax.sharding import PartitionSpec as P

VMEM_LIMIT = 32 * 1024 * 1024
VMEM_ALL = 61 * 1024 * 1024
IN_VMEM = pl.BlockSpec(memory_space=pltpu.VMEM)
IN_SMEM = pl.BlockSpec(memory_space=pltpu.SMEM)
IN_HBM = pl.BlockSpec(memory_space=pltpu.HBM)


def params(limit=VMEM_LIMIT):
    return pltpu.CompilerParams(vmem_limit_bytes=limit)


def bf16(*shape):
    return jax.ShapeDtypeStruct(shape, jnp.bfloat16)


def wide(value):
    return value.astype(jnp.float32)


def shifted(value, axis, by):
    size = lax.axis_size(axis)
    pairs = [(i, i + by) for i in range(size) if 0 <= i + by < size]
    return lax.ppermute(value, axis, pairs)


def swapped(value, axis, by):
    size = lax.axis_size(axis)
    return lax.ppermute(value, axis, [(i, i ^ by) for i in range(size)])


def exchanged(value, axis):
    return lax.all_to_all(value, axis, split_axis=0, concat_axis=0, tiled=True)


def masked_grad(grad, pre, slope):
    return jnp.where(pre > 0, grad, (wide(grad) * slope).astype(jnp.bfloat16))


def find_places(index, shuffle, blocks, slots, places, used):
    for i in range(used.shape[0]):
        used[i] = 0
    for block in range(blocks):
        owner = shuffle[index[0] * blocks + block] // blocks
        slot = used[owner]
        used[owner] = slot + 1
        places[block] = owner * slots + slot


def aggregate_kernel(
    reach, groups, send_slots, me, shuffle, cols, count, gc, pc, gx, px, slopes, adj, features, weight, *refs
):
    clean, outgoing, *refs = refs
    sides, packed, refs = refs[:4], refs[4 : 4 + groups], refs[4 + groups :]
    data, tiles, rhs, stage, results, halos, packs, places, used, sems, pack_sems, out_sems = refs
    blocks, slots, rows, _ = adj.shape
    width = gc.shape[1]
    quarter = features.shape[0] // groups
    spare = blocks + 2 * reach
    pad = 2 * reach * rows

    def copies(step):
        span = slice(2 * step, 2 * step + 2)
        out = [
            pltpu.make_async_copy(
                ref.at[2 * step * rows : (2 * step + 2) * rows], data.at[i, step], sems.at[i, step]
            )
            for i, ref in enumerate((gc, pc, gx, px))
        ]
        return out + [pltpu.make_async_copy(adj.at[span], tiles.at[span], sems.at[4, step])]

    inputs = [copies(step) for step in range(blocks // 2)]
    for copy in sum(inputs, []):
        copy.start()
    to_vmem, to_hbm = [], []
    for i in range(groups):
        span = pl.ds(pl.multiple_of((me[1] ^ i) * quarter, quarter), quarter)
        to_vmem.append(
            pltpu.make_async_copy(features.at[span], packs.at[i, :quarter], pack_sems.at[0, i])
        )
        to_vmem.append(pltpu.make_async_copy(weight, packs.at[i, quarter:], pack_sems.at[1, i]))
        to_hbm.append(pltpu.make_async_copy(packs.at[i], packed[i], pack_sems.at[2, i]))
    for copy in to_vmem:
        copy.start()
    stage[...] = jnp.zeros_like(stage)
    rhs[:pad] = jnp.zeros((pad, 2 * width), jnp.bfloat16)
    rhs[pad + blocks * rows :] = jnp.zeros((pad, 2 * width), jnp.bfloat16)
    shape = (rows, rows)
    identity = (
        lax.broadcasted_iota(jnp.int32, shape, 0) == lax.broadcasted_iota(jnp.int32, shape, 1)
    ).astype(jnp.float32).astype(jnp.bfloat16)
    slope = slopes[...]
    find_places(me, shuffle, blocks, send_slots, places, used)

    def take(step):
        gradients = [masked_grad(data[i, step], data[i + 1, step], slope) for i in (0, 2)]
        rhs[pad + 2 * step * rows : pad + (2 * step + 2) * rows] = jnp.concatenate(gradients, axis=1)
        turned = lax.dot_general(
            identity,
            tiles[2 * step : 2 * step + 2].reshape(2 * slots * rows, rows),
            (((1,), (1,)), ((), ())),
            preferred_element_type=jnp.float32,
        )
        for i in range(2 * slots):
            block, k = 2 * step + i // slots, i % slots
            live = k < count[block]
            target = cols[k, block] - me[0] * blocks
            place = jnp.where(live, target + reach, spare)
            distance = jnp.where(live, block - target + reach, 0)
            part = turned[:, i * rows : (i + 1) * rows]
            stage[place, distance] = (wide(stage[place, distance]) + part).astype(jnp.bfloat16)

    blank = jnp.zeros(shape, jnp.bfloat16)

    def pair(first):
        lhs = jnp.concatenate(
            [
                jnp.concatenate(
                    [blank] * i + [stage[first + i, j] for j in range(2 * reach + 1)] + [blank] * (1 - i),
                    axis=1,
                )
                for i in range(2)
            ],
            axis=0,
        )
        span = slice(first * rows, (first + 2 * reach + 2) * rows)
        product = jnp.dot(lhs, rhs[span], preferred_element_type=jnp.float32)
        product = product.astype(jnp.bfloat16).reshape(2, rows, 2 * width)
        return product[:, :, :width], product[:, :, width:]

    writes = []

    def finish(first):
        block = first - reach
        if 0 <= block < blocks:
            span = slice(block, block + 2)
            results[0, span], results[1, span] = pair(first)
            done = [pltpu.make_async_copy(results.at[0, span], clean.at[span], out_sems.at[0, block])]
            for i in range(block, block + 2):
                target = outgoing.at[places[i]]
                done.append(pltpu.make_async_copy(results.at[1, i], target, out_sems.at[1, i]))
        else:
            side, at = int(block >= 0), first % (blocks + reach)
            halos[side, 0, at : at + 2], halos[side, 1, at : at + 2] = pair(first)
            done = []
            for i in range(2):
                source, target = halos.at[side, i, at : at + 2], sides[2 * i + side].at[at : at + 2]
                done.append(pltpu.make_async_copy(source, target, out_sems.at[2 + i, first]))
        for copy in done:
            copy.start()
        writes.extend(done)

    for step in range(blocks // 2):
        for copy in inputs[step]:
            copy.wait()
        if step:
            finish(2 * step - 2)
        take(step)
    for copy in to_vmem:
        copy.wait()
    for copy in to_hbm:
        copy.start()
    for first in range(blocks + 2 * reach - 2, blocks - 4, -2):
        finish(first)
    for copy in writes + to_hbm:
        copy.wait()


def aggregate(index, shuffle, cols, count, gc, pc, gx, px, slopes, adj, features, weight, reach, devs, groups):
    blocks, slots, rows, _ = adj.shape
    width = gc.shape[1]
    send_slots = -(-blocks // devs)
    assert reach % 2 == 0 and blocks % 2 == 0
    packed = features.shape[0] // groups + weight.shape[0]
    return pl.pallas_call(
        functools.partial(aggregate_kernel, reach, groups, send_slots),
        in_specs=[IN_SMEM] * 4 + [IN_HBM] * 4 + [IN_VMEM] + [IN_HBM] * 3,
        out_specs=[IN_HBM] * (6 + groups),
        out_shape=[bf16(blocks, rows, width), bf16(devs * send_slots, rows, width)]
        + [bf16(reach, rows, width)] * 4
        + [bf16(packed, width)] * groups,
        scratch_shapes=[
            pltpu.VMEM((4, blocks // 2, 2 * rows, width), jnp.bfloat16),
            pltpu.VMEM((blocks, slots, rows, rows), jnp.bfloat16),
            pltpu.VMEM(((blocks + 4 * reach) * rows, 2 * width), jnp.bfloat16),
            pltpu.VMEM((blocks + 2 * reach + 1, 2 * reach + 1, rows, rows), jnp.bfloat16),
            pltpu.VMEM((2, blocks, rows, width), jnp.bfloat16),
            pltpu.VMEM((2, 2, reach, rows, width), jnp.bfloat16),
            pltpu.VMEM((groups, packed, width), jnp.bfloat16),
            pltpu.SMEM((blocks,), jnp.int32),
            pltpu.SMEM((devs,), jnp.int32),
            pltpu.SemaphoreType.DMA((5, blocks // 2)),
            pltpu.SemaphoreType.DMA((3, groups)),
            pltpu.SemaphoreType.DMA((4, blocks + 2 * reach)),
        ],
        compiler_params=params(VMEM_ALL),
        cost_estimate=pl.CostEstimate(
            flops=4 * blocks * slots * rows * rows * width,
            bytes_accessed=12 * blocks * rows * width + 2 * blocks * slots * rows * rows,
            transcendentals=0,
        ),
        name="aggregate",
    )(index, shuffle, cols, count, gc, pc, gx, px, slopes, adj, features, weight)


def patch_kernel(reach, blocks, slots, index, shuffle, outgoing, low, high, out, *scratch):
    held, other, ready, places, used, sems = scratch
    arrivals = [
        pltpu.make_async_copy(side, other.at[i * reach : (i + 1) * reach], sems.at[2, i])
        for i, side in enumerate((low, high))
    ]
    for copy in arrivals:
        copy.start()
    find_places(index, shuffle, blocks, slots, places, used)
    border = [*range(reach), *range(blocks - reach, blocks)]
    reads, writes = [], []
    for i, block in enumerate(border):
        place = places[block]
        reads.append(pltpu.make_async_copy(outgoing.at[place], held.at[i], sems.at[0, i]))
        writes.append(pltpu.make_async_copy(ready.at[i], out.at[place], sems.at[1, i]))
    for copy in reads:
        copy.start()
    for copy in arrivals:
        copy.wait()
    for i, (read, write) in enumerate(zip(reads, writes)):
        read.wait()
        ready[i] = (wide(held[i]) + wide(other[i])).astype(jnp.bfloat16)
        write.start()
    for copy in writes:
        copy.wait()


def patch(index, shuffle, outgoing, low, high, blocks, slots):
    sent, rows, width = outgoing.shape
    reach = low.shape[0]
    border = pltpu.VMEM((2 * reach, rows, width), jnp.bfloat16)
    return pl.pallas_call(
        functools.partial(patch_kernel, reach, blocks, slots),
        in_specs=[IN_SMEM] * 2 + [IN_HBM] * 3,
        out_specs=IN_HBM,
        out_shape=bf16(*outgoing.shape),
        input_output_aliases={2: 0},
        scratch_shapes=[
            border,
            border,
            border,
            pltpu.SMEM((blocks,), jnp.int32),
            pltpu.SMEM((sent // slots,), jnp.int32),
            pltpu.SemaphoreType.DMA((3, 2 * reach)),
        ],
        compiler_params=params(VMEM_ALL),
        name="patch",
    )(index, shuffle, outgoing, low, high)


def merge_kernel(quarter, index, landing, clean, low, high, incoming, *refs):
    *packed, out, tiles, whole = refs
    blocks, rows, _ = clean.shape
    for i, piece in enumerate(packed):
        tiles[i] = piece[quarter:]
    reach = low.shape[0]
    group = index[1]
    piece = math.gcd(rows, quarter)
    for block in range(blocks):
        whole[block] = wide(clean[block])
    for i in range(reach):
        whole[i] += wide(low[i])
        whole[blocks - reach + i] += wide(high[i])
    for place in range(incoming.shape[0]):
        block = landing[place]

        @pl.when(block >= 0)
        def _():
            total = (whole[block] + wide(incoming[place])).astype(jnp.bfloat16)
            for part in range(rows // piece):
                at = block * (rows // piece) + part
                owner = at // (quarter // piece)
                offset = (at - owner * (quarter // piece)) * piece
                out[owner ^ group, pl.ds(pl.multiple_of(offset, piece), piece)] = total[
                    part * piece : (part + 1) * piece
                ]


def merge(index, landing, clean, low, high, incoming, packed):
    blocks, rows, width = clean.shape
    groups = len(packed)
    quarter = blocks * rows // groups
    height = packed[0].shape[0] - quarter
    return pl.pallas_call(
        functools.partial(merge_kernel, quarter),
        in_specs=[IN_SMEM] * 2 + [IN_VMEM] * (4 + groups),
        out_specs=[IN_VMEM] * 2,
        out_shape=[bf16(groups, quarter, width), bf16(groups, height, width)],
        scratch_shapes=[pltpu.VMEM((blocks, rows, width), jnp.float32)],
        compiler_params=params(),
        name="merge",
    )(index, landing, clean, low, high, incoming, *packed)


def weight_kernel(devs, index, *refs):
    groups = (len(refs) - 2) // 2
    packed, summed, (keep, send) = refs[:groups], refs[groups : 2 * groups], refs[2 * groups :]
    me, group = index[0], index[1]
    shares = devs // groups
    height, width = keep.shape[2:]
    rhs = jnp.concatenate([piece[...] for piece in summed], axis=1)
    for relative in range(groups):
        product = lax.dot_general(
            packed[relative][: rhs.shape[0]],
            rhs,
            (((0,), (0,)), ((), ())),
            preferred_element_type=jnp.float32,
        ).astype(jnp.bfloat16)
        for share in range(shares):
            node = ((group ^ relative) * shares + share) ^ me
            rows = product[share * height : (share + 1) * height]

            def store(out):
                for i in range(groups):
                    out[node >> 1, i] = rows[:, i * width : (i + 1) * width]

            pl.when((node & 1) == 0)(functools.partial(store, keep))
            pl.when((node & 1) == 1)(functools.partial(store, send))


def weight_partial(index, packed, summed, devs):
    groups = len(packed)
    rows, width = summed[0].shape
    height = groups * width // devs
    return pl.pallas_call(
        functools.partial(weight_kernel, devs),
        in_specs=[IN_SMEM] + [IN_VMEM] * (2 * groups),
        out_specs=[IN_VMEM] * 2,
        out_shape=[bf16(devs // 2, groups, height, width)] * 2,
        compiler_params=params(),
        cost_estimate=pl.CostEstimate(
            flops=2 * rows * (groups * width) ** 2,
            bytes_accessed=2 * (groups * width) ** 2 + 4 * groups * rows * width,
            transcendentals=0,
        ),
        name="weight_partial",
    )(index, *packed, *summed)


def feature_kernel(first, index, *refs):
    *summed, even, odd, out = refs
    groups = len(summed)
    devs = 2 * even.shape[0]
    me, group = index[0], index[1]
    shares = devs // groups
    height = even.shape[2]
    low = me & (shares - 1)
    lhs = jnp.concatenate([piece[...] for piece in summed], axis=1)
    for relative in range(first, first + out.shape[0]):
        rows = []
        for i in range(shares):
            node = (((group ^ relative) * shares) ^ (me - low)) + i
            half = odd if i % 2 else even
            rows.append(jnp.concatenate([half[node >> 1, j] for j in range(groups)], axis=1))
        product = lax.dot_general(
            lhs,
            jnp.concatenate(rows, axis=0),
            (((1,), (1,)), ((), ())),
            preferred_element_type=jnp.float32,
        ).astype(jnp.bfloat16)
        parts = [product[:, i * height : (i + 1) * height] for i in range(shares)]

        def store(flip):
            out[relative - first] = jnp.concatenate([parts[i ^ flip] for i in range(shares)], axis=1)

        for flip in range(shares):
            pl.when(low == flip)(functools.partial(store, flip))


def feature_rows(index, summed, even, odd, first, count):
    groups = len(summed)
    rows, width = summed[0].shape
    return pl.pallas_call(
        functools.partial(feature_kernel, first),
        in_specs=[IN_SMEM] + [IN_VMEM] * (groups + 2),
        out_specs=IN_VMEM,
        out_shape=bf16(count, rows, width),
        compiler_params=params(),
        cost_estimate=pl.CostEstimate(
            flops=2 * rows * groups * count * width**2,
            bytes_accessed=2 * groups * count * width**2 + 2 * (groups + count) * rows * width,
            transcendentals=0,
        ),
        name="feature_rows",
    )(index, *summed, even, odd)


def gather_kernel(index, *refs):
    *pieces, out, sems = refs
    rows = pieces[0].shape[0]
    copies = [
        pltpu.make_async_copy(
            piece, out.at[pl.ds(pl.multiple_of((index[1] ^ i) * rows, rows), rows)], sems.at[i]
        )
        for i, piece in enumerate(pieces)
    ]
    for copy in copies:
        copy.start()
    for copy in copies:
        copy.wait()


def laid_out(index, pieces):
    rows, width = pieces[0].shape
    return pl.pallas_call(
        gather_kernel,
        in_specs=[IN_SMEM] + [IN_VMEM] * len(pieces),
        out_specs=IN_HBM,
        out_shape=bf16(len(pieces) * rows, width),
        scratch_shapes=[pltpu.SemaphoreType.DMA((len(pieces),))],
        compiler_params=params(),
        name="laid_out",
    )(index, *pieces)


def landing_blocks(shuffle_from, me, blocks, devs, slots):
    owner = (shuffle_from // blocks).reshape(devs, blocks)
    within = (shuffle_from % blocks).reshape(devs, blocks)
    for_me = owner == me
    earlier = jnp.arange(blocks)[None, :] < jnp.arange(blocks)[:, None]
    rank = jnp.sum((for_me[:, None, :] & earlier[None]).astype(jnp.int32), axis=2)
    picked = for_me[:, None, :] & (rank[:, None, :] == jnp.arange(slots)[None, :, None])
    return (jnp.sum(jnp.where(picked, within[:, None, :] + 1, 0), axis=2) - 1).reshape(-1)


def exchange_order(groups):
    return sorted(range(1, groups), reverse=True)


def local(
    features,
    weight,
    pre_clean,
    pre_corrupt,
    grad_clean,
    grad_corrupt,
    slopes,
    adj_vals,
    adj_cols,
    adj_count,
    shuffle_from,
):
    row_count = features.shape[0]
    blocks, tile_slots, _, _ = adj_vals.shape
    reach = (tile_slots - 1) // 2
    me = lax.axis_index("node")
    group = lax.axis_index("chan")
    devs = lax.axis_size("node")
    groups = lax.axis_size("chan")
    slots = -(-blocks // devs)
    index = jnp.stack([me, group])

    args = (index, shuffle_from, adj_cols.T, adj_count)
    args += (grad_clean, pre_clean, grad_corrupt, pre_corrupt, slopes[None, :], adj_vals)
    clean, outgoing, *sides = aggregate(*args, features, weight, reach, devs, groups)
    sides, packed = sides[:4], sides[4:]
    low, high = shifted(sides[3], "node", 1), shifted(sides[2], "node", -1)
    for i in exchange_order(groups):
        packed[i] = swapped(packed[i], "chan", i)

    outgoing = patch(index, shuffle_from, outgoing, low, high, blocks, slots)
    shuffle_from, outgoing, clean, sides = lax.optimization_barrier(
        (shuffle_from, outgoing, clean, sides)
    )
    low, high = shifted(sides[1], "node", 1), shifted(sides[0], "node", -1)
    landing = landing_blocks(shuffle_from, me, blocks, devs, slots)
    incoming = exchanged(outgoing, "node")
    incoming, packed = lax.optimization_barrier((incoming, packed))
    merged, tiles = merge(index, landing, clean, low, high, incoming, packed)

    summed = [merged[0]] + [None] * (groups - 1)
    for i in exchange_order(groups):
        summed[i] = swapped(merged[i], "chan", i)
    even = [tiles] + [swapped(tiles, "node", 2 * i) for i in range(1, devs // 2)]
    even = jnp.stack(even)
    summed, even = lax.optimization_barrier((summed, even))
    odd = swapped(even, "node", 1)

    keep, send = weight_partial(index, packed, summed, devs)
    odd, send = lax.optimization_barrier((odd, send))
    arrived = swapped(send, "node", 1)
    sent = feature_rows(index, summed, even, odd, 1, groups - 1)
    arrived, sent, summed, even, odd = lax.optimization_barrier((arrived, sent, summed, even, odd))
    pieces = [feature_rows(index, summed, even, odd, 0, 1)[0]] + [None] * (groups - 1)
    for i in exchange_order(groups):
        pieces[i] = swapped(sent[i - 1], "chan", i)
    total = wide(keep) + wide(arrived)
    share = total[0]
    for i in range(1, devs // 2):
        share = share + wide(swapped(total[i].astype(jnp.bfloat16), "node", 2 * i))
    grad_weight = share[0]
    for i in range(1, groups):
        grad_weight = grad_weight + wide(swapped(share[i].astype(jnp.bfloat16), "chan", i))
    return (grad_weight, laid_out(index, pieces))


def solution(mesh):
    placed = (
        P("node", "chan"),
        P("node", "chan"),
        P("node", "chan"),
        P("node", "chan"),
        P("node", "chan"),
        P("node", "chan"),
        P("chan"),
        P("node", None, None, None),
        P("node", None),
        P("node"),
        P(),
    )
    return jax.shard_map(
        local,
        mesh=mesh,
        in_specs=placed,
        out_specs=(P("node", "chan"), P("node", "chan")),
        check_vma=False,
    )
```

```python
import functools
import math

import jax
import jax.numpy as jnp
from jax import lax
from jax.experimental import pallas as pl
from jax.experimental.pallas import tpu as pltpu
from jax.sharding import PartitionSpec as P

VMEM_LIMIT = 32 * 1024 * 1024
VMEM_ALL = 61 * 1024 * 1024
IN_VMEM = pl.BlockSpec(memory_space=pltpu.VMEM)
IN_SMEM = pl.BlockSpec(memory_space=pltpu.SMEM)
IN_HBM = pl.BlockSpec(memory_space=pltpu.HBM)


def params(limit=VMEM_LIMIT):
    return pltpu.CompilerParams(vmem_limit_bytes=limit)


def bf16(*shape):
    return jax.ShapeDtypeStruct(shape, jnp.bfloat16)


def wide(value):
    return value.astype(jnp.float32)


def shifted(value, axis, by):
    size = lax.axis_size(axis)
    pairs = [(i, i + by) for i in range(size) if 0 <= i + by < size]
    return lax.ppermute(value, axis, pairs)


def swapped(value, axis, by):
    size = lax.axis_size(axis)
    return lax.ppermute(value, axis, [(i, i ^ by) for i in range(size)])


def exchanged(value, axis):
    return lax.all_to_all(value, axis, split_axis=0, concat_axis=0, tiled=True)


def masked_grad(grad, pre, slope):
    return jnp.where(pre > 0, grad, (wide(grad) * slope).astype(jnp.bfloat16))


def find_places(index, shuffle, blocks, slots, places, used):
    for i in range(used.shape[0]):
        used[i] = 0
    for block in range(blocks):
        owner = shuffle[index[0] * blocks + block] // blocks
        slot = used[owner]
        used[owner] = slot + 1
        places[block] = owner * slots + slot


def aggregate_kernel(
    reach, groups, send_slots, shuffle, cols, count, gc, pc, gx, px, slopes, adj, features, weight, *refs
):
    clean, outgoing, *refs = refs
    sides, packed, refs = refs[:4], refs[4 : 4 + groups], refs[4 + groups :]
    data, tiles, rhs, stage, results, halos, packs, places, used, sems, pack_sems, out_sems = refs
    blocks, slots, rows, _ = adj.shape
    width = gc.shape[1]
    me = (lax.axis_index("node"), lax.axis_index("chan"))
    quarter = features.shape[0] // groups
    spare = blocks + 2 * reach
    pad = 2 * reach * rows

    def copies(step):
        span = slice(2 * step, 2 * step + 2)
        out = [
            pltpu.make_async_copy(
                ref.at[2 * step * rows : (2 * step + 2) * rows], data.at[i, step], sems.at[i, step]
            )
            for i, ref in enumerate((gc, pc, gx, px))
        ]
        return out + [pltpu.make_async_copy(adj.at[span], tiles.at[span], sems.at[4, step])]

    inputs = [copies(step) for step in range(blocks // 2)]
    ahead = 3
    for copy in sum(inputs[:ahead], []):
        copy.start()
    to_vmem, to_hbm = [], []
    for i in range(groups):
        span = pl.ds(pl.multiple_of((me[1] ^ i) * quarter, quarter), quarter)
        to_vmem.append(
            pltpu.make_async_copy(features.at[span], packs.at[i, :quarter], pack_sems.at[0, i])
        )
        to_vmem.append(pltpu.make_async_copy(weight, packs.at[i, quarter:], pack_sems.at[1, i]))
        to_hbm.append(pltpu.make_async_copy(packs.at[i], packed[i], pack_sems.at[2, i]))
    stage[...] = jnp.zeros_like(stage)
    rhs[:pad] = jnp.zeros((pad, 2 * width), jnp.bfloat16)
    rhs[pad + blocks * rows :] = jnp.zeros((pad, 2 * width), jnp.bfloat16)
    shape = (rows, rows)
    identity = (
        lax.broadcasted_iota(jnp.int32, shape, 0) == lax.broadcasted_iota(jnp.int32, shape, 1)
    ).astype(jnp.float32).astype(jnp.bfloat16)
    slope = slopes[...]
    find_places(me, shuffle, blocks, send_slots, places, used)

    def take(step):
        gradients = [masked_grad(data[i, step], data[i + 1, step], slope) for i in (0, 2)]
        rhs[pad + 2 * step * rows : pad + (2 * step + 2) * rows] = jnp.concatenate(gradients, axis=1)
        turned = lax.dot_general(
            identity,
            tiles[2 * step : 2 * step + 2].reshape(2 * slots * rows, rows),
            (((1,), (1,)), ((), ())),
            preferred_element_type=jnp.float32,
        )
        for i in range(2 * slots):
            block, k = 2 * step + i // slots, i % slots
            live = k < count[block]
            target = cols[k, block] - me[0] * blocks
            place = jnp.where(live, target + reach, spare)
            distance = jnp.where(live, block - target + reach, 0)
            part = turned[:, i * rows : (i + 1) * rows]
            stage[place, distance] = (wide(stage[place, distance]) + part).astype(jnp.bfloat16)

    blank = jnp.zeros(shape, jnp.bfloat16)

    def pair(first):
        lhs = jnp.concatenate(
            [
                jnp.concatenate(
                    [blank] * i + [stage[first + i, j] for j in range(2 * reach + 1)] + [blank] * (1 - i),
                    axis=1,
                )
                for i in range(2)
            ],
            axis=0,
        )
        span = slice(first * rows, (first + 2 * reach + 2) * rows)
        product = jnp.dot(lhs, rhs[span], preferred_element_type=jnp.float32)
        product = product.astype(jnp.bfloat16).reshape(2, rows, 2 * width)
        return product[:, :, :width], product[:, :, width:]

    writes = []

    def finish(first):
        block = first - reach
        if 0 <= block < blocks:
            span = slice(block, block + 2)
            results[0, span], results[1, span] = pair(first)
            done = [pltpu.make_async_copy(results.at[0, span], clean.at[span], out_sems.at[0, block])]
            for i in range(block, block + 2):
                target = outgoing.at[places[i]]
                done.append(pltpu.make_async_copy(results.at[1, i], target, out_sems.at[1, i]))
        else:
            side, at = int(block >= 0), first % (blocks + reach)
            halos[side, 0, at : at + 2], halos[side, 1, at : at + 2] = pair(first)
            done = []
            for i in range(2):
                source, target = halos.at[side, i, at : at + 2], sides[2 * i + side].at[at : at + 2]
                done.append(pltpu.make_async_copy(source, target, out_sems.at[2 + i, first]))
        for copy in done:
            copy.start()
        writes.extend(done)

    for step in range(blocks // 2):
        for copy in inputs[step]:
            copy.wait()
        for copy in inputs[step + ahead] if step + ahead < blocks // 2 else []:
            copy.start()
        if step == 1:
            for copy in to_vmem:
                copy.start()
        if step:
            finish(2 * step - 2)
        take(step)
    for copy in to_vmem:
        copy.wait()
    for copy in to_hbm:
        copy.start()
    for first in range(blocks + 2 * reach - 2, blocks - 4, -2):
        finish(first)
    for copy in writes + to_hbm:
        copy.wait()


def aggregate(shuffle, cols, count, gc, pc, gx, px, slopes, adj, features, weight, reach, devs, groups):
    blocks, slots, rows, _ = adj.shape
    width = gc.shape[1]
    send_slots = -(-blocks // devs)
    assert reach % 2 == 0 and blocks % 2 == 0
    packed = features.shape[0] // groups + weight.shape[0]
    return pl.pallas_call(
        functools.partial(aggregate_kernel, reach, groups, send_slots),
        in_specs=[IN_SMEM] * 3 + [IN_HBM] * 4 + [IN_VMEM] + [IN_HBM] * 3,
        out_specs=[IN_HBM] * (6 + groups),
        out_shape=[bf16(blocks, rows, width), bf16(devs * send_slots, rows, width)]
        + [bf16(reach, rows, width)] * 4
        + [bf16(packed, width)] * groups,
        scratch_shapes=[
            pltpu.VMEM((4, blocks // 2, 2 * rows, width), jnp.bfloat16),
            pltpu.VMEM((blocks, slots, rows, rows), jnp.bfloat16),
            pltpu.VMEM(((blocks + 4 * reach) * rows, 2 * width), jnp.bfloat16),
            pltpu.VMEM((blocks + 2 * reach + 1, 2 * reach + 1, rows, rows), jnp.bfloat16),
            pltpu.VMEM((2, blocks, rows, width), jnp.bfloat16),
            pltpu.VMEM((2, 2, reach, rows, width), jnp.bfloat16),
            pltpu.VMEM((groups, packed, width), jnp.bfloat16),
            pltpu.SMEM((blocks,), jnp.int32),
            pltpu.SMEM((devs,), jnp.int32),
            pltpu.SemaphoreType.DMA((5, blocks // 2)),
            pltpu.SemaphoreType.DMA((3, groups)),
            pltpu.SemaphoreType.DMA((4, blocks + 2 * reach)),
        ],
        compiler_params=params(VMEM_ALL),
        cost_estimate=pl.CostEstimate(
            flops=4 * blocks * slots * rows * rows * width,
            bytes_accessed=12 * blocks * rows * width + 2 * blocks * slots * rows * rows,
            transcendentals=0,
        ),
        name="aggregate",
    )(shuffle, cols, count, gc, pc, gx, px, slopes, adj, features, weight)


def patch_kernel(reach, blocks, slots, index, shuffle, outgoing, low, high, out, *scratch):
    held, other, ready, places, used, sems = scratch
    arrivals = [
        pltpu.make_async_copy(side, other.at[i * reach : (i + 1) * reach], sems.at[2, i])
        for i, side in enumerate((low, high))
    ]
    for copy in arrivals:
        copy.start()
    find_places(index, shuffle, blocks, slots, places, used)
    border = [*range(reach), *range(blocks - reach, blocks)]
    reads, writes = [], []
    for i, block in enumerate(border):
        place = places[block]
        reads.append(pltpu.make_async_copy(outgoing.at[place], held.at[i], sems.at[0, i]))
        writes.append(pltpu.make_async_copy(ready.at[i], out.at[place], sems.at[1, i]))
    for copy in reads:
        copy.start()
    for copy in arrivals:
        copy.wait()
    for i, (read, write) in enumerate(zip(reads, writes)):
        read.wait()
        ready[i] = (wide(held[i]) + wide(other[i])).astype(jnp.bfloat16)
        write.start()
    for copy in writes:
        copy.wait()


def patch(index, shuffle, outgoing, low, high, blocks, slots):
    sent, rows, width = outgoing.shape
    reach = low.shape[0]
    border = pltpu.VMEM((2 * reach, rows, width), jnp.bfloat16)
    return pl.pallas_call(
        functools.partial(patch_kernel, reach, blocks, slots),
        in_specs=[IN_SMEM] * 2 + [IN_HBM] * 3,
        out_specs=IN_HBM,
        out_shape=bf16(*outgoing.shape),
        input_output_aliases={2: 0},
        scratch_shapes=[
            border,
            border,
            border,
            pltpu.SMEM((blocks,), jnp.int32),
            pltpu.SMEM((sent // slots,), jnp.int32),
            pltpu.SemaphoreType.DMA((3, 2 * reach)),
        ],
        compiler_params=params(VMEM_ALL),
        name="patch",
    )(index, shuffle, outgoing, low, high)


def merge_kernel(quarter, index, landing, clean, low, high, incoming, out, whole):
    blocks, rows, _ = clean.shape
    reach = low.shape[0]
    group = index[1]
    piece = math.gcd(rows, quarter)
    for block in range(blocks):
        whole[block] = wide(clean[block])
    for i in range(reach):
        whole[i] += wide(low[i])
        whole[blocks - reach + i] += wide(high[i])
    for place in range(incoming.shape[0]):
        block = landing[place]

        @pl.when(block >= 0)
        def _():
            total = (whole[block] + wide(incoming[place])).astype(jnp.bfloat16)
            for part in range(rows // piece):
                at = block * (rows // piece) + part
                owner = at // (quarter // piece)
                offset = (at - owner * (quarter // piece)) * piece
                out[owner ^ group, pl.ds(pl.multiple_of(offset, piece), piece)] = total[
                    part * piece : (part + 1) * piece
                ]


def merge(index, landing, clean, low, high, incoming, groups):
    blocks, rows, width = clean.shape
    quarter = blocks * rows // groups
    return pl.pallas_call(
        functools.partial(merge_kernel, quarter),
        in_specs=[IN_SMEM] * 2 + [IN_VMEM] * 4,
        out_specs=IN_VMEM,
        out_shape=bf16(groups, quarter, width),
        scratch_shapes=[pltpu.VMEM((blocks, rows, width), jnp.float32)],
        compiler_params=params(),
        name="merge",
    )(index, landing, clean, low, high, incoming)


def weight_kernel(devs, index, *refs):
    groups = (len(refs) - 2) // 2
    packed, summed, (keep, send) = refs[:groups], refs[groups : 2 * groups], refs[2 * groups :]
    me, group = index[0], index[1]
    shares = devs // groups
    height, width = keep.shape[2:]
    rhs = jnp.concatenate([piece[...] for piece in summed], axis=1)
    for relative in range(groups):
        product = lax.dot_general(
            packed[relative][: rhs.shape[0]],
            rhs,
            (((0,), (0,)), ((), ())),
            preferred_element_type=jnp.float32,
        ).astype(jnp.bfloat16)
        for share in range(shares):
            node = ((group ^ relative) * shares + share) ^ me
            rows = product[share * height : (share + 1) * height]

            def store(out):
                for i in range(groups):
                    out[node >> 1, i] = rows[:, i * width : (i + 1) * width]

            pl.when((node & 1) == 0)(functools.partial(store, keep))
            pl.when((node & 1) == 1)(functools.partial(store, send))


def weight_partial(index, packed, summed, devs):
    groups = len(packed)
    rows, width = summed[0].shape
    height = groups * width // devs
    return pl.pallas_call(
        functools.partial(weight_kernel, devs),
        in_specs=[IN_SMEM] + [IN_VMEM] * (2 * groups),
        out_specs=[IN_VMEM] * 2,
        out_shape=[bf16(devs // 2, groups, height, width)] * 2,
        compiler_params=params(),
        cost_estimate=pl.CostEstimate(
            flops=2 * rows * (groups * width) ** 2,
            bytes_accessed=2 * (groups * width) ** 2 + 4 * groups * rows * width,
            transcendentals=0,
        ),
        name="weight_partial",
    )(index, *packed, *summed)


def feature_kernel(first, index, *refs):
    *summed, even, odd, out = refs
    groups = len(summed)
    devs = 2 * even.shape[0]
    me, group = index[0], index[1]
    shares = devs // groups
    height = even.shape[2]
    low = me & (shares - 1)
    lhs = jnp.concatenate([piece[...] for piece in summed], axis=1)
    for relative in range(first, first + out.shape[0]):
        rows = []
        for i in range(shares):
            node = (((group ^ relative) * shares) ^ (me - low)) + i
            half = odd if i % 2 else even
            rows.append(jnp.concatenate([half[node >> 1, j] for j in range(groups)], axis=1))
        product = lax.dot_general(
            lhs,
            jnp.concatenate(rows, axis=0),
            (((1,), (1,)), ((), ())),
            preferred_element_type=jnp.float32,
        ).astype(jnp.bfloat16)
        parts = [product[:, i * height : (i + 1) * height] for i in range(shares)]

        def store(flip):
            out[relative - first] = jnp.concatenate([parts[i ^ flip] for i in range(shares)], axis=1)

        for flip in range(shares):
            pl.when(low == flip)(functools.partial(store, flip))


def feature_rows(index, summed, even, odd, first, count):
    groups = len(summed)
    rows, width = summed[0].shape
    return pl.pallas_call(
        functools.partial(feature_kernel, first),
        in_specs=[IN_SMEM] + [IN_VMEM] * (groups + 2),
        out_specs=IN_VMEM,
        out_shape=bf16(count, rows, width),
        compiler_params=params(),
        cost_estimate=pl.CostEstimate(
            flops=2 * rows * groups * count * width**2,
            bytes_accessed=2 * groups * count * width**2 + 2 * (groups + count) * rows * width,
            transcendentals=0,
        ),
        name="feature_rows",
    )(index, *summed, even, odd)


def gather_kernel(index, *refs):
    *pieces, out, sems = refs
    rows = pieces[0].shape[0]
    copies = [
        pltpu.make_async_copy(
            piece, out.at[pl.ds(pl.multiple_of((index[1] ^ i) * rows, rows), rows)], sems.at[i]
        )
        for i, piece in enumerate(pieces)
    ]
    for copy in copies:
        copy.start()
    for copy in copies:
        copy.wait()


def laid_out(index, pieces):
    rows, width = pieces[0].shape
    return pl.pallas_call(
        gather_kernel,
        in_specs=[IN_SMEM] + [IN_VMEM] * len(pieces),
        out_specs=IN_HBM,
        out_shape=bf16(len(pieces) * rows, width),
        scratch_shapes=[pltpu.SemaphoreType.DMA((len(pieces),))],
        compiler_params=params(),
        name="laid_out",
    )(index, *pieces)


def landing_blocks(shuffle_from, me, blocks, devs, slots):
    owner = (shuffle_from // blocks).reshape(devs, blocks)
    within = (shuffle_from % blocks).reshape(devs, blocks)
    for_me = owner == me
    earlier = jnp.arange(blocks)[None, :] < jnp.arange(blocks)[:, None]
    rank = jnp.sum((for_me[:, None, :] & earlier[None]).astype(jnp.int32), axis=2)
    picked = for_me[:, None, :] & (rank[:, None, :] == jnp.arange(slots)[None, :, None])
    return (jnp.sum(jnp.where(picked, within[:, None, :] + 1, 0), axis=2) - 1).reshape(-1)


def exchange_order(groups):
    return sorted(range(1, groups), reverse=True)


def local(
    features,
    weight,
    pre_clean,
    pre_corrupt,
    grad_clean,
    grad_corrupt,
    slopes,
    adj_vals,
    adj_cols,
    adj_count,
    shuffle_from,
):
    row_count = features.shape[0]
    blocks, tile_slots, _, _ = adj_vals.shape
    reach = (tile_slots - 1) // 2
    me = lax.axis_index("node")
    group = lax.axis_index("chan")
    devs = lax.axis_size("node")
    groups = lax.axis_size("chan")
    slots = -(-blocks // devs)
    index = jnp.stack([me, group])

    args = (shuffle_from, adj_cols.T, adj_count)
    args += (grad_clean, pre_clean, grad_corrupt, pre_corrupt, slopes[None, :], adj_vals)
    clean, outgoing, *sides = aggregate(*args, features, weight, reach, devs, groups)
    sides, packed = sides[:4], sides[4:]
    low, high = shifted(sides[3], "node", 1), shifted(sides[2], "node", -1)
    for i in exchange_order(groups):
        packed[i] = swapped(packed[i], "chan", i)

    outgoing = patch(index, shuffle_from, outgoing, low, high, blocks, slots)
    shuffle_from, outgoing, clean, sides = lax.optimization_barrier(
        (shuffle_from, outgoing, clean, sides)
    )
    low, high = shifted(sides[1], "node", 1), shifted(sides[0], "node", -1)
    landing = landing_blocks(shuffle_from, me, blocks, devs, slots)
    incoming = exchanged(outgoing, "node")
    incoming, packed = lax.optimization_barrier((incoming, packed))
    merged = merge(index, landing, clean, low, high, incoming, groups)

    quarter = row_count // groups
    summed = [merged[0]] + [None] * (groups - 1)
    for i in exchange_order(groups):
        summed[i] = swapped(merged[i], "chan", i)
    tiles = jnp.stack([piece[quarter:] for piece in packed])
    even = [tiles] + [swapped(tiles, "node", 2 * i) for i in range(1, devs // 2)]
    order = [0, *range(2, groups - 1), 1, groups - 1]
    listed, even = lax.optimization_barrier(([summed[i] for i in order], even))
    summed = [listed[order.index(i)] for i in range(groups)]
    even = jnp.stack(even)
    odd = swapped(even, "node", 1)

    keep, send = weight_partial(index, packed, summed, devs)
    odd, send = lax.optimization_barrier((odd, send))
    arrived = swapped(send, "node", 1)
    sent = feature_rows(index, summed, even, odd, 1, groups - 1)
    arrived, sent, summed, even, odd = lax.optimization_barrier((arrived, sent, summed, even, odd))
    pieces = [feature_rows(index, summed, even, odd, 0, 1)[0]] + [None] * (groups - 1)
    for i in exchange_order(groups):
        pieces[i] = swapped(sent[i - 1], "chan", i)
    total = wide(keep) + wide(arrived)
    share = total[0]
    for i in range(1, devs // 2):
        share = share + wide(swapped(total[i].astype(jnp.bfloat16), "node", 2 * i))
    grad_weight = share[0]
    for i in range(1, groups):
        grad_weight = grad_weight + wide(swapped(share[i].astype(jnp.bfloat16), "chan", i))
    return (grad_weight, laid_out(index, pieces))


def solution(mesh):
    placed = (
        P("node", "chan"),
        P("node", "chan"),
        P("node", "chan"),
        P("node", "chan"),
        P("node", "chan"),
        P("node", "chan"),
        P("chan"),
        P("node", None, None, None),
        P("node", None),
        P("node"),
        P(),
    )
    return jax.shard_map(
        local,
        mesh=mesh,
        in_specs=placed,
        out_specs=(P("node", "chan"), P("node", "chan")),
        check_vma=False,
    )
```

```python
import functools
import math

import jax
import jax.numpy as jnp
from jax import lax
from jax.experimental import pallas as pl
from jax.experimental.pallas import tpu as pltpu
from jax.sharding import PartitionSpec as P

VMEM_LIMIT = 32 * 1024 * 1024
VMEM_ALL = 61 * 1024 * 1024
IN_VMEM = pl.BlockSpec(memory_space=pltpu.VMEM)
IN_SMEM = pl.BlockSpec(memory_space=pltpu.SMEM)
IN_HBM = pl.BlockSpec(memory_space=pltpu.HBM)


def params(limit=VMEM_LIMIT):
    return pltpu.CompilerParams(vmem_limit_bytes=limit)


def bf16(*shape):
    return jax.ShapeDtypeStruct(shape, jnp.bfloat16)


def wide(value):
    return value.astype(jnp.float32)


def shifted(value, axis, by):
    size = lax.axis_size(axis)
    pairs = [(i, i + by) for i in range(size) if 0 <= i + by < size]
    return lax.ppermute(value, axis, pairs)


def swapped(value, axis, by):
    size = lax.axis_size(axis)
    return lax.ppermute(value, axis, [(i, i ^ by) for i in range(size)])


def exchanged(value, axis):
    return lax.all_to_all(value, axis, split_axis=0, concat_axis=0, tiled=True)


def masked_grad(grad, pre, slope):
    return jnp.where(pre > 0, grad, grad * slope)


def find_places(index, shuffle, blocks, slots, places, used):
    for i in range(used.shape[0]):
        used[i] = 0
    for block in range(blocks):
        owner = shuffle[index[0] * blocks + block] // blocks
        slot = used[owner]
        used[owner] = slot + 1
        places[block] = owner * slots + slot


def aggregate_kernel(
    reach, groups, send_slots, shuffle, cols, count, gc, pc, gx, px, slopes, adj, features, weight, *refs
):
    clean, outgoing, *refs = refs
    sides, packed, refs = refs[:4], refs[4 : 4 + groups], refs[4 + groups :]
    data, tiles, rhs, stage, results, halos, packs, places, used, sems, pack_sems, out_sems = refs
    blocks, slots, rows, _ = adj.shape
    width = gc.shape[1]
    me = (lax.axis_index("node"), lax.axis_index("chan"))
    quarter = features.shape[0] // groups
    spare = blocks + 2 * reach

    def copies(step):
        span = slice(2 * step, 2 * step + 2)
        out = [
            pltpu.make_async_copy(
                ref.at[2 * step * rows : (2 * step + 2) * rows], data.at[i, step], sems.at[i, step]
            )
            for i, ref in enumerate((gc, pc, gx, px))
        ]
        return out + [pltpu.make_async_copy(adj.at[span], tiles.at[span], sems.at[4, step])]

    inputs = [copies(step) for step in range(blocks // 2)]
    ahead = 3
    for copy in sum(inputs[:ahead], []):
        copy.start()
    to_vmem, to_hbm = [], []
    for i in range(groups):
        span = pl.ds(pl.multiple_of((me[1] ^ i) * quarter, quarter), quarter)
        to_vmem.append(
            pltpu.make_async_copy(features.at[span], packs.at[i, :quarter], pack_sems.at[0, i])
        )
        to_vmem.append(pltpu.make_async_copy(weight, packs.at[i, quarter:], pack_sems.at[1, i]))
        to_hbm.append(pltpu.make_async_copy(packs.at[i], packed[i], pack_sems.at[2, i]))
    stage[...] = jnp.zeros_like(stage)
    shape = (rows, rows)
    identity = (
        lax.broadcasted_iota(jnp.int32, shape, 0) == lax.broadcasted_iota(jnp.int32, shape, 1)
    ).astype(jnp.float32).astype(jnp.bfloat16)
    slope = slopes[...].astype(jnp.bfloat16)
    find_places(me, shuffle, blocks, send_slots, places, used)

    def take(step):
        gradients = [masked_grad(data[i, step], data[i + 1, step], slope) for i in (0, 2)]
        rhs[2 * step * rows : (2 * step + 2) * rows] = jnp.concatenate(gradients, axis=1)
        turned = lax.dot_general(
            identity,
            tiles[2 * step : 2 * step + 2].reshape(2 * slots * rows, rows),
            (((1,), (1,)), ((), ())),
            preferred_element_type=jnp.float32,
        )
        for i in range(2 * slots):
            block, k = 2 * step + i // slots, i % slots
            live = k < count[block]
            target = cols[k, block] - me[0] * blocks
            place = jnp.where(live, target + reach, spare)
            distance = jnp.where(live, block - target + reach, 0)
            stage[place, distance] += turned[:, i * rows : (i + 1) * rows].astype(jnp.bfloat16)

    blank = jnp.zeros(shape, jnp.bfloat16)

    def pair(first):
        targets = [first - reach, first - reach + 1]
        sources = range(max(0, targets[0] - reach), min(blocks, targets[1] + reach + 1))

        def tile(i, source):
            distance = source - targets[i] + reach
            return stage[first + i, distance] if 0 <= distance <= 2 * reach else blank

        lhs = jnp.concatenate(
            [jnp.concatenate([tile(i, b) for b in sources], axis=1) for i in range(2)], axis=0
        )
        span = slice(sources.start * rows, sources.stop * rows)
        product = jnp.dot(lhs, rhs[span], preferred_element_type=jnp.float32)
        product = product.astype(jnp.bfloat16).reshape(2, rows, 2 * width)
        return product[:, :, :width], product[:, :, width:]

    writes = []

    def finish(first):
        block = first - reach
        if 0 <= block < blocks:
            span = slice(block, block + 2)
            results[0, span], results[1, span] = pair(first)
            done = [pltpu.make_async_copy(results.at[0, span], clean.at[span], out_sems.at[0, block])]
            for i in range(block, block + 2):
                target = outgoing.at[places[i]]
                done.append(pltpu.make_async_copy(results.at[1, i], target, out_sems.at[1, i]))
        else:
            side, at = int(block >= 0), first % (blocks + reach)
            halos[side, 0, at : at + 2], halos[side, 1, at : at + 2] = pair(first)
            done = []
            for i in range(2):
                source, target = halos.at[side, i, at : at + 2], sides[2 * i + side].at[at : at + 2]
                done.append(pltpu.make_async_copy(source, target, out_sems.at[2 + i, first]))
        for copy in done:
            copy.start()
        writes.extend(done)

    for step in range(blocks // 2):
        for copy in inputs[step]:
            copy.wait()
        for copy in inputs[step + ahead] if step + ahead < blocks // 2 else []:
            copy.start()
        if step == 1:
            for copy in to_vmem:
                copy.start()
        if step:
            finish(2 * step - 2)
        take(step)
    for copy in to_vmem:
        copy.wait()
    for copy in to_hbm:
        copy.start()
    for first in range(blocks + 2 * reach - 2, blocks - 4, -2):
        finish(first)
    for copy in writes + to_hbm:
        copy.wait()


def aggregate(shuffle, cols, count, gc, pc, gx, px, slopes, adj, features, weight, reach, devs, groups):
    blocks, slots, rows, _ = adj.shape
    width = gc.shape[1]
    send_slots = -(-blocks // devs)
    assert reach % 2 == 0 and blocks % 2 == 0
    packed = features.shape[0] // groups + weight.shape[0]
    return pl.pallas_call(
        functools.partial(aggregate_kernel, reach, groups, send_slots),
        in_specs=[IN_SMEM] * 3 + [IN_HBM] * 4 + [IN_VMEM] + [IN_HBM] * 3,
        out_specs=[IN_HBM] * (6 + groups),
        out_shape=[bf16(blocks, rows, width), bf16(devs * send_slots, rows, width)]
        + [bf16(reach, rows, width)] * 4
        + [bf16(packed, width)] * groups,
        scratch_shapes=[
            pltpu.VMEM((4, blocks // 2, 2 * rows, width), jnp.bfloat16),
            pltpu.VMEM((blocks, slots, rows, rows), jnp.bfloat16),
            pltpu.VMEM((blocks * rows, 2 * width), jnp.bfloat16),
            pltpu.VMEM((blocks + 2 * reach + 1, 2 * reach + 1, rows, rows), jnp.bfloat16),
            pltpu.VMEM((2, blocks, rows, width), jnp.bfloat16),
            pltpu.VMEM((2, 2, reach, rows, width), jnp.bfloat16),
            pltpu.VMEM((groups, packed, width), jnp.bfloat16),
            pltpu.SMEM((blocks,), jnp.int32),
            pltpu.SMEM((devs,), jnp.int32),
            pltpu.SemaphoreType.DMA((5, blocks // 2)),
            pltpu.SemaphoreType.DMA((3, groups)),
            pltpu.SemaphoreType.DMA((4, blocks + 2 * reach)),
        ],
        compiler_params=params(VMEM_ALL),
        cost_estimate=pl.CostEstimate(
            flops=4 * blocks * slots * rows * rows * width,
            bytes_accessed=12 * blocks * rows * width + 2 * blocks * slots * rows * rows,
            transcendentals=0,
        ),
        name="aggregate",
    )(shuffle, cols, count, gc, pc, gx, px, slopes, adj, features, weight)


def patch_kernel(reach, blocks, slots, index, shuffle, outgoing, low, high, out, *scratch):
    held, other, ready, places, used, sems = scratch
    arrivals = [
        pltpu.make_async_copy(side, other.at[i * reach : (i + 1) * reach], sems.at[2, i])
        for i, side in enumerate((low, high))
    ]
    for copy in arrivals:
        copy.start()
    find_places(index, shuffle, blocks, slots, places, used)
    border = [*range(reach), *range(blocks - reach, blocks)]
    reads, writes = [], []
    for i, block in enumerate(border):
        place = places[block]
        reads.append(pltpu.make_async_copy(outgoing.at[place], held.at[i], sems.at[0, i]))
        writes.append(pltpu.make_async_copy(ready.at[i], out.at[place], sems.at[1, i]))
    for copy in reads:
        copy.start()
    for copy in arrivals:
        copy.wait()
    for i, (read, write) in enumerate(zip(reads, writes)):
        read.wait()
        ready[i] = (wide(held[i]) + wide(other[i])).astype(jnp.bfloat16)
        write.start()
    for copy in writes:
        copy.wait()


def patch(index, shuffle, outgoing, low, high, blocks, slots):
    sent, rows, width = outgoing.shape
    reach = low.shape[0]
    border = pltpu.VMEM((2 * reach, rows, width), jnp.bfloat16)
    return pl.pallas_call(
        functools.partial(patch_kernel, reach, blocks, slots),
        in_specs=[IN_SMEM] * 2 + [IN_HBM] * 3,
        out_specs=IN_HBM,
        out_shape=bf16(*outgoing.shape),
        input_output_aliases={2: 0},
        scratch_shapes=[
            border,
            border,
            border,
            pltpu.SMEM((blocks,), jnp.int32),
            pltpu.SMEM((sent // slots,), jnp.int32),
            pltpu.SemaphoreType.DMA((3, 2 * reach)),
        ],
        compiler_params=params(VMEM_ALL),
        name="patch",
    )(index, shuffle, outgoing, low, high)


def merge_kernel(quarter, index, landing, clean, low, high, incoming, out, whole):
    blocks, rows, _ = clean.shape
    reach = low.shape[0]
    group = index[1]
    piece = math.gcd(rows, quarter)
    for block in range(blocks):
        whole[block] = wide(clean[block])
    for i in range(reach):
        whole[i] += wide(low[i])
        whole[blocks - reach + i] += wide(high[i])
    for place in range(incoming.shape[0]):
        block = landing[place]

        @pl.when(block >= 0)
        def _():
            total = (whole[block] + wide(incoming[place])).astype(jnp.bfloat16)
            for part in range(rows // piece):
                at = block * (rows // piece) + part
                owner = at // (quarter // piece)
                offset = (at - owner * (quarter // piece)) * piece
                out[owner ^ group, pl.ds(pl.multiple_of(offset, piece), piece)] = total[
                    part * piece : (part + 1) * piece
                ]


def merge(index, landing, clean, low, high, incoming, groups):
    blocks, rows, width = clean.shape
    quarter = blocks * rows // groups
    return pl.pallas_call(
        functools.partial(merge_kernel, quarter),
        in_specs=[IN_SMEM] * 2 + [IN_VMEM] * 4,
        out_specs=IN_VMEM,
        out_shape=bf16(groups, quarter, width),
        scratch_shapes=[pltpu.VMEM((blocks, rows, width), jnp.float32)],
        compiler_params=params(),
        name="merge",
    )(index, landing, clean, low, high, incoming)


def weight_kernel(devs, index, *refs):
    groups = (len(refs) - 2) // 2
    packed, summed, (keep, send) = refs[:groups], refs[groups : 2 * groups], refs[2 * groups :]
    me, group = index[0], index[1]
    shares = devs // groups
    height, width = keep.shape[2:]
    rhs = jnp.concatenate([piece[...] for piece in summed], axis=1)
    for relative in range(groups):
        product = lax.dot_general(
            packed[relative][: rhs.shape[0]],
            rhs,
            (((0,), (0,)), ((), ())),
            preferred_element_type=jnp.float32,
        ).astype(jnp.bfloat16)
        for share in range(shares):
            node = ((group ^ relative) * shares + share) ^ me
            rows = product[share * height : (share + 1) * height]

            def store(out):
                for i in range(groups):
                    out[node >> 1, i] = rows[:, i * width : (i + 1) * width]

            pl.when((node & 1) == 0)(functools.partial(store, keep))
            pl.when((node & 1) == 1)(functools.partial(store, send))


def weight_partial(index, packed, summed, devs):
    groups = len(packed)
    rows, width = summed[0].shape
    height = groups * width // devs
    return pl.pallas_call(
        functools.partial(weight_kernel, devs),
        in_specs=[IN_SMEM] + [IN_VMEM] * (2 * groups),
        out_specs=[IN_VMEM] * 2,
        out_shape=[bf16(devs // 2, groups, height, width)] * 2,
        compiler_params=params(),
        cost_estimate=pl.CostEstimate(
            flops=2 * rows * (groups * width) ** 2,
            bytes_accessed=2 * (groups * width) ** 2 + 4 * groups * rows * width,
            transcendentals=0,
        ),
        name="weight_partial",
    )(index, *packed, *summed)


def feature_kernel(first, index, *refs):
    *summed, even, odd, out = refs
    groups = len(summed)
    devs = 2 * even.shape[0]
    me, group = index[0], index[1]
    shares = devs // groups
    height = even.shape[2]
    low = me & (shares - 1)
    lhs = jnp.concatenate([piece[...] for piece in summed], axis=1)
    for relative in range(first, first + out.shape[0]):
        rows = []
        for i in range(shares):
            node = (((group ^ relative) * shares) ^ (me - low)) + i
            half = odd if i % 2 else even
            rows.append(jnp.concatenate([half[node >> 1, j] for j in range(groups)], axis=1))
        product = lax.dot_general(
            lhs,
            jnp.concatenate(rows, axis=0),
            (((1,), (1,)), ((), ())),
            preferred_element_type=jnp.float32,
        ).astype(jnp.bfloat16)
        parts = [product[:, i * height : (i + 1) * height] for i in range(shares)]

        def store(flip):
            out[relative - first] = jnp.concatenate([parts[i ^ flip] for i in range(shares)], axis=1)

        for flip in range(shares):
            pl.when(low == flip)(functools.partial(store, flip))


def feature_rows(index, summed, even, odd, first, count):
    groups = len(summed)
    rows, width = summed[0].shape
    return pl.pallas_call(
        functools.partial(feature_kernel, first),
        in_specs=[IN_SMEM] + [IN_VMEM] * (groups + 2),
        out_specs=IN_VMEM,
        out_shape=bf16(count, rows, width),
        compiler_params=params(),
        cost_estimate=pl.CostEstimate(
            flops=2 * rows * groups * count * width**2,
            bytes_accessed=2 * groups * count * width**2 + 2 * (groups + count) * rows * width,
            transcendentals=0,
        ),
        name="feature_rows",
    )(index, *summed, even, odd)


def gather_kernel(index, *refs):
    *pieces, out, sems = refs
    rows = pieces[0].shape[0]
    copies = [
        pltpu.make_async_copy(
            piece, out.at[pl.ds(pl.multiple_of((index[1] ^ i) * rows, rows), rows)], sems.at[i]
        )
        for i, piece in enumerate(pieces)
    ]
    for copy in copies:
        copy.start()
    for copy in copies:
        copy.wait()


def laid_out(index, pieces):
    rows, width = pieces[0].shape
    return pl.pallas_call(
        gather_kernel,
        in_specs=[IN_SMEM] + [IN_VMEM] * len(pieces),
        out_specs=IN_HBM,
        out_shape=bf16(len(pieces) * rows, width),
        scratch_shapes=[pltpu.SemaphoreType.DMA((len(pieces),))],
        compiler_params=params(),
        name="laid_out",
    )(index, *pieces)


def landing_blocks(shuffle_from, me, blocks, devs, slots):
    owner = (shuffle_from // blocks).reshape(devs, blocks)
    within = (shuffle_from % blocks).reshape(devs, blocks)
    for_me = owner == me
    earlier = jnp.arange(blocks)[None, :] < jnp.arange(blocks)[:, None]
    rank = jnp.sum((for_me[:, None, :] & earlier[None]).astype(jnp.int32), axis=2)
    picked = for_me[:, None, :] & (rank[:, None, :] == jnp.arange(slots)[None, :, None])
    return (jnp.sum(jnp.where(picked, within[:, None, :] + 1, 0), axis=2) - 1).reshape(-1)


def exchange_order(groups):
    return sorted(range(1, groups), reverse=True)


def local(
    features,
    weight,
    pre_clean,
    pre_corrupt,
    grad_clean,
    grad_corrupt,
    slopes,
    adj_vals,
    adj_cols,
    adj_count,
    shuffle_from,
):
    row_count = features.shape[0]
    blocks, tile_slots, _, _ = adj_vals.shape
    reach = (tile_slots - 1) // 2
    me = lax.axis_index("node")
    group = lax.axis_index("chan")
    devs = lax.axis_size("node")
    groups = lax.axis_size("chan")
    slots = -(-blocks // devs)
    index = jnp.stack([me, group])

    args = (shuffle_from, adj_cols.T, adj_count)
    args += (grad_clean, pre_clean, grad_corrupt, pre_corrupt, slopes[None, :], adj_vals)
    clean, outgoing, *sides = aggregate(*args, features, weight, reach, devs, groups)
    sides, packed = sides[:4], sides[4:]
    low, high = shifted(sides[3], "node", 1), shifted(sides[2], "node", -1)
    for i in exchange_order(groups):
        packed[i] = swapped(packed[i], "chan", i)

    outgoing = patch(index, shuffle_from, outgoing, low, high, blocks, slots)
    shuffle_from, outgoing, clean, sides = lax.optimization_barrier(
        (shuffle_from, outgoing, clean, sides)
    )
    low, high = shifted(sides[1], "node", 1), shifted(sides[0], "node", -1)
    landing = landing_blocks(shuffle_from, me, blocks, devs, slots)
    incoming = exchanged(outgoing, "node")
    incoming, packed = lax.optimization_barrier((incoming, packed))
    merged = merge(index, landing, clean, low, high, incoming, groups)

    quarter = row_count // groups
    summed = [merged[0]] + [None] * (groups - 1)
    for i in exchange_order(groups):
        summed[i] = swapped(merged[i], "chan", i)
    tiles = jnp.stack([piece[quarter:] for piece in packed])
    even = [tiles] + [swapped(tiles, "node", 2 * i) for i in range(1, devs // 2)]
    order = [0, *range(2, groups - 1), 1, groups - 1]
    listed, even = lax.optimization_barrier(([summed[i] for i in order], even))
    summed = [listed[order.index(i)] for i in range(groups)]
    even = jnp.stack(even)
    odd = swapped(even, "node", 1)

    keep, send = weight_partial(index, packed, summed, devs)
    odd, send = lax.optimization_barrier((odd, send))
    arrived = swapped(send, "node", 1)
    sent = feature_rows(index, summed, even, odd, 1, groups - 1)
    arrived, sent, summed, even, odd = lax.optimization_barrier((arrived, sent, summed, even, odd))
    pieces = [feature_rows(index, summed, even, odd, 0, 1)[0]] + [None] * (groups - 1)
    for i in exchange_order(groups):
        pieces[i] = swapped(sent[i - 1], "chan", i)
    total = wide(keep) + wide(arrived)
    share = total[0]
    for i in range(1, devs // 2):
        share = share + wide(swapped(total[i].astype(jnp.bfloat16), "node", 2 * i))
    grad_weight = share[0]
    for i in range(1, groups):
        grad_weight = grad_weight + wide(swapped(share[i].astype(jnp.bfloat16), "chan", i))
    return (grad_weight, laid_out(index, pieces))


def solution(mesh):
    placed = (
        P("node", "chan"),
        P("node", "chan"),
        P("node", "chan"),
        P("node", "chan"),
        P("node", "chan"),
        P("node", "chan"),
        P("chan"),
        P("node", None, None, None),
        P("node", None),
        P("node"),
        P(),
    )
    return jax.shard_map(
        local,
        mesh=mesh,
        in_specs=placed,
        out_specs=(P("node", "chan"), P("node", "chan")),
        check_vma=False,
    )
```

```python
import functools
import math

import jax
import jax.numpy as jnp
from jax import lax
from jax.experimental import pallas as pl
from jax.experimental.pallas import tpu as pltpu
from jax.sharding import PartitionSpec as P

VMEM_LIMIT = 32 * 1024 * 1024
VMEM_ALL = 61 * 1024 * 1024
IN_VMEM = pl.BlockSpec(memory_space=pltpu.VMEM)
IN_SMEM = pl.BlockSpec(memory_space=pltpu.SMEM)
IN_HBM = pl.BlockSpec(memory_space=pltpu.HBM)


def params(limit=VMEM_LIMIT):
    return pltpu.CompilerParams(vmem_limit_bytes=limit)


def bf16(*shape):
    return jax.ShapeDtypeStruct(shape, jnp.bfloat16)


def wide(value):
    return value.astype(jnp.float32)


def swapped_beside(value, axis):
    size = lax.axis_size(axis)
    pairs = [(i, (i + 1) % size) for i in range(1, size, 2)]
    return lax.ppermute(value, axis, pairs + [(j, i) for i, j in pairs])


def swapped(value, axis, by):
    size = lax.axis_size(axis)
    return lax.ppermute(value, axis, [(i, i ^ by) for i in range(size)])


def exchanged(value, axis):
    return lax.all_to_all(value, axis, split_axis=0, concat_axis=0, tiled=True)


def masked_grad(grad, pre, slope):
    return jnp.where(pre > 0, grad, grad * slope)


def find_places(index, shuffle, blocks, slots, places, used):
    for i in range(used.shape[0]):
        used[i] = 0
    for block in range(blocks):
        owner = shuffle[index[0] * blocks + block] // blocks
        slot = used[owner]
        used[owner] = slot + 1
        places[block] = owner * slots + slot


def aggregate_kernel(
    reach, groups, send_slots, shuffle, cols, count, gc, pc, gx, px, slopes, adj, features, weight, *refs
):
    clean, outgoing, *refs = refs
    sides, packed, refs = refs[:2], refs[2 : 2 + groups], refs[2 + groups :]
    data, tiles, rhs, stage, results, halos, packs, places, used, sems, pack_sems, out_sems = refs
    blocks, slots, rows, _ = adj.shape
    width = gc.shape[1]
    me = (lax.axis_index("node"), lax.axis_index("chan"))
    quarter = features.shape[0] // groups
    spare = blocks + 2 * reach

    def copies(step):
        span = slice(2 * step, 2 * step + 2)
        out = [
            pltpu.make_async_copy(
                ref.at[2 * step * rows : (2 * step + 2) * rows], data.at[i, step], sems.at[i, step]
            )
            for i, ref in enumerate((gc, pc, gx, px))
        ]
        return out + [pltpu.make_async_copy(adj.at[span], tiles.at[span], sems.at[4, step])]

    inputs = [copies(step) for step in range(blocks // 2)]
    ahead = 3
    for copy in sum(inputs[:ahead], []):
        copy.start()
    to_vmem, to_hbm = [], []
    for i in range(groups):
        span = pl.ds(pl.multiple_of((me[1] ^ i) * quarter, quarter), quarter)
        to_vmem.append(
            pltpu.make_async_copy(features.at[span], packs.at[i, :quarter], pack_sems.at[0, i])
        )
        to_vmem.append(pltpu.make_async_copy(weight, packs.at[i, quarter:], pack_sems.at[1, i]))
        to_hbm.append(pltpu.make_async_copy(packs.at[i], packed[i], pack_sems.at[2, i]))
    stage[...] = jnp.zeros_like(stage)
    shape = (rows, rows)
    identity = (
        lax.broadcasted_iota(jnp.int32, shape, 0) == lax.broadcasted_iota(jnp.int32, shape, 1)
    ).astype(jnp.float32).astype(jnp.bfloat16)
    slope = slopes[...].astype(jnp.bfloat16)
    find_places(me, shuffle, blocks, send_slots, places, used)

    def take(step):
        gradients = [masked_grad(data[i, step], data[i + 1, step], slope) for i in (0, 2)]
        rhs[2 * step * rows : (2 * step + 2) * rows] = jnp.concatenate(gradients, axis=1)
        turned = lax.dot_general(
            identity,
            tiles[2 * step : 2 * step + 2].reshape(2 * slots * rows, rows),
            (((1,), (1,)), ((), ())),
            preferred_element_type=jnp.float32,
        )
        for i in range(2 * slots):
            block, k = 2 * step + i // slots, i % slots
            live = k < count[block]
            target = cols[k, block] - me[0] * blocks
            place = jnp.where(live, target + reach, spare)
            distance = jnp.where(live, block - target + reach, 0)
            stage[place, distance] += turned[:, i * rows : (i + 1) * rows].astype(jnp.bfloat16)

    blank = jnp.zeros(shape, jnp.bfloat16)

    def pair(first):
        targets = [first - reach, first - reach + 1]
        sources = range(max(0, targets[0] - reach), min(blocks, targets[1] + reach + 1))

        def tile(i, source):
            distance = source - targets[i] + reach
            return stage[first + i, distance] if 0 <= distance <= 2 * reach else blank

        lhs = jnp.concatenate(
            [jnp.concatenate([tile(i, b) for b in sources], axis=1) for i in range(2)], axis=0
        )
        span = slice(sources.start * rows, sources.stop * rows)
        product = jnp.dot(lhs, rhs[span], preferred_element_type=jnp.float32)
        product = product.astype(jnp.bfloat16).reshape(2, rows, 2 * width)
        return product[:, :, :width], product[:, :, width:]

    writes = []

    def finish(first):
        block = first - reach
        if 0 <= block < blocks:
            span = slice(block, block + 2)
            results[0, span], results[1, span] = pair(first)
            done = [pltpu.make_async_copy(results.at[0, span], clean.at[span], out_sems.at[0, block])]
            for i in range(block, block + 2):
                target = outgoing.at[places[i]]
                done.append(pltpu.make_async_copy(results.at[1, i], target, out_sems.at[1, i]))
        else:
            side, at = int(block >= 0), first % (blocks + reach)
            halos[side, 0, at : at + 2], halos[side, 1, at : at + 2] = pair(first)
            slot = (me[0] & 1) ^ (1 - side)
            done = []
            for i in range(2):
                source, target = halos.at[side, i, at : at + 2], sides[i].at[slot, at : at + 2]
                done.append(pltpu.make_async_copy(source, target, out_sems.at[2 + i, first]))
        for copy in done:
            copy.start()
        writes.extend(done)

    for step in range(blocks // 2):
        for copy in inputs[step]:
            copy.wait()
        for copy in inputs[step + ahead] if step + ahead < blocks // 2 else []:
            copy.start()
        if step == 1:
            for copy in to_vmem:
                copy.start()
        if step:
            finish(2 * step - 2)
        take(step)
    for copy in to_vmem:
        copy.wait()
    for copy in to_hbm:
        copy.start()
    for first in range(blocks + 2 * reach - 2, blocks - 4, -2):
        finish(first)
    for copy in writes + to_hbm:
        copy.wait()


def aggregate(shuffle, cols, count, gc, pc, gx, px, slopes, adj, features, weight, reach, devs, groups):
    blocks, slots, rows, _ = adj.shape
    width = gc.shape[1]
    send_slots = -(-blocks // devs)
    assert reach % 2 == 0 and blocks % 2 == 0
    packed = features.shape[0] // groups + weight.shape[0]
    return pl.pallas_call(
        functools.partial(aggregate_kernel, reach, groups, send_slots),
        in_specs=[IN_SMEM] * 3 + [IN_HBM] * 4 + [IN_VMEM] + [IN_HBM] * 3,
        out_specs=[IN_HBM] * (4 + groups),
        out_shape=[bf16(blocks, rows, width), bf16(devs * send_slots, rows, width)]
        + [bf16(2, reach, rows, width)] * 2
        + [bf16(packed, width)] * groups,
        scratch_shapes=[
            pltpu.VMEM((4, blocks // 2, 2 * rows, width), jnp.bfloat16),
            pltpu.VMEM((blocks, slots, rows, rows), jnp.bfloat16),
            pltpu.VMEM((blocks * rows, 2 * width), jnp.bfloat16),
            pltpu.VMEM((blocks + 2 * reach + 1, 2 * reach + 1, rows, rows), jnp.bfloat16),
            pltpu.VMEM((2, blocks, rows, width), jnp.bfloat16),
            pltpu.VMEM((2, 2, reach, rows, width), jnp.bfloat16),
            pltpu.VMEM((groups, packed, width), jnp.bfloat16),
            pltpu.SMEM((blocks,), jnp.int32),
            pltpu.SMEM((devs,), jnp.int32),
            pltpu.SemaphoreType.DMA((5, blocks // 2)),
            pltpu.SemaphoreType.DMA((3, groups)),
            pltpu.SemaphoreType.DMA((4, blocks + 2 * reach)),
        ],
        compiler_params=params(VMEM_ALL),
        cost_estimate=pl.CostEstimate(
            flops=4 * blocks * slots * rows * rows * width,
            bytes_accessed=12 * blocks * rows * width + 2 * blocks * slots * rows * rows,
            transcendentals=0,
        ),
        name="aggregate",
    )(shuffle, cols, count, gc, pc, gx, px, slopes, adj, features, weight)


def patch_kernel(reach, blocks, slots, index, shuffle, outgoing, pair, beside, out, *scratch):
    held, other, ready, places, used, sems = scratch
    odd = index[0] & 1
    arrivals = [
        pltpu.make_async_copy(pair, other.at[pl.ds((1 - odd) * reach, reach)], sems.at[2, 0]),
        pltpu.make_async_copy(beside, other.at[pl.ds(odd * reach, reach)], sems.at[2, 1]),
    ]
    for copy in arrivals:
        copy.start()
    find_places(index, shuffle, blocks, slots, places, used)
    border = [*range(reach), *range(blocks - reach, blocks)]
    reads, writes = [], []
    for i, block in enumerate(border):
        place = places[block]
        reads.append(pltpu.make_async_copy(outgoing.at[place], held.at[i], sems.at[0, i]))
        writes.append(pltpu.make_async_copy(ready.at[i], out.at[place], sems.at[1, i]))
    for copy in reads:
        copy.start()
    for copy in arrivals:
        copy.wait()
    for i, (read, write) in enumerate(zip(reads, writes)):
        read.wait()
        ready[i] = (wide(held[i]) + wide(other[i])).astype(jnp.bfloat16)
        write.start()
    for copy in writes:
        copy.wait()


def patch(index, shuffle, outgoing, pair, beside, blocks, slots):
    sent, rows, width = outgoing.shape
    reach = pair.shape[0]
    border = pltpu.VMEM((2 * reach, rows, width), jnp.bfloat16)
    return pl.pallas_call(
        functools.partial(patch_kernel, reach, blocks, slots),
        in_specs=[IN_SMEM] * 2 + [IN_HBM] * 3,
        out_specs=IN_HBM,
        out_shape=bf16(*outgoing.shape),
        input_output_aliases={2: 0},
        scratch_shapes=[
            border,
            border,
            border,
            pltpu.SMEM((blocks,), jnp.int32),
            pltpu.SMEM((sent // slots,), jnp.int32),
            pltpu.SemaphoreType.DMA((3, 2 * reach)),
        ],
        compiler_params=params(VMEM_ALL),
        name="patch",
    )(index, shuffle, outgoing, pair, beside)


def merge_kernel(quarter, index, landing, clean, pair, beside, incoming, out, whole):
    blocks, rows, _ = clean.shape
    reach = pair.shape[0]
    group = index[1]
    piece = math.gcd(rows, quarter)
    for block in range(blocks):
        whole[block] = wide(clean[block])
    odd = index[0] & 1
    for i in range(reach):
        whole[(1 - odd) * (blocks - reach) + i] += wide(pair[i])
        whole[odd * (blocks - reach) + i] += wide(beside[i])
    for place in range(incoming.shape[0]):
        block = landing[place]

        @pl.when(block >= 0)
        def _():
            total = (whole[block] + wide(incoming[place])).astype(jnp.bfloat16)
            for part in range(rows // piece):
                at = block * (rows // piece) + part
                owner = at // (quarter // piece)
                offset = (at - owner * (quarter // piece)) * piece
                out[owner ^ group, pl.ds(pl.multiple_of(offset, piece), piece)] = total[
                    part * piece : (part + 1) * piece
                ]


def merge(index, landing, clean, pair, beside, incoming, groups):
    blocks, rows, width = clean.shape
    quarter = blocks * rows // groups
    return pl.pallas_call(
        functools.partial(merge_kernel, quarter),
        in_specs=[IN_SMEM] * 2 + [IN_VMEM] * 4,
        out_specs=IN_VMEM,
        out_shape=bf16(groups, quarter, width),
        scratch_shapes=[pltpu.VMEM((blocks, rows, width), jnp.float32)],
        compiler_params=params(),
        name="merge",
    )(index, landing, clean, pair, beside, incoming)


def weight_kernel(devs, index, *refs):
    groups = (len(refs) - 2) // 2
    packed, summed, (keep, send) = refs[:groups], refs[groups : 2 * groups], refs[2 * groups :]
    me, group = index[0], index[1]
    shares = devs // groups
    height, width = keep.shape[2:]
    rhs = jnp.concatenate([piece[...] for piece in summed], axis=1)
    for relative in range(groups):
        product = lax.dot_general(
            packed[relative][: rhs.shape[0]],
            rhs,
            (((0,), (0,)), ((), ())),
            preferred_element_type=jnp.float32,
        ).astype(jnp.bfloat16)
        for share in range(shares):
            node = ((group ^ relative) * shares + share) ^ me
            rows = product[share * height : (share + 1) * height]

            def store(out):
                for i in range(groups):
                    out[node >> 1, i] = rows[:, i * width : (i + 1) * width]

            pl.when((node & 1) == 0)(functools.partial(store, keep))
            pl.when((node & 1) == 1)(functools.partial(store, send))


def weight_partial(index, packed, summed, devs):
    groups = len(packed)
    rows, width = summed[0].shape
    height = groups * width // devs
    return pl.pallas_call(
        functools.partial(weight_kernel, devs),
        in_specs=[IN_SMEM] + [IN_VMEM] * (2 * groups),
        out_specs=[IN_VMEM] * 2,
        out_shape=[bf16(devs // 2, groups, height, width)] * 2,
        compiler_params=params(),
        cost_estimate=pl.CostEstimate(
            flops=2 * rows * (groups * width) ** 2,
            bytes_accessed=2 * (groups * width) ** 2 + 4 * groups * rows * width,
            transcendentals=0,
        ),
        name="weight_partial",
    )(index, *packed, *summed)


def feature_kernel(first, index, *refs):
    *summed, even, odd, out = refs
    groups = len(summed)
    devs = 2 * even.shape[0]
    me, group = index[0], index[1]
    shares = devs // groups
    height = even.shape[2]
    low = me & (shares - 1)
    lhs = jnp.concatenate([piece[...] for piece in summed], axis=1)
    for relative in range(first, first + out.shape[0]):
        rows = []
        for i in range(shares):
            node = (((group ^ relative) * shares) ^ (me - low)) + i
            half = odd if i % 2 else even
            rows.append(jnp.concatenate([half[node >> 1, j] for j in range(groups)], axis=1))
        product = lax.dot_general(
            lhs,
            jnp.concatenate(rows, axis=0),
            (((1,), (1,)), ((), ())),
            preferred_element_type=jnp.float32,
        ).astype(jnp.bfloat16)
        parts = [product[:, i * height : (i + 1) * height] for i in range(shares)]

        def store(flip):
            out[relative - first] = jnp.concatenate([parts[i ^ flip] for i in range(shares)], axis=1)

        for flip in range(shares):
            pl.when(low == flip)(functools.partial(store, flip))


def feature_rows(index, summed, even, odd, first, count):
    groups = len(summed)
    rows, width = summed[0].shape
    return pl.pallas_call(
        functools.partial(feature_kernel, first),
        in_specs=[IN_SMEM] + [IN_VMEM] * (groups + 2),
        out_specs=IN_VMEM,
        out_shape=bf16(count, rows, width),
        compiler_params=params(),
        cost_estimate=pl.CostEstimate(
            flops=2 * rows * groups * count * width**2,
            bytes_accessed=2 * groups * count * width**2 + 2 * (groups + count) * rows * width,
            transcendentals=0,
        ),
        name="feature_rows",
    )(index, *summed, even, odd)


def gather_kernel(index, *refs):
    *pieces, out, sems = refs
    rows = pieces[0].shape[0]
    copies = [
        pltpu.make_async_copy(
            piece, out.at[pl.ds(pl.multiple_of((index[1] ^ i) * rows, rows), rows)], sems.at[i]
        )
        for i, piece in enumerate(pieces)
    ]
    for copy in copies:
        copy.start()
    for copy in copies:
        copy.wait()


def laid_out(index, pieces):
    rows, width = pieces[0].shape
    return pl.pallas_call(
        gather_kernel,
        in_specs=[IN_SMEM] + [IN_VMEM] * len(pieces),
        out_specs=IN_HBM,
        out_shape=bf16(len(pieces) * rows, width),
        scratch_shapes=[pltpu.SemaphoreType.DMA((len(pieces),))],
        compiler_params=params(),
        name="laid_out",
    )(index, *pieces)


def landing_blocks(shuffle_from, me, blocks, devs, slots):
    owner = (shuffle_from // blocks).reshape(devs, blocks)
    within = (shuffle_from % blocks).reshape(devs, blocks)
    for_me = owner == me
    earlier = jnp.arange(blocks)[None, :] < jnp.arange(blocks)[:, None]
    rank = jnp.sum((for_me[:, None, :] & earlier[None]).astype(jnp.int32), axis=2)
    picked = for_me[:, None, :] & (rank[:, None, :] == jnp.arange(slots)[None, :, None])
    return (jnp.sum(jnp.where(picked, within[:, None, :] + 1, 0), axis=2) - 1).reshape(-1)


def exchange_order(groups):
    return sorted(range(1, groups), reverse=True)


def local(
    features,
    weight,
    pre_clean,
    pre_corrupt,
    grad_clean,
    grad_corrupt,
    slopes,
    adj_vals,
    adj_cols,
    adj_count,
    shuffle_from,
):
    row_count = features.shape[0]
    blocks, tile_slots, _, _ = adj_vals.shape
    reach = (tile_slots - 1) // 2
    me = lax.axis_index("node")
    group = lax.axis_index("chan")
    devs = lax.axis_size("node")
    groups = lax.axis_size("chan")
    slots = -(-blocks // devs)
    index = jnp.stack([me, group])

    args = (shuffle_from, adj_cols.T, adj_count)
    args += (grad_clean, pre_clean, grad_corrupt, pre_corrupt, slopes[None, :], adj_vals)
    clean, outgoing, *sides = aggregate(*args, features, weight, reach, devs, groups)
    (clean_side, side), packed = sides[:2], sides[2:]
    pair, beside = swapped(side[0], "node", 1), swapped_beside(side[1], "node")
    for i in exchange_order(groups):
        packed[i] = swapped(packed[i], "chan", i)

    outgoing = patch(index, shuffle_from, outgoing, pair, beside, blocks, slots)
    shuffle_from, outgoing, clean, clean_side = lax.optimization_barrier(
        (shuffle_from, outgoing, clean, clean_side)
    )
    clean_pair = swapped(clean_side[0], "node", 1)
    clean_beside = swapped_beside(clean_side[1], "node")
    landing = landing_blocks(shuffle_from, me, blocks, devs, slots)
    incoming = exchanged(outgoing, "node")
    incoming, packed = lax.optimization_barrier((incoming, packed))
    merged = merge(index, landing, clean, clean_pair, clean_beside, incoming, groups)

    quarter = row_count // groups
    summed = [merged[0]] + [None] * (groups - 1)
    for i in exchange_order(groups):
        summed[i] = swapped(merged[i], "chan", i)
    tiles = jnp.stack([piece[quarter:] for piece in packed])
    even = [tiles] + [swapped(tiles, "node", 2 * i) for i in range(1, devs // 2)]
    order = [0, *range(2, groups - 1), 1, groups - 1]
    listed, even = lax.optimization_barrier(([summed[i] for i in order], even))
    summed = [listed[order.index(i)] for i in range(groups)]
    even = jnp.stack(even)
    odd = swapped(even, "node", 1)

    keep, send = weight_partial(index, packed, summed, devs)
    odd, send = lax.optimization_barrier((odd, send))
    arrived = swapped(send, "node", 1)
    sent = feature_rows(index, summed, even, odd, 1, groups - 1)
    arrived, sent, summed, even, odd = lax.optimization_barrier((arrived, sent, summed, even, odd))
    pieces = [feature_rows(index, summed, even, odd, 0, 1)[0]] + [None] * (groups - 1)
    for i in exchange_order(groups):
        pieces[i] = swapped(sent[i - 1], "chan", i)
    total = wide(keep) + wide(arrived)
    share = total[0]
    for i in range(1, devs // 2):
        share = share + wide(swapped(total[i].astype(jnp.bfloat16), "node", 2 * i))
    grad_weight = share[0]
    for i in range(1, groups):
        grad_weight = grad_weight + wide(swapped(share[i].astype(jnp.bfloat16), "chan", i))
    return (grad_weight, laid_out(index, pieces))


def solution(mesh):
    placed = (
        P("node", "chan"),
        P("node", "chan"),
        P("node", "chan"),
        P("node", "chan"),
        P("node", "chan"),
        P("node", "chan"),
        P("chan"),
        P("node", None, None, None),
        P("node", None),
        P("node"),
        P(),
    )
    return jax.shard_map(
        local,
        mesh=mesh,
        in_specs=placed,
        out_specs=(P("node", "chan"), P("node", "chan")),
        check_vma=False,
    )
```

```python
import functools
import math

import jax
import jax.numpy as jnp
from jax import lax
from jax.experimental import pallas as pl
from jax.experimental.pallas import tpu as pltpu
from jax.sharding import PartitionSpec as P

VMEM_LIMIT = 32 * 1024 * 1024
VMEM_ALL = 61 * 1024 * 1024
IN_VMEM = pl.BlockSpec(memory_space=pltpu.VMEM)
IN_SMEM = pl.BlockSpec(memory_space=pltpu.SMEM)
IN_HBM = pl.BlockSpec(memory_space=pltpu.HBM)


def params(limit=VMEM_LIMIT):
    return pltpu.CompilerParams(vmem_limit_bytes=limit)


def bf16(*shape):
    return jax.ShapeDtypeStruct(shape, jnp.bfloat16)


def wide(value):
    return value.astype(jnp.float32)


def swapped_beside(value, axis):
    size = lax.axis_size(axis)
    pairs = [(i, i + 1) for i in range(1, size - 1, 2)]
    return lax.ppermute(value, axis, pairs + [(j, i) for i, j in pairs])


def swapped(value, axis, by):
    size = lax.axis_size(axis)
    return lax.ppermute(value, axis, [(i, i ^ by) for i in range(size)])


def exchanged(value, axis):
    return lax.all_to_all(value, axis, split_axis=0, concat_axis=0, tiled=True)


def masked_grad(grad, pre, slope):
    return jnp.where(pre > 0, grad, grad * slope)


def find_places(index, shuffle, blocks, slots, places, used):
    for i in range(used.shape[0]):
        used[i] = 0
    for block in range(blocks):
        owner = shuffle[index[0] * blocks + block] // blocks
        slot = used[owner]
        used[owner] = slot + 1
        places[block] = owner * slots + slot


def aggregate_kernel(
    reach, groups, send_slots, shuffle, cols, count, gc, pc, gx, px, slopes, adj, features, weight, *refs
):
    clean, outgoing, *refs = refs
    sides, packed, refs = refs[:2], refs[2 : 2 + groups], refs[2 + groups :]
    data, tiles, rhs, stage, results, halos, packs, places, used, sems, pack_sems, out_sems = refs
    blocks, slots, rows, _ = adj.shape
    width = gc.shape[1]
    me = (lax.axis_index("node"), lax.axis_index("chan"))
    quarter = features.shape[0] // groups
    spare = blocks + 2 * reach

    def copies(step):
        span = slice(2 * step, 2 * step + 2)
        out = [
            pltpu.make_async_copy(
                ref.at[2 * step * rows : (2 * step + 2) * rows], data.at[i, step], sems.at[i, step]
            )
            for i, ref in enumerate((gc, pc, gx, px))
        ]
        return out + [pltpu.make_async_copy(adj.at[span], tiles.at[span], sems.at[4, step])]

    inputs = [copies(step) for step in range(blocks // 2)]
    ahead = 3
    for copy in sum(inputs[:ahead], []):
        copy.start()
    to_vmem, to_hbm = [], []
    for i in range(groups):
        span = pl.ds(pl.multiple_of((me[1] ^ i) * quarter, quarter), quarter)
        to_vmem.append(
            pltpu.make_async_copy(features.at[span], packs.at[i, :quarter], pack_sems.at[0, i])
        )
        to_vmem.append(pltpu.make_async_copy(weight, packs.at[i, quarter:], pack_sems.at[1, i]))
        to_hbm.append(pltpu.make_async_copy(packs.at[i], packed[i], pack_sems.at[2, i]))
    stage[...] = jnp.zeros_like(stage)
    shape = (rows, rows)
    identity = (
        lax.broadcasted_iota(jnp.int32, shape, 0) == lax.broadcasted_iota(jnp.int32, shape, 1)
    ).astype(jnp.float32).astype(jnp.bfloat16)
    slope = slopes[...].astype(jnp.bfloat16)
    find_places(me, shuffle, blocks, send_slots, places, used)

    def take(step):
        gradients = [masked_grad(data[i, step], data[i + 1, step], slope) for i in (0, 2)]
        rhs[2 * step * rows : (2 * step + 2) * rows] = jnp.concatenate(gradients, axis=1)
        turned = lax.dot_general(
            identity,
            tiles[2 * step : 2 * step + 2].reshape(2 * slots * rows, rows),
            (((1,), (1,)), ((), ())),
            preferred_element_type=jnp.float32,
        )
        for i in range(2 * slots):
            block, k = 2 * step + i // slots, i % slots
            live = k < count[block]
            target = cols[k, block] - me[0] * blocks
            place = jnp.where(live, target + reach, spare)
            distance = jnp.where(live, block - target + reach, 0)
            stage[place, distance] += turned[:, i * rows : (i + 1) * rows].astype(jnp.bfloat16)

    blank = jnp.zeros(shape, jnp.bfloat16)

    def pair(first):
        targets = [first - reach, first - reach + 1]
        sources = range(max(0, targets[0] - reach), min(blocks, targets[1] + reach + 1))

        def tile(i, source):
            distance = source - targets[i] + reach
            return stage[first + i, distance] if 0 <= distance <= 2 * reach else blank

        lhs = jnp.concatenate(
            [jnp.concatenate([tile(i, b) for b in sources], axis=1) for i in range(2)], axis=0
        )
        span = slice(sources.start * rows, sources.stop * rows)
        product = jnp.dot(lhs, rhs[span], preferred_element_type=jnp.float32)
        product = product.astype(jnp.bfloat16).reshape(2, rows, 2 * width)
        return product[:, :, :width], product[:, :, width:]

    writes = []

    def finish(first):
        block = first - reach
        if 0 <= block < blocks:
            span = slice(block, block + 2)
            results[0, span], results[1, span] = pair(first)
            done = [pltpu.make_async_copy(results.at[0, span], clean.at[span], out_sems.at[0, block])]
            for i in range(block, block + 2):
                target = outgoing.at[places[i]]
                done.append(pltpu.make_async_copy(results.at[1, i], target, out_sems.at[1, i]))
        else:
            side, at = int(block >= 0), first % (blocks + reach)
            halos[side, 0, at : at + 2], halos[side, 1, at : at + 2] = pair(first)
            slot = (me[0] & 1) ^ (1 - side)
            done = []
            for i in range(2):
                source, target = halos.at[side, i, at : at + 2], sides[i].at[slot, at : at + 2]
                done.append(pltpu.make_async_copy(source, target, out_sems.at[2 + i, first]))
        for copy in done:
            copy.start()
        writes.extend(done)

    for step in range(blocks // 2):
        for copy in inputs[step]:
            copy.wait()
        for copy in inputs[step + ahead] if step + ahead < blocks // 2 else []:
            copy.start()
        if step == 1:
            for copy in to_vmem:
                copy.start()
        if step:
            finish(2 * step - 2)
        take(step)
    for copy in to_vmem:
        copy.wait()
    for copy in to_hbm:
        copy.start()
    for first in range(blocks + 2 * reach - 2, blocks - 4, -2):
        finish(first)
    for copy in writes + to_hbm:
        copy.wait()


def aggregate(shuffle, cols, count, gc, pc, gx, px, slopes, adj, features, weight, reach, devs, groups):
    blocks, slots, rows, _ = adj.shape
    width = gc.shape[1]
    send_slots = -(-blocks // devs)
    assert reach % 2 == 0 and blocks % 2 == 0
    packed = features.shape[0] // groups + weight.shape[0]
    return pl.pallas_call(
        functools.partial(aggregate_kernel, reach, groups, send_slots),
        in_specs=[IN_SMEM] * 3 + [IN_HBM] * 4 + [IN_VMEM] + [IN_HBM] * 3,
        out_specs=[IN_HBM] * (4 + groups),
        out_shape=[bf16(blocks, rows, width), bf16(devs * send_slots, rows, width)]
        + [bf16(2, reach, rows, width)] * 2
        + [bf16(packed, width)] * groups,
        scratch_shapes=[
            pltpu.VMEM((4, blocks // 2, 2 * rows, width), jnp.bfloat16),
            pltpu.VMEM((blocks, slots, rows, rows), jnp.bfloat16),
            pltpu.VMEM((blocks * rows, 2 * width), jnp.bfloat16),
            pltpu.VMEM((blocks + 2 * reach + 1, 2 * reach + 1, rows, rows), jnp.bfloat16),
            pltpu.VMEM((2, blocks, rows, width), jnp.bfloat16),
            pltpu.VMEM((2, 2, reach, rows, width), jnp.bfloat16),
            pltpu.VMEM((groups, packed, width), jnp.bfloat16),
            pltpu.SMEM((blocks,), jnp.int32),
            pltpu.SMEM((devs,), jnp.int32),
            pltpu.SemaphoreType.DMA((5, blocks // 2)),
            pltpu.SemaphoreType.DMA((3, groups)),
            pltpu.SemaphoreType.DMA((4, blocks + 2 * reach)),
        ],
        compiler_params=params(VMEM_ALL),
        cost_estimate=pl.CostEstimate(
            flops=4 * blocks * slots * rows * rows * width,
            bytes_accessed=12 * blocks * rows * width + 2 * blocks * slots * rows * rows,
            transcendentals=0,
        ),
        name="aggregate",
    )(shuffle, cols, count, gc, pc, gx, px, slopes, adj, features, weight)


def patch_kernel(reach, blocks, slots, index, shuffle, outgoing, pair, beside, out, *scratch):
    held, other, ready, places, used, sems = scratch
    odd = index[0] & 1
    arrivals = [
        pltpu.make_async_copy(pair, other.at[pl.ds((1 - odd) * reach, reach)], sems.at[2, 0]),
        pltpu.make_async_copy(beside, other.at[pl.ds(odd * reach, reach)], sems.at[2, 1]),
    ]
    for copy in arrivals:
        copy.start()
    find_places(index, shuffle, blocks, slots, places, used)
    border = [*range(reach), *range(blocks - reach, blocks)]
    reads, writes = [], []
    for i, block in enumerate(border):
        place = places[block]
        reads.append(pltpu.make_async_copy(outgoing.at[place], held.at[i], sems.at[0, i]))
        writes.append(pltpu.make_async_copy(ready.at[i], out.at[place], sems.at[1, i]))
    for copy in reads:
        copy.start()
    for copy in arrivals:
        copy.wait()
    for i, (read, write) in enumerate(zip(reads, writes)):
        read.wait()
        ready[i] = (wide(held[i]) + wide(other[i])).astype(jnp.bfloat16)
        write.start()
    for copy in writes:
        copy.wait()


def patch(index, shuffle, outgoing, pair, beside, blocks, slots):
    sent, rows, width = outgoing.shape
    reach = pair.shape[0]
    border = pltpu.VMEM((2 * reach, rows, width), jnp.bfloat16)
    return pl.pallas_call(
        functools.partial(patch_kernel, reach, blocks, slots),
        in_specs=[IN_SMEM] * 2 + [IN_HBM] * 3,
        out_specs=IN_HBM,
        out_shape=bf16(*outgoing.shape),
        input_output_aliases={2: 0},
        scratch_shapes=[
            border,
            border,
            border,
            pltpu.SMEM((blocks,), jnp.int32),
            pltpu.SMEM((sent // slots,), jnp.int32),
            pltpu.SemaphoreType.DMA((3, 2 * reach)),
        ],
        compiler_params=params(VMEM_ALL),
        name="patch",
    )(index, shuffle, outgoing, pair, beside)


def merge_kernel(quarter, index, landing, clean, pair, beside, incoming, out, whole):
    blocks, rows, _ = clean.shape
    reach = pair.shape[0]
    group = index[1]
    piece = math.gcd(rows, quarter)
    for block in range(blocks):
        whole[block] = wide(clean[block])
    odd = index[0] & 1
    for i in range(reach):
        whole[(1 - odd) * (blocks - reach) + i] += wide(pair[i])
        whole[odd * (blocks - reach) + i] += wide(beside[i])
    for place in range(incoming.shape[0]):
        block = landing[place]

        @pl.when(block >= 0)
        def _():
            total = (whole[block] + wide(incoming[place])).astype(jnp.bfloat16)
            for part in range(rows // piece):
                at = block * (rows // piece) + part
                owner = at // (quarter // piece)
                offset = (at - owner * (quarter // piece)) * piece
                out[owner ^ group, pl.ds(pl.multiple_of(offset, piece), piece)] = total[
                    part * piece : (part + 1) * piece
                ]


def merge(index, landing, clean, pair, beside, incoming, groups):
    blocks, rows, width = clean.shape
    quarter = blocks * rows // groups
    return pl.pallas_call(
        functools.partial(merge_kernel, quarter),
        in_specs=[IN_SMEM] * 2 + [IN_VMEM] * 4,
        out_specs=IN_VMEM,
        out_shape=bf16(groups, quarter, width),
        scratch_shapes=[pltpu.VMEM((blocks, rows, width), jnp.float32)],
        compiler_params=params(),
        name="merge",
    )(index, landing, clean, pair, beside, incoming)


def weight_kernel(devs, index, *refs):
    groups = (len(refs) - 2) // 2
    packed, summed, (keep, send) = refs[:groups], refs[groups : 2 * groups], refs[2 * groups :]
    me, group = index[0], index[1]
    shares = devs // groups
    height, width = keep.shape[2:]
    rhs = jnp.concatenate([piece[...] for piece in summed], axis=1)
    for relative in range(groups):
        product = lax.dot_general(
            packed[relative][: rhs.shape[0]],
            rhs,
            (((0,), (0,)), ((), ())),
            preferred_element_type=jnp.float32,
        ).astype(jnp.bfloat16)
        for share in range(shares):
            node = ((group ^ relative) * shares + share) ^ me
            rows = product[share * height : (share + 1) * height]

            def store(out):
                for i in range(groups):
                    out[node >> 1, i] = rows[:, i * width : (i + 1) * width]

            pl.when((node & 1) == 0)(functools.partial(store, keep))
            pl.when((node & 1) == 1)(functools.partial(store, send))


def weight_partial(index, packed, summed, devs):
    groups = len(packed)
    rows, width = summed[0].shape
    height = groups * width // devs
    return pl.pallas_call(
        functools.partial(weight_kernel, devs),
        in_specs=[IN_SMEM] + [IN_VMEM] * (2 * groups),
        out_specs=[IN_VMEM] * 2,
        out_shape=[bf16(devs // 2, groups, height, width)] * 2,
        compiler_params=params(),
        cost_estimate=pl.CostEstimate(
            flops=2 * rows * (groups * width) ** 2,
            bytes_accessed=2 * (groups * width) ** 2 + 4 * groups * rows * width,
            transcendentals=0,
        ),
        name="weight_partial",
    )(index, *packed, *summed)


def feature_kernel(first, index, *refs):
    *summed, even, odd, out = refs
    groups = len(summed)
    devs = 2 * even.shape[0]
    me, group = index[0], index[1]
    shares = devs // groups
    height = even.shape[2]
    low = me & (shares - 1)
    lhs = jnp.concatenate([piece[...] for piece in summed], axis=1)
    for relative in range(first, first + out.shape[0]):
        rows = []
        for i in range(shares):
            node = (((group ^ relative) * shares) ^ (me - low)) + i
            half = odd if i % 2 else even
            rows.append(jnp.concatenate([half[node >> 1, j] for j in range(groups)], axis=1))
        product = lax.dot_general(
            lhs,
            jnp.concatenate(rows, axis=0),
            (((1,), (1,)), ((), ())),
            preferred_element_type=jnp.float32,
        ).astype(jnp.bfloat16)
        parts = [product[:, i * height : (i + 1) * height] for i in range(shares)]

        def store(flip):
            out[relative - first] = jnp.concatenate([parts[i ^ flip] for i in range(shares)], axis=1)

        for flip in range(shares):
            pl.when(low == flip)(functools.partial(store, flip))


def feature_rows(index, summed, even, odd, first, count):
    groups = len(summed)
    rows, width = summed[0].shape
    return pl.pallas_call(
        functools.partial(feature_kernel, first),
        in_specs=[IN_SMEM] + [IN_VMEM] * (groups + 2),
        out_specs=IN_VMEM,
        out_shape=bf16(count, rows, width),
        compiler_params=params(),
        cost_estimate=pl.CostEstimate(
            flops=2 * rows * groups * count * width**2,
            bytes_accessed=2 * groups * count * width**2 + 2 * (groups + count) * rows * width,
            transcendentals=0,
        ),
        name="feature_rows",
    )(index, *summed, even, odd)


def gather_kernel(index, *refs):
    *pieces, out, sems = refs
    rows = pieces[0].shape[0]
    copies = [
        pltpu.make_async_copy(
            piece, out.at[pl.ds(pl.multiple_of((index[1] ^ i) * rows, rows), rows)], sems.at[i]
        )
        for i, piece in enumerate(pieces)
    ]
    for copy in copies:
        copy.start()
    for copy in copies:
        copy.wait()


def laid_out(index, pieces):
    rows, width = pieces[0].shape
    return pl.pallas_call(
        gather_kernel,
        in_specs=[IN_SMEM] + [IN_VMEM] * len(pieces),
        out_specs=IN_HBM,
        out_shape=bf16(len(pieces) * rows, width),
        scratch_shapes=[pltpu.SemaphoreType.DMA((len(pieces),))],
        compiler_params=params(),
        name="laid_out",
    )(index, *pieces)


def landing_blocks(shuffle_from, me, blocks, devs, slots):
    owner = (shuffle_from // blocks).reshape(devs, blocks)
    within = (shuffle_from % blocks).reshape(devs, blocks)
    for_me = owner == me
    earlier = jnp.arange(blocks)[None, :] < jnp.arange(blocks)[:, None]
    rank = jnp.sum((for_me[:, None, :] & earlier[None]).astype(jnp.int32), axis=2)
    picked = for_me[:, None, :] & (rank[:, None, :] == jnp.arange(slots)[None, :, None])
    return (jnp.sum(jnp.where(picked, within[:, None, :] + 1, 0), axis=2) - 1).reshape(-1)


def exchange_order(groups):
    return sorted(range(1, groups), reverse=True)


def local(
    features,
    weight,
    pre_clean,
    pre_corrupt,
    grad_clean,
    grad_corrupt,
    slopes,
    adj_vals,
    adj_cols,
    adj_count,
    shuffle_from,
):
    row_count = features.shape[0]
    blocks, tile_slots, _, _ = adj_vals.shape
    reach = (tile_slots - 1) // 2
    me = lax.axis_index("node")
    group = lax.axis_index("chan")
    devs = lax.axis_size("node")
    groups = lax.axis_size("chan")
    slots = -(-blocks // devs)
    index = jnp.stack([me, group])

    args = (shuffle_from, adj_cols.T, adj_count)
    args += (grad_clean, pre_clean, grad_corrupt, pre_corrupt, slopes[None, :], adj_vals)
    clean, outgoing, *sides = aggregate(*args, features, weight, reach, devs, groups)
    (clean_side, side), packed = sides[:2], sides[2:]
    pair, beside = swapped(side[0], "node", 1), swapped_beside(side[1], "node")
    for i in exchange_order(groups):
        packed[i] = swapped(packed[i], "chan", i)

    outgoing = patch(index, shuffle_from, outgoing, pair, beside, blocks, slots)
    shuffle_from, outgoing, clean, clean_side = lax.optimization_barrier(
        (shuffle_from, outgoing, clean, clean_side)
    )
    clean_pair = swapped(clean_side[0], "node", 1)
    clean_beside = swapped_beside(clean_side[1], "node")
    landing = landing_blocks(shuffle_from, me, blocks, devs, slots)
    incoming = exchanged(outgoing, "node")
    incoming, packed = lax.optimization_barrier((incoming, packed))
    merged = merge(index, landing, clean, clean_pair, clean_beside, incoming, groups)

    quarter = row_count // groups
    summed = [merged[0]] + [None] * (groups - 1)
    for i in exchange_order(groups):
        summed[i] = swapped(merged[i], "chan", i)
    tiles = jnp.stack([piece[quarter:] for piece in packed])
    even = [tiles] + [swapped(tiles, "node", 2 * i) for i in range(1, devs // 2)]
    order = [0, *range(2, groups - 1), 1, groups - 1]
    listed, even = lax.optimization_barrier(([summed[i] for i in order], even))
    summed = [listed[order.index(i)] for i in range(groups)]
    even = jnp.stack(even)
    odd = swapped(even, "node", 1)

    keep, send = weight_partial(index, packed, summed, devs)
    odd, send = lax.optimization_barrier((odd, send))
    arrived = swapped(send, "node", 1)
    sent = feature_rows(index, summed, even, odd, 1, groups - 1)
    arrived, sent, summed, even, odd = lax.optimization_barrier((arrived, sent, summed, even, odd))
    pieces = [feature_rows(index, summed, even, odd, 0, 1)[0]] + [None] * (groups - 1)
    for i in exchange_order(groups):
        pieces[i] = swapped(sent[i - 1], "chan", i)
    total = wide(keep) + wide(arrived)
    share = total[0]
    for i in range(1, devs // 2):
        share = share + wide(swapped(total[i].astype(jnp.bfloat16), "node", 2 * i))
    grad_weight = share[0]
    for i in range(1, groups):
        grad_weight = grad_weight + wide(swapped(share[i].astype(jnp.bfloat16), "chan", i))
    return (grad_weight, laid_out(index, pieces))


def solution(mesh):
    placed = (
        P("node", "chan"),
        P("node", "chan"),
        P("node", "chan"),
        P("node", "chan"),
        P("node", "chan"),
        P("node", "chan"),
        P("chan"),
        P("node", None, None, None),
        P("node", None),
        P("node"),
        P(),
    )
    return jax.shard_map(
        local,
        mesh=mesh,
        in_specs=placed,
        out_specs=(P("node", "chan"), P("node", "chan")),
        check_vma=False,
    )
```

```python
import functools
import math

import jax
import jax.numpy as jnp
from jax import lax
from jax.experimental import pallas as pl
from jax.experimental.pallas import tpu as pltpu
from jax.sharding import PartitionSpec as P

VMEM_LIMIT = 32 * 1024 * 1024
VMEM_ALL = 61 * 1024 * 1024
IN_VMEM = pl.BlockSpec(memory_space=pltpu.VMEM)
IN_SMEM = pl.BlockSpec(memory_space=pltpu.SMEM)
IN_HBM = pl.BlockSpec(memory_space=pltpu.HBM)


def params(limit=VMEM_LIMIT):
    return pltpu.CompilerParams(vmem_limit_bytes=limit)


def bf16(*shape):
    return jax.ShapeDtypeStruct(shape, jnp.bfloat16)


def wide(value):
    return value.astype(jnp.float32)


def swapped_beside(value, axis):
    size = lax.axis_size(axis)
    pairs = [(i, (i + 1) % size) for i in range(1, size, 2)]
    return lax.ppermute(value, axis, pairs + [(j, i) for i, j in pairs])


def swapped(value, axis, by):
    size = lax.axis_size(axis)
    return lax.ppermute(value, axis, [(i, i ^ by) for i in range(size)])


def exchanged(value, axis):
    return lax.all_to_all(value, axis, split_axis=0, concat_axis=0, tiled=True)


def masked_grad(grad, pre, slope):
    return jnp.where(pre > 0, grad, grad * slope)


def find_places(index, shuffle, blocks, slots, places, used):
    for i in range(used.shape[0]):
        used[i] = 0
    for block in range(blocks):
        owner = shuffle[index[0] * blocks + block] // blocks
        slot = used[owner]
        used[owner] = slot + 1
        places[block] = owner * slots + slot


def aggregate_kernel(
    reach, groups, send_slots, shuffle, cols, count, gc, pc, gx, px, slopes, adj, features, weight, *refs
):
    clean, outgoing, *refs = refs
    sides, late, packed, refs = refs[:2], refs[2], refs[3 : 3 + groups], refs[3 + groups :]
    moved = late.shape[1]
    data, tiles, rhs, stage, results, halos, packs, held, places, used, sems, pack_sems, out_sems = refs
    blocks, slots, rows, _ = adj.shape
    width = gc.shape[1]
    me = (lax.axis_index("node"), lax.axis_index("chan"))
    quarter = features.shape[0] // groups
    early = quarter - moved
    spare = blocks + 2 * reach

    def copies(step):
        span = slice(2 * step, 2 * step + 2)
        out = [
            pltpu.make_async_copy(
                ref.at[2 * step * rows : (2 * step + 2) * rows], data.at[i, step], sems.at[i, step]
            )
            for i, ref in enumerate((gc, pc, gx, px))
        ]
        return out + [pltpu.make_async_copy(adj.at[span], tiles.at[span], sems.at[4, step])]

    inputs = [copies(step) for step in range(blocks // 2)]
    ahead = 3
    for copy in sum(inputs[:ahead], []):
        copy.start()
    to_vmem, to_hbm = [], []
    for i in range(groups):
        start = pl.multiple_of((me[1] ^ i) * quarter, 16)
        rest = pl.multiple_of((me[1] ^ i) * quarter + early, 16)
        sources = (features.at[pl.ds(start, early)], weight, features.at[pl.ds(rest, moved)])
        targets = (packs.at[i, :early], packs.at[i, early:], held.at[i])
        for j, (source, target) in enumerate(zip(sources, targets)):
            to_vmem.append(pltpu.make_async_copy(source, target, pack_sems.at[j, i]))
        to_hbm.append(pltpu.make_async_copy(packs.at[i], packed[i], pack_sems.at[3, i]))
        to_hbm.append(pltpu.make_async_copy(held.at[i], late.at[i], pack_sems.at[4, i]))
    stage[...] = jnp.zeros_like(stage)
    shape = (rows, rows)
    identity = (
        lax.broadcasted_iota(jnp.int32, shape, 0) == lax.broadcasted_iota(jnp.int32, shape, 1)
    ).astype(jnp.float32).astype(jnp.bfloat16)
    slope = slopes[...].astype(jnp.bfloat16)
    find_places(me, shuffle, blocks, send_slots, places, used)

    def take(step):
        gradients = [masked_grad(data[i, step], data[i + 1, step], slope) for i in (0, 2)]
        rhs[2 * step * rows : (2 * step + 2) * rows] = jnp.concatenate(gradients, axis=1)
        turned = lax.dot_general(
            identity,
            tiles[2 * step : 2 * step + 2].reshape(2 * slots * rows, rows),
            (((1,), (1,)), ((), ())),
            preferred_element_type=jnp.float32,
        )
        for i in range(2 * slots):
            block, k = 2 * step + i // slots, i % slots
            live = k < count[block]
            target = cols[k, block] - me[0] * blocks
            place = jnp.where(live, target + reach, spare)
            distance = jnp.where(live, block - target + reach, 0)
            stage[place, distance] += turned[:, i * rows : (i + 1) * rows].astype(jnp.bfloat16)

    blank = jnp.zeros(shape, jnp.bfloat16)

    def pair(first):
        targets = [first - reach, first - reach + 1]
        sources = range(max(0, targets[0] - reach), min(blocks, targets[1] + reach + 1))

        def tile(i, source):
            distance = source - targets[i] + reach
            return stage[first + i, distance] if 0 <= distance <= 2 * reach else blank

        lhs = jnp.concatenate(
            [jnp.concatenate([tile(i, b) for b in sources], axis=1) for i in range(2)], axis=0
        )
        span = slice(sources.start * rows, sources.stop * rows)
        product = jnp.dot(lhs, rhs[span], preferred_element_type=jnp.float32)
        product = product.astype(jnp.bfloat16).reshape(2, rows, 2 * width)
        return product[:, :, :width], product[:, :, width:]

    writes = []

    def finish(first):
        block = first - reach
        if 0 <= block < blocks:
            span = slice(block, block + 2)
            results[0, span], results[1, span] = pair(first)
            done = [pltpu.make_async_copy(results.at[0, span], clean.at[span], out_sems.at[0, block])]
            for i in range(block, block + 2):
                target = outgoing.at[places[i]]
                done.append(pltpu.make_async_copy(results.at[1, i], target, out_sems.at[1, i]))
        else:
            side, at = int(block >= 0), first % (blocks + reach)
            halos[side, 0, at : at + 2], halos[side, 1, at : at + 2] = pair(first)
            slot = (me[0] & 1) ^ (1 - side)
            done = []
            for i in range(2):
                source, target = halos.at[side, i, at : at + 2], sides[i].at[slot, at : at + 2]
                done.append(pltpu.make_async_copy(source, target, out_sems.at[2 + i, first]))
        for copy in done:
            copy.start()
        writes.extend(done)

    for step in range(blocks // 2):
        for copy in inputs[step]:
            copy.wait()
        for copy in inputs[step + ahead] if step + ahead < blocks // 2 else []:
            copy.start()
        if step == 1:
            for copy in to_vmem:
                copy.start()
        if step:
            finish(2 * step - 2)
        take(step)
    for copy in to_vmem:
        copy.wait()
    for copy in to_hbm:
        copy.start()
    for first in range(blocks + 2 * reach - 2, blocks - 4, -2):
        finish(first)
    for copy in writes + to_hbm:
        copy.wait()


def moved_rows(quarter, weight_rows):
    return min(weight_rows - quarter + 16, quarter // 64 * 16)


def aggregate(shuffle, cols, count, gc, pc, gx, px, slopes, adj, features, weight, reach, devs, groups):
    blocks, slots, rows, _ = adj.shape
    width = gc.shape[1]
    send_slots = -(-blocks // devs)
    assert reach % 2 == 0 and blocks % 2 == 0
    quarter = features.shape[0] // groups
    moved = moved_rows(quarter, groups * weight.shape[0])
    packed = quarter - moved + weight.shape[0]
    return pl.pallas_call(
        functools.partial(aggregate_kernel, reach, groups, send_slots),
        in_specs=[IN_SMEM] * 3 + [IN_HBM] * 4 + [IN_VMEM] + [IN_HBM] * 3,
        out_specs=[IN_HBM] * (5 + groups),
        out_shape=[bf16(blocks, rows, width), bf16(devs * send_slots, rows, width)]
        + [bf16(2, reach, rows, width)] * 2
        + [bf16(groups, moved, width)]
        + [bf16(packed, width)] * groups,
        scratch_shapes=[
            pltpu.VMEM((4, blocks // 2, 2 * rows, width), jnp.bfloat16),
            pltpu.VMEM((blocks, slots, rows, rows), jnp.bfloat16),
            pltpu.VMEM((blocks * rows, 2 * width), jnp.bfloat16),
            pltpu.VMEM((blocks + 2 * reach + 1, 2 * reach + 1, rows, rows), jnp.bfloat16),
            pltpu.VMEM((2, blocks, rows, width), jnp.bfloat16),
            pltpu.VMEM((2, 2, reach, rows, width), jnp.bfloat16),
            pltpu.VMEM((groups, packed, width), jnp.bfloat16),
            pltpu.VMEM((groups, moved, width), jnp.bfloat16),
            pltpu.SMEM((blocks,), jnp.int32),
            pltpu.SMEM((devs,), jnp.int32),
            pltpu.SemaphoreType.DMA((5, blocks // 2)),
            pltpu.SemaphoreType.DMA((5, groups)),
            pltpu.SemaphoreType.DMA((4, blocks + 2 * reach)),
        ],
        compiler_params=params(VMEM_ALL),
        cost_estimate=pl.CostEstimate(
            flops=4 * blocks * slots * rows * rows * width,
            bytes_accessed=12 * blocks * rows * width + 2 * blocks * slots * rows * rows,
            transcendentals=0,
        ),
        name="aggregate",
    )(shuffle, cols, count, gc, pc, gx, px, slopes, adj, features, weight)


def patch_kernel(reach, blocks, slots, index, shuffle, outgoing, pair, beside, out, *scratch):
    held, other, ready, places, used, sems = scratch
    odd = index[0] & 1
    arrivals = [
        pltpu.make_async_copy(pair, other.at[pl.ds((1 - odd) * reach, reach)], sems.at[2, 0]),
        pltpu.make_async_copy(beside, other.at[pl.ds(odd * reach, reach)], sems.at[2, 1]),
    ]
    for copy in arrivals:
        copy.start()
    find_places(index, shuffle, blocks, slots, places, used)
    border = [*range(reach), *range(blocks - reach, blocks)]
    reads, writes = [], []
    for i, block in enumerate(border):
        place = places[block]
        reads.append(pltpu.make_async_copy(outgoing.at[place], held.at[i], sems.at[0, i]))
        writes.append(pltpu.make_async_copy(ready.at[i], out.at[place], sems.at[1, i]))
    for copy in reads:
        copy.start()
    for copy in arrivals:
        copy.wait()
    for i, (read, write) in enumerate(zip(reads, writes)):
        read.wait()
        ready[i] = (wide(held[i]) + wide(other[i])).astype(jnp.bfloat16)
        write.start()
    for copy in writes:
        copy.wait()


def patch(index, shuffle, outgoing, pair, beside, blocks, slots):
    sent, rows, width = outgoing.shape
    reach = pair.shape[0]
    border = pltpu.VMEM((2 * reach, rows, width), jnp.bfloat16)
    return pl.pallas_call(
        functools.partial(patch_kernel, reach, blocks, slots),
        in_specs=[IN_SMEM] * 2 + [IN_HBM] * 3,
        out_specs=IN_HBM,
        out_shape=bf16(*outgoing.shape),
        input_output_aliases={2: 0},
        scratch_shapes=[
            border,
            border,
            border,
            pltpu.SMEM((blocks,), jnp.int32),
            pltpu.SMEM((sent // slots,), jnp.int32),
            pltpu.SemaphoreType.DMA((3, 2 * reach)),
        ],
        compiler_params=params(VMEM_ALL),
        name="patch",
    )(index, shuffle, outgoing, pair, beside)


def merge_kernel(quarter, index, landing, clean, pair, beside, incoming, late, out, whole):
    out[:, quarter:] = late[...]
    blocks, rows, _ = clean.shape
    reach = pair.shape[0]
    group = index[1]
    piece = math.gcd(rows, quarter)
    for block in range(blocks):
        whole[block] = wide(clean[block])
    odd = index[0] & 1
    for i in range(reach):
        whole[(1 - odd) * (blocks - reach) + i] += wide(pair[i])
        whole[odd * (blocks - reach) + i] += wide(beside[i])
    for place in range(incoming.shape[0]):
        block = landing[place]

        @pl.when(block >= 0)
        def _():
            total = (whole[block] + wide(incoming[place])).astype(jnp.bfloat16)
            for part in range(rows // piece):
                at = block * (rows // piece) + part
                owner = at // (quarter // piece)
                offset = (at - owner * (quarter // piece)) * piece
                out[owner ^ group, pl.ds(pl.multiple_of(offset, piece), piece)] = total[
                    part * piece : (part + 1) * piece
                ]


def merge(index, landing, clean, pair, beside, incoming, late):
    blocks, rows, width = clean.shape
    groups, moved, _ = late.shape
    quarter = blocks * rows // groups
    return pl.pallas_call(
        functools.partial(merge_kernel, quarter),
        in_specs=[IN_SMEM] * 2 + [IN_VMEM] * 5,
        out_specs=IN_VMEM,
        out_shape=bf16(groups, quarter + moved, width),
        scratch_shapes=[pltpu.VMEM((blocks, rows, width), jnp.float32)],
        compiler_params=params(),
        name="merge",
    )(index, landing, clean, pair, beside, incoming, late)


def weight_kernel(devs, index, *refs):
    groups = (len(refs) - 2) // 2
    packed, summed, (keep, send) = refs[:groups], refs[groups : 2 * groups], refs[2 * groups :]
    me, group = index[0], index[1]
    shares = devs // groups
    height, width = keep.shape[2:]
    early = packed[0].shape[0] - height
    quarter = (summed[0].shape[0] + early) // 2
    rhs = jnp.concatenate([piece[:quarter] for piece in summed], axis=1)
    for relative in range(groups):
        product = lax.dot_general(
            jnp.concatenate([packed[relative][:early], summed[relative][quarter:]], axis=0),
            rhs,
            (((0,), (0,)), ((), ())),
            preferred_element_type=jnp.float32,
        ).astype(jnp.bfloat16)
        for share in range(shares):
            node = ((group ^ relative) * shares + share) ^ me
            rows = product[share * height : (share + 1) * height]

            def store(out):
                for i in range(groups):
                    out[node >> 1, i] = rows[:, i * width : (i + 1) * width]

            pl.when((node & 1) == 0)(functools.partial(store, keep))
            pl.when((node & 1) == 1)(functools.partial(store, send))


def weight_partial(index, packed, summed, devs):
    groups = len(packed)
    rows, width = summed[0].shape
    height = groups * width // devs
    return pl.pallas_call(
        functools.partial(weight_kernel, devs),
        in_specs=[IN_SMEM] + [IN_VMEM] * (2 * groups),
        out_specs=[IN_VMEM] * 2,
        out_shape=[bf16(devs // 2, groups, height, width)] * 2,
        compiler_params=params(),
        cost_estimate=pl.CostEstimate(
            flops=2 * rows * (groups * width) ** 2,
            bytes_accessed=2 * (groups * width) ** 2 + 4 * groups * rows * width,
            transcendentals=0,
        ),
        name="weight_partial",
    )(index, *packed, *summed)


def feature_kernel(first, index, *refs):
    *summed, even, odd, out = refs
    groups = len(summed)
    devs = 2 * even.shape[0]
    me, group = index[0], index[1]
    shares = devs // groups
    height = even.shape[2]
    low = me & (shares - 1)
    lhs = jnp.concatenate([piece[: out.shape[1]] for piece in summed], axis=1)
    for relative in range(first, first + out.shape[0]):
        rows = []
        for i in range(shares):
            node = (((group ^ relative) * shares) ^ (me - low)) + i
            half = odd if i % 2 else even
            rows.append(jnp.concatenate([half[node >> 1, j] for j in range(groups)], axis=1))
        product = lax.dot_general(
            lhs,
            jnp.concatenate(rows, axis=0),
            (((1,), (1,)), ((), ())),
            preferred_element_type=jnp.float32,
        ).astype(jnp.bfloat16)
        parts = [product[:, i * height : (i + 1) * height] for i in range(shares)]

        def store(flip):
            out[relative - first] = jnp.concatenate([parts[i ^ flip] for i in range(shares)], axis=1)

        for flip in range(shares):
            pl.when(low == flip)(functools.partial(store, flip))


def feature_rows(index, summed, even, odd, first, count, rows):
    groups = len(summed)
    width = summed[0].shape[1]
    return pl.pallas_call(
        functools.partial(feature_kernel, first),
        in_specs=[IN_SMEM] + [IN_VMEM] * (groups + 2),
        out_specs=IN_VMEM,
        out_shape=bf16(count, rows, width),
        compiler_params=params(),
        cost_estimate=pl.CostEstimate(
            flops=2 * rows * groups * count * width**2,
            bytes_accessed=2 * groups * count * width**2 + 2 * (groups + count) * rows * width,
            transcendentals=0,
        ),
        name="feature_rows",
    )(index, *summed, even, odd)


def gather_kernel(index, *refs):
    *pieces, out, sems = refs
    rows = pieces[0].shape[0]
    copies = [
        pltpu.make_async_copy(
            piece, out.at[pl.ds(pl.multiple_of((index[1] ^ i) * rows, rows), rows)], sems.at[i]
        )
        for i, piece in enumerate(pieces)
    ]
    for copy in copies:
        copy.start()
    for copy in copies:
        copy.wait()


def laid_out(index, pieces):
    rows, width = pieces[0].shape
    return pl.pallas_call(
        gather_kernel,
        in_specs=[IN_SMEM] + [IN_VMEM] * len(pieces),
        out_specs=IN_HBM,
        out_shape=bf16(len(pieces) * rows, width),
        scratch_shapes=[pltpu.SemaphoreType.DMA((len(pieces),))],
        compiler_params=params(),
        name="laid_out",
    )(index, *pieces)


def landing_blocks(shuffle_from, me, blocks, devs, slots):
    owner = (shuffle_from // blocks).reshape(devs, blocks)
    within = (shuffle_from % blocks).reshape(devs, blocks)
    for_me = owner == me
    earlier = jnp.arange(blocks)[None, :] < jnp.arange(blocks)[:, None]
    rank = jnp.sum((for_me[:, None, :] & earlier[None]).astype(jnp.int32), axis=2)
    picked = for_me[:, None, :] & (rank[:, None, :] == jnp.arange(slots)[None, :, None])
    return (jnp.sum(jnp.where(picked, within[:, None, :] + 1, 0), axis=2) - 1).reshape(-1)


def exchange_order(groups):
    return sorted(range(1, groups), reverse=True)


def local(
    features,
    weight,
    pre_clean,
    pre_corrupt,
    grad_clean,
    grad_corrupt,
    slopes,
    adj_vals,
    adj_cols,
    adj_count,
    shuffle_from,
):
    row_count = features.shape[0]
    blocks, tile_slots, _, _ = adj_vals.shape
    reach = (tile_slots - 1) // 2
    me = lax.axis_index("node")
    group = lax.axis_index("chan")
    devs = lax.axis_size("node")
    groups = lax.axis_size("chan")
    slots = -(-blocks // devs)
    index = jnp.stack([me, group])

    args = (shuffle_from, adj_cols.T, adj_count)
    args += (grad_clean, pre_clean, grad_corrupt, pre_corrupt, slopes[None, :], adj_vals)
    clean, outgoing, *sides = aggregate(*args, features, weight, reach, devs, groups)
    (clean_side, side, late), packed = sides[:3], sides[3:]
    pair, beside = swapped(side[0], "node", 1), swapped_beside(side[1], "node")
    for i in exchange_order(groups):
        packed[i] = swapped(packed[i], "chan", i)

    outgoing = patch(index, shuffle_from, outgoing, pair, beside, blocks, slots)
    shuffle_from, outgoing, clean, clean_side = lax.optimization_barrier(
        (shuffle_from, outgoing, clean, clean_side)
    )
    clean_pair = swapped(clean_side[0], "node", 1)
    clean_beside = swapped_beside(clean_side[1], "node")
    landing = landing_blocks(shuffle_from, me, blocks, devs, slots)
    incoming = exchanged(outgoing, "node")
    incoming, packed = lax.optimization_barrier((incoming, packed))
    merged = merge(index, landing, clean, clean_pair, clean_beside, incoming, late)

    quarter = row_count // groups
    tiles = jnp.stack([piece[quarter - late.shape[1] :] for piece in packed])
    merged, tiles = lax.optimization_barrier((merged, tiles))
    summed = [merged[0]] + [None] * (groups - 1)
    for i in exchange_order(groups):
        summed[i] = swapped(merged[i], "chan", i)
    even = [tiles] + [swapped(tiles, "node", 2 * i) for i in range(1, devs // 2)]
    order = [0, *range(2, groups - 1), 1, groups - 1]
    listed, even = lax.optimization_barrier(([summed[i] for i in order], even))
    summed = [listed[order.index(i)] for i in range(groups)]
    even = jnp.stack(even)
    odd = swapped(even, "node", 1)

    keep, send = weight_partial(index, packed, summed, devs)
    odd, send = lax.optimization_barrier((odd, send))
    arrived = swapped(send, "node", 1)
    sent = feature_rows(index, summed, even, odd, 1, groups - 1, quarter)
    arrived, sent, summed, even, odd = lax.optimization_barrier((arrived, sent, summed, even, odd))
    pieces = [feature_rows(index, summed, even, odd, 0, 1, quarter)[0]] + [None] * (groups - 1)
    for i in exchange_order(groups):
        pieces[i] = swapped(sent[i - 1], "chan", i)
    total = wide(keep) + wide(arrived)
    share = total[0]
    for i in range(1, devs // 2):
        share = share + wide(swapped(total[i].astype(jnp.bfloat16), "node", 2 * i))
    grad_weight = share[0]
    for i in range(1, groups):
        grad_weight = grad_weight + wide(swapped(share[i].astype(jnp.bfloat16), "chan", i))
    return (grad_weight, laid_out(index, pieces))


def solution(mesh):
    placed = (
        P("node", "chan"),
        P("node", "chan"),
        P("node", "chan"),
        P("node", "chan"),
        P("node", "chan"),
        P("node", "chan"),
        P("chan"),
        P("node", None, None, None),
        P("node", None),
        P("node"),
        P(),
    )
    return jax.shard_map(
        local,
        mesh=mesh,
        in_specs=placed,
        out_specs=(P("node", "chan"), P("node", "chan")),
        check_vma=False,
    )
```

```python
import functools
import math

import jax
import jax.numpy as jnp
from jax import lax
from jax.experimental import pallas as pl
from jax.experimental.pallas import tpu as pltpu
from jax.sharding import PartitionSpec as P

VMEM_LIMIT = 32 * 1024 * 1024
VMEM_ALL = 61 * 1024 * 1024
IN_VMEM = pl.BlockSpec(memory_space=pltpu.VMEM)
IN_SMEM = pl.BlockSpec(memory_space=pltpu.SMEM)
IN_HBM = pl.BlockSpec(memory_space=pltpu.HBM)


def params(limit=VMEM_LIMIT):
    return pltpu.CompilerParams(vmem_limit_bytes=limit)


def bf16(*shape):
    return jax.ShapeDtypeStruct(shape, jnp.bfloat16)


def wide(value):
    return value.astype(jnp.float32)


def swapped_beside(value, axis, round):
    size = lax.axis_size(axis)
    pairs = [(i, (i + 1) % size) for i in range(1, size if round else size - 1, 2)]
    return lax.ppermute(value, axis, pairs + [(j, i) for i, j in pairs])


def swapped(value, axis, by):
    size = lax.axis_size(axis)
    return lax.ppermute(value, axis, [(i, i ^ by) for i in range(size)])


def exchanged(value, axis):
    return lax.all_to_all(value, axis, split_axis=0, concat_axis=0, tiled=True)


def masked_grad(grad, pre, slope):
    return jnp.where(pre > 0, grad, grad * slope)


def find_places(index, shuffle, blocks, slots, places, used):
    for i in range(used.shape[0]):
        used[i] = 0
    for block in range(blocks):
        owner = shuffle[index[0] * blocks + block] // blocks
        slot = used[owner]
        used[owner] = slot + 1
        places[block] = owner * slots + slot


def aggregate_kernel(
    reach, groups, send_slots, shuffle, cols, count, gc, pc, gx, px, slopes, adj, features, weight, *refs
):
    clean, outgoing, *refs = refs
    sides, packed, refs = refs[:2], refs[2 : 2 + groups], refs[2 + groups :]
    data, tiles, rhs, stage, results, halos, packs, places, used, sems, pack_sems, out_sems = refs
    blocks, slots, rows, _ = adj.shape
    width = gc.shape[1]
    me = (lax.axis_index("node"), lax.axis_index("chan"))
    quarter = features.shape[0] // groups
    spare = blocks + 2 * reach

    def copies(step):
        span = slice(2 * step, 2 * step + 2)
        out = [
            pltpu.make_async_copy(
                ref.at[2 * step * rows : (2 * step + 2) * rows], data.at[i, step], sems.at[i, step]
            )
            for i, ref in enumerate((gc, pc, gx, px))
        ]
        return out + [pltpu.make_async_copy(adj.at[span], tiles.at[span], sems.at[4, step])]

    inputs = [copies(step) for step in range(blocks // 2)]
    ahead = 3
    for copy in sum(inputs[:ahead], []):
        copy.start()
    to_vmem, to_hbm = [], []
    for i in range(groups):
        span = pl.ds(pl.multiple_of((me[1] ^ i) * quarter, quarter), quarter)
        to_vmem.append(
            pltpu.make_async_copy(features.at[span], packs.at[i, :quarter], pack_sems.at[0, i])
        )
        to_vmem.append(pltpu.make_async_copy(weight, packs.at[i, quarter:], pack_sems.at[1, i]))
        to_hbm.append(pltpu.make_async_copy(packs.at[i], packed[i], pack_sems.at[2, i]))
    stage[...] = jnp.zeros_like(stage)
    shape = (rows, rows)
    identity = (
        lax.broadcasted_iota(jnp.int32, shape, 0) == lax.broadcasted_iota(jnp.int32, shape, 1)
    ).astype(jnp.float32).astype(jnp.bfloat16)
    slope = slopes[...].astype(jnp.bfloat16)
    find_places(me, shuffle, blocks, send_slots, places, used)

    def take(step):
        gradients = [masked_grad(data[i, step], data[i + 1, step], slope) for i in (0, 2)]
        rhs[2 * step * rows : (2 * step + 2) * rows] = jnp.concatenate(gradients, axis=1)
        turned = lax.dot_general(
            identity,
            tiles[2 * step : 2 * step + 2].reshape(2 * slots * rows, rows),
            (((1,), (1,)), ((), ())),
            preferred_element_type=jnp.float32,
        )
        for i in range(2 * slots):
            block, k = 2 * step + i // slots, i % slots
            live = k < count[block]
            target = cols[k, block] - me[0] * blocks
            place = jnp.where(live, target + reach, spare)
            distance = jnp.where(live, block - target + reach, 0)
            stage[place, distance] += turned[:, i * rows : (i + 1) * rows].astype(jnp.bfloat16)

    blank = jnp.zeros(shape, jnp.bfloat16)

    def pair(first):
        targets = [first - reach, first - reach + 1]
        sources = range(max(0, targets[0] - reach), min(blocks, targets[1] + reach + 1))

        def tile(i, source):
            distance = source - targets[i] + reach
            return stage[first + i, distance] if 0 <= distance <= 2 * reach else blank

        lhs = jnp.concatenate(
            [jnp.concatenate([tile(i, b) for b in sources], axis=1) for i in range(2)], axis=0
        )
        span = slice(sources.start * rows, sources.stop * rows)
        product = jnp.dot(lhs, rhs[span], preferred_element_type=jnp.float32)
        product = product.astype(jnp.bfloat16).reshape(2, rows, 2 * width)
        return product[:, :, :width], product[:, :, width:]

    writes = []

    def finish(first):
        block = first - reach
        if 0 <= block < blocks:
            span = slice(block, block + 2)
            results[0, span], results[1, span] = pair(first)
            done = [pltpu.make_async_copy(results.at[0, span], clean.at[span], out_sems.at[0, block])]
            for i in range(block, block + 2):
                target = outgoing.at[places[i]]
                done.append(pltpu.make_async_copy(results.at[1, i], target, out_sems.at[1, i]))
        else:
            side, at = int(block >= 0), first % (blocks + reach)
            halos[side, 0, at : at + 2], halos[side, 1, at : at + 2] = pair(first)
            slot = (me[0] & 1) ^ (1 - side)
            done = []
            for i in range(2):
                source, target = halos.at[side, i, at : at + 2], sides[i].at[slot, at : at + 2]
                done.append(pltpu.make_async_copy(source, target, out_sems.at[2 + i, first]))
        for copy in done:
            copy.start()
        writes.extend(done)

    for step in range(blocks // 2):
        for copy in inputs[step]:
            copy.wait()
        for copy in inputs[step + ahead] if step + ahead < blocks // 2 else []:
            copy.start()
        if step == 1:
            for copy in to_vmem:
                copy.start()
        if step:
            finish(2 * step - 2)
        take(step)
    for copy in to_vmem:
        copy.wait()
    for copy in to_hbm:
        copy.start()
    for first in range(blocks + 2 * reach - 2, blocks - 4, -2):
        finish(first)
    for copy in writes + to_hbm:
        copy.wait()


def aggregate(shuffle, cols, count, gc, pc, gx, px, slopes, adj, features, weight, reach, devs, groups):
    blocks, slots, rows, _ = adj.shape
    width = gc.shape[1]
    send_slots = -(-blocks // devs)
    assert reach % 2 == 0 and blocks % 2 == 0
    packed = features.shape[0] // groups + weight.shape[0]
    return pl.pallas_call(
        functools.partial(aggregate_kernel, reach, groups, send_slots),
        in_specs=[IN_SMEM] * 3 + [IN_HBM] * 4 + [IN_VMEM] + [IN_HBM] * 3,
        out_specs=[IN_HBM] * (4 + groups),
        out_shape=[bf16(blocks, rows, width), bf16(devs * send_slots, rows, width)]
        + [bf16(2, reach, rows, width)] * 2
        + [bf16(packed, width)] * groups,
        scratch_shapes=[
            pltpu.VMEM((4, blocks // 2, 2 * rows, width), jnp.bfloat16),
            pltpu.VMEM((blocks, slots, rows, rows), jnp.bfloat16),
            pltpu.VMEM((blocks * rows, 2 * width), jnp.bfloat16),
            pltpu.VMEM((blocks + 2 * reach + 1, 2 * reach + 1, rows, rows), jnp.bfloat16),
            pltpu.VMEM((2, blocks, rows, width), jnp.bfloat16),
            pltpu.VMEM((2, 2, reach, rows, width), jnp.bfloat16),
            pltpu.VMEM((groups, packed, width), jnp.bfloat16),
            pltpu.SMEM((blocks,), jnp.int32),
            pltpu.SMEM((devs,), jnp.int32),
            pltpu.SemaphoreType.DMA((5, blocks // 2)),
            pltpu.SemaphoreType.DMA((3, groups)),
            pltpu.SemaphoreType.DMA((4, blocks + 2 * reach)),
        ],
        compiler_params=params(VMEM_ALL),
        cost_estimate=pl.CostEstimate(
            flops=4 * blocks * slots * rows * rows * width,
            bytes_accessed=12 * blocks * rows * width + 2 * blocks * slots * rows * rows,
            transcendentals=0,
        ),
        name="aggregate",
    )(shuffle, cols, count, gc, pc, gx, px, slopes, adj, features, weight)


def patch_kernel(reach, blocks, slots, shuffle, outgoing, pair, beside, out, *scratch):
    held, other, ready, places, used, sems = scratch
    index = (lax.axis_index("node"),)
    odd = index[0] & 1
    arrivals = [
        pltpu.make_async_copy(pair, other.at[pl.ds((1 - odd) * reach, reach)], sems.at[2, 0]),
        pltpu.make_async_copy(beside, other.at[pl.ds(odd * reach, reach)], sems.at[2, 1]),
    ]
    for copy in arrivals:
        copy.start()
    find_places(index, shuffle, blocks, slots, places, used)
    border = [*range(reach), *range(blocks - reach, blocks)]
    reads, writes = [], []
    for i, block in enumerate(border):
        place = places[block]
        reads.append(pltpu.make_async_copy(outgoing.at[place], held.at[i], sems.at[0, i]))
        writes.append(pltpu.make_async_copy(ready.at[i], out.at[place], sems.at[1, i]))
    for copy in reads:
        copy.start()
    for copy in arrivals:
        copy.wait()
    for i, (read, write) in enumerate(zip(reads, writes)):
        read.wait()
        ready[i] = (wide(held[i]) + wide(other[i])).astype(jnp.bfloat16)
        write.start()
    for copy in writes:
        copy.wait()


def patch(shuffle, outgoing, pair, beside, blocks, slots):
    sent, rows, width = outgoing.shape
    reach = pair.shape[0]
    border = pltpu.VMEM((2 * reach, rows, width), jnp.bfloat16)
    return pl.pallas_call(
        functools.partial(patch_kernel, reach, blocks, slots),
        in_specs=[IN_SMEM] + [IN_HBM] * 3,
        out_specs=IN_HBM,
        out_shape=bf16(*outgoing.shape),
        input_output_aliases={1: 0},
        scratch_shapes=[
            border,
            border,
            border,
            pltpu.SMEM((blocks,), jnp.int32),
            pltpu.SMEM((sent // slots,), jnp.int32),
            pltpu.SemaphoreType.DMA((3, 2 * reach)),
        ],
        compiler_params=params(VMEM_ALL),
        name="patch",
    )(shuffle, outgoing, pair, beside)


def merge_kernel(quarter, index, landing, clean, pair, beside, incoming, out, whole):
    blocks, rows, _ = clean.shape
    reach = pair.shape[0]
    group = index[1]
    piece = math.gcd(rows, quarter)
    for block in range(blocks):
        whole[block] = wide(clean[block])
    odd = index[0] & 1
    for i in range(reach):
        whole[(1 - odd) * (blocks - reach) + i] += wide(pair[i])
        whole[odd * (blocks - reach) + i] += wide(beside[i])
    for place in range(incoming.shape[0]):
        block = landing[place]

        @pl.when(block >= 0)
        def _():
            total = (whole[block] + wide(incoming[place])).astype(jnp.bfloat16)
            for part in range(rows // piece):
                at = block * (rows // piece) + part
                owner = at // (quarter // piece)
                offset = (at - owner * (quarter // piece)) * piece
                out[owner ^ group, pl.ds(pl.multiple_of(offset, piece), piece)] = total[
                    part * piece : (part + 1) * piece
                ]


def merge(index, landing, clean, pair, beside, incoming, groups):
    blocks, rows, width = clean.shape
    quarter = blocks * rows // groups
    return pl.pallas_call(
        functools.partial(merge_kernel, quarter),
        in_specs=[IN_SMEM] * 2 + [IN_VMEM] * 4,
        out_specs=IN_VMEM,
        out_shape=bf16(groups, quarter, width),
        scratch_shapes=[pltpu.VMEM((blocks, rows, width), jnp.float32)],
        compiler_params=params(),
        name="merge",
    )(index, landing, clean, pair, beside, incoming)


def weight_kernel(devs, index, *refs):
    groups = (len(refs) - 2) // 2
    packed, summed, (keep, send) = refs[:groups], refs[groups : 2 * groups], refs[2 * groups :]
    me, group = index[0], index[1]
    shares = devs // groups
    height, width = keep.shape[2:]
    rhs = jnp.concatenate([piece[...] for piece in summed], axis=1)
    for relative in range(groups):
        product = lax.dot_general(
            packed[relative][: rhs.shape[0]],
            rhs,
            (((0,), (0,)), ((), ())),
            preferred_element_type=jnp.float32,
        ).astype(jnp.bfloat16)
        for share in range(shares):
            node = ((group ^ relative) * shares + share) ^ me
            rows = product[share * height : (share + 1) * height]

            def store(out):
                for i in range(groups):
                    out[node >> 1, i] = rows[:, i * width : (i + 1) * width]

            pl.when((node & 1) == 0)(functools.partial(store, keep))
            pl.when((node & 1) == 1)(functools.partial(store, send))


def weight_partial(index, packed, summed, devs):
    groups = len(packed)
    rows, width = summed[0].shape
    height = groups * width // devs
    return pl.pallas_call(
        functools.partial(weight_kernel, devs),
        in_specs=[IN_SMEM] + [IN_VMEM] * (2 * groups),
        out_specs=[IN_VMEM] * 2,
        out_shape=[bf16(devs // 2, groups, height, width)] * 2,
        compiler_params=params(),
        cost_estimate=pl.CostEstimate(
            flops=2 * rows * (groups * width) ** 2,
            bytes_accessed=2 * (groups * width) ** 2 + 4 * groups * rows * width,
            transcendentals=0,
        ),
        name="weight_partial",
    )(index, *packed, *summed)


def feature_kernel(first, index, *refs):
    *summed, even, odd, out = refs
    groups = len(summed)
    devs = 2 * even.shape[0]
    me, group = index[0], index[1]
    shares = devs // groups
    height = even.shape[2]
    low = me & (shares - 1)
    lhs = jnp.concatenate([piece[...] for piece in summed], axis=1)
    for relative in range(first, first + out.shape[0]):
        rows = []
        for i in range(shares):
            node = (((group ^ relative) * shares) ^ (me - low)) + i
            half = odd if i % 2 else even
            rows.append(jnp.concatenate([half[node >> 1, j] for j in range(groups)], axis=1))
        product = lax.dot_general(
            lhs,
            jnp.concatenate(rows, axis=0),
            (((1,), (1,)), ((), ())),
            preferred_element_type=jnp.float32,
        ).astype(jnp.bfloat16)
        parts = [product[:, i * height : (i + 1) * height] for i in range(shares)]

        def store(flip):
            out[relative - first] = jnp.concatenate([parts[i ^ flip] for i in range(shares)], axis=1)

        for flip in range(shares):
            pl.when(low == flip)(functools.partial(store, flip))


def feature_rows(index, summed, even, odd, first, count):
    groups = len(summed)
    rows, width = summed[0].shape
    return pl.pallas_call(
        functools.partial(feature_kernel, first),
        in_specs=[IN_SMEM] + [IN_VMEM] * (groups + 2),
        out_specs=IN_VMEM,
        out_shape=bf16(count, rows, width),
        compiler_params=params(),
        cost_estimate=pl.CostEstimate(
            flops=2 * rows * groups * count * width**2,
            bytes_accessed=2 * groups * count * width**2 + 2 * (groups + count) * rows * width,
            transcendentals=0,
        ),
        name="feature_rows",
    )(index, *summed, even, odd)


def gather_kernel(index, *refs):
    *pieces, out, sems = refs
    rows = pieces[0].shape[0]
    copies = [
        pltpu.make_async_copy(
            piece, out.at[pl.ds(pl.multiple_of((index[1] ^ i) * rows, rows), rows)], sems.at[i]
        )
        for i, piece in enumerate(pieces)
    ]
    for copy in copies:
        copy.start()
    for copy in copies:
        copy.wait()


def laid_out(index, pieces):
    rows, width = pieces[0].shape
    return pl.pallas_call(
        gather_kernel,
        in_specs=[IN_SMEM] + [IN_VMEM] * len(pieces),
        out_specs=IN_HBM,
        out_shape=bf16(len(pieces) * rows, width),
        scratch_shapes=[pltpu.SemaphoreType.DMA((len(pieces),))],
        compiler_params=params(),
        name="laid_out",
    )(index, *pieces)


def landing_blocks(shuffle_from, me, blocks, devs, slots):
    owner = (shuffle_from // blocks).reshape(devs, blocks)
    within = (shuffle_from % blocks).reshape(devs, blocks)
    for_me = owner == me
    earlier = jnp.arange(blocks)[None, :] < jnp.arange(blocks)[:, None]
    rank = jnp.sum((for_me[:, None, :] & earlier[None]).astype(jnp.int32), axis=2)
    picked = for_me[:, None, :] & (rank[:, None, :] == jnp.arange(slots)[None, :, None])
    return (jnp.sum(jnp.where(picked, within[:, None, :] + 1, 0), axis=2) - 1).reshape(-1)


def exchange_order(groups):
    return sorted(range(1, groups), reverse=True)


def local(
    features,
    weight,
    pre_clean,
    pre_corrupt,
    grad_clean,
    grad_corrupt,
    slopes,
    adj_vals,
    adj_cols,
    adj_count,
    shuffle_from,
):
    row_count = features.shape[0]
    blocks, tile_slots, _, _ = adj_vals.shape
    reach = (tile_slots - 1) // 2
    me = lax.axis_index("node")
    group = lax.axis_index("chan")
    devs = lax.axis_size("node")
    groups = lax.axis_size("chan")
    slots = -(-blocks // devs)
    index = jnp.stack([me, group])

    args = (shuffle_from, adj_cols.T, adj_count)
    args += (grad_clean, pre_clean, grad_corrupt, pre_corrupt, slopes[None, :], adj_vals)
    clean, outgoing, *sides = aggregate(*args, features, weight, reach, devs, groups)
    (clean_side, side), packed = sides[:2], sides[2:]
    pair, beside = swapped(side[0], "node", 1), swapped_beside(side[1], "node", True)
    for i in exchange_order(groups):
        packed[i] = swapped(packed[i], "chan", i)

    outgoing = patch(shuffle_from, outgoing, pair, beside, blocks, slots)
    shuffle_from, outgoing, clean, clean_side = lax.optimization_barrier(
        (shuffle_from, outgoing, clean, clean_side)
    )
    clean_pair = swapped(clean_side[0], "node", 1)
    clean_beside = swapped_beside(clean_side[1], "node", False)
    landing = landing_blocks(shuffle_from, me, blocks, devs, slots)
    incoming = exchanged(outgoing, "node")
    incoming, packed = lax.optimization_barrier((incoming, packed))
    merged = merge(index, landing, clean, clean_pair, clean_beside, incoming, groups)

    quarter = row_count // groups
    summed = [merged[0]] + [None] * (groups - 1)
    for i in exchange_order(groups):
        summed[i] = swapped(merged[i], "chan", i)
    tiles = jnp.stack([piece[quarter:] for piece in packed])
    even = [tiles] + [swapped(tiles, "node", 2 * i) for i in range(1, devs // 2)]
    order = [0, *range(2, groups - 1), 1, groups - 1]
    listed, even = lax.optimization_barrier(([summed[i] for i in order], even))
    summed = [listed[order.index(i)] for i in range(groups)]
    even = jnp.stack(even)
    odd = swapped(even, "node", 1)

    keep, send = weight_partial(index, packed, summed, devs)
    odd, send = lax.optimization_barrier((odd, send))
    arrived = swapped(send, "node", 1)
    sent = feature_rows(index, summed, even, odd, 1, groups - 1)
    arrived, sent, summed, even, odd = lax.optimization_barrier((arrived, sent, summed, even, odd))
    pieces = [feature_rows(index, summed, even, odd, 0, 1)[0]] + [None] * (groups - 1)
    for i in exchange_order(groups):
        pieces[i] = swapped(sent[i - 1], "chan", i)
    total = wide(keep) + wide(arrived)
    share = total[0]
    for i in range(1, devs // 2):
        share = share + wide(swapped(total[i].astype(jnp.bfloat16), "node", 2 * i))
    grad_weight = share[0]
    for i in range(1, groups):
        grad_weight = grad_weight + wide(swapped(share[i].astype(jnp.bfloat16), "chan", i))
    return (grad_weight, laid_out(index, pieces))


def solution(mesh):
    placed = (
        P("node", "chan"),
        P("node", "chan"),
        P("node", "chan"),
        P("node", "chan"),
        P("node", "chan"),
        P("node", "chan"),
        P("chan"),
        P("node", None, None, None),
        P("node", None),
        P("node"),
        P(),
    )
    return jax.shard_map(
        local,
        mesh=mesh,
        in_specs=placed,
        out_specs=(P("node", "chan"), P("node", "chan")),
        check_vma=False,
    )
```

```python
import functools
import math

import jax
import jax.numpy as jnp
from jax import lax
from jax.experimental import pallas as pl
from jax.experimental.pallas import tpu as pltpu
from jax.sharding import PartitionSpec as P

VMEM_LIMIT = 32 * 1024 * 1024
VMEM_ALL = 61 * 1024 * 1024
IN_VMEM = pl.BlockSpec(memory_space=pltpu.VMEM)
IN_SMEM = pl.BlockSpec(memory_space=pltpu.SMEM)
IN_HBM = pl.BlockSpec(memory_space=pltpu.HBM)


def params(limit=VMEM_LIMIT):
    return pltpu.CompilerParams(vmem_limit_bytes=limit)


def bf16(*shape):
    return jax.ShapeDtypeStruct(shape, jnp.bfloat16)


def wide(value):
    return value.astype(jnp.float32)


def swapped_beside(value, axis, round):
    size = lax.axis_size(axis)
    pairs = [(i, (i + 1) % size) for i in range(1, size if round else size - 1, 2)]
    return lax.ppermute(value, axis, pairs + [(j, i) for i, j in pairs])


def swapped(value, axis, by):
    size = lax.axis_size(axis)
    return lax.ppermute(value, axis, [(i, i ^ by) for i in range(size)])


def exchanged(value, axis):
    return lax.all_to_all(value, axis, split_axis=0, concat_axis=0, tiled=True)


def masked_grad(grad, pre, slope):
    return jnp.where(pre > 0, grad, grad * slope)


def find_places(index, shuffle, blocks, slots, places, used):
    for i in range(used.shape[0]):
        used[i] = 0
    for block in range(blocks):
        owner = shuffle[index[0] * blocks + block] // blocks
        slot = used[owner]
        used[owner] = slot + 1
        places[block] = owner * slots + slot


def aggregate_kernel(
    reach, groups, send_slots, shuffle, cols, count, gc, pc, gx, px, slopes, adj, features, weight, *refs
):
    clean, outgoing, *refs = refs
    sides, packed, refs = refs[:2], refs[2 : 2 + groups], refs[2 + groups :]
    data, tiles, rhs, stage, results, halos, packs, places, used, sems, pack_sems, out_sems = refs
    blocks, slots, rows, _ = adj.shape
    width = gc.shape[1]
    me = (lax.axis_index("node"), lax.axis_index("chan"))
    quarter = features.shape[0] // groups
    spare = blocks + 2 * reach

    def copies(step):
        span = slice(2 * step, 2 * step + 2)
        out = [
            pltpu.make_async_copy(
                ref.at[2 * step * rows : (2 * step + 2) * rows], data.at[i, step], sems.at[i, step]
            )
            for i, ref in enumerate((gc, pc, gx, px))
        ]
        return out + [pltpu.make_async_copy(adj.at[span], tiles.at[span], sems.at[4, step])]

    inputs = [copies(step) for step in range(blocks // 2)]
    ahead = 3
    for copy in sum(inputs[:ahead], []):
        copy.start()
    to_vmem, to_hbm = [], []
    for i in range(groups):
        span = pl.ds(pl.multiple_of((me[1] ^ i) * quarter, quarter), quarter)
        to_vmem.append(
            pltpu.make_async_copy(features.at[span], packs.at[i, :quarter], pack_sems.at[0, i])
        )
        to_vmem.append(pltpu.make_async_copy(weight, packs.at[i, quarter:], pack_sems.at[1, i]))
        to_hbm.append(pltpu.make_async_copy(packs.at[i], packed[i], pack_sems.at[2, i]))
    stage[...] = jnp.zeros_like(stage)
    shape = (rows, rows)
    identity = (
        lax.broadcasted_iota(jnp.int32, shape, 0) == lax.broadcasted_iota(jnp.int32, shape, 1)
    ).astype(jnp.float32).astype(jnp.bfloat16)
    slope = slopes[...].astype(jnp.bfloat16)
    find_places(me, shuffle, blocks, send_slots, places, used)

    def take(step):
        gradients = [masked_grad(data[i, step], data[i + 1, step], slope) for i in (0, 2)]
        rhs[2 * step * rows : (2 * step + 2) * rows] = jnp.concatenate(gradients, axis=1)
        turned = lax.dot_general(
            identity,
            tiles[2 * step : 2 * step + 2].reshape(2 * slots * rows, rows),
            (((1,), (1,)), ((), ())),
            preferred_element_type=jnp.float32,
        )
        for i in range(2 * slots):
            block, k = 2 * step + i // slots, i % slots
            live = k < count[block]
            target = cols[k, block] - me[0] * blocks
            place = jnp.where(live, target + reach, spare)
            distance = jnp.where(live, block - target + reach, 0)
            stage[place, distance] += turned[:, i * rows : (i + 1) * rows].astype(jnp.bfloat16)

    blank = jnp.zeros(shape, jnp.bfloat16)

    def pair(first):
        targets = [first - reach, first - reach + 1]
        sources = range(max(0, targets[0] - reach), min(blocks, targets[1] + reach + 1))

        def tile(i, source):
            distance = source - targets[i] + reach
            return stage[first + i, distance] if 0 <= distance <= 2 * reach else blank

        lhs = jnp.concatenate(
            [jnp.concatenate([tile(i, b) for b in sources], axis=1) for i in range(2)], axis=0
        )
        span = slice(sources.start * rows, sources.stop * rows)
        product = jnp.dot(lhs, rhs[span], preferred_element_type=jnp.float32)
        product = product.astype(jnp.bfloat16).reshape(2, rows, 2 * width)
        return product[:, :, :width], product[:, :, width:]

    writes = []

    def finish(first):
        block = first - reach
        if 0 <= block < blocks:
            span = slice(block, block + 2)
            results[0, span], results[1, span] = pair(first)
            done = [pltpu.make_async_copy(results.at[0, span], clean.at[span], out_sems.at[0, block])]
            for i in range(block, block + 2):
                target = outgoing.at[places[i]]
                done.append(pltpu.make_async_copy(results.at[1, i], target, out_sems.at[1, i]))
        else:
            side, at = int(block >= 0), first % (blocks + reach)
            halos[side, 0, at : at + 2], halos[side, 1, at : at + 2] = pair(first)
            slot = (me[0] & 1) ^ (1 - side)
            done = []
            for i in range(2):
                source, target = halos.at[side, i, at : at + 2], sides[i].at[slot, at : at + 2]
                done.append(pltpu.make_async_copy(source, target, out_sems.at[2 + i, first]))
        for copy in done:
            copy.start()
        writes.extend(done)

    for step in range(blocks // 2):
        for copy in inputs[step]:
            copy.wait()
        for copy in inputs[step + ahead] if step + ahead < blocks // 2 else []:
            copy.start()
        if step == 1:
            for copy in to_vmem:
                copy.start()
        if step:
            finish(2 * step - 2)
        take(step)
    for copy in to_vmem:
        copy.wait()
    for copy in to_hbm:
        copy.start()
    for first in range(blocks + 2 * reach - 2, blocks - 4, -2):
        finish(first)
    for copy in writes + to_hbm:
        copy.wait()


def aggregate(shuffle, cols, count, gc, pc, gx, px, slopes, adj, features, weight, reach, devs, groups):
    blocks, slots, rows, _ = adj.shape
    width = gc.shape[1]
    send_slots = -(-blocks // devs)
    assert reach % 2 == 0 and blocks % 2 == 0
    packed = features.shape[0] // groups + weight.shape[0]
    return pl.pallas_call(
        functools.partial(aggregate_kernel, reach, groups, send_slots),
        in_specs=[IN_SMEM] * 3 + [IN_HBM] * 4 + [IN_VMEM] + [IN_HBM] * 3,
        out_specs=[IN_HBM] * (4 + groups),
        out_shape=[bf16(blocks, rows, width), bf16(devs * send_slots, rows, width)]
        + [bf16(2, reach, rows, width)] * 2
        + [bf16(packed, width)] * groups,
        scratch_shapes=[
            pltpu.VMEM((4, blocks // 2, 2 * rows, width), jnp.bfloat16),
            pltpu.VMEM((blocks, slots, rows, rows), jnp.bfloat16),
            pltpu.VMEM((blocks * rows, 2 * width), jnp.bfloat16),
            pltpu.VMEM((blocks + 2 * reach + 1, 2 * reach + 1, rows, rows), jnp.bfloat16),
            pltpu.VMEM((2, blocks, rows, width), jnp.bfloat16),
            pltpu.VMEM((2, 2, reach, rows, width), jnp.bfloat16),
            pltpu.VMEM((groups, packed, width), jnp.bfloat16),
            pltpu.SMEM((blocks,), jnp.int32),
            pltpu.SMEM((devs,), jnp.int32),
            pltpu.SemaphoreType.DMA((5, blocks // 2)),
            pltpu.SemaphoreType.DMA((3, groups)),
            pltpu.SemaphoreType.DMA((4, blocks + 2 * reach)),
        ],
        compiler_params=params(VMEM_ALL),
        cost_estimate=pl.CostEstimate(
            flops=4 * blocks * slots * rows * rows * width,
            bytes_accessed=12 * blocks * rows * width + 2 * blocks * slots * rows * rows,
            transcendentals=0,
        ),
        name="aggregate",
    )(shuffle, cols, count, gc, pc, gx, px, slopes, adj, features, weight)


def patch_kernel(reach, blocks, slots, shuffle, outgoing, pair, beside, out, *scratch):
    held, other, ready, places, used, sems = scratch
    index = (lax.axis_index("node"),)
    odd = index[0] & 1
    arrivals = [
        pltpu.make_async_copy(pair, other.at[pl.ds((1 - odd) * reach, reach)], sems.at[2, 0]),
        pltpu.make_async_copy(beside, other.at[pl.ds(odd * reach, reach)], sems.at[2, 1]),
    ]
    for copy in arrivals:
        copy.start()
    find_places(index, shuffle, blocks, slots, places, used)
    border = [*range(reach), *range(blocks - reach, blocks)]
    reads, writes = [], []
    for i, block in enumerate(border):
        place = places[block]
        reads.append(pltpu.make_async_copy(outgoing.at[place], held.at[i], sems.at[0, i]))
        writes.append(pltpu.make_async_copy(ready.at[i], out.at[place], sems.at[1, i]))
    for copy in reads:
        copy.start()
    for copy in arrivals:
        copy.wait()
    for i, (read, write) in enumerate(zip(reads, writes)):
        read.wait()
        ready[i] = (wide(held[i]) + wide(other[i])).astype(jnp.bfloat16)
        write.start()
    for copy in writes:
        copy.wait()


def patch(shuffle, outgoing, pair, beside, blocks, slots):
    sent, rows, width = outgoing.shape
    reach = pair.shape[0]
    border = pltpu.VMEM((2 * reach, rows, width), jnp.bfloat16)
    return pl.pallas_call(
        functools.partial(patch_kernel, reach, blocks, slots),
        in_specs=[IN_SMEM] + [IN_HBM] * 3,
        out_specs=IN_HBM,
        out_shape=bf16(*outgoing.shape),
        input_output_aliases={1: 0},
        scratch_shapes=[
            border,
            border,
            border,
            pltpu.SMEM((blocks,), jnp.int32),
            pltpu.SMEM((sent // slots,), jnp.int32),
            pltpu.SemaphoreType.DMA((3, 2 * reach)),
        ],
        compiler_params=params(VMEM_ALL),
        name="patch",
    )(shuffle, outgoing, pair, beside)


def merge_kernel(quarter, index, landing, clean, pair, beside, incoming, out, whole):
    blocks, rows, _ = clean.shape
    reach = pair.shape[0]
    group = index[1]
    piece = math.gcd(rows, quarter)
    for block in range(blocks):
        whole[block] = wide(clean[block])
    odd = index[0] & 1
    for i in range(reach):
        whole[(1 - odd) * (blocks - reach) + i] += wide(pair[i])
        whole[odd * (blocks - reach) + i] += wide(beside[i])
    for place in range(incoming.shape[0]):
        block = landing[place]

        @pl.when(block >= 0)
        def _():
            total = (whole[block] + wide(incoming[place])).astype(jnp.bfloat16)
            for part in range(rows // piece):
                at = block * (rows // piece) + part
                owner = at // (quarter // piece)
                offset = (at - owner * (quarter // piece)) * piece
                out[owner ^ group, pl.ds(pl.multiple_of(offset, piece), piece)] = total[
                    part * piece : (part + 1) * piece
                ]


def merge(index, landing, clean, pair, beside, incoming, groups):
    blocks, rows, width = clean.shape
    quarter = blocks * rows // groups
    return pl.pallas_call(
        functools.partial(merge_kernel, quarter),
        in_specs=[IN_SMEM] * 2 + [IN_VMEM] * 4,
        out_specs=IN_VMEM,
        out_shape=bf16(groups, quarter, width),
        scratch_shapes=[pltpu.VMEM((blocks, rows, width), jnp.float32)],
        compiler_params=params(),
        name="merge",
    )(index, landing, clean, pair, beside, incoming)


def weight_kernel(devs, index, *refs):
    groups = (len(refs) - 2) // 2
    packed, summed, (keep, send) = refs[:groups], refs[groups : 2 * groups], refs[2 * groups :]
    me, group = index[0], index[1]
    shares = devs // groups
    height, width = keep.shape[2:]
    rhs = jnp.concatenate([piece[...] for piece in summed], axis=1)
    for relative in range(groups):
        product = lax.dot_general(
            packed[relative][: rhs.shape[0]],
            rhs,
            (((0,), (0,)), ((), ())),
            preferred_element_type=jnp.float32,
        ).astype(jnp.bfloat16)
        for share in range(shares):
            node = ((group ^ relative) * shares + share) ^ me
            rows = product[share * height : (share + 1) * height]

            def store(out):
                for i in range(groups):
                    out[node >> 1, i] = rows[:, i * width : (i + 1) * width]

            pl.when((node & 1) == 0)(functools.partial(store, keep))
            pl.when((node & 1) == 1)(functools.partial(store, send))


def weight_partial(index, packed, summed, devs):
    groups = len(packed)
    rows, width = summed[0].shape
    height = groups * width // devs
    return pl.pallas_call(
        functools.partial(weight_kernel, devs),
        in_specs=[IN_SMEM] + [IN_VMEM] * (2 * groups),
        out_specs=[IN_VMEM] * 2,
        out_shape=[bf16(devs // 2, groups, height, width)] * 2,
        compiler_params=params(),
        cost_estimate=pl.CostEstimate(
            flops=2 * rows * (groups * width) ** 2,
            bytes_accessed=2 * (groups * width) ** 2 + 4 * groups * rows * width,
            transcendentals=0,
        ),
        name="weight_partial",
    )(index, *packed, *summed)


def feature_kernel(first, index, *refs):
    *summed, even, odd, out = refs
    groups = len(summed)
    devs = 2 * even.shape[0]
    me, group = index[0], index[1]
    shares = devs // groups
    height = even.shape[2]
    low = me & (shares - 1)
    lhs = jnp.concatenate([piece[...] for piece in summed], axis=1)
    for relative in range(first, first + out.shape[0]):
        rows = []
        for i in range(shares):
            node = (((group ^ relative) * shares) ^ (me - low)) + i
            half = odd if i % 2 else even
            rows.append(jnp.concatenate([half[node >> 1, j] for j in range(groups)], axis=1))
        product = lax.dot_general(
            lhs,
            jnp.concatenate(rows, axis=0),
            (((1,), (1,)), ((), ())),
            preferred_element_type=jnp.float32,
        ).astype(jnp.bfloat16)
        parts = [product[:, i * height : (i + 1) * height] for i in range(shares)]

        def store(flip):
            out[relative - first] = jnp.concatenate([parts[i ^ flip] for i in range(shares)], axis=1)

        for flip in range(shares):
            pl.when(low == flip)(functools.partial(store, flip))


def feature_rows(index, summed, even, odd, first, count):
    groups = len(summed)
    rows, width = summed[0].shape
    return pl.pallas_call(
        functools.partial(feature_kernel, first),
        in_specs=[IN_SMEM] + [IN_VMEM] * (groups + 2),
        out_specs=IN_VMEM,
        out_shape=bf16(count, rows, width),
        compiler_params=params(),
        cost_estimate=pl.CostEstimate(
            flops=2 * rows * groups * count * width**2,
            bytes_accessed=2 * groups * count * width**2 + 2 * (groups + count) * rows * width,
            transcendentals=0,
        ),
        name="feature_rows",
    )(index, *summed, even, odd)


def gather_kernel(index, *refs):
    *pieces, out, sems = refs
    rows = pieces[0].shape[0]
    copies = [
        pltpu.make_async_copy(
            piece, out.at[pl.ds(pl.multiple_of((index[1] ^ i) * rows, rows), rows)], sems.at[i]
        )
        for i, piece in enumerate(pieces)
    ]
    for copy in copies:
        copy.start()
    for copy in copies:
        copy.wait()


def laid_out(index, pieces):
    rows, width = pieces[0].shape
    return pl.pallas_call(
        gather_kernel,
        in_specs=[IN_SMEM] + [IN_VMEM] * len(pieces),
        out_specs=IN_HBM,
        out_shape=bf16(len(pieces) * rows, width),
        scratch_shapes=[pltpu.SemaphoreType.DMA((len(pieces),))],
        compiler_params=params(),
        name="laid_out",
    )(index, *pieces)


def landing_blocks(shuffle_from, me, blocks, devs, slots):
    owner = (shuffle_from // blocks).reshape(devs, blocks)
    within = (shuffle_from % blocks).reshape(devs, blocks)
    for_me = owner == me
    earlier = jnp.arange(blocks)[None, :] < jnp.arange(blocks)[:, None]
    rank = jnp.sum((for_me[:, None, :] & earlier[None]).astype(jnp.int32), axis=2)
    picked = for_me[:, None, :] & (rank[:, None, :] == jnp.arange(slots)[None, :, None])
    return (jnp.sum(jnp.where(picked, within[:, None, :] + 1, 0), axis=2) - 1).reshape(-1)


def exchange_order(groups):
    return sorted(range(1, groups), reverse=True)


def local(
    features,
    weight,
    pre_clean,
    pre_corrupt,
    grad_clean,
    grad_corrupt,
    slopes,
    adj_vals,
    adj_cols,
    adj_count,
    shuffle_from,
):
    row_count = features.shape[0]
    blocks, tile_slots, _, _ = adj_vals.shape
    reach = (tile_slots - 1) // 2
    me = lax.axis_index("node")
    group = lax.axis_index("chan")
    devs = lax.axis_size("node")
    groups = lax.axis_size("chan")
    slots = -(-blocks // devs)
    index = jnp.stack([me, group])

    args = (shuffle_from, adj_cols.T, adj_count)
    args += (grad_clean, pre_clean, grad_corrupt, pre_corrupt, slopes[None, :], adj_vals)
    clean, outgoing, *sides = aggregate(*args, features, weight, reach, devs, groups)
    (clean_side, side), packed = sides[:2], sides[2:]
    pair, beside = swapped(side[0], "node", 1), swapped_beside(side[1], "node", True)
    for i in exchange_order(groups):
        packed[i] = swapped(packed[i], "chan", i)

    outgoing = patch(shuffle_from, outgoing, pair, beside, blocks, slots)
    shuffle_from, outgoing, clean, clean_side = lax.optimization_barrier(
        (shuffle_from, outgoing, clean, clean_side)
    )
    clean_pair = swapped(clean_side[0], "node", 1)
    clean_beside = swapped_beside(clean_side[1], "node", True)
    landing = landing_blocks(shuffle_from, me, blocks, devs, slots)
    incoming = exchanged(outgoing, "node")
    incoming, packed = lax.optimization_barrier((incoming, packed))
    merged = merge(index, landing, clean, clean_pair, clean_beside, incoming, groups)

    quarter = row_count // groups
    summed = [merged[0]] + [None] * (groups - 1)
    for i in exchange_order(groups):
        summed[i] = swapped(merged[i], "chan", i)
    tiles = jnp.stack([piece[quarter:] for piece in packed])
    even = [tiles] + [swapped(tiles, "node", 2 * i) for i in range(1, devs // 2)]
    order = [0, *range(2, groups - 1), 1, groups - 1]
    listed, even = lax.optimization_barrier(([summed[i] for i in order], even))
    summed = [listed[order.index(i)] for i in range(groups)]
    even = jnp.stack(even)
    odd = swapped(even, "node", 1)

    keep, send = weight_partial(index, packed, summed, devs)
    odd, send = lax.optimization_barrier((odd, send))
    arrived = swapped(send, "node", 1)
    sent = feature_rows(index, summed, even, odd, 1, groups - 1)
    arrived, sent, summed, even, odd = lax.optimization_barrier((arrived, sent, summed, even, odd))
    pieces = [feature_rows(index, summed, even, odd, 0, 1)[0]] + [None] * (groups - 1)
    for i in exchange_order(groups):
        pieces[i] = swapped(sent[i - 1], "chan", i)
    total = wide(keep) + wide(arrived)
    share = total[0]
    for i in range(1, devs // 2):
        share = share + wide(swapped(total[i].astype(jnp.bfloat16), "node", 2 * i))
    grad_weight = share[0]
    for i in range(1, groups):
        grad_weight = grad_weight + wide(swapped(share[i].astype(jnp.bfloat16), "chan", i))
    return (grad_weight, laid_out(index, pieces))


def solution(mesh):
    placed = (
        P("node", "chan"),
        P("node", "chan"),
        P("node", "chan"),
        P("node", "chan"),
        P("node", "chan"),
        P("node", "chan"),
        P("chan"),
        P("node", None, None, None),
        P("node", None),
        P("node"),
        P(),
    )
    return jax.shard_map(
        local,
        mesh=mesh,
        in_specs=placed,
        out_specs=(P("node", "chan"), P("node", "chan")),
        check_vma=False,
    )
```
